128 devices in a mesh: batch: 8 (over x_hi, y), tensor: 16 (over x_lo, z, core).
Axes of the slice: x: 4 (x_hi: 2, x_lo: 2; x = x_hi * 2 + x_lo), y: 4, z: 4, core: 2. Of those that a mesh axis runs over, the one named last changes fastest.
Arguments:
- tokens: bfloat16 [16384, 2048], P('batch'), may hold values from -6 to 6
- ln1_gain: float32 [2048], replicated, may hold values from 0.5 to 1.5
- ln1_shift: float32 [2048], replicated, may hold values from -0.12 to 0.12
- qkv_weight: bfloat16 [3, 2048, 2048], P(None, None, 'tensor'), may hold values from -0.125 to 0.125
- out_weight: bfloat16 [2048, 2048], P('tensor'), may hold values from -2 to 2
- ln2_gain: float32 [2048], replicated, may hold values from 0.5 to 1.5
- ln2_shift: float32 [2048], replicated, may hold values from -0.6 to 0.6
- up_weight: bfloat16 [2048, 8192], P(None, 'tensor'), may hold values from -0.125 to 0.125
- down_weight: bfloat16 [8192, 2048], P('tensor'), may hold values from -0.0625 to 0.0625
- lengths: int32 [8], P('batch'), may hold values from 512 to 2048, as said below
- cotangent: bfloat16 [16384, 2048], P(('batch', 'tensor')), may hold values from -6 to 6
Outputs:
- output: bfloat16 [16384, 2048], P(('batch', 'tensor'))
- grad_tokens: bfloat16 [16384, 2048], P(('batch', 'tensor'))
- grad_qkv: float32 [3, 2048, 2048], P(None, 'batch', 'tensor')
- grad_out: float32 [2048, 2048], P('tensor', 'batch')
- grad_up: float32 [2048, 8192], P('batch', 'tensor')
- grad_down: float32 [8192, 2048], P('tensor', 'batch')
- grad_gains: float32 [2, 2048], replicated
- grad_shifts: float32 [2, 2048], replicated
The draws below stay inside these ranges and needn't reach their ends.
Inputs may be any that keep to these rules, and one draw needn't show every extreme that they name: `lengths`: live tokens of each sequence; the rest of its 2048 slots are padding.
All inputs are finite; a program needn't handle non-finite values.
Results may differ from the reference program's by a relative error of at most 0.025.
Values may be sent and summed in bfloat16 or wider, within the bound.
No kernel may reach another device: no remote copies, remote signals or barrier semaphores. Data moves between devices by JAX's collectives and lax.ppermute only.
A program may use at most 256 MiB of HBM per device.

```python
import jax
import jax.numpy as jnp
from jax import lax

D = 2048
H = 16
HD = 128
FF = 8192
LEN = 2048
SEQ_ALL = 8
TOKENS = 16384
N_TENSOR = 16


def draw_lengths(key, part):
    key = jax.random.fold_in(key, 7)
    drawn = jax.random.randint(jax.random.fold_in(key, 1), (SEQ_ALL,), LEN // 4, LEN + 1, dtype=jnp.int32)
    ranking = jax.random.permutation(jax.random.fold_in(key, 2), SEQ_ALL)
    drawn = drawn.at[ranking[0]].set(LEN)
    drawn = drawn.at[ranking[1]].set(LEN // 4)
    return drawn.astype(jnp.int32)


def levels(own_key, extent, pieces, smallest, top_value):
    factor_of = 1.0
    for position, parts in pieces:
        draws = jax.random.uniform(jax.random.fold_in(jax.random.fold_in(own_key, 6), position), (parts,), jnp.float32, smallest / len(pieces), top_value / len(pieces))
        factor_of = factor_of * jnp.repeat(jnp.exp(draws), extent[position] // parts).reshape((-1,) + (1,) * (len(extent) - 1 - position))
    return factor_of


def centred(rng, extent, deviation, bound, shards=(), kind=jnp.bfloat16):
    level = levels(rng, extent, shards, -0.22, 0.18) if shards else 1.0
    values = jax.random.normal(rng, extent, jnp.float32) * deviation * level
    return jnp.minimum(jnp.maximum(values, -bound), bound).astype(kind)


def setup_inputs(seed: int = 0) -> dict:
    seeds = jax.random.split(jax.random.key(seed), 12)
    return {
        "tokens": centred(seeds[0], (TOKENS, D), 1.0, 6.0, ((0, 8),)),
        "ln1_gain": jnp.clip(1.0 + 0.1 * jax.random.normal(seeds[1], (D,), jnp.float32), 0.5, 1.5),
        "ln1_shift": centred(seeds[2], (D,), 0.02, 0.12, (), jnp.float32),
        "qkv_weight": centred(seeds[3], (3, D, H * HD), D ** -0.5, 0.125, ((2, 16),)),
        "out_weight": centred(seeds[4], (H * HD, D), (max(1, 8 * H * HD // LEN)) ** -0.5, 2.0, ((0, 16),)),
        "ln2_gain": jnp.clip(1.0 + 0.1 * jax.random.normal(seeds[5], (D,), jnp.float32), 0.5, 1.5),
        "ln2_shift": centred(seeds[6], (D,), 0.1, 0.6, (), jnp.float32),
        "up_weight": centred(seeds[7], (D, FF), D ** -0.5, 0.125, ((1, 16),)),
        "down_weight": centred(seeds[8], (FF, D), FF ** -0.5, 0.0625, ((0, 16),)),
        "lengths": draw_lengths(jax.random.fold_in(seeds[11], 71), 0),
        "cotangent": centred(seeds[10], (TOKENS, D), 1.0, 6.0, ((0, 128),)),
    }


@jax.custom_vjp
def low(v):
    return lax.optimization_barrier(v.astype(jnp.bfloat16)).astype(jnp.float32)

@jax.custom_vjp
def low_back(v):
    return v

def low_keep(v):
    return (low(v), None)

def low_pass(kept, grad):
    return (grad,)

def back_keep(v):
    return (v, None)

def back_low(kept, grad):
    return (low(grad),)
low.defvjp(low_keep, low_pass)
low_back.defvjp(back_keep, back_low)
EPS = 1e-05
MASKED_SCORE = -1e+30

def matmul(left, right):
    return jnp.dot(left, right, precision=lax.Precision.HIGHEST, preferred_element_type=jnp.float32)

def norm_rows(values, gain, shift):
    centre = lax.optimization_barrier(jnp.mean(values, axis=-1, keepdims=True))
    offsets = values - centre
    spread = lax.optimization_barrier(jnp.mean(offsets * offsets, axis=-1, keepdims=True))
    return offsets * lax.rsqrt(spread + EPS) * gain + shift

def one_sequence(params, inputs, length):
    ln1_gain, ln1_shift, qkv_weight, out_weight, ln2_gain, ln2_shift, up_weight, down_weight = params
    seq_len = inputs.shape[0]
    head_width = H * HD
    normed_first = low(norm_rows(inputs, ln1_gain, ln1_shift))
    projected = jnp.einsum('td,cdh->cth', normed_first, qkv_weight, precision=lax.Precision.HIGHEST)
    projected = low(low_back(projected))
    queries = projected[0].reshape(seq_len, H, HD)
    key_rows = projected[1].reshape(seq_len, H, HD)
    value_rows = projected[2].reshape(seq_len, H, HD)
    scores = jnp.einsum('qhe,khe->hqk', queries, key_rows, precision=lax.Precision.HIGHEST) * HD ** (-0.5)
    scores = low_back(scores)
    query_index = jnp.arange(seq_len, dtype=jnp.int32)[:, None]
    key_index = jnp.arange(seq_len, dtype=jnp.int32)[None, :]
    allowed = (key_index <= query_index) & (key_index < length)
    scores = jnp.where(allowed[None], scores, MASKED_SCORE)
    attn_probs = low(jax.nn.softmax(scores, axis=-1))
    attended = jnp.einsum('hqk,khe->qhe', attn_probs, value_rows, precision=lax.Precision.HIGHEST)
    attended = low(low_back(attended.reshape(seq_len, head_width)))
    group_width = head_width // N_TENSOR
    branch = jnp.zeros((seq_len, D), jnp.float32)
    for group_index in range(N_TENSOR):
        col_start = group_index * group_width
        branch = branch + low(matmul(attended[:, col_start:col_start + group_width], out_weight[col_start:col_start + group_width]))
    branch = low_back(branch)
    middle = inputs + branch
    normed_second = low(norm_rows(middle, ln2_gain, ln2_shift))
    hidden = low_back(matmul(normed_second, up_weight))
    activated = low(jax.nn.gelu(hidden, approximate=True))
    unit_width = FF // N_TENSOR
    mixed = jnp.zeros((seq_len, D), jnp.float32)
    for group_index in range(N_TENSOR):
        col_start = group_index * unit_width
        mixed = mixed + low(matmul(activated[:, col_start:col_start + unit_width], down_weight[col_start:col_start + unit_width]))
    mixed = low_back(mixed)
    return middle + mixed

def reference(tokens, ln1_gain, ln1_shift, qkv_weight, out_weight, ln2_gain, ln2_shift, up_weight, down_weight, lengths, cotangent):
    params = tuple((array_in.astype(jnp.float32) for array_in in (ln1_gain, ln1_shift, qkv_weight, out_weight, ln2_gain, ln2_shift, up_weight, down_weight)))
    inputs = tokens.astype(jnp.float32).reshape(SEQ_ALL, LEN, D)

    def forward(weights, sequences):

        def per_sequence(packed):
            return one_sequence(weights, packed[0], packed[1])
        return lax.map(jax.checkpoint(per_sequence), (sequences, lengths))
    outputs, pullback = jax.vjp(forward, params, inputs)
    positions = jnp.arange(LEN, dtype=jnp.int32)[None, :]
    live = (positions < lengths[:, None]).astype(jnp.float32)
    incoming = cotangent.astype(jnp.float32).reshape(SEQ_ALL, LEN, D) * live[:, :, None]
    grad_params, grad_inputs = pullback(incoming)
    grad_gains = jnp.stack([grad_params[0], grad_params[4]])
    grad_shifts = jnp.stack([grad_params[1], grad_params[5]])
    return (outputs.reshape(TOKENS, D).astype(jnp.bfloat16), grad_inputs.reshape(TOKENS, D).astype(jnp.bfloat16), grad_params[2], grad_params[3], grad_params[6], grad_params[7], grad_gains, grad_shifts)
```

```python
from functools import partial

import jax
import jax.numpy as jnp
from jax import lax
from jax.sharding import PartitionSpec as P

HD = 128
EPS = 1e-05
MASKED_SCORE = -1e30
BF = jnp.bfloat16
F32 = jnp.float32


def place(index):
    batch, tensor = divmod(index, 16)
    return [batch // 4, batch % 4, tensor // 8, (tensor // 2) % 4, tensor % 2]


def index_of(at):
    x_hi, y, x_lo, z, core = at
    return (x_hi * 4 + y) * 16 + x_lo * 8 + z * 2 + core


def mover(step):
    pairs = [(i, index_of(step(place(i)))) for i in range(128)]
    return lambda values: lax.ppermute(values, ("batch", "tensor"), pairs)


def along_z(by):
    return mover(lambda a: [a[0], a[1], a[2], (a[3] + by) % 4, a[4]])


def along_y(by):
    return mover(lambda a: [a[0], (a[1] + by) % 4, a[2], a[3], a[4]])


def along_x(by):
    def step(a):
        ring = (a[0] * 2 + a[2] + by) % 4
        return [ring // 2, a[1], ring % 2, a[3], a[4]]

    return mover(step)


z_up, z_down, z_far = along_z(1), along_z(-1), along_z(2)
y_up, y_down, y_far = along_y(1), along_y(-1), along_y(2)
x_up, x_down, x_far = along_x(1), along_x(-1), along_x(2)
x_pair = mover(lambda a: [a[0], a[1], 1 - a[2], a[3], a[4]])
core_swap = mover(lambda a: [a[0], a[1], a[2], a[3], 1 - a[4]])


def norm_stats(values):
    centre = jnp.mean(values, axis=-1, keepdims=True)
    offsets = values - centre
    spread = jnp.mean(offsets * offsets, axis=-1, keepdims=True)
    inverse = lax.rsqrt(spread + EPS)
    return (offsets * inverse, inverse)


def norm_back(grad_normed, gain, unit_rows, inverse):
    scaled = grad_normed * gain
    return inverse * (
        scaled
        - jnp.mean(scaled, axis=-1, keepdims=True)
        - unit_rows * jnp.mean(scaled * unit_rows, axis=-1, keepdims=True)
    )


def dot(left, right, dims):
    return lax.dot_general(left, right, ((dims[:1], dims[1:]), ((), ())), preferred_element_type=F32)


def block_scores(queries, key_rows, start_row, stop_row, length):
    scores = dot(queries[start_row:stop_row], key_rows[:stop_row], (1, 1)) * HD ** (-0.5)
    query_index = start_row + jnp.arange(stop_row - start_row, dtype=jnp.int32)[:, None]
    key_index = jnp.arange(stop_row, dtype=jnp.int32)[None, :]
    return jnp.where((key_index <= query_index) & (key_index < length), scores, MASKED_SCORE)


def attend_forward(queries, key_rows, value_rows, length):
    seq_len = queries.shape[0]
    pieces = []
    totals = []
    for start_row in range(0, seq_len, 512):
        stop_row = start_row + 512
        scores = block_scores(queries, key_rows, start_row, stop_row, length)
        row_peak = jnp.max(scores, axis=-1, keepdims=True)
        log_total = jnp.log(jnp.sum(jnp.exp(scores - row_peak), axis=-1, keepdims=True)) + row_peak
        attn_probs = jnp.exp(scores - log_total).astype(BF)
        pieces.append(dot(attn_probs, value_rows[:stop_row], (1, 0)).astype(BF))
        totals.append(log_total)
    return (jnp.concatenate(pieces, axis=0), jnp.concatenate(totals, axis=0))


def attend_backward(queries, key_rows, value_rows, grad_attended, totals, length):
    seq_len = queries.shape[0]
    score_scale = HD ** (-0.5)
    grad_queries = []
    grad_keys = jnp.zeros(key_rows.shape, F32)
    grad_values = jnp.zeros(value_rows.shape, F32)
    for start_row in range(0, seq_len, 512):
        stop_row = start_row + 512
        scores = block_scores(queries, key_rows, start_row, stop_row, length)
        attn_probs = jnp.exp(scores - totals[start_row:stop_row])
        grad_probs = dot(grad_attended[start_row:stop_row], value_rows[:stop_row], (1, 1))
        centre = jnp.sum(attn_probs * grad_probs, axis=-1, keepdims=True)
        grad_scores = (attn_probs * (grad_probs - centre)).astype(BF)
        grad_queries.append(dot(grad_scores, key_rows[:stop_row], (1, 0)) * score_scale)
        grad_keys = grad_keys.at[:stop_row].add(
            dot(grad_scores, queries[start_row:stop_row], (0, 0)) * score_scale
        )
        grad_values = grad_values.at[:stop_row].add(
            dot(attn_probs.astype(BF), grad_attended[start_row:stop_row], (0, 0))
        )
    grad_queries = jnp.concatenate(grad_queries, axis=0)
    return (grad_queries.astype(BF), grad_keys.astype(BF), grad_values.astype(BF))


def gather_rows(rows):
    mine = jnp.concatenate([rows, z_up(rows), z_down(rows), z_far(rows)], axis=0)
    return mine, core_swap(mine)


def scatter_rows(mine, others):
    halves = (mine.astype(F32) + core_swap(others).astype(F32)).astype(BF)
    part = [halves[i * 128 : (i + 1) * 128] for i in range(4)]
    return (
        part[0].astype(F32)
        + z_down(part[1]).astype(F32)
        + z_up(part[2]).astype(F32)
        + z_far(part[3]).astype(F32)
    )


def take(values, index, size, axis):
    return lax.dynamic_slice_in_dim(values, index * size, size, axis)


def sum_along_y(values, y, axis):
    size = values.shape[axis] // 4
    parts = [take(values, (y + by) % 4, size, axis) for by in range(4)]
    return (
        parts[0].astype(F32)
        + y_up(parts[1]).astype(F32)
        + y_far(parts[2]).astype(F32)
        + y_down(parts[3]).astype(F32)
    )


def sum_along_x(own, partner, x_hi, x_lo, axis):
    size = own.shape[axis] // 2
    up_hi = jnp.where(x_lo == 0, x_hi, 1 - x_hi)
    return (
        take(own, x_hi, size, axis).astype(F32)
        + x_far(take(own, 1 - x_hi, size, axis)).astype(F32)
        + x_up(take(partner, up_hi, size, axis)).astype(F32)
        + x_down(take(partner, 1 - up_hi, size, axis)).astype(F32)
    )


def sum_of_all(values):
    for move in (core_swap, z_far, z_up, x_far, x_up, y_far, y_up):
        values = values + move(values)
    return values


def body(
    tokens,
    ln1_gain,
    ln1_shift,
    qkv_weight,
    out_weight,
    ln2_gain,
    ln2_shift,
    up_weight,
    down_weight,
    lengths,
    cotangent,
):
    batch, tensor = lax.axis_index("batch"), lax.axis_index("tensor")
    x_hi, y = batch // 4, batch % 4
    x_lo, z, core = tensor // 8, (tensor // 2) % 4, tensor % 2
    length = lengths[0]
    first_row = tensor * 128

    out_full = lax.all_gather(out_weight, "tensor", axis=0, tiled=True)
    live_rows = (first_row + jnp.arange(128, dtype=jnp.int32) < length).astype(F32)[:, None]
    incoming_rows = cotangent.astype(F32) * live_rows
    incoming = jnp.concatenate(gather_rows(incoming_rows.astype(BF)), axis=0)
    up_both = jnp.concatenate(
        [
            up_weight,
            jnp.concatenate([x_up(up_weight[:1024]), x_down(up_weight[1024:])], axis=0),
        ],
        axis=1,
    )
    down_both = jnp.concatenate(
        [down_weight, x_up(down_weight[:256]), x_down(down_weight[256:])], axis=0
    )

    inputs = tokens.astype(F32)
    unit_first, _ = norm_stats(inputs)
    normed_first = (unit_first * ln1_gain + ln1_shift).astype(BF)
    projected = jnp.einsum("td,cdh->cth", normed_first, qkv_weight, preferred_element_type=F32).astype(BF)
    attended, totals = attend_forward(projected[0], projected[1], projected[2], length)
    attended_rows = lax.all_to_all(attended, "tensor", 0, 1, tiled=True)
    branch_rows = dot(attended_rows, out_full, (1, 0))
    token_rows = take(tokens, tensor, 128, 0).astype(F32)
    middle_rows = token_rows + branch_rows
    unit_second, inverse_second = norm_stats(middle_rows)
    normed_rows = (unit_second * ln2_gain + ln2_shift).astype(BF)

    normed_second = jnp.concatenate(gather_rows(normed_rows), axis=0)
    hidden = dot(normed_second, up_both, (1, 0))
    activated, gelu_pull = jax.vjp(partial(jax.nn.gelu, approximate=True), hidden)
    activated = activated.astype(BF)
    grad_act = dot(incoming, down_both, (1, 1))
    grad_hidden = gelu_pull(grad_act)[0].astype(BF)
    grad_normed_part = dot(grad_hidden, up_both, (1, 1)).astype(BF)
    grad_normed_second = scatter_rows(grad_normed_part[:512], grad_normed_part[512:])

    mixed_part = dot(activated, down_both, (1, 0)).astype(BF)
    grad_down = dot(activated, incoming, (0, 0)).astype(BF)
    grad_up = dot(normed_second, grad_hidden, (0, 0)).astype(BF)

    grad_middle = incoming_rows + norm_back(grad_normed_second, ln2_gain, unit_second, inverse_second)
    gain_second = jnp.sum(grad_normed_second * unit_second, axis=0)
    shift_second = jnp.sum(grad_normed_second, axis=0)
    grad_branch = grad_middle.astype(BF)
    grad_attended = lax.all_to_all(dot(grad_branch, out_full, (1, 1)).astype(BF), "tensor", 1, 0, tiled=True)

    mixed_rows = scatter_rows(mixed_part[:512], mixed_part[512:])
    output = (middle_rows + mixed_rows).astype(BF)

    branch_back = jnp.concatenate(gather_rows(grad_branch), axis=0)
    order = [(0, 0), (-1, 0), (1, 0), (2, 0), (0, 1), (-1, 1), (1, 1), (2, 1)]
    spots = [((z + by) % 4) * 2 + (core + swap) % 2 for by, swap in order]
    own_half = jnp.concatenate([take(attended, x_lo * 8 + spot, 128, 0) for spot in spots], axis=0)
    sent_half = jnp.concatenate([take(attended, (1 - x_lo) * 8 + spot, 128, 0) for spot in spots], axis=0)
    both_heads = jnp.concatenate([own_half, x_pair(sent_half)], axis=1)
    grad_out = dot(both_heads, branch_back, (0, 0)).astype(BF)

    grad_queries, grad_keys, grad_values = attend_backward(
        projected[0], projected[1], projected[2], grad_attended, totals, length
    )
    stacked = jnp.stack([grad_queries, grad_keys, grad_values])
    grad_first_part = jnp.einsum("cth,cdh->td", stacked, qkv_weight, preferred_element_type=F32).astype(BF)
    grad_qkv_part = jnp.einsum("td,cth->cdh", normed_first, stacked, preferred_element_type=F32)

    columns = jnp.sum(stacked.astype(F32), axis=1)
    weights = qkv_weight.astype(F32)
    shift_first = jnp.sum(weights * columns[:, None, :], axis=(0, 2))
    gain_first = (jnp.sum(weights * grad_qkv_part, axis=(0, 2)) - ln1_shift * shift_first) / ln1_gain
    sums = sum_of_all(jnp.stack([gain_first, gain_second, shift_first, shift_second]))

    by_core = grad_first_part.reshape(8, 2, 128, 2048)
    kept = lax.dynamic_index_in_dim(by_core, core, 1, False)
    sent = lax.dynamic_index_in_dim(by_core, 1 - core, 1, False)
    halves = (kept.astype(F32) + core_swap(sent).astype(F32)).astype(BF).reshape(2, 4, 128, 2048)

    def over_x(values):
        return take(values, x_lo, 1, 0)[0].astype(F32) + x_pair(take(values, 1 - x_lo, 1, 0)[0]).astype(F32)

    def over_z(values):
        part = [lax.dynamic_index_in_dim(values, (z + by) % 4, values.ndim - 3, False) for by in range(4)]
        return (
            part[0].astype(F32)
            + z_up(part[1]).astype(F32)
            + z_far(part[2]).astype(F32)
            + z_down(part[3]).astype(F32)
        )

    left, right = halves[..., :1024], halves[..., 1024:]
    grad_normed_first = jnp.concatenate(
        [over_x(over_z(left).astype(BF)), over_z(over_x(right).astype(BF))], axis=-1
    )
    unit_rows, inverse_rows = norm_stats(token_rows)
    grad_tokens = (grad_middle + norm_back(grad_normed_first, ln1_gain, unit_rows, inverse_rows)).astype(BF)

    grad_down = sum_along_y(
        sum_along_x(grad_down[:512], grad_down[512:], x_hi, x_lo, 1).astype(BF), y, 1
    )
    up_sums = sum_along_y(grad_up.reshape(2, 4, 256, 1024), y, 1)[:, 0].astype(BF)
    up_sums = up_sums.reshape(512, 1024)
    grad_up = sum_along_x(up_sums[:, :512], up_sums[:, 512:], x_hi, x_lo, 0)
    grad_out = sum_along_y(
        sum_along_x(grad_out[:128], grad_out[128:], x_hi, x_lo, 1).astype(BF), y, 1
    )
    qkv_sums = sum_along_y(grad_qkv_part.astype(BF).reshape(3, 2, 4, 256, 128), y, 2)[:, :, 0].astype(BF)
    grad_qkv = lax.dynamic_index_in_dim(qkv_sums, x_hi, 1, False).astype(F32) + x_far(
        lax.dynamic_index_in_dim(qkv_sums, 1 - x_hi, 1, False)
    ).astype(F32)
    return (output, grad_tokens, grad_qkv, grad_out, grad_up, grad_down, sums[:2], sums[2:])


def solution(mesh):
    return jax.shard_map(
        body,
        mesh=mesh,
        in_specs=(
            P("batch", None),
            P(),
            P(),
            P(None, None, "tensor"),
            P("tensor", None),
            P(),
            P(),
            P(None, "tensor"),
            P("tensor", None),
            P("batch"),
            P(("batch", "tensor"), None),
        ),
        out_specs=(
            P(("batch", "tensor"), None),
            P(("batch", "tensor"), None),
            P(None, "batch", "tensor"),
            P("tensor", "batch"),
            P("batch", "tensor"),
            P("tensor", "batch"),
            P(),
            P(),
        ),
        check_vma=False,
    )
```

```python
from functools import partial

import jax
import jax.numpy as jnp
from jax import lax
from jax.sharding import Mesh
from jax.sharding import PartitionSpec as P

HD = 128
EPS = 1e-05
MASKED_SCORE = -1e30
BF = jnp.bfloat16
F32 = jnp.float32


AXES = ("x_hi", "y", "x_lo", "z", "core")
BATCH, TENSOR = AXES[:2], AXES[2:]


def core_swap(values):
    return lax.ppermute(values, "core", [(0, 1), (1, 0)])


def x_pair(values):
    return lax.ppermute(values, "x_lo", [(0, 1), (1, 0)])


def x_partner(values):
    pairs = [(r * 2 + c, ((r + (1, -1)[c]) % 4) * 2 + c) for r in range(4) for c in range(2)]
    return lax.ppermute(values, ("x_hi", "x_lo", "core"), pairs)


def exchange(values, axes):
    return lax.all_to_all(values, axes, 0, 0)


def spread(values, axes, count=4):
    return exchange(jnp.broadcast_to(values[None], (count, *values.shape)), axes)


def total(values):
    return jnp.sum(values.astype(F32), axis=0)


def norm_stats(values):
    centre = jnp.mean(values, axis=-1, keepdims=True)
    offsets = values - centre
    spread = jnp.mean(offsets * offsets, axis=-1, keepdims=True)
    inverse = lax.rsqrt(spread + EPS)
    return (offsets * inverse, inverse)


def norm_back(grad_normed, gain, unit_rows, inverse):
    scaled = grad_normed * gain
    return inverse * (
        scaled
        - jnp.mean(scaled, axis=-1, keepdims=True)
        - unit_rows * jnp.mean(scaled * unit_rows, axis=-1, keepdims=True)
    )


def dot(left, right, dims):
    return lax.dot_general(left, right, ((dims[:1], dims[1:]), ((), ())), preferred_element_type=F32)


def block_scores(queries, key_rows, start_row, stop_row, length):
    scores = dot(queries[start_row:stop_row], key_rows[:stop_row], (1, 1)) * HD ** (-0.5)
    query_index = start_row + jnp.arange(stop_row - start_row, dtype=jnp.int32)[:, None]
    key_index = jnp.arange(stop_row, dtype=jnp.int32)[None, :]
    return jnp.where((key_index <= query_index) & (key_index < length), scores, MASKED_SCORE)


def attend_forward(queries, key_rows, value_rows, length):
    seq_len = queries.shape[0]
    pieces = []
    totals = []
    for start_row in range(0, seq_len, 512):
        stop_row = start_row + 512
        scores = block_scores(queries, key_rows, start_row, stop_row, length)
        row_peak = jnp.max(scores, axis=-1, keepdims=True)
        log_total = jnp.log(jnp.sum(jnp.exp(scores - row_peak), axis=-1, keepdims=True)) + row_peak
        attn_probs = jnp.exp(scores - log_total).astype(BF)
        pieces.append(dot(attn_probs, value_rows[:stop_row], (1, 0)).astype(BF))
        totals.append(log_total)
    return (jnp.concatenate(pieces, axis=0), jnp.concatenate(totals, axis=0))


def attend_backward(queries, key_rows, value_rows, grad_attended, totals, length):
    seq_len = queries.shape[0]
    score_scale = HD ** (-0.5)
    grad_queries = []
    grad_keys = jnp.zeros(key_rows.shape, F32)
    grad_values = jnp.zeros(value_rows.shape, F32)
    for start_row in range(0, seq_len, 512):
        stop_row = start_row + 512
        scores = block_scores(queries, key_rows, start_row, stop_row, length)
        attn_probs = jnp.exp(scores - totals[start_row:stop_row])
        grad_probs = dot(grad_attended[start_row:stop_row], value_rows[:stop_row], (1, 1))
        centre = jnp.sum(attn_probs * grad_probs, axis=-1, keepdims=True)
        grad_scores = (attn_probs * (grad_probs - centre)).astype(BF)
        grad_queries.append(dot(grad_scores, key_rows[:stop_row], (1, 0)) * score_scale)
        grad_keys = grad_keys.at[:stop_row].add(
            dot(grad_scores, queries[start_row:stop_row], (0, 0)) * score_scale
        )
        grad_values = grad_values.at[:stop_row].add(
            dot(attn_probs.astype(BF), grad_attended[start_row:stop_row], (0, 0))
        )
    grad_queries = jnp.concatenate(grad_queries, axis=0)
    return (grad_queries.astype(BF), grad_keys.astype(BF), grad_values.astype(BF))


def gather_rows(rows):
    mine = spread(rows, "z").reshape(512, rows.shape[1])
    return jnp.concatenate([mine, core_swap(mine)], axis=0)


def scatter_rows(partial_sums):
    mine, others = partial_sums[:512], partial_sums[512:]
    halves = (mine.astype(F32) + core_swap(others).astype(F32)).astype(BF)
    return total(exchange(halves.reshape(4, 128, 2048), "z"))


def pick(values, index, axis):
    return lax.dynamic_index_in_dim(values, index, axis, False)


def sum_of_all(values):
    values = values + core_swap(values)
    for axes in ("z", ("x_hi", "x_lo"), "y"):
        values = total(spread(values, axes))
    return values


def body(
    tokens,
    ln1_gain,
    ln1_shift,
    qkv_weight,
    out_weight,
    ln2_gain,
    ln2_shift,
    up_weight,
    down_weight,
    lengths,
    cotangent,
):
    x_hi, y, x_lo, z, core = (lax.axis_index(axis) for axis in AXES)
    tensor = x_lo * 8 + z * 2 + core
    length = lengths[0]

    out_groups = []
    for half in range(2):
        mine = spread(out_weight[:, half * 1024 : (half + 1) * 1024], "z").reshape(512, 1024)
        both = [mine, x_partner(mine)]
        out_groups.append([group for part in both for group in (part, core_swap(part))])
    live_rows = (tensor * 128 + jnp.arange(128, dtype=jnp.int32) < length).astype(F32)[:, None]
    incoming_rows = cotangent.astype(F32) * live_rows
    up_both = jnp.concatenate([up_weight, x_partner(up_weight)], axis=1)
    down_both = jnp.concatenate([down_weight, x_partner(down_weight)], axis=0)
    incoming = gather_rows(incoming_rows.astype(BF))

    inputs = tokens.astype(F32)
    unit_first, _ = norm_stats(inputs)
    normed_first = (unit_first * ln1_gain + ln1_shift).astype(BF)
    projected = jnp.einsum("td,cdh->cth", normed_first, qkv_weight, preferred_element_type=F32).astype(BF)
    attended, totals = attend_forward(projected[0], projected[1], projected[2], length)
    attended_rows = exchange(attended.reshape(16, 128, HD), TENSOR).reshape(2, 4, 2, 128, HD)
    head_groups = [
        pick(pick(attended_rows, at_x, 0), at_core, 1).transpose(1, 0, 2).reshape(128, 512)
        for at_x in (x_lo, 1 - x_lo)
        for at_core in (core, 1 - core)
    ]
    branch_rows = jnp.concatenate(
        [sum(dot(heads, w, (1, 0)) for heads, w in zip(head_groups, groups)) for groups in out_groups], axis=1
    )
    token_rows = lax.dynamic_slice_in_dim(tokens, tensor * 128, 128, 0).astype(F32)
    middle_rows = token_rows + branch_rows
    unit_second, inverse_second = norm_stats(middle_rows)
    normed_rows = (unit_second * ln2_gain + ln2_shift).astype(BF)

    normed_second = gather_rows(normed_rows)
    hidden = dot(normed_second, up_both, (1, 0))
    activated, gelu_pull = jax.vjp(partial(jax.nn.gelu, approximate=True), hidden)
    activated = activated.astype(BF)
    grad_act = dot(incoming, down_both, (1, 1))
    grad_hidden = gelu_pull(grad_act)[0].astype(BF)
    grad_normed_part = dot(grad_hidden, up_both, (1, 1)).astype(BF)
    grad_normed_second = scatter_rows(grad_normed_part)

    mixed_part = dot(activated, down_both, (1, 0)).astype(BF)
    grad_down = dot(activated, incoming, (0, 0)).astype(BF)
    grad_up = dot(normed_second, grad_hidden, (0, 0)).astype(BF)

    grad_middle = incoming_rows + norm_back(grad_normed_second, ln2_gain, unit_second, inverse_second)
    gain_second = jnp.sum(grad_normed_second * unit_second, axis=0)
    shift_second = jnp.sum(grad_normed_second, axis=0)
    grad_branch = grad_middle.astype(BF)
    grad_heads = jnp.stack(
        [
            sum(dot(grad_branch[:, i * 1024 : (i + 1) * 1024], out_groups[i][g], (1, 1)) for i in range(2)).astype(BF)
            for g in range(4)
        ]
    ).reshape(2, 2, 128, 4, HD)
    grad_heads = jnp.where(x_lo == 0, grad_heads, grad_heads[::-1])
    grad_heads = jnp.where(core == 0, grad_heads, grad_heads[:, ::-1])
    grad_attended = exchange(grad_heads.transpose(0, 3, 1, 2, 4).reshape(16, 128, HD), TENSOR).reshape(2048, HD)

    mixed_rows = scatter_rows(mixed_part)
    output = (middle_rows + mixed_rows).astype(BF)

    branch_back = gather_rows(grad_branch)
    by_place = attended.reshape(2, 4, 2, 128, HD)
    own_half, sent_half = (
        jnp.concatenate([pick(pick(by_place, at_x, 0), at_core, 1) for at_core in (core, 1 - core)]).reshape(1024, HD)
        for at_x in (x_lo, 1 - x_lo)
    )
    both_heads = jnp.concatenate([own_half, x_pair(sent_half)], axis=1)
    grad_out = dot(both_heads, branch_back, (0, 0)).astype(BF)

    grad_queries, grad_keys, grad_values = attend_backward(
        projected[0], projected[1], projected[2], grad_attended, totals, length
    )
    stacked = jnp.stack([grad_queries, grad_keys, grad_values])
    grad_first_part = jnp.einsum("cth,cdh->td", stacked, qkv_weight, preferred_element_type=F32).astype(BF)
    grad_qkv_part = jnp.einsum("td,cth->cdh", normed_first, stacked, preferred_element_type=F32)

    columns = jnp.sum(stacked.astype(F32), axis=1)
    weights = qkv_weight.astype(F32)
    shift_first = jnp.sum(weights * columns[:, None, :], axis=(0, 2))
    gain_first = (jnp.sum(weights * grad_qkv_part, axis=(0, 2)) - ln1_shift * shift_first) / ln1_gain
    sums = sum_of_all(jnp.stack([gain_first, gain_second, shift_first, shift_second]))

    by_core = grad_first_part.reshape(8, 2, 128, 2048)
    sent = core_swap(pick(by_core, 1 - core, 1))
    halves = (pick(by_core, core, 1).astype(F32) + sent.astype(F32)).astype(BF).reshape(2, 4, 128, 2048)

    def over_x(values):
        return pick(values, x_lo, 0).astype(F32) + x_pair(pick(values, 1 - x_lo, 0)).astype(F32)

    left = total(exchange(halves[..., :1024].transpose(1, 0, 2, 3), "z")).astype(BF)
    right = over_x(halves[..., 1024:]).astype(BF)
    grad_normed_first = jnp.concatenate([over_x(left), total(exchange(right, "z"))], axis=-1)
    unit_rows, inverse_rows = norm_stats(token_rows)
    grad_tokens = (grad_middle + norm_back(grad_normed_first, ln1_gain, unit_rows, inverse_rows)).astype(BF)

    def own_first(values):
        return jnp.where(x_lo == 0, values, values[::-1])

    def sum_columns(grad):
        rows = grad.shape[0] // 2
        blocks = own_first(grad.reshape(2, rows, 2, 1024)).transpose(2, 0, 1, 3).reshape(4, rows, 1024)
        over_x = total(exchange(blocks, ("x_hi", "x_lo"))).astype(BF)
        return total(exchange(over_x.reshape(rows, 4, 256).transpose(1, 0, 2), "y"))

    grad_down = sum_columns(grad_down)
    grad_out = sum_columns(grad_out)
    up_sums = total(exchange(grad_up.reshape(2, 4, 256, 1024).transpose(1, 0, 2, 3), "y")).astype(BF)
    up_blocks = own_first(up_sums.reshape(2, 256, 2, 512).transpose(2, 0, 1, 3)).transpose(1, 0, 2, 3)
    grad_up = total(exchange(up_blocks.reshape(4, 256, 512), ("x_hi", "x_lo")))
    qkv_sums = total(
        exchange(grad_qkv_part.astype(BF).reshape(3, 2, 4, 256, 128).transpose(2, 1, 0, 3, 4), "y")
    ).astype(BF)
    grad_qkv = total(exchange(qkv_sums, "x_hi"))
    return (output, grad_tokens, grad_qkv, grad_out, grad_up, grad_down, sums[:2], sums[2:])


def solution(mesh):
    return jax.shard_map(
        body,
        mesh=Mesh(mesh.devices.reshape(2, 4, 2, 4, 2), AXES),
        in_specs=(
            P(BATCH, None),
            P(),
            P(),
            P(None, None, TENSOR),
            P(TENSOR, None),
            P(),
            P(),
            P(None, TENSOR),
            P(TENSOR, None),
            P(BATCH),
            P(AXES, None),
        ),
        out_specs=(
            P(AXES, None),
            P(AXES, None),
            P(None, BATCH, TENSOR),
            P(TENSOR, BATCH),
            P(BATCH, TENSOR),
            P(TENSOR, BATCH),
            P(),
            P(),
        ),
        check_vma=False,
    )
```

```python
from functools import partial

import jax
import jax.numpy as jnp
from jax import lax
from jax.sharding import Mesh
from jax.sharding import PartitionSpec as P

HD = 128
EPS = 1e-05
MASKED_SCORE = -1e30
BF = jnp.bfloat16
F32 = jnp.float32


AXES = ("x_hi", "y", "x_lo", "z", "core")
BATCH, TENSOR = AXES[:2], AXES[2:]


def core_swap(values):
    return lax.ppermute(values, "core", [(0, 1), (1, 0)])


def x_pair(values):
    return lax.ppermute(values, "x_lo", [(0, 1), (1, 0)])


def x_partner(values):
    pairs = [(r * 2 + c, ((r + (1, -1)[c]) % 4) * 2 + c) for r in range(4) for c in range(2)]
    return lax.ppermute(values, ("x_hi", "x_lo", "core"), pairs)


def shift(axes, sizes, step):
    return lambda values: lax.ppermute(values, axes, [(i, (i + step) % sizes) for i in range(sizes)])


z_up, z_down, z_far = (shift("z", 4, step) for step in (1, -1, 2))
y_up, y_down, y_far = (shift("y", 4, step) for step in (1, -1, 2))
x_up, x_down, x_far = (shift(("x_hi", "x_lo"), 4, step) for step in (1, -1, 2))


def norm_stats(values):
    centre = jnp.mean(values, axis=-1, keepdims=True)
    offsets = values - centre
    variance = jnp.mean(offsets * offsets, axis=-1, keepdims=True)
    inverse = lax.rsqrt(variance + EPS)
    return (offsets * inverse, inverse)


def norm_back(grad_normed, gain, unit_rows, inverse):
    scaled = grad_normed * gain
    return inverse * (
        scaled
        - jnp.mean(scaled, axis=-1, keepdims=True)
        - unit_rows * jnp.mean(scaled * unit_rows, axis=-1, keepdims=True)
    )


def dot(left, right, dims):
    return lax.dot_general(left, right, ((dims[:1], dims[1:]), ((), ())), preferred_element_type=F32)


def block_scores(queries, key_rows, start_row, stop_row, length):
    scores = dot(queries[start_row:stop_row], key_rows[:stop_row], (1, 1)) * HD ** (-0.5)
    query_index = start_row + jnp.arange(stop_row - start_row, dtype=jnp.int32)[:, None]
    key_index = jnp.arange(stop_row, dtype=jnp.int32)[None, :]
    return jnp.where((key_index <= query_index) & (key_index < length), scores, MASKED_SCORE)


def attend_forward(queries, key_rows, value_rows, length):
    seq_len = queries.shape[0]
    pieces = []
    totals = []
    for start_row in range(0, seq_len, 512):
        stop_row = start_row + 512
        scores = block_scores(queries, key_rows, start_row, stop_row, length)
        row_peak = jnp.max(scores, axis=-1, keepdims=True)
        log_total = jnp.log(jnp.sum(jnp.exp(scores - row_peak), axis=-1, keepdims=True)) + row_peak
        attn_probs = jnp.exp(scores - log_total).astype(BF)
        pieces.append(dot(attn_probs, value_rows[:stop_row], (1, 0)).astype(BF))
        totals.append(log_total)
    return (jnp.concatenate(pieces, axis=0), jnp.concatenate(totals, axis=0))


def attend_backward(queries, key_rows, value_rows, grad_attended, totals, length):
    seq_len = queries.shape[0]
    score_scale = HD ** (-0.5)
    grad_queries = []
    grad_keys = jnp.zeros(key_rows.shape, F32)
    grad_values = jnp.zeros(value_rows.shape, F32)
    for start_row in range(0, seq_len, 512):
        stop_row = start_row + 512
        scores = block_scores(queries, key_rows, start_row, stop_row, length)
        attn_probs = jnp.exp(scores - totals[start_row:stop_row])
        grad_probs = dot(grad_attended[start_row:stop_row], value_rows[:stop_row], (1, 1))
        centre = jnp.sum(attn_probs * grad_probs, axis=-1, keepdims=True)
        grad_scores = (attn_probs * (grad_probs - centre)).astype(BF)
        grad_queries.append(dot(grad_scores, key_rows[:stop_row], (1, 0)) * score_scale)
        grad_keys = grad_keys.at[:stop_row].add(
            dot(grad_scores, queries[start_row:stop_row], (0, 0)) * score_scale
        )
        grad_values = grad_values.at[:stop_row].add(
            dot(attn_probs.astype(BF), grad_attended[start_row:stop_row], (0, 0))
        )
    grad_queries = jnp.concatenate(grad_queries, axis=0)
    return (grad_queries.astype(BF), grad_keys.astype(BF), grad_values.astype(BF))


def scatter(values, axes):
    return lax.psum_scatter(values, axes, scatter_dimension=0, tiled=True).astype(F32)


def pick(values, index, axis):
    return lax.dynamic_index_in_dim(values, index, axis, False)


def reduce_ring(values, place, up, down, far):
    parts = [pick(values, (place + by) % 4, 0) for by in range(4)]
    return sum(
        move(part).astype(F32) for move, part in zip((lambda v: v, up, far, down), parts)
    )


def sum_of_all(values):
    for move in (core_swap, z_far, z_up, x_far, x_up, y_far, y_up):
        values = values + move(values)
    return values


def body(
    tokens,
    ln1_gain,
    ln1_shift,
    qkv_weight,
    out_weight,
    ln2_gain,
    ln2_shift,
    up_weight,
    down_weight,
    lengths,
    cotangent,
):
    x_hi, y, x_lo, z, core = (lax.axis_index(axis) for axis in AXES)
    tensor = x_lo * 8 + z * 2 + core
    length = lengths[0]

    out_full = lax.all_gather(out_weight, TENSOR, axis=0, tiled=True)
    live_rows = (tensor * 128 + jnp.arange(128, dtype=jnp.int32) < length).astype(F32)[:, None]
    incoming_rows = cotangent.astype(F32) * live_rows
    sent_rows = incoming_rows.astype(BF)
    along_z = jnp.stack([sent_rows, z_down(sent_rows), z_far(sent_rows), z_up(sent_rows)])
    along_z = lax.dynamic_slice_in_dim(jnp.concatenate([along_z, along_z[:3]]), (4 - z) % 4, 4, 0)
    from_core = core_swap(along_z)
    incoming = jnp.stack(
        [jnp.where(core == 0, along_z, from_core), jnp.where(core == 0, from_core, along_z)], axis=1
    ).reshape(1024, 2048)
    up_both = jnp.concatenate([up_weight, x_partner(up_weight)], axis=1)
    down_both = jnp.concatenate([down_weight, x_partner(down_weight)], axis=0)

    inputs = tokens.astype(F32)
    unit_first, _ = norm_stats(inputs)
    normed_first = (unit_first * ln1_gain + ln1_shift).astype(BF)
    projected = jnp.einsum("td,cdh->cth", normed_first, qkv_weight, preferred_element_type=F32).astype(BF)
    attended, totals = attend_forward(projected[0], projected[1], projected[2], length)
    attended_rows = lax.all_to_all(attended, TENSOR, 0, 1, tiled=True)
    branch_rows = dot(attended_rows, out_full, (1, 0))
    token_rows = lax.dynamic_slice_in_dim(tokens, tensor * 128, 128, 0).astype(F32)
    middle_rows = token_rows + branch_rows
    unit_second, inverse_second = norm_stats(middle_rows)
    normed_rows = (unit_second * ln2_gain + ln2_shift).astype(BF)

    normed_second = lax.all_gather(normed_rows, ("z", "core"), axis=0, tiled=True)
    hidden = dot(normed_second, up_both, (1, 0))
    activated, gelu_pull = jax.vjp(partial(jax.nn.gelu, approximate=True), hidden)
    activated = activated.astype(BF)
    grad_act = dot(incoming, down_both, (1, 1))
    grad_hidden = gelu_pull(grad_act)[0].astype(BF)
    grad_normed_part = dot(grad_hidden, up_both, (1, 1)).astype(BF)
    grad_normed_second = scatter(grad_normed_part, ("z", "core"))

    mixed_part = dot(activated, down_both, (1, 0)).astype(BF)
    grad_down = dot(activated, incoming, (0, 0)).astype(BF)
    grad_up = dot(normed_second, grad_hidden, (0, 0)).astype(BF)

    grad_middle = incoming_rows + norm_back(grad_normed_second, ln2_gain, unit_second, inverse_second)
    gain_second = jnp.sum(grad_normed_second * unit_second, axis=0)
    shift_second = jnp.sum(grad_normed_second, axis=0)
    grad_branch = grad_middle.astype(BF)
    grad_attended = lax.all_to_all(dot(grad_branch, out_full, (1, 1)).astype(BF), TENSOR, 1, 0, tiled=True)
    mixed_rows = scatter(mixed_part, ("z", "core"))
    output = (middle_rows + mixed_rows).astype(BF)

    branch_back = lax.all_gather(grad_branch, ("z", "core"), axis=0, tiled=True)
    by_half = attended.reshape(2, 1024, HD)
    both_heads = jnp.concatenate([pick(by_half, x_lo, 0), x_pair(pick(by_half, 1 - x_lo, 0))], axis=1)
    grad_out = dot(both_heads, branch_back, (0, 0)).astype(BF)

    grad_queries, grad_keys, grad_values = attend_backward(
        projected[0], projected[1], projected[2], grad_attended, totals, length
    )
    stacked = jnp.stack([grad_queries, grad_keys, grad_values])
    grad_first_part = jnp.einsum("cth,cdh->td", stacked, qkv_weight, preferred_element_type=F32).astype(BF)
    grad_qkv_part = jnp.einsum("td,cth->cdh", normed_first, stacked, preferred_element_type=F32)

    columns = jnp.sum(stacked.astype(F32), axis=1)
    weights = qkv_weight.astype(F32)
    shift_first = jnp.sum(weights * columns[:, None, :], axis=(0, 2))
    gain_first = (jnp.sum(weights * grad_qkv_part, axis=(0, 2)) - ln1_shift * shift_first) / ln1_gain
    sums = sum_of_all(jnp.stack([gain_first, gain_second, shift_first, shift_second]))

    by_core = grad_first_part.reshape(8, 2, 128, 2048)
    sent = core_swap(pick(by_core, 1 - core, 1))
    halves = (pick(by_core, core, 1).astype(F32) + sent.astype(F32)).astype(BF).reshape(2, 4, 128, 2048)

    def over_x(values):
        return pick(values, x_lo, 0).astype(F32) + x_pair(pick(values, 1 - x_lo, 0)).astype(F32)

    def over_z(values):
        return reduce_ring(values, z, z_up, z_down, z_far)

    left = over_z(halves[..., :1024].transpose(1, 0, 2, 3)).astype(BF)
    right = over_x(halves[..., 1024:]).astype(BF)
    grad_normed_first = jnp.concatenate([over_x(left), over_z(right)], axis=-1)
    unit_rows, inverse_rows = norm_stats(token_rows)
    grad_tokens = (grad_middle + norm_back(grad_normed_first, ln1_gain, unit_rows, inverse_rows)).astype(BF)

    def own_first(values):
        return jnp.where(x_lo == 0, values, values[::-1])

    def over_y(values):
        return reduce_ring(values, y, y_up, y_down, y_far)

    def over_ring(values):
        return reduce_ring(values, x_hi * 2 + x_lo, x_up, x_down, x_far)

    def sum_columns(grad):
        rows = grad.shape[0] // 2
        blocks = own_first(grad.reshape(2, rows, 2, 1024)).transpose(2, 0, 1, 3).reshape(4, rows, 1024)
        return over_y(over_ring(blocks).astype(BF).reshape(rows, 4, 256).transpose(1, 0, 2))

    grad_down = sum_columns(grad_down)
    grad_out = sum_columns(grad_out)
    up_sums = over_y(grad_up.reshape(2, 4, 256, 1024).transpose(1, 0, 2, 3)).astype(BF)
    up_blocks = own_first(up_sums.reshape(2, 256, 2, 512).transpose(2, 0, 1, 3)).transpose(1, 0, 2, 3)
    grad_up = over_ring(up_blocks.reshape(4, 256, 512))
    qkv_sums = over_y(grad_qkv_part.astype(BF).reshape(3, 2, 4, 256, 128).transpose(2, 1, 0, 3, 4)).astype(BF)
    grad_qkv = pick(qkv_sums, x_hi, 0).astype(F32) + shift("x_hi", 2, 1)(pick(qkv_sums, 1 - x_hi, 0)).astype(F32)
    return (output, grad_tokens, grad_qkv, grad_out, grad_up, grad_down, sums[:2], sums[2:])


def solution(mesh):
    return jax.shard_map(
        body,
        mesh=Mesh(mesh.devices.reshape(2, 4, 2, 4, 2), AXES),
        in_specs=(
            P(BATCH, None),
            P(),
            P(),
            P(None, None, TENSOR),
            P(TENSOR, None),
            P(),
            P(),
            P(None, TENSOR),
            P(TENSOR, None),
            P(BATCH),
            P(AXES, None),
        ),
        out_specs=(
            P(AXES, None),
            P(AXES, None),
            P(None, BATCH, TENSOR),
            P(TENSOR, BATCH),
            P(BATCH, TENSOR),
            P(TENSOR, BATCH),
            P(),
            P(),
        ),
        check_vma=False,
    )
```

```python
import functools

import jax
import jax.numpy as jnp
from jax import lax
from jax.experimental import pallas as pl
from jax.experimental.pallas import tpu as pltpu
from jax.sharding import Mesh
from jax.sharding import PartitionSpec as P

HD = 128
EPS = 1e-05
MASKED_SCORE = -1e30
BF = jnp.bfloat16
F32 = jnp.float32

AXES = ("x_hi", "y", "x_lo", "z", "core")
BATCH, TENSOR = AXES[:2], AXES[2:]


def core_swap(values):
    return lax.ppermute(values, "core", [(0, 1), (1, 0)])


def x_pair(values):
    return lax.ppermute(values, "x_lo", [(0, 1), (1, 0)])


def x_partner(values):
    pairs = [(r * 2 + c, ((r + (1, -1)[c]) % 4) * 2 + c) for r in range(4) for c in range(2)]
    return lax.ppermute(values, ("x_hi", "x_lo", "core"), pairs)


def shift(axes, sizes, step):
    return lambda values: lax.ppermute(values, axes, [(i, (i + step) % sizes) for i in range(sizes)])


z_up, z_down, z_far = (shift("z", 4, step) for step in (1, -1, 2))
y_up, y_down, y_far = (shift("y", 4, step) for step in (1, -1, 2))
x_up, x_down, x_far = (shift(("x_hi", "x_lo"), 4, step) for step in (1, -1, 2))


def norm_stats(values):
    centre = jnp.mean(values, axis=-1, keepdims=True)
    offsets = values - centre
    variance = jnp.mean(offsets * offsets, axis=-1, keepdims=True)
    inverse = lax.rsqrt(variance + EPS)
    return (offsets * inverse, inverse)


def norm_back(grad_normed, gain, unit_rows, inverse):
    scaled = grad_normed * gain
    return inverse * (
        scaled
        - jnp.mean(scaled, axis=-1, keepdims=True)
        - unit_rows * jnp.mean(scaled * unit_rows, axis=-1, keepdims=True)
    )


def dot(left, right, dims):
    return lax.dot_general(left, right, ((dims[:1], dims[1:]), ((), ())), preferred_element_type=F32)


def params(limit=60, **kw):
    return pltpu.CompilerParams(vmem_limit_bytes=limit * 2**20, **kw)


def qkv_kernel(x_ref, gain_ref, shift_ref, w_ref, normed_ref, out_ref, weights):
    @pl.when(pl.program_id(0) == 0)
    def _():
        for c in range(3):
            weights[:, c * HD : (c + 1) * HD] = w_ref[c]

    x = x_ref[...].astype(F32)
    offsets = x - jnp.mean(x, axis=-1, keepdims=True)
    inverse = lax.rsqrt(jnp.mean(offsets * offsets, axis=-1, keepdims=True) + EPS)
    normed = (offsets * inverse * gain_ref[...] + shift_ref[...]).astype(BF)
    normed_ref[...] = normed
    out_ref[...] = dot(normed, weights[...], (1, 0)).astype(BF)

def project(tokens, gain, shift, weight):
    rows = 256
    return pl.pallas_call(
        qkv_kernel,
        grid=(2048 // rows,),
        in_specs=[
            pl.BlockSpec((rows, 2048), lambda i: (i, 0)),
            pl.BlockSpec((1, 2048), lambda i: (0, 0)),
            pl.BlockSpec((1, 2048), lambda i: (0, 0)),
            pl.BlockSpec((3, 2048, HD), lambda i: (0, 0, 0)),
        ],
        out_specs=[pl.BlockSpec((rows, 2048), lambda i: (i, 0)), pl.BlockSpec((rows, 3 * HD), lambda i: (i, 0))],
        out_shape=[jax.ShapeDtypeStruct((2048, 2048), BF), jax.ShapeDtypeStruct((2048, 3 * HD), BF)],
        scratch_shapes=[pltpu.VMEM((2048, 3 * HD), BF)],
        compiler_params=params(),
        cost_estimate=pl.CostEstimate(flops=2 * 2048 * 2048 * 384, bytes_accessed=20 << 20, transcendentals=0),
    )(tokens, gain[None], shift[None], weight)


QB = 512
SCALE = HD ** -0.5

def masked(scores, first_query, first_key, length):
    query = first_query + lax.broadcasted_iota(jnp.int32, scores.shape, 0)
    key = first_key + lax.broadcasted_iota(jnp.int32, scores.shape, 1)
    return jnp.where((key <= query) & (key < length), scores, MASKED_SCORE)

def forward_kernel(length_ref, qkv_ref, out_ref, total_ref):
    length = length_ref[0]
    for i in range(2048 // QB):
        q = qkv_ref[i * QB : (i + 1) * QB, :HD]
        parts = []
        for j in range(i + 1):
            k = qkv_ref[j * QB : (j + 1) * QB, HD : 2 * HD]
            parts.append(masked(dot(q, k, (1, 1)) * SCALE, i * QB, j * QB, length))
        peak = functools.reduce(jnp.maximum, [jnp.max(p, axis=-1, keepdims=True) for p in parts])
        total = jnp.zeros((QB, 1), F32)
        acc = jnp.zeros((QB, HD), F32)
        for j in range(i + 1):
            e = jnp.exp(parts[j] - peak)
            total += jnp.sum(e, axis=-1, keepdims=True)
            acc += dot(e.astype(BF), qkv_ref[j * QB : (j + 1) * QB, 2 * HD :], (1, 0))
        out_ref[i * QB : (i + 1) * QB] = (acc / total).astype(BF)
        total_ref[i * QB : (i + 1) * QB] = peak + jnp.log(total)

def attend(qkv, lengths):
    return pl.pallas_call(
        forward_kernel,
        in_specs=[pl.BlockSpec(memory_space=pltpu.SMEM), pl.BlockSpec(memory_space=pltpu.VMEM)],
        out_specs=[pl.BlockSpec(memory_space=pltpu.VMEM)] * 2,
        out_shape=[jax.ShapeDtypeStruct((2048, HD), BF), jax.ShapeDtypeStruct((2048, 1), F32)],
        compiler_params=params(),
        cost_estimate=pl.CostEstimate(flops=2 * 2 * 2048 * 2048 * 128, bytes_accessed=3 << 20, transcendentals=2048 * 1280),
    )(lengths, qkv)

def backward_kernel(length_ref, qkv_ref, grad_ref, total_ref, out_ref, gk, gv, probs, gprobs):
    length = length_ref[0]
    n = 2048 // QB
    gk[...] = jnp.zeros_like(gk)
    gv[...] = jnp.zeros_like(gv)
    for i in range(n):
        rows = slice(i * QB, (i + 1) * QB)
        q = qkv_ref[rows, :HD]
        g = grad_ref[rows]
        total = total_ref[rows]
        centre = jnp.zeros((QB, 1), F32)
        for j in range(i + 1):
            keys = slice(j * QB, (j + 1) * QB)
            s = masked(dot(q, qkv_ref[keys, HD : 2 * HD], (1, 1)) * SCALE, i * QB, j * QB, length)
            p = jnp.exp(s - total)
            gp = dot(g, qkv_ref[keys, 2 * HD :], (1, 1))
            centre += jnp.sum(p * gp, axis=-1, keepdims=True)
            probs[:, keys] = p
            gprobs[:, keys] = gp
        gq = jnp.zeros((QB, HD), F32)
        for j in range(i + 1):
            keys = slice(j * QB, (j + 1) * QB)
            p = probs[:, keys]
            gs = (p * (gprobs[:, keys] - centre)).astype(BF)
            gq += dot(gs, qkv_ref[keys, HD : 2 * HD], (1, 0))
            gk[keys] += dot(gs, q, (0, 0))
            gv[keys] += dot(p.astype(BF), g, (0, 0))
        out_ref[rows, :HD] = (gq * SCALE).astype(BF)
    out_ref[:, HD : 2 * HD] = (gk[...] * SCALE).astype(BF)
    out_ref[:, 2 * HD :] = gv[...].astype(BF)

def attend_back(qkv, grad, totals, lengths):
    return pl.pallas_call(
        backward_kernel,
        in_specs=[pl.BlockSpec(memory_space=pltpu.SMEM)] + [pl.BlockSpec(memory_space=pltpu.VMEM)] * 3,
        out_specs=pl.BlockSpec(memory_space=pltpu.VMEM),
        out_shape=jax.ShapeDtypeStruct((2048, 3 * HD), BF),
        scratch_shapes=[pltpu.VMEM((2048, HD), F32), pltpu.VMEM((2048, HD), F32), pltpu.VMEM((QB, 2048), F32), pltpu.VMEM((QB, 2048), F32)],
        compiler_params=params(),
        cost_estimate=pl.CostEstimate(flops=5 * 2 * 2048 * 1280 * 128, bytes_accessed=4 << 20, transcendentals=2048 * 1280),
    )(lengths, qkv, grad, totals)


GELU_A = 0.7978845608028654
GELU_B = 0.044715

def front_kernel(place_ref, n_ref, mine_ref, other_ref, uo, up, do, dp, act_ref, gh_ref, part_ref, inc_ref):
    core = place_ref[0]
    inc_ref[0, core] = mine_ref[0]
    inc_ref[0, 1 - core] = other_ref[0]
    n = n_ref[0].reshape(256, 2048)
    inc = inc_ref[0].reshape(256, 2048)
    part = jnp.zeros((256, 2048), F32)
    for h, (u, d) in enumerate(((uo, do), (up, dp))):
        cols = slice(h * 512, (h + 1) * 512)
        hidden = dot(n, u[...], (1, 0))
        square = hidden * hidden
        t = jnp.tanh(GELU_A * (hidden + GELU_B * hidden * square))
        act_ref[:, cols] = (0.5 * hidden * (1 + t)).astype(BF)
        slope = 0.5 * (1 + t) + 0.5 * hidden * (1 - t * t) * (GELU_A * (1 + 3 * GELU_B * square))
        gh = (dot(inc, d[...], (1, 1)) * slope).astype(BF)
        gh_ref[:, cols] = gh
        part += dot(gh, u[...], (1, 1))
    part_ref[0] = part.astype(BF).reshape(2, 128, 2048)

def front(place, normed, mine, other, uo, up, do, dp):
    whole = lambda a: pl.BlockSpec(a.shape, lambda i, p: (0,) * a.ndim)
    blk = pl.BlockSpec((1, 2, 128, 2048), lambda i, p: (i, 0, 0, 0))
    one = pl.BlockSpec((1, 128, 2048), lambda i, p: ((i + 4 - p[1]) % 4, 0, 0))
    col = pl.BlockSpec((256, 1024), lambda i, p: (i, 0))
    return pl.pallas_call(
        front_kernel,
        grid_spec=pltpu.PrefetchScalarGridSpec(
            num_scalar_prefetch=1, grid=(4,),
            in_specs=[blk, one, one, whole(uo), whole(up), whole(do), whole(dp)],
            out_specs=[col, col, blk, blk],
        ),
        out_shape=[jax.ShapeDtypeStruct((1024, 1024), BF)] * 2 + [jax.ShapeDtypeStruct((4, 2, 128, 2048), BF)] * 2,
        compiler_params=params(),
        cost_estimate=pl.CostEstimate(flops=6 * 1024 * 1024 * 2048, bytes_accessed=28 << 20, transcendentals=1 << 20),
    )(place, normed, mine, other, uo, up, do, dp)


def mixed_kernel(act_ref, do, dp, out_ref):
    a = act_ref[...]
    out_ref[...] = (dot(a[:, :512], do[...], (1, 0)) + dot(a[:, 512:], dp[...], (1, 0))).astype(BF)

def mix(act, do, dp):
    whole = lambda a: pl.BlockSpec(a.shape, lambda i: (0,) * a.ndim)
    return pl.pallas_call(
        mixed_kernel, grid=(4,),
        in_specs=[pl.BlockSpec((256, 1024), lambda i: (i, 0)), whole(do), whole(dp)],
        out_specs=pl.BlockSpec((256, 2048), lambda i: (i, 0)),
        out_shape=jax.ShapeDtypeStruct((1024, 2048), BF),
        compiler_params=params(),
        cost_estimate=pl.CostEstimate(flops=2 * 1024 * 1024 * 2048, bytes_accessed=10 << 20, transcendentals=0),
    )(act, do, dp)


def grads_kernel(n_ref, inc_ref, act_ref, gh_ref, down_ref, up_ref):
    down_ref[...] = dot(act_ref[...], inc_ref[...], (0, 0)).astype(BF)
    up_ref[...] = dot(n_ref[...], gh_ref[...], (0, 0)).astype(BF)

def weight_grads(n, inc, act, gh):
    return pl.pallas_call(
        grads_kernel, grid=(4,),
        in_specs=[pl.BlockSpec((1024, 2048), lambda j: (0, 0))] * 2 + [pl.BlockSpec((1024, 256), lambda j: (0, j))] * 2,
        out_specs=[pl.BlockSpec((256, 2048), lambda j: (j, 0)), pl.BlockSpec((2048, 256), lambda j: (0, j))],
        out_shape=[jax.ShapeDtypeStruct((1024, 2048), BF), jax.ShapeDtypeStruct((2048, 1024), BF)],
        compiler_params=params(),
        cost_estimate=pl.CostEstimate(flops=4 * 1024 * 1024 * 2048, bytes_accessed=20 << 20, transcendentals=0),
    )(n, inc, act, gh)


def first_kernel(gp_ref, w_ref, out_ref):
    g = gp_ref[...]
    out_ref[...] = sum(dot(g[:, c * HD : (c + 1) * HD], w_ref[c], (1, 1)) for c in range(3)).astype(BF)

def first_back(gp, w):
    return pl.pallas_call(
        first_kernel, grid=(8,),
        in_specs=[pl.BlockSpec((256, 384), lambda i: (i, 0)), pl.BlockSpec((3, 2048, HD), lambda i: (0, 0, 0))],
        out_specs=pl.BlockSpec((256, 2048), lambda i: (i, 0)),
        out_shape=jax.ShapeDtypeStruct((2048, 2048), BF),
        compiler_params=params(),
        cost_estimate=pl.CostEstimate(flops=2 * 2048 * 2048 * 384, bytes_accessed=11 << 20, transcendentals=0),
    )(gp, w)

def stack_kernel(*refs):
    out, sem = refs[-2:]
    copies = [pltpu.make_async_copy(ref, out.at[i], sem.at[i]) for i, ref in enumerate(refs[:-2])]
    for copy in copies:
        copy.start()
    for copy in copies:
        copy.wait()

def stack(*arrays):
    return pl.pallas_call(
        stack_kernel,
        in_specs=[pl.BlockSpec(memory_space=pl.ANY)] * len(arrays),
        out_specs=pl.BlockSpec(memory_space=pl.ANY),
        out_shape=jax.ShapeDtypeStruct((len(arrays), *arrays[0].shape), arrays[0].dtype),
        scratch_shapes=[pltpu.SemaphoreType.DMA((len(arrays),))],
    )(*arrays)

def qkv_grads_kernel(n_ref, gp_ref, w_ref, out_ref, gain_ref, shift_ref, sums):
    @pl.when(pl.program_id(0) == 0)
    def _():
        sums[...] = jnp.sum(gp_ref[...].astype(F32), axis=0, keepdims=True)

    grad = dot(n_ref[...], gp_ref[...], (0, 0))
    out_ref[...] = grad.astype(BF)
    gain = jnp.zeros((256, 1), F32)
    shift = jnp.zeros((256, 1), F32)
    for c in range(3):
        cols = slice(c * HD, (c + 1) * HD)
        w = w_ref[c].astype(F32)
        gain += jnp.sum(w * grad[:, cols], axis=-1, keepdims=True)
        shift += jnp.sum(w * sums[:, cols], axis=-1, keepdims=True)
    gain_ref[...] = gain
    shift_ref[...] = shift

def qkv_grads(normed, gp, w):
    return pl.pallas_call(
        qkv_grads_kernel, grid=(8,),
        in_specs=[
            pl.BlockSpec((2048, 256), lambda i: (0, i)),
            pl.BlockSpec((2048, 384), lambda i: (0, 0)),
            pl.BlockSpec((3, 256, HD), lambda i: (0, i, 0)),
        ],
        out_specs=[pl.BlockSpec((256, 384), lambda i: (i, 0))] + [pl.BlockSpec((256, 1), lambda i: (i, 0))] * 2,
        out_shape=[jax.ShapeDtypeStruct((2048, 384), BF)] + [jax.ShapeDtypeStruct((2048, 1), F32)] * 2,
        scratch_shapes=[pltpu.VMEM((1, 384), F32)],
        compiler_params=params(),
        cost_estimate=pl.CostEstimate(flops=2 * 2048 * 2048 * 384, bytes_accessed=12 << 20, transcendentals=0),
    )(normed, gp, w)


def scatter(values, axes):
    return lax.psum_scatter(values, axes, scatter_dimension=0, tiled=True).astype(F32)


def pick(values, index, axis):
    return lax.dynamic_index_in_dim(values, index, axis, False)


def over_y(values, y, axis):
    parts = [pick(values, (y + by) % 4, axis) for by in range(4)]
    return sum(move(part).astype(F32) for move, part in zip((lambda v: v, y_up, y_far, y_down), parts))


def over_x(own, partner, x_hi, x_lo, axis):
    size = own.shape[axis] // 2
    up_hi = jnp.where(x_lo == 0, x_hi, 1 - x_hi)

    def part(values, at):
        return lax.dynamic_slice_in_dim(values, at * size, size, axis)

    return (
        part(own, x_hi).astype(F32)
        + x_far(part(own, 1 - x_hi)).astype(F32)
        + x_up(part(partner, up_hi)).astype(F32)
        + x_down(part(partner, 1 - up_hi)).astype(F32)
    )


def sum_of_all(values):
    for move in (core_swap, z_far, z_up, x_far, x_up, y_far, y_up):
        values = values + move(values)
    return values


def body(
    tokens,
    ln1_gain,
    ln1_shift,
    qkv_weight,
    out_weight,
    ln2_gain,
    ln2_shift,
    up_weight,
    down_weight,
    lengths,
    cotangent,
):
    x_hi, y, x_lo, z, core = (lax.axis_index(axis) for axis in AXES)
    tensor = x_lo * 8 + z * 2 + core
    length = lengths[0]

    out_full = lax.all_gather(out_weight, TENSOR, axis=0, tiled=True)
    live_rows = (tensor * 128 + jnp.arange(128, dtype=jnp.int32) < length).astype(F32)[:, None]
    incoming_rows = cotangent.astype(F32) * live_rows
    sent_rows = incoming_rows.astype(BF)
    along_z = stack(sent_rows, z_down(sent_rows), z_far(sent_rows), z_up(sent_rows))
    up_partner = x_partner(up_weight)
    down_partner = x_partner(down_weight)

    normed_first, projected = project(tokens, ln1_gain, ln1_shift, qkv_weight)
    attended, totals = attend(projected, lengths)
    attended, along_z = lax.optimization_barrier((attended, along_z))
    from_core = core_swap(along_z)
    attended_rows = lax.all_to_all(attended, TENSOR, 0, 1, tiled=True)
    attended_rows, from_core, up_partner = lax.optimization_barrier((attended_rows, from_core, up_partner))
    branch_rows = dot(attended_rows, out_full, (1, 0))
    token_rows = lax.dynamic_slice_in_dim(tokens, tensor * 128, 128, 0).astype(F32)
    middle_rows = token_rows + branch_rows
    unit_second, inverse_second = norm_stats(middle_rows)
    normed_rows = (unit_second * ln2_gain + ln2_shift).astype(BF)

    normed_second = lax.all_gather(normed_rows, ("z", "core"), axis=0, tiled=True)
    activated, grad_hidden, grad_normed_part, incoming = front(
        jnp.stack([core, z]),
        normed_second.reshape(4, 2, 128, 2048),
        along_z,
        from_core,
        up_weight,
        up_partner,
        down_weight,
        down_partner,
    )
    incoming = incoming.reshape(1024, 2048)
    grad_normed_second = scatter(grad_normed_part.reshape(1024, 2048), ("z", "core"))
    grad_down, grad_up = weight_grads(normed_second, incoming, activated, grad_hidden)
    mixed_part = mix(activated, down_weight, down_partner)

    grad_middle = incoming_rows + norm_back(grad_normed_second, ln2_gain, unit_second, inverse_second)
    gain_second = jnp.sum(grad_normed_second * unit_second, axis=0)
    shift_second = jnp.sum(grad_normed_second, axis=0)
    grad_branch = grad_middle.astype(BF)
    grad_attended = lax.all_to_all(dot(grad_branch, out_full, (1, 1)).astype(BF), TENSOR, 1, 0, tiled=True)
    mixed_rows = scatter(mixed_part, ("z", "core"))
    output = (middle_rows + mixed_rows).astype(BF)

    branch_back = lax.all_gather(grad_branch, ("z", "core"), axis=0, tiled=True)
    by_half = attended.reshape(2, 1024, HD)
    both_heads = jnp.concatenate([pick(by_half, x_lo, 0), x_pair(pick(by_half, 1 - x_lo, 0))], axis=1)
    grad_out = dot(both_heads, branch_back, (0, 0)).astype(BF)

    grad_projected = attend_back(projected, grad_attended, totals, lengths)
    grad_normed_first = scatter(first_back(grad_projected, qkv_weight), TENSOR)
    grad_qkv, gain_first, shift_first = qkv_grads(normed_first, grad_projected, qkv_weight)
    shift_first = shift_first[:, 0]
    gain_first = (gain_first[:, 0] - ln1_shift * shift_first) / ln1_gain
    sums = sum_of_all(jnp.stack([gain_first, gain_second, shift_first, shift_second]))

    unit_rows, inverse_rows = norm_stats(token_rows)
    grad_tokens = (grad_middle + norm_back(grad_normed_first, ln1_gain, unit_rows, inverse_rows)).astype(BF)

    def sum_columns(grad):
        rows = grad.shape[0] // 2
        along_x = over_x(grad[:rows], grad[rows:], x_hi, x_lo, 1).astype(BF)
        return over_y(along_x.reshape(rows, 4, 256), y, 1)

    grad_down = sum_columns(grad_down)
    grad_out = sum_columns(grad_out)
    up_sums = over_y(grad_up.reshape(2, 4, 256, 1024), y, 1).astype(BF)
    up_sums = up_sums.reshape(512, 1024)
    grad_up = over_x(up_sums[:, :512], up_sums[:, 512:], x_hi, x_lo, 0)
    qkv_sums = over_y(grad_qkv.reshape(2, 4, 256, 384), y, 1).astype(BF)
    grad_qkv = pick(qkv_sums, x_hi, 0).astype(F32) + shift("x_hi", 2, 1)(pick(qkv_sums, 1 - x_hi, 0)).astype(F32)
    grad_qkv = grad_qkv.reshape(256, 3, HD).transpose(1, 0, 2)
    return (output, grad_tokens, grad_qkv, grad_out, grad_up, grad_down, sums[:2], sums[2:])


def solution(mesh):
    return jax.shard_map(
        body,
        mesh=Mesh(mesh.devices.reshape(2, 4, 2, 4, 2), AXES),
        in_specs=(
            P(BATCH, None),
            P(),
            P(),
            P(None, None, TENSOR),
            P(TENSOR, None),
            P(),
            P(),
            P(None, TENSOR),
            P(TENSOR, None),
            P(BATCH),
            P(AXES, None),
        ),
        out_specs=(
            P(AXES, None),
            P(AXES, None),
            P(None, BATCH, TENSOR),
            P(TENSOR, BATCH),
            P(BATCH, TENSOR),
            P(TENSOR, BATCH),
            P(),
            P(),
        ),
        check_vma=False,
    )
```

```python
import functools

import jax
import jax.numpy as jnp
from jax import lax
from jax.experimental import pallas as pl
from jax.experimental.pallas import tpu as pltpu
from jax.sharding import Mesh
from jax.sharding import PartitionSpec as P

HD = 128
EPS = 1e-05
MASKED_SCORE = -1e30
BF = jnp.bfloat16
F32 = jnp.float32

AXES = ("x_hi", "y", "x_lo", "z", "core")
BATCH, TENSOR = AXES[:2], AXES[2:]


def core_swap(values):
    return lax.ppermute(values, "core", [(0, 1), (1, 0)])


def x_pair(values):
    return lax.ppermute(values, "x_lo", [(0, 1), (1, 0)])


def x_partner(values):
    pairs = [(r * 2 + c, ((r + (1, -1)[c]) % 4) * 2 + c) for r in range(4) for c in range(2)]
    return lax.ppermute(values, ("x_hi", "x_lo", "core"), pairs)


def neighbours(axis):
    pairs = [(i * 2 + c, ((i ^ 1) if c == 0 else 3 - i) * 2 + c) for i in range(4) for c in range(2)]
    return lambda values: lax.ppermute(values, (axis, "core"), pairs)


y_pair, z_pair = neighbours("y"), neighbours("z")


def shift(axes, sizes, step):
    return lambda values: lax.ppermute(values, axes, [(i, (i + step) % sizes) for i in range(sizes)])


z_up, z_down, z_far = (shift("z", 4, step) for step in (1, -1, 2))
y_up, y_far = (shift("y", 4, step) for step in (1, 2))
x_up, x_far = (shift(("x_hi", "x_lo"), 4, step) for step in (1, 2))


def norm_stats(values):
    centre = jnp.mean(values, axis=-1, keepdims=True)
    offsets = values - centre
    variance = jnp.mean(offsets * offsets, axis=-1, keepdims=True)
    inverse = lax.rsqrt(variance + EPS)
    return (offsets * inverse, inverse)


def norm_back(grad_normed, gain, unit_rows, inverse):
    scaled = grad_normed * gain
    return inverse * (
        scaled
        - jnp.mean(scaled, axis=-1, keepdims=True)
        - unit_rows * jnp.mean(scaled * unit_rows, axis=-1, keepdims=True)
    )


def dot(left, right, dims):
    return lax.dot_general(left, right, ((dims[:1], dims[1:]), ((), ())), preferred_element_type=F32)


def params(limit=60, **kw):
    return pltpu.CompilerParams(vmem_limit_bytes=limit * 2**20, **kw)


def qkv_kernel(x_ref, gain_ref, shift_ref, w_ref, normed_ref, out_ref, weights):
    @pl.when(pl.program_id(0) == 0)
    def _():
        for c in range(3):
            weights[:, c * HD : (c + 1) * HD] = w_ref[c]

    x = x_ref[...].astype(F32)
    offsets = x - jnp.mean(x, axis=-1, keepdims=True)
    inverse = lax.rsqrt(jnp.mean(offsets * offsets, axis=-1, keepdims=True) + EPS)
    normed = (offsets * inverse * gain_ref[...] + shift_ref[...]).astype(BF)
    normed_ref[...] = normed
    out_ref[...] = dot(normed, weights[...], (1, 0)).astype(BF)

def project(tokens, gain, shift, weight):
    rows = 256
    return pl.pallas_call(
        qkv_kernel,
        grid=(2048 // rows,),
        in_specs=[
            pl.BlockSpec((rows, 2048), lambda i: (i, 0)),
            pl.BlockSpec((1, 2048), lambda i: (0, 0)),
            pl.BlockSpec((1, 2048), lambda i: (0, 0)),
            pl.BlockSpec((3, 2048, HD), lambda i: (0, 0, 0)),
        ],
        out_specs=[
            pl.BlockSpec((rows, 2048), lambda i: (i, 0)),
            pl.BlockSpec((rows, 3 * HD), lambda i: (i, 0)),
            pl.BlockSpec((2048, 3 * HD), lambda i: (0, 0)),
        ],
        out_shape=[jax.ShapeDtypeStruct((2048, 2048), BF)] + [jax.ShapeDtypeStruct((2048, 3 * HD), BF)] * 2,
        compiler_params=params(),
        cost_estimate=pl.CostEstimate(flops=2 * 2048 * 2048 * 384, bytes_accessed=20 << 20, transcendentals=0),
    )(tokens, gain[None], shift[None], weight)


QB = 512
SCALE = HD ** -0.5

def masked(scores, first_query, first_key, length):
    query = first_query + lax.broadcasted_iota(jnp.int32, scores.shape, 0)
    key = first_key + lax.broadcasted_iota(jnp.int32, scores.shape, 1)
    return jnp.where((key <= query) & (key < length), scores, MASKED_SCORE)

def forward_kernel(length_ref, qkv_ref, out_ref, total_ref):
    length = length_ref[0]
    for i in range(2048 // QB):
        q = qkv_ref[i * QB : (i + 1) * QB, :HD]
        parts = []
        for j in range(i + 1):
            k = qkv_ref[j * QB : (j + 1) * QB, HD : 2 * HD]
            parts.append(masked(dot(q, k, (1, 1)) * SCALE, i * QB, j * QB, length))
        peak = functools.reduce(jnp.maximum, [jnp.max(p, axis=-1, keepdims=True) for p in parts])
        total = jnp.zeros((QB, 1), F32)
        acc = jnp.zeros((QB, HD), F32)
        for j in range(i + 1):
            e = jnp.exp(parts[j] - peak)
            total += jnp.sum(e, axis=-1, keepdims=True)
            acc += dot(e.astype(BF), qkv_ref[j * QB : (j + 1) * QB, 2 * HD :], (1, 0))
        out_ref[i * QB : (i + 1) * QB] = (acc / total).astype(BF)
        total_ref[i * QB : (i + 1) * QB] = peak + jnp.log(total)

def attend(qkv, lengths):
    return pl.pallas_call(
        forward_kernel,
        in_specs=[pl.BlockSpec(memory_space=pltpu.SMEM), pl.BlockSpec(memory_space=pltpu.VMEM)],
        out_specs=[pl.BlockSpec(memory_space=pltpu.VMEM)] * 2,
        out_shape=[jax.ShapeDtypeStruct((2048, HD), BF), jax.ShapeDtypeStruct((2048, 1), F32)],
        compiler_params=params(),
        cost_estimate=pl.CostEstimate(flops=2 * 2 * 2048 * 2048 * 128, bytes_accessed=3 << 20, transcendentals=2048 * 1280),
    )(lengths, qkv)

def backward_kernel(length_ref, qkv_ref, grad_ref, total_ref, out_ref, gk, gv, probs, gprobs):
    length = length_ref[0]
    n = 2048 // QB
    gk[...] = jnp.zeros_like(gk)
    gv[...] = jnp.zeros_like(gv)
    for i in range(n):
        rows = slice(i * QB, (i + 1) * QB)
        q = qkv_ref[rows, :HD]
        g = grad_ref[rows]
        total = total_ref[rows]
        centre = jnp.zeros((QB, 1), F32)
        for j in range(i + 1):
            keys = slice(j * QB, (j + 1) * QB)
            s = masked(dot(q, qkv_ref[keys, HD : 2 * HD], (1, 1)) * SCALE, i * QB, j * QB, length)
            p = jnp.exp(s - total)
            gp = dot(g, qkv_ref[keys, 2 * HD :], (1, 1))
            centre += jnp.sum(p * gp, axis=-1, keepdims=True)
            probs[:, keys] = p
            gprobs[:, keys] = gp
        gq = jnp.zeros((QB, HD), F32)
        for j in range(i + 1):
            keys = slice(j * QB, (j + 1) * QB)
            p = probs[:, keys]
            gs = (p * (gprobs[:, keys] - centre)).astype(BF)
            gq += dot(gs, qkv_ref[keys, HD : 2 * HD], (1, 0))
            gk[keys] += dot(gs, q, (0, 0))
            gv[keys] += dot(p.astype(BF), g, (0, 0))
        out_ref[rows, :HD] = (gq * SCALE).astype(BF)
    out_ref[:, HD : 2 * HD] = (gk[...] * SCALE).astype(BF)
    out_ref[:, 2 * HD :] = gv[...].astype(BF)

def attend_back(qkv, grad, totals, lengths):
    return pl.pallas_call(
        backward_kernel,
        in_specs=[pl.BlockSpec(memory_space=pltpu.SMEM)] + [pl.BlockSpec(memory_space=pltpu.VMEM)] * 3,
        out_specs=pl.BlockSpec(memory_space=pltpu.VMEM),
        out_shape=jax.ShapeDtypeStruct((2048, 3 * HD), BF),
        scratch_shapes=[pltpu.VMEM((2048, HD), F32), pltpu.VMEM((2048, HD), F32), pltpu.VMEM((QB, 2048), F32), pltpu.VMEM((QB, 2048), F32)],
        compiler_params=params(),
        cost_estimate=pl.CostEstimate(flops=5 * 2 * 2048 * 1280 * 128, bytes_accessed=4 << 20, transcendentals=2048 * 1280),
    )(lengths, qkv, grad, totals)


GELU_A = 0.7978845608028654
GELU_B = 0.044715

def front_kernel(place_ref, n_ref, mine_ref, other_ref, uo, up, do, dp, act_ref, gh_ref, part_ref, inc_ref):
    core = place_ref[0]
    inc_ref[0, core] = mine_ref[0]
    inc_ref[0, 1 - core] = other_ref[0]
    n = n_ref[0].reshape(256, 2048)
    inc = inc_ref[0].reshape(256, 2048)
    part = jnp.zeros((256, 2048), F32)
    for h, (u, d) in enumerate(((uo, do), (up, dp))):
        cols = slice(h * 512, (h + 1) * 512)
        hidden = dot(n, u[...], (1, 0))
        square = hidden * hidden
        t = jnp.tanh(GELU_A * (hidden + GELU_B * hidden * square))
        act_ref[:, cols] = (0.5 * hidden * (1 + t)).astype(BF)
        slope = 0.5 * (1 + t) + 0.5 * hidden * (1 - t * t) * (GELU_A * (1 + 3 * GELU_B * square))
        gh = (dot(inc, d[...], (1, 1)) * slope).astype(BF)
        gh_ref[:, cols] = gh
        part += dot(gh, u[...], (1, 1))
    part_ref[0] = part.astype(BF).reshape(2, 128, 2048)

def front(place, normed, mine, other, uo, up, do, dp):
    whole = lambda a: pl.BlockSpec(a.shape, lambda i, p: (0,) * a.ndim)
    blk = pl.BlockSpec((1, 2, 128, 2048), lambda i, p: (i, 0, 0, 0))
    one = pl.BlockSpec((1, 128, 2048), lambda i, p: ((i + 4 - p[1]) % 4, 0, 0))
    col = pl.BlockSpec((256, 1024), lambda i, p: (i, 0))
    return pl.pallas_call(
        front_kernel,
        grid_spec=pltpu.PrefetchScalarGridSpec(
            num_scalar_prefetch=1, grid=(4,),
            in_specs=[blk, one, one, whole(uo), whole(up), whole(do), whole(dp)],
            out_specs=[col, col, blk, blk],
        ),
        out_shape=[jax.ShapeDtypeStruct((1024, 1024), BF)] * 2 + [jax.ShapeDtypeStruct((4, 2, 128, 2048), BF)] * 2,
        compiler_params=params(),
        cost_estimate=pl.CostEstimate(flops=6 * 1024 * 1024 * 2048, bytes_accessed=28 << 20, transcendentals=1 << 20),
    )(place, normed, mine, other, uo, up, do, dp)


def mixed_kernel(place_ref, act_ref, do, dp, mine_ref, other_ref, rows):
    a = act_ref[...]
    rows[...] = (dot(a[:, :512], do[...], (1, 0)) + dot(a[:, 512:], dp[...], (1, 0))).astype(BF).reshape(2, 128, 2048)
    mine_ref[0] = rows[place_ref[0]]
    other_ref[0] = rows[1 - place_ref[0]]

def mix(place, act, do, dp):
    whole = lambda a: pl.BlockSpec(a.shape, lambda i, p: (0,) * a.ndim)
    return pl.pallas_call(
        mixed_kernel,
        grid_spec=pltpu.PrefetchScalarGridSpec(
            num_scalar_prefetch=1, grid=(4,),
            in_specs=[pl.BlockSpec((256, 1024), lambda i, p: (i, 0)), whole(do), whole(dp)],
            out_specs=[pl.BlockSpec((1, 128, 2048), lambda i, p: (i, 0, 0))] * 2,
            scratch_shapes=[pltpu.VMEM((2, 128, 2048), BF)],
        ),
        out_shape=[jax.ShapeDtypeStruct((4, 128, 2048), BF)] * 2,
        compiler_params=params(),
        cost_estimate=pl.CostEstimate(flops=2 * 1024 * 1024 * 2048, bytes_accessed=10 << 20, transcendentals=0),
    )(place, act, do, dp)

def grads_kernel(n_ref, inc_ref, act_ref, gh_ref, down_ref, up_ref):
    down_ref[...] = dot(act_ref[...], inc_ref[...], (0, 0)).astype(BF)
    up_ref[...] = dot(n_ref[...], gh_ref[...], (0, 0)).astype(BF)

def weight_grads(n, inc, act, gh):
    return pl.pallas_call(
        grads_kernel, grid=(4,),
        in_specs=[pl.BlockSpec((1024, 2048), lambda j: (0, 0))] * 2 + [pl.BlockSpec((1024, 256), lambda j: (0, j))] * 2,
        out_specs=[pl.BlockSpec((256, 2048), lambda j: (j, 0)), pl.BlockSpec((2048, 256), lambda j: (0, j))],
        out_shape=[jax.ShapeDtypeStruct((1024, 2048), BF), jax.ShapeDtypeStruct((2048, 1024), BF)],
        compiler_params=params(),
        cost_estimate=pl.CostEstimate(flops=4 * 1024 * 1024 * 2048, bytes_accessed=20 << 20, transcendentals=0),
    )(n, inc, act, gh)


def first_kernel(gp_ref, w_ref, out_ref):
    out_ref[...] = dot(gp_ref[...], w_ref[...], (1, 1)).astype(BF)

def first_back(gp, w):
    return pl.pallas_call(
        first_kernel, grid=(8,),
        in_specs=[pl.BlockSpec((256, 384), lambda i: (i, 0)), pl.BlockSpec((2048, 384), lambda i: (0, 0))],
        out_specs=pl.BlockSpec((256, 2048), lambda i: (i, 0)),
        out_shape=jax.ShapeDtypeStruct((2048, 2048), BF),
        compiler_params=params(),
        cost_estimate=pl.CostEstimate(flops=2 * 2048 * 2048 * 384, bytes_accessed=11 << 20, transcendentals=0),
    )(gp, w)


def stack_kernel(*refs):
    for i, ref in enumerate(refs[:-1]):
        refs[-1][i] = ref[...]

def stack(*arrays):
    return pl.pallas_call(
        stack_kernel,
        in_specs=[pl.BlockSpec(memory_space=pltpu.VMEM)] * len(arrays),
        out_specs=pl.BlockSpec(memory_space=pltpu.VMEM),
        out_shape=jax.ShapeDtypeStruct((len(arrays), *arrays[0].shape), arrays[0].dtype),
        compiler_params=params(),
    )(*arrays)

def qkv_grads_kernel(n_ref, gp_ref, w_ref, out_ref, gain_ref, shift_ref, sums):
    @pl.when(pl.program_id(0) == 0)
    def _():
        sums[...] = jnp.sum(gp_ref[...].astype(F32), axis=0, keepdims=True)

    grad = dot(n_ref[...], gp_ref[...], (0, 0))
    out_ref[...] = grad.astype(BF)
    gain = jnp.zeros((256, 1), F32)
    shift = jnp.zeros((256, 1), F32)
    for c in range(3):
        cols = slice(c * HD, (c + 1) * HD)
        w = w_ref[c].astype(F32)
        gain += jnp.sum(w * grad[:, cols], axis=-1, keepdims=True)
        shift += jnp.sum(w * sums[:, cols], axis=-1, keepdims=True)
    gain_ref[...] = gain
    shift_ref[...] = shift

def qkv_grads(normed, gp, w):
    return pl.pallas_call(
        qkv_grads_kernel, grid=(8,),
        in_specs=[
            pl.BlockSpec((2048, 256), lambda i: (0, i)),
            pl.BlockSpec((2048, 384), lambda i: (0, 0)),
            pl.BlockSpec((3, 256, HD), lambda i: (0, i, 0)),
        ],
        out_specs=[pl.BlockSpec((256, 384), lambda i: (i, 0))] + [pl.BlockSpec((256, 1), lambda i: (i, 0))] * 2,
        out_shape=[jax.ShapeDtypeStruct((2048, 384), BF)] + [jax.ShapeDtypeStruct((2048, 1), F32)] * 2,
        scratch_shapes=[pltpu.VMEM((1, 384), F32)],
        compiler_params=params(),
        cost_estimate=pl.CostEstimate(flops=2 * 2048 * 2048 * 384, bytes_accessed=12 << 20, transcendentals=0),
    )(normed, gp, w)


def scatter(values, axes):
    return lax.psum_scatter(values, axes, scatter_dimension=0, tiled=True).astype(F32)


def pick(values, index, axis):
    return lax.dynamic_index_in_dim(values, index, axis, False)


def after(values, *others):
    return lax.optimization_barrier((values, *others))[0]


def add(left, right):
    return (left.astype(F32) + right.astype(F32)).astype(BF)


def halve(values, place, axis, pair, far, pair_gate=(), far_gate=()):
    high, low = place // 2, place % 2
    values = add(pick(values, low, axis + 1), after(pair(pick(values, 1 - low, axis + 1)), *pair_gate))
    sent = far(pick(values, 1 - high, axis))
    return pick(values, high, axis).astype(F32) + after(sent, *far_gate).astype(F32)


def over_x(own, partner, x_hi, axis, pair_gate=(), far_gate=()):
    size = own.shape[axis] // 2
    own = add(own, after(x_partner(partner), *pair_gate))

    def part(at):
        return lax.dynamic_slice_in_dim(own, at * size, size, axis)

    return part(x_hi).astype(F32) + after(x_far(part(1 - x_hi)), *far_gate).astype(F32)


def sum_of_all(values):
    for move in (core_swap, z_far, z_up, x_far, x_up, y_far, y_up):
        values = values + move(values)
    return values


def body(
    tokens,
    ln1_gain,
    ln1_shift,
    qkv_weight,
    out_weight,
    ln2_gain,
    ln2_shift,
    up_weight,
    down_weight,
    lengths,
    cotangent,
):
    x_hi, y, x_lo, z, core = (lax.axis_index(axis) for axis in AXES)
    tensor = x_lo * 8 + z * 2 + core
    length = lengths[0]

    out_full = lax.all_gather(out_weight, TENSOR, axis=0, tiled=True)
    live_rows = (tensor * 128 + jnp.arange(128, dtype=jnp.int32) < length).astype(F32)[:, None]
    incoming_rows = cotangent.astype(F32) * live_rows
    sent_rows = incoming_rows.astype(BF)
    along_z = stack(sent_rows, z_down(sent_rows), z_far(sent_rows), z_up(sent_rows))
    up_partner = x_partner(up_weight)

    normed_first, projected, weights = project(tokens, ln1_gain, ln1_shift, qkv_weight)
    attended, totals = attend(projected, lengths)
    from_core = core_swap(along_z)
    attended_rows = lax.all_to_all(after(attended, along_z), TENSOR, 0, 1, tiled=True)
    attended_rows = after(attended_rows, from_core, up_partner)
    down_partner = x_partner(after(down_weight, out_full))
    branch_rows = dot(attended_rows, out_full, (1, 0))
    token_rows = lax.dynamic_slice_in_dim(tokens, tensor * 128, 128, 0).astype(F32)
    middle_rows = token_rows + branch_rows
    unit_second, inverse_second = norm_stats(middle_rows)
    normed_rows = (unit_second * ln2_gain + ln2_shift).astype(BF)

    normed_second = lax.all_gather(normed_rows, ("z", "core"), axis=0, tiled=True)
    place = jnp.stack([core, z])
    activated, grad_hidden, grad_normed_part, incoming = front(
        place,
        normed_second.reshape(4, 2, 128, 2048),
        along_z,
        from_core,
        up_weight,
        up_partner,
        down_weight,
        down_partner,
    )
    incoming = incoming.reshape(1024, 2048)
    grad_normed_second = scatter(grad_normed_part.reshape(1024, 2048), ("z", "core"))
    grad_down, grad_up = weight_grads(normed_second, incoming, activated, grad_hidden)
    mixed_mine, mixed_other = mix(place, after(activated, grad_up), down_weight, down_partner)
    mixed = add(mixed_mine, core_swap(mixed_other)).reshape(2, 2, 128, 2048)
    grad_normed_second = after(grad_normed_second, grad_down, grad_up, mixed)

    grad_middle = incoming_rows + norm_back(grad_normed_second, ln2_gain, unit_second, inverse_second)
    gain_second = jnp.sum(grad_normed_second * unit_second, axis=0)
    shift_second = jnp.sum(grad_normed_second, axis=0)
    grad_branch = grad_middle.astype(BF)
    grad_attended_rows = dot(grad_branch, out_full, (1, 1)).astype(BF)
    grad_attended = lax.all_to_all(grad_attended_rows, TENSOR, 1, 0, tiled=True)

    branch_back = lax.all_gather(grad_branch, ("z", "core"), axis=0, tiled=True)
    by_half = attended.reshape(2, 1024, HD)
    both_heads = jnp.concatenate([pick(by_half, x_lo, 0), x_pair(pick(by_half, 1 - x_lo, 0))], axis=1)
    grad_out = dot(both_heads, branch_back, (0, 0)).astype(BF)

    grad_projected = attend_back(projected, grad_attended, totals, lengths)
    grad_first_part = first_back(grad_projected, weights)
    grad_normed_first = scatter(grad_first_part, TENSOR)

    gates = ((grad_attended_rows,), (grad_first_part,))
    output = (middle_rows + halve(mixed, z, 0, z_pair, z_far, gates[1])).astype(BF)
    grad_down = over_x(grad_down[:512], grad_down[512:], x_hi, 1, *gates).astype(BF)
    up_sums = halve(grad_up.reshape(2, 2, 2, 256, 1024), y, 1, y_pair, y_far, *gates).astype(BF)
    grad_qkv, gain_first, shift_first = qkv_grads(normed_first, after(grad_projected, grad_first_part), qkv_weight)
    shift_first = shift_first[:, 0]
    gain_first = (gain_first[:, 0] - ln1_shift * shift_first) / ln1_gain
    sums = sum_of_all(jnp.stack([gain_first, gain_second, shift_first, shift_second]))

    unit_rows, inverse_rows = norm_stats(token_rows)
    grad_tokens = (grad_middle + norm_back(grad_normed_first, ln1_gain, unit_rows, inverse_rows)).astype(BF)

    def columns_over_y(grad):
        return halve(grad.reshape(grad.shape[0], 2, 2, 256), y, 1, y_pair, y_far)

    grad_down = columns_over_y(grad_down)
    grad_out = columns_over_y(over_x(grad_out[:128], grad_out[128:], x_hi, 1).astype(BF))
    up_sums = up_sums.reshape(512, 1024)
    grad_up = over_x(up_sums[:, :512], up_sums[:, 512:], x_hi, 0)
    qkv_sums = halve(grad_qkv.reshape(2, 2, 2, 256, 384), y, 1, y_pair, y_far).astype(BF)
    grad_qkv = pick(qkv_sums, x_hi, 0).astype(F32) + x_far(pick(qkv_sums, 1 - x_hi, 0)).astype(F32)
    grad_qkv = grad_qkv.reshape(256, 3, HD).transpose(1, 0, 2)
    return (output, grad_tokens, grad_qkv, grad_out, grad_up, grad_down, sums[:2], sums[2:])


def solution(mesh):
    return jax.shard_map(
        body,
        mesh=Mesh(mesh.devices.reshape(2, 4, 2, 4, 2), AXES),
        in_specs=(
            P(BATCH, None),
            P(),
            P(),
            P(None, None, TENSOR),
            P(TENSOR, None),
            P(),
            P(),
            P(None, TENSOR),
            P(TENSOR, None),
            P(BATCH),
            P(AXES, None),
        ),
        out_specs=(
            P(AXES, None),
            P(AXES, None),
            P(None, BATCH, TENSOR),
            P(TENSOR, BATCH),
            P(BATCH, TENSOR),
            P(TENSOR, BATCH),
            P(),
            P(),
        ),
        check_vma=False,
    )
```

```python
import functools

import jax
import jax.numpy as jnp
from jax import lax
from jax.experimental import pallas as pl
from jax.experimental.pallas import tpu as pltpu
from jax.sharding import Mesh
from jax.sharding import PartitionSpec as P

HD = 128
EPS = 1e-05
MASKED_SCORE = -1e30
BF = jnp.bfloat16
F32 = jnp.float32

AXES = ("x_hi", "y", "x_lo", "z", "core")
BATCH, TENSOR = AXES[:2], AXES[2:]


def core_swap(values):
    return lax.ppermute(values, "core", [(0, 1), (1, 0)])


def x_pair(values):
    return lax.ppermute(values, "x_lo", [(0, 1), (1, 0)])


def x_partner(values):
    pairs = [(r * 2 + c, ((r + (1, -1)[c]) % 4) * 2 + c) for r in range(4) for c in range(2)]
    return lax.ppermute(values, ("x_hi", "x_lo", "core"), pairs)


def neighbours(axis):
    pairs = [(i * 2 + c, ((i ^ 1) if c == 0 else 3 - i) * 2 + c) for i in range(4) for c in range(2)]
    return lambda values: lax.ppermute(values, (axis, "core"), pairs)


y_pair, z_pair = neighbours("y"), neighbours("z")


def shift(axes, sizes, step):
    return lambda values: lax.ppermute(values, axes, [(i, (i + step) % sizes) for i in range(sizes)])


z_up, z_down, z_far = (shift("z", 4, step) for step in (1, -1, 2))
y_up, y_far = (shift("y", 4, step) for step in (1, 2))
x_up, x_far = (shift(("x_hi", "x_lo"), 4, step) for step in (1, 2))


def norm_stats(values):
    centre = jnp.mean(values, axis=-1, keepdims=True)
    offsets = values - centre
    variance = jnp.mean(offsets * offsets, axis=-1, keepdims=True)
    inverse = lax.rsqrt(variance + EPS)
    return (offsets * inverse, inverse)


def norm_back(grad_normed, gain, unit_rows, inverse):
    scaled = grad_normed * gain
    return inverse * (
        scaled
        - jnp.mean(scaled, axis=-1, keepdims=True)
        - unit_rows * jnp.mean(scaled * unit_rows, axis=-1, keepdims=True)
    )


def dot(left, right, dims):
    return lax.dot_general(left, right, ((dims[:1], dims[1:]), ((), ())), preferred_element_type=F32)


def params(limit=60, **kw):
    return pltpu.CompilerParams(vmem_limit_bytes=limit * 2**20, **kw)


def qkv_kernel(x_ref, gain_ref, shift_ref, w_ref, normed_ref, out_ref, weights):
    @pl.when(pl.program_id(0) == 0)
    def _():
        for c in range(3):
            weights[:, c * HD : (c + 1) * HD] = w_ref[c]

    x = x_ref[...].astype(F32)
    offsets = x - jnp.mean(x, axis=-1, keepdims=True)
    inverse = lax.rsqrt(jnp.mean(offsets * offsets, axis=-1, keepdims=True) + EPS)
    normed = (offsets * inverse * gain_ref[...] + shift_ref[...]).astype(BF)
    normed_ref[...] = normed
    out_ref[...] = dot(normed, weights[...], (1, 0)).astype(BF)

def project(tokens, gain, shift, weight):
    rows = 256
    return pl.pallas_call(
        qkv_kernel,
        grid=(2048 // rows,),
        in_specs=[
            pl.BlockSpec((rows, 2048), lambda i: (i, 0)),
            pl.BlockSpec((1, 2048), lambda i: (0, 0)),
            pl.BlockSpec((1, 2048), lambda i: (0, 0)),
            pl.BlockSpec((3, 2048, HD), lambda i: (0, 0, 0)),
        ],
        out_specs=[
            pl.BlockSpec((rows, 2048), lambda i: (i, 0)),
            pl.BlockSpec((rows, 3 * HD), lambda i: (i, 0)),
            pl.BlockSpec((2048, 3 * HD), lambda i: (0, 0)),
        ],
        out_shape=[jax.ShapeDtypeStruct((2048, 2048), BF)] + [jax.ShapeDtypeStruct((2048, 3 * HD), BF)] * 2,
        compiler_params=params(),
        cost_estimate=pl.CostEstimate(flops=2 * 2048 * 2048 * 384, bytes_accessed=20 << 20, transcendentals=0),
    )(tokens, gain[None], shift[None], weight)


QB = 512
SCALE = HD ** -0.5

def masked(scores, first_query, first_key, length):
    query = first_query + lax.broadcasted_iota(jnp.int32, scores.shape, 0)
    key = first_key + lax.broadcasted_iota(jnp.int32, scores.shape, 1)
    return jnp.where((key <= query) & (key < length), scores, MASKED_SCORE)

def forward_kernel(length_ref, qkv_ref, out_ref, total_ref):
    length = length_ref[0]
    for i in range(2048 // QB):
        q = qkv_ref[i * QB : (i + 1) * QB, :HD]
        parts = []
        for j in range(i + 1):
            k = qkv_ref[j * QB : (j + 1) * QB, HD : 2 * HD]
            parts.append(masked(dot(q, k, (1, 1)) * SCALE, i * QB, j * QB, length))
        peak = functools.reduce(jnp.maximum, [jnp.max(p, axis=-1, keepdims=True) for p in parts])
        total = jnp.zeros((QB, 1), F32)
        acc = jnp.zeros((QB, HD), F32)
        for j in range(i + 1):
            e = jnp.exp(parts[j] - peak)
            total += jnp.sum(e, axis=-1, keepdims=True)
            acc += dot(e.astype(BF), qkv_ref[j * QB : (j + 1) * QB, 2 * HD :], (1, 0))
        out_ref[i * QB : (i + 1) * QB] = (acc / total).astype(BF)
        total_ref[i * QB : (i + 1) * QB] = peak + jnp.log(total)

def attend(qkv, lengths):
    return pl.pallas_call(
        forward_kernel,
        in_specs=[pl.BlockSpec(memory_space=pltpu.SMEM), pl.BlockSpec(memory_space=pltpu.VMEM)],
        out_specs=[pl.BlockSpec(memory_space=pltpu.VMEM)] * 2,
        out_shape=[jax.ShapeDtypeStruct((2048, HD), BF), jax.ShapeDtypeStruct((2048, 1), F32)],
        compiler_params=params(),
        cost_estimate=pl.CostEstimate(flops=2 * 2 * 2048 * 2048 * 128, bytes_accessed=3 << 20, transcendentals=2048 * 1280),
    )(lengths, qkv)

def backward_kernel(length_ref, qkv_ref, grad_ref, total_ref, out_ref, gk, gv, probs, gprobs):
    length = length_ref[0]
    n = 2048 // QB
    gk[...] = jnp.zeros_like(gk)
    gv[...] = jnp.zeros_like(gv)
    for i in range(n):
        rows = slice(i * QB, (i + 1) * QB)
        q = qkv_ref[rows, :HD]
        g = grad_ref[rows]
        total = total_ref[rows]
        centre = jnp.zeros((QB, 1), F32)
        for j in range(i + 1):
            keys = slice(j * QB, (j + 1) * QB)
            s = masked(dot(q, qkv_ref[keys, HD : 2 * HD], (1, 1)) * SCALE, i * QB, j * QB, length)
            p = jnp.exp(s - total)
            gp = dot(g, qkv_ref[keys, 2 * HD :], (1, 1))
            centre += jnp.sum(p * gp, axis=-1, keepdims=True)
            probs[:, keys] = p
            gprobs[:, keys] = gp
        gq = jnp.zeros((QB, HD), F32)
        for j in range(i + 1):
            keys = slice(j * QB, (j + 1) * QB)
            p = probs[:, keys]
            gs = (p * (gprobs[:, keys] - centre)).astype(BF)
            gq += dot(gs, qkv_ref[keys, HD : 2 * HD], (1, 0))
            gk[keys] += dot(gs, q, (0, 0))
            gv[keys] += dot(p.astype(BF), g, (0, 0))
        out_ref[rows, :HD] = (gq * SCALE).astype(BF)
    out_ref[:, HD : 2 * HD] = (gk[...] * SCALE).astype(BF)
    out_ref[:, 2 * HD :] = gv[...].astype(BF)

def attend_back(qkv, grad, totals, lengths):
    return pl.pallas_call(
        backward_kernel,
        in_specs=[pl.BlockSpec(memory_space=pltpu.SMEM)] + [pl.BlockSpec(memory_space=pltpu.VMEM)] * 3,
        out_specs=pl.BlockSpec(memory_space=pltpu.VMEM),
        out_shape=jax.ShapeDtypeStruct((2048, 3 * HD), BF),
        scratch_shapes=[pltpu.VMEM((2048, HD), F32), pltpu.VMEM((2048, HD), F32), pltpu.VMEM((QB, 2048), F32), pltpu.VMEM((QB, 2048), F32)],
        compiler_params=params(),
        cost_estimate=pl.CostEstimate(flops=5 * 2 * 2048 * 1280 * 128, bytes_accessed=4 << 20, transcendentals=2048 * 1280),
    )(lengths, qkv, grad, totals)


GELU_A = 0.7978845608028654
GELU_B = 0.044715

def front_kernel(place_ref, n_ref, mine_ref, other_ref, uo, up, do, dp, act_ref, gh_ref, part_ref, inc_ref):
    core = place_ref[0]
    inc_ref[0, core] = mine_ref[0]
    inc_ref[0, 1 - core] = other_ref[0]
    n = n_ref[0].reshape(256, 2048)
    inc = inc_ref[0].reshape(256, 2048)
    part = jnp.zeros((256, 2048), F32)
    for h, (u, d) in enumerate(((uo, do), (up, dp))):
        cols = slice(h * 512, (h + 1) * 512)
        hidden = dot(n, u[...], (1, 0))
        square = hidden * hidden
        t = jnp.tanh(GELU_A * (hidden + GELU_B * hidden * square))
        act_ref[:, cols] = (0.5 * hidden * (1 + t)).astype(BF)
        slope = 0.5 * (1 + t) + 0.5 * hidden * (1 - t * t) * (GELU_A * (1 + 3 * GELU_B * square))
        gh = (dot(inc, d[...], (1, 1)) * slope).astype(BF)
        gh_ref[:, cols] = gh
        part += dot(gh, u[...], (1, 1))
    part_ref[0] = part.astype(BF).reshape(2, 128, 2048)

def front(place, normed, mine, other, uo, up, do, dp):
    whole = lambda a: pl.BlockSpec(a.shape, lambda i, p: (0,) * a.ndim)
    blk = pl.BlockSpec((1, 2, 128, 2048), lambda i, p: (i, 0, 0, 0))
    one = pl.BlockSpec((1, 128, 2048), lambda i, p: ((i + 4 - p[1]) % 4, 0, 0))
    col = pl.BlockSpec((256, 1024), lambda i, p: (i, 0))
    return pl.pallas_call(
        front_kernel,
        grid_spec=pltpu.PrefetchScalarGridSpec(
            num_scalar_prefetch=1, grid=(4,),
            in_specs=[blk, one, one, whole(uo), whole(up), whole(do), whole(dp)],
            out_specs=[col, col, blk, blk],
        ),
        out_shape=[jax.ShapeDtypeStruct((1024, 1024), BF)] * 2 + [jax.ShapeDtypeStruct((4, 2, 128, 2048), BF)] * 2,
        compiler_params=params(),
        cost_estimate=pl.CostEstimate(flops=6 * 1024 * 1024 * 2048, bytes_accessed=28 << 20, transcendentals=1 << 20),
    )(place, normed, mine, other, uo, up, do, dp)


def mixed_kernel(place_ref, act_ref, do, dp, mine_ref, other_ref, rows):
    a = act_ref[...]
    rows[...] = (dot(a[:, :512], do[...], (1, 0)) + dot(a[:, 512:], dp[...], (1, 0))).astype(BF).reshape(2, 128, 2048)
    mine_ref[0] = rows[place_ref[0]]
    other_ref[0] = rows[1 - place_ref[0]]

def mix(place, act, do, dp):
    whole = lambda a: pl.BlockSpec(a.shape, lambda i, p: (0,) * a.ndim)
    return pl.pallas_call(
        mixed_kernel,
        grid_spec=pltpu.PrefetchScalarGridSpec(
            num_scalar_prefetch=1, grid=(4,),
            in_specs=[pl.BlockSpec((256, 1024), lambda i, p: (i, 0)), whole(do), whole(dp)],
            out_specs=[pl.BlockSpec((1, 128, 2048), lambda i, p: (i, 0, 0))] * 2,
            scratch_shapes=[pltpu.VMEM((2, 128, 2048), BF)],
        ),
        out_shape=[jax.ShapeDtypeStruct((4, 128, 2048), BF)] * 2,
        compiler_params=params(),
        cost_estimate=pl.CostEstimate(flops=2 * 1024 * 1024 * 2048, bytes_accessed=10 << 20, transcendentals=0),
    )(place, act, do, dp)

def grads_kernel(n_ref, inc_ref, act_ref, gh_ref, down_ref, up_ref):
    down_ref[...] = dot(act_ref[...], inc_ref[...], (0, 0)).astype(BF)
    up_ref[...] = dot(n_ref[...], gh_ref[...], (0, 0)).astype(BF)

def weight_grads(n, inc, act, gh):
    return pl.pallas_call(
        grads_kernel, grid=(4,),
        in_specs=[pl.BlockSpec((1024, 2048), lambda j: (0, 0))] * 2 + [pl.BlockSpec((1024, 256), lambda j: (0, j))] * 2,
        out_specs=[pl.BlockSpec((256, 2048), lambda j: (j, 0)), pl.BlockSpec((2048, 256), lambda j: (0, j))],
        out_shape=[jax.ShapeDtypeStruct((1024, 2048), BF), jax.ShapeDtypeStruct((2048, 1024), BF)],
        compiler_params=params(),
        cost_estimate=pl.CostEstimate(flops=4 * 1024 * 1024 * 2048, bytes_accessed=20 << 20, transcendentals=0),
    )(n, inc, act, gh)


def first_kernel(gp_ref, w_ref, out_ref):
    out_ref[...] = dot(gp_ref[...], w_ref[...], (1, 1)).astype(BF)

def first_back(gp, w):
    return pl.pallas_call(
        first_kernel, grid=(8,),
        in_specs=[pl.BlockSpec((256, 384), lambda i: (i, 0)), pl.BlockSpec((2048, 384), lambda i: (0, 0))],
        out_specs=pl.BlockSpec((256, 2048), lambda i: (i, 0)),
        out_shape=jax.ShapeDtypeStruct((2048, 2048), BF),
        compiler_params=params(),
        cost_estimate=pl.CostEstimate(flops=2 * 2048 * 2048 * 384, bytes_accessed=11 << 20, transcendentals=0),
    )(gp, w)


def stack_kernel(*refs):
    for i, ref in enumerate(refs[:-1]):
        refs[-1][i] = ref[...]

def stack(*arrays):
    return pl.pallas_call(
        stack_kernel,
        in_specs=[pl.BlockSpec(memory_space=pltpu.VMEM)] * len(arrays),
        out_specs=pl.BlockSpec(memory_space=pltpu.VMEM),
        out_shape=jax.ShapeDtypeStruct((len(arrays), *arrays[0].shape), arrays[0].dtype),
        compiler_params=params(),
    )(*arrays)

def out_kernel(place_ref, mine_ref, partner_ref, grad_ref, out_ref):
    grad = grad_ref[...]
    out_ref[0, place_ref[0]] = dot(mine_ref[...], grad, (0, 0)).astype(BF)
    out_ref[0, 1 - place_ref[0]] = dot(partner_ref[...], grad, (0, 0)).astype(BF)

def out_grads(place, mine, partner, grad):
    heads = pl.BlockSpec((1024, HD), lambda i, p: (0, 0))
    return pl.pallas_call(
        out_kernel,
        grid_spec=pltpu.PrefetchScalarGridSpec(
            num_scalar_prefetch=1, grid=(8,),
            in_specs=[heads, heads, pl.BlockSpec((1024, 256), lambda i, p: (0, i))],
            out_specs=pl.BlockSpec((1, 2, HD, 256), lambda i, p: (i, 0, 0, 0)),
        ),
        out_shape=jax.ShapeDtypeStruct((8, 2, HD, 256), BF),
        compiler_params=params(),
        cost_estimate=pl.CostEstimate(flops=2 * 1024 * 256 * 2048, bytes_accessed=6 << 20, transcendentals=0),
    )(place, mine, partner, grad)


def qkv_grads_kernel(n_ref, gp_ref, w_ref, out_ref, gain_ref, shift_ref, sums):
    @pl.when(pl.program_id(0) == 0)
    def _():
        sums[...] = jnp.sum(gp_ref[...].astype(F32), axis=0, keepdims=True)

    grad = dot(n_ref[...], gp_ref[...], (0, 0))
    out_ref[...] = grad.astype(BF)
    gain = jnp.zeros((256, 1), F32)
    shift = jnp.zeros((256, 1), F32)
    for c in range(3):
        cols = slice(c * HD, (c + 1) * HD)
        w = w_ref[c].astype(F32)
        gain += jnp.sum(w * grad[:, cols], axis=-1, keepdims=True)
        shift += jnp.sum(w * sums[:, cols], axis=-1, keepdims=True)
    gain_ref[...] = gain
    shift_ref[...] = shift

def qkv_grads(normed, gp, w):
    return pl.pallas_call(
        qkv_grads_kernel, grid=(8,),
        in_specs=[
            pl.BlockSpec((2048, 256), lambda i: (0, i)),
            pl.BlockSpec((2048, 384), lambda i: (0, 0)),
            pl.BlockSpec((3, 256, HD), lambda i: (0, i, 0)),
        ],
        out_specs=[pl.BlockSpec((256, 384), lambda i: (i, 0))] + [pl.BlockSpec((256, 1), lambda i: (i, 0))] * 2,
        out_shape=[jax.ShapeDtypeStruct((2048, 384), BF)] + [jax.ShapeDtypeStruct((2048, 1), F32)] * 2,
        scratch_shapes=[pltpu.VMEM((1, 384), F32)],
        compiler_params=params(),
        cost_estimate=pl.CostEstimate(flops=2 * 2048 * 2048 * 384, bytes_accessed=12 << 20, transcendentals=0),
    )(normed, gp, w)


def scatter(values, axes):
    return lax.psum_scatter(values, axes, scatter_dimension=0, tiled=True).astype(F32)


def pick(values, index, axis):
    return lax.dynamic_index_in_dim(values, index, axis, False)


def after(values, *others):
    return lax.optimization_barrier((values, *others))[0]


def add(left, right):
    return (left.astype(F32) + right.astype(F32)).astype(BF)


def halve(values, place, axis, pair, far):
    high, low = place // 2, place % 2
    values = add(pick(values, low, axis + 1), pair(pick(values, 1 - low, axis + 1)))
    return pick(values, high, axis).astype(F32) + far(pick(values, 1 - high, axis)).astype(F32)


def over_x(own, partner, x_hi, axis):
    size = own.shape[axis] // 2
    own = add(own, x_partner(partner))

    def part(at):
        return lax.dynamic_slice_in_dim(own, at * size, size, axis)

    return part(x_hi).astype(F32) + x_far(part(1 - x_hi)).astype(F32)


def exchange(values, axes):
    return jnp.sum(lax.all_to_all(values, axes, 0, 0).astype(F32), axis=0)


def sum_of_all(values):
    for axes, count in ((("z", "core"), 8), (("x_hi", "y", "x_lo"), 16)):
        values = exchange(jnp.broadcast_to(values[None], (count, *values.shape)), axes)
    return values


def body(
    tokens,
    ln1_gain,
    ln1_shift,
    qkv_weight,
    out_weight,
    ln2_gain,
    ln2_shift,
    up_weight,
    down_weight,
    lengths,
    cotangent,
):
    x_hi, y, x_lo, z, core = (lax.axis_index(axis) for axis in AXES)
    tensor = x_lo * 8 + z * 2 + core
    length = lengths[0]

    out_full = lax.all_gather(out_weight, TENSOR, axis=0, tiled=True)
    live_rows = (tensor * 128 + jnp.arange(128, dtype=jnp.int32) < length).astype(F32)[:, None]
    incoming_rows = cotangent.astype(F32) * live_rows
    sent_rows = incoming_rows.astype(BF)
    along_z = [z_down(sent_rows), z_far(sent_rows), z_up(sent_rows)]
    up_partner = x_partner(up_weight)

    normed_first, projected, weights = project(tokens, ln1_gain, ln1_shift, qkv_weight)
    attended, totals = attend(projected, lengths)
    along_z = stack(after(sent_rows, attended), *along_z)
    from_core = core_swap(along_z)
    attended_rows = lax.all_to_all(attended, TENSOR, 0, 1, tiled=True)
    attended_rows = after(attended_rows, from_core, up_partner)
    down_partner = x_partner(after(down_weight, out_full))
    branch_rows = dot(attended_rows, out_full, (1, 0))
    token_rows = lax.dynamic_slice_in_dim(tokens, tensor * 128, 128, 0).astype(F32)
    middle_rows = token_rows + branch_rows
    unit_second, inverse_second = norm_stats(middle_rows)
    normed_rows = (unit_second * ln2_gain + ln2_shift).astype(BF)

    normed_second = lax.all_gather(normed_rows, ("z", "core"), axis=0, tiled=True)
    place = jnp.stack([core, z])
    activated, grad_hidden, grad_normed_part, incoming = front(
        place,
        normed_second.reshape(4, 2, 128, 2048),
        along_z,
        from_core,
        up_weight,
        up_partner,
        down_weight,
        down_partner,
    )
    incoming = incoming.reshape(1024, 2048)
    grad_normed_second = scatter(grad_normed_part.reshape(1024, 2048), ("z", "core"))
    grad_down, grad_up = weight_grads(normed_second, incoming, activated, grad_hidden)
    mixed_mine, mixed_other = mix(place, after(activated, grad_up), down_weight, down_partner)
    mixed = add(mixed_mine, core_swap(mixed_other)).reshape(2, 2, 128, 2048)
    grad_normed_second = after(grad_normed_second, grad_down, grad_up, mixed)

    grad_middle = incoming_rows + norm_back(grad_normed_second, ln2_gain, unit_second, inverse_second)
    gain_second = jnp.sum(grad_normed_second * unit_second, axis=0)
    shift_second = jnp.sum(grad_normed_second, axis=0)
    grad_branch = grad_middle.astype(BF)
    grad_attended_rows = dot(grad_branch, out_full, (1, 1)).astype(BF)
    grad_attended = lax.all_to_all(grad_attended_rows, TENSOR, 1, 0, tiled=True)

    branch_back = lax.all_gather(grad_branch, ("z", "core"), axis=0, tiled=True)
    down_sums = add(grad_down[:512], after(x_partner(grad_down[512:]), grad_attended_rows))
    up_blocks = grad_up.reshape(2, 2, 2, 256, 1024)
    up_sums = add(pick(up_blocks, y % 2, 2), after(y_pair(pick(up_blocks, 1 - y % 2, 2)), grad_attended_rows))
    by_half = attended.reshape(2, 1024, HD)
    partner_heads = x_pair(pick(by_half, 1 - x_lo, 0))

    grad_projected = attend_back(projected, after(grad_attended, down_sums, up_sums), totals, lengths)
    grad_first_part = first_back(grad_projected, weights)
    grad_normed_first = scatter(grad_first_part, TENSOR)

    down_sums, up_sums = (
        pick(values, at, axis).astype(F32) + after(far(pick(values, 1 - at, axis)), grad_first_part).astype(F32)
        for values, at, axis, far in ((down_sums.reshape(512, 2, 1024), x_hi, 1, x_far), (up_sums, y // 2, 1, y_far))
    )
    grad_down = exchange(down_sums.astype(BF).reshape(512, 4, 256).transpose(1, 0, 2), "y")
    out_blocks = out_grads(
        x_lo[None], after(pick(by_half, x_lo, 0), grad_first_part), partner_heads, branch_back
    )
    grad_out = exchange(out_blocks.reshape(16, HD, 256), ("x_hi", "y", "x_lo"))
    grad_qkv, gain_first, shift_first = qkv_grads(normed_first, after(grad_projected, out_blocks), qkv_weight)
    shift_first = shift_first[:, 0]
    gain_first = (gain_first[:, 0] - ln1_shift * shift_first) / ln1_gain
    sums = sum_of_all(jnp.stack([gain_first, gain_second, shift_first, shift_second]))
    grad_qkv = exchange(grad_qkv.reshape(8, 256, 384), BATCH)
    grad_qkv = grad_qkv.reshape(256, 3, HD).transpose(1, 0, 2)
    up_sums = up_sums.astype(BF).reshape(512, 1024)
    grad_up = over_x(up_sums[:, :512], up_sums[:, 512:], x_hi, 0)
    output = (middle_rows + halve(after(mixed, grad_first_part), z, 0, z_pair, z_far)).astype(BF)

    unit_rows, inverse_rows = norm_stats(token_rows)
    grad_tokens = (grad_middle + norm_back(grad_normed_first, ln1_gain, unit_rows, inverse_rows)).astype(BF)
    return (output, grad_tokens, grad_qkv, grad_out, grad_up, grad_down, sums[:2], sums[2:])


def solution(mesh):
    return jax.shard_map(
        body,
        mesh=Mesh(mesh.devices.reshape(2, 4, 2, 4, 2), AXES),
        in_specs=(
            P(BATCH, None),
            P(),
            P(),
            P(None, None, TENSOR),
            P(TENSOR, None),
            P(),
            P(),
            P(None, TENSOR),
            P(TENSOR, None),
            P(BATCH),
            P(AXES, None),
        ),
        out_specs=(
            P(AXES, None),
            P(AXES, None),
            P(None, BATCH, TENSOR),
            P(TENSOR, BATCH),
            P(BATCH, TENSOR),
            P(TENSOR, BATCH),
            P(),
            P(),
        ),
        check_vma=False,
    )
```

```python
import functools

import jax
import jax.numpy as jnp
from jax import lax
from jax.experimental import pallas as pl
from jax.experimental.pallas import tpu as pltpu
from jax.sharding import Mesh
from jax.sharding import PartitionSpec as P

HD = 128
EPS = 1e-05
MASKED_SCORE = -1e30
BF = jnp.bfloat16
F32 = jnp.float32

AXES = ("x_hi", "y", "x_lo", "z", "core")
BATCH, TENSOR = AXES[:2], AXES[2:]


def core_swap(values):
    return lax.ppermute(values, "core", [(0, 1), (1, 0)])


def x_pair(values):
    return lax.ppermute(values, "x_lo", [(0, 1), (1, 0)])


def x_partner(values):
    pairs = [(r * 2 + c, ((r + (1, -1)[c]) % 4) * 2 + c) for r in range(4) for c in range(2)]
    return lax.ppermute(values, ("x_hi", "x_lo", "core"), pairs)


def neighbours(axis):
    pairs = [(i * 2 + c, ((i ^ 1) if c == 0 else 3 - i) * 2 + c) for i in range(4) for c in range(2)]
    return lambda values: lax.ppermute(values, (axis, "core"), pairs)


y_pair, z_pair = neighbours("y"), neighbours("z")


def shift(axes, sizes, step):
    return lambda values: lax.ppermute(values, axes, [(i, (i + step) % sizes) for i in range(sizes)])


z_up, z_down, z_far = (shift("z", 4, step) for step in (1, -1, 2))
y_up, y_far = (shift("y", 4, step) for step in (1, 2))
x_up, x_far = (shift(("x_hi", "x_lo"), 4, step) for step in (1, 2))


def norm_stats(values):
    centre = jnp.mean(values, axis=-1, keepdims=True)
    offsets = values - centre
    variance = jnp.mean(offsets * offsets, axis=-1, keepdims=True)
    inverse = lax.rsqrt(variance + EPS)
    return (offsets * inverse, inverse)


def norm_back(grad_normed, gain, unit_rows, inverse):
    scaled = grad_normed * gain
    return inverse * (
        scaled
        - jnp.mean(scaled, axis=-1, keepdims=True)
        - unit_rows * jnp.mean(scaled * unit_rows, axis=-1, keepdims=True)
    )


def dot(left, right, dims):
    return lax.dot_general(left, right, ((dims[:1], dims[1:]), ((), ())), preferred_element_type=F32)


def short(flops, moved):
    return pl.CostEstimate(flops=flops // 64, bytes_accessed=moved // 64, transcendentals=0)


def params(limit=60, **kw):
    return pltpu.CompilerParams(vmem_limit_bytes=limit * 2**20, **kw)


def qkv_kernel(x_ref, gain_ref, shift_ref, w_ref, normed_ref, out_ref, weights):
    @pl.when(pl.program_id(0) == 0)
    def _():
        for c in range(3):
            weights[:, c * HD : (c + 1) * HD] = w_ref[c]

    x = x_ref[...].astype(F32)
    offsets = x - jnp.mean(x, axis=-1, keepdims=True)
    inverse = lax.rsqrt(jnp.mean(offsets * offsets, axis=-1, keepdims=True) + EPS)
    normed = (offsets * inverse * gain_ref[...] + shift_ref[...]).astype(BF)
    normed_ref[...] = normed
    out_ref[...] = dot(normed, weights[...], (1, 0)).astype(BF)

def project(tokens, gain, shift, weight):
    rows = 256
    return pl.pallas_call(
        qkv_kernel,
        grid=(2048 // rows,),
        in_specs=[
            pl.BlockSpec((rows, 2048), lambda i: (i, 0)),
            pl.BlockSpec((1, 2048), lambda i: (0, 0)),
            pl.BlockSpec((1, 2048), lambda i: (0, 0)),
            pl.BlockSpec((3, 2048, HD), lambda i: (0, 0, 0)),
        ],
        out_specs=[
            pl.BlockSpec((rows, 2048), lambda i: (i, 0)),
            pl.BlockSpec((rows, 3 * HD), lambda i: (i, 0)),
            pl.BlockSpec((2048, 3 * HD), lambda i: (0, 0)),
        ],
        out_shape=[jax.ShapeDtypeStruct((2048, 2048), BF)] + [jax.ShapeDtypeStruct((2048, 3 * HD), BF)] * 2,
        compiler_params=params(),
        cost_estimate=short(2 * 2048 * 2048 * 384, 20 << 20),
    )(tokens, gain[None], shift[None], weight)


QB = 512
SCALE = HD ** -0.5

def masked(scores, first_query, first_key, length):
    query = first_query + lax.broadcasted_iota(jnp.int32, scores.shape, 0)
    key = first_key + lax.broadcasted_iota(jnp.int32, scores.shape, 1)
    return jnp.where((key <= query) & (key < length), scores, MASKED_SCORE)

def forward_kernel(length_ref, qkv_ref, out_ref, total_ref):
    length = length_ref[0]
    for i in range(2048 // QB):
        q = qkv_ref[i * QB : (i + 1) * QB, :HD]
        parts = []
        for j in range(i + 1):
            k = qkv_ref[j * QB : (j + 1) * QB, HD : 2 * HD]
            parts.append(masked(dot(q, k, (1, 1)) * SCALE, i * QB, j * QB, length))
        peak = functools.reduce(jnp.maximum, [jnp.max(p, axis=-1, keepdims=True) for p in parts])
        total = jnp.zeros((QB, 1), F32)
        acc = jnp.zeros((QB, HD), F32)
        for j in range(i + 1):
            e = jnp.exp(parts[j] - peak)
            total += jnp.sum(e, axis=-1, keepdims=True)
            acc += dot(e.astype(BF), qkv_ref[j * QB : (j + 1) * QB, 2 * HD :], (1, 0))
        out = (acc / total).astype(BF)
        for b in range(QB // HD):
            block = i * (QB // HD) + b
            out_ref[block % 8, block // 8] = out[b * HD : (b + 1) * HD]
        total_ref[i * QB : (i + 1) * QB] = peak + jnp.log(total)

def attend(qkv, lengths):
    return pl.pallas_call(
        forward_kernel,
        in_specs=[pl.BlockSpec(memory_space=pltpu.SMEM), pl.BlockSpec(memory_space=pltpu.VMEM)],
        out_specs=[pl.BlockSpec(memory_space=pltpu.VMEM)] * 2,
        out_shape=[jax.ShapeDtypeStruct((8, 2, 128, HD), BF), jax.ShapeDtypeStruct((2048, 1), F32)],
        compiler_params=params(),
        cost_estimate=short(2 * 2 * 2048 * 2048 * 128, 3 << 20),
    )(lengths, qkv)

def backward_kernel(length_ref, qkv_ref, grad_ref, total_ref, out_ref, gk, gv, probs, gprobs):
    length = length_ref[0]
    n = 2048 // QB
    gk[...] = jnp.zeros_like(gk)
    gv[...] = jnp.zeros_like(gv)
    for i in range(n):
        rows = slice(i * QB, (i + 1) * QB)
        q = qkv_ref[rows, :HD]
        g = grad_ref[rows]
        total = total_ref[rows]
        centre = jnp.zeros((QB, 1), F32)
        for j in range(i + 1):
            keys = slice(j * QB, (j + 1) * QB)
            s = masked(dot(q, qkv_ref[keys, HD : 2 * HD], (1, 1)) * SCALE, i * QB, j * QB, length)
            p = jnp.exp(s - total)
            gp = dot(g, qkv_ref[keys, 2 * HD :], (1, 1))
            centre += jnp.sum(p * gp, axis=-1, keepdims=True)
            probs[:, keys] = p
            gprobs[:, keys] = gp
        gq = jnp.zeros((QB, HD), F32)
        for j in range(i + 1):
            keys = slice(j * QB, (j + 1) * QB)
            p = probs[:, keys]
            gs = (p * (gprobs[:, keys] - centre)).astype(BF)
            gq += dot(gs, qkv_ref[keys, HD : 2 * HD], (1, 0))
            gk[keys] += dot(gs, q, (0, 0))
            gv[keys] += dot(p.astype(BF), g, (0, 0))
        out_ref[rows, :HD] = (gq * SCALE).astype(BF)
    out_ref[:, HD : 2 * HD] = (gk[...] * SCALE).astype(BF)
    out_ref[:, 2 * HD :] = gv[...].astype(BF)

def attend_back(qkv, grad, totals, lengths):
    return pl.pallas_call(
        backward_kernel,
        in_specs=[pl.BlockSpec(memory_space=pltpu.SMEM)] + [pl.BlockSpec(memory_space=pltpu.VMEM)] * 3,
        out_specs=pl.BlockSpec(memory_space=pltpu.VMEM),
        out_shape=jax.ShapeDtypeStruct((2048, 3 * HD), BF),
        scratch_shapes=[pltpu.VMEM((2048, HD), F32), pltpu.VMEM((2048, HD), F32), pltpu.VMEM((QB, 2048), F32), pltpu.VMEM((QB, 2048), F32)],
        compiler_params=params(),
        cost_estimate=short(5 * 2 * 2048 * 1280 * 128, 4 << 20),
    )(lengths, qkv, grad, totals)


GELU_A = 0.7978845608028654
GELU_B = 0.044715

def front_kernel(place_ref, n_ref, mine_ref, other_ref, uo, up, do, dp, act_ref, gh_ref, part_ref, inc_ref):
    core = place_ref[0]
    inc_ref[0, core] = mine_ref[0]
    inc_ref[0, 1 - core] = other_ref[0]
    n = n_ref[0].reshape(256, 2048)
    inc = inc_ref[0].reshape(256, 2048)
    part = jnp.zeros((256, 2048), F32)
    for h, (u, d) in enumerate(((uo, do), (up, dp))):
        cols = slice(h * 512, (h + 1) * 512)
        hidden = dot(n, u[...], (1, 0))
        square = hidden * hidden
        t = jnp.tanh(GELU_A * (hidden + GELU_B * hidden * square))
        act_ref[:, cols] = (0.5 * hidden * (1 + t)).astype(BF)
        slope = 0.5 * (1 + t) + 0.5 * hidden * (1 - t * t) * (GELU_A * (1 + 3 * GELU_B * square))
        gh = (dot(inc, d[...], (1, 1)) * slope).astype(BF)
        gh_ref[:, cols] = gh
        part += dot(gh, u[...], (1, 1))
    part_ref[0] = part.astype(BF).reshape(2, 128, 2048)

def front(place, normed, mine, other, uo, up, do, dp):
    whole = lambda a: pl.BlockSpec(a.shape, lambda i, p: (0,) * a.ndim)
    blk = pl.BlockSpec((1, 2, 128, 2048), lambda i, p: (i, 0, 0, 0))
    one = pl.BlockSpec((1, 128, 2048), lambda i, p: ((i + 4 - p[1]) % 4, 0, 0))
    col = pl.BlockSpec((256, 1024), lambda i, p: (i, 0))
    return pl.pallas_call(
        front_kernel,
        grid_spec=pltpu.PrefetchScalarGridSpec(
            num_scalar_prefetch=1, grid=(4,),
            in_specs=[blk, one, one, whole(uo), whole(up), whole(do), whole(dp)],
            out_specs=[col, col, blk, blk],
        ),
        out_shape=[jax.ShapeDtypeStruct((1024, 1024), BF)] * 2 + [jax.ShapeDtypeStruct((4, 2, 128, 2048), BF)] * 2,
        compiler_params=params(),
        cost_estimate=short(6 * 1024 * 1024 * 2048, 28 << 20),
    )(place, normed, mine, other, uo, up, do, dp)


def mixed_kernel(place_ref, act_ref, do, dp, mine_ref, other_ref, rows):
    a = act_ref[...]
    rows[...] = (dot(a[:, :512], do[...], (1, 0)) + dot(a[:, 512:], dp[...], (1, 0))).astype(BF).reshape(2, 128, 2048)
    mine_ref[0] = rows[place_ref[0]]
    other_ref[0] = rows[1 - place_ref[0]]

def mix(place, act, do, dp):
    whole = lambda a: pl.BlockSpec(a.shape, lambda i, p: (0,) * a.ndim)
    return pl.pallas_call(
        mixed_kernel,
        grid_spec=pltpu.PrefetchScalarGridSpec(
            num_scalar_prefetch=1, grid=(4,),
            in_specs=[pl.BlockSpec((256, 1024), lambda i, p: (i, 0)), whole(do), whole(dp)],
            out_specs=[pl.BlockSpec((1, 128, 2048), lambda i, p: (i, 0, 0))] * 2,
            scratch_shapes=[pltpu.VMEM((2, 128, 2048), BF)],
        ),
        out_shape=[jax.ShapeDtypeStruct((4, 128, 2048), BF)] * 2,
        compiler_params=params(),
        cost_estimate=short(2 * 1024 * 1024 * 2048, 10 << 20),
    )(place, act, do, dp)

def branch_kernel(place_ref, heads_ref, w_ref, mine_ref, other_ref, left, out):
    @pl.when(pl.program_id(0) == 0)
    def _():
        for h in range(8):
            left[:, h * HD : (h + 1) * HD] = heads_ref[h].reshape(256, HD)

    out[...] = dot(left[...], w_ref[...], (1, 0)).reshape(2, 128, 512)
    mine_ref[...] = out[place_ref[0]]
    other_ref[...] = out[1 - place_ref[0]].astype(BF)

def branch(place, heads, w):
    col = pl.BlockSpec((128, 512), lambda i, p: (0, i))
    return pl.pallas_call(
        branch_kernel,
        grid_spec=pltpu.PrefetchScalarGridSpec(
            num_scalar_prefetch=1, grid=(4,),
            in_specs=[pl.BlockSpec((8, 2, 128, HD), lambda i, p: (0, 0, 0, 0)), pl.BlockSpec((1024, 512), lambda i, p: (0, i))],
            out_specs=[col, col],
            scratch_shapes=[pltpu.VMEM((256, 1024), BF), pltpu.VMEM((2, 128, 512), F32)],
        ),
        out_shape=[jax.ShapeDtypeStruct((128, 2048), F32), jax.ShapeDtypeStruct((128, 2048), BF)],
        compiler_params=params(),
        cost_estimate=short(2 * 256 * 1024 * 2048, 6 << 20),
    )(place, heads, w)

def grads_kernel(place_ref, n_ref, inc_ref, act_ref, gh_ref, mine_ref, partner_ref, keep_ref, send_ref, up):
    def down(ref):
        ref[...] = dot(act_ref[...], inc_ref[...], (0, 0)).astype(BF)

    @pl.when(pl.program_id(0) < 2)
    def _():
        down(mine_ref)

    @pl.when(pl.program_id(0) >= 2)
    def _():
        down(partner_ref)

    up[...] = dot(n_ref[...], gh_ref[...], (0, 0)).astype(BF).reshape(2, 2, 2, 256, 256)
    keep_ref[...] = up[:, :, place_ref[0]]
    send_ref[...] = up[:, :, 1 - place_ref[0]]

def weight_grads(place, n, inc, act, gh):
    rows = pl.BlockSpec((1024, 2048), lambda j, p: (0, 0))
    cols = pl.BlockSpec((1024, 256), lambda j, p: (0, j))
    part = pl.BlockSpec((2, 2, 256, 256), lambda j, p: (0, 0, 0, j))
    return pl.pallas_call(
        grads_kernel,
        grid_spec=pltpu.PrefetchScalarGridSpec(
            num_scalar_prefetch=1, grid=(4,),
            in_specs=[rows, rows, cols, cols],
            out_specs=[
                pl.BlockSpec((256, 2048), lambda j, p: (jnp.minimum(j, 1), 0)),
                pl.BlockSpec((256, 2048), lambda j, p: (jnp.maximum(j - 2, 0), 0)),
                part, part,
            ],
            scratch_shapes=[pltpu.VMEM((2, 2, 2, 256, 256), BF)],
        ),
        out_shape=[jax.ShapeDtypeStruct((512, 2048), BF)] * 2 + [jax.ShapeDtypeStruct((2, 2, 256, 1024), BF)] * 2,
        compiler_params=params(),
        cost_estimate=short(4 * 1024 * 1024 * 2048, 20 << 20),
    )(place, n, inc, act, gh)

def stack_kernel(*refs):
    for i, ref in enumerate(refs[:-1]):
        refs[-1][i] = ref[...]

def stack(*arrays):
    return pl.pallas_call(
        stack_kernel,
        in_specs=[pl.BlockSpec(memory_space=pltpu.VMEM)] * len(arrays),
        out_specs=pl.BlockSpec(memory_space=pltpu.VMEM),
        out_shape=jax.ShapeDtypeStruct((len(arrays), *arrays[0].shape), arrays[0].dtype),
        compiler_params=params(),
    )(*arrays)

def out_kernel(place_ref, mine_ref, partner_ref, grad_ref, out_ref):
    grad = grad_ref[...]
    out_ref[0, place_ref[0]] = dot(mine_ref[...], grad, (0, 0)).astype(BF)
    out_ref[0, 1 - place_ref[0]] = dot(partner_ref[...], grad, (0, 0)).astype(BF)

def out_grads(place, mine, partner, grad):
    heads = pl.BlockSpec((1024, HD), lambda i, p: (0, 0))
    return pl.pallas_call(
        out_kernel,
        grid_spec=pltpu.PrefetchScalarGridSpec(
            num_scalar_prefetch=1, grid=(8,),
            in_specs=[heads, heads, pl.BlockSpec((1024, 256), lambda i, p: (0, i))],
            out_specs=pl.BlockSpec((1, 2, HD, 256), lambda i, p: (i, 0, 0, 0)),
        ),
        out_shape=jax.ShapeDtypeStruct((8, 2, HD, 256), BF),
        compiler_params=params(),
        cost_estimate=short(2 * 1024 * 256 * 2048, 6 << 20),
    )(place, mine, partner, grad)


def qkv_grads_kernel(n_ref, gp_ref, w_ref, out_ref, sums_ref, columns):
    @pl.when(pl.program_id(0) == 0)
    def _():
        columns[...] = jnp.sum(gp_ref[...].astype(F32), axis=0, keepdims=True)

    grad = dot(n_ref[...], gp_ref[...], (0, 0))
    out_ref[...] = grad.astype(BF)
    ones = jnp.ones((8, HD), F32)
    gain = jnp.zeros((8, 256), F32)
    shift = jnp.zeros((8, 256), F32)
    for c in range(3):
        cols = slice(c * HD, (c + 1) * HD)
        w = w_ref[c].astype(F32)
        total = lambda v: lax.dot_general(ones, v, (((1,), (1,)), ((), ())), precision=lax.Precision.HIGHEST, preferred_element_type=F32)
        gain += total(w * grad[:, cols])
        shift += total(w * columns[:, cols])
    sums_ref[0] = gain[0:1]
    sums_ref[1] = shift[0:1]

def qkv_grads(normed, gp, w):
    return pl.pallas_call(
        qkv_grads_kernel, grid=(8,),
        in_specs=[
            pl.BlockSpec((2048, 256), lambda i: (0, i)),
            pl.BlockSpec((2048, 384), lambda i: (0, 0)),
            pl.BlockSpec((3, 256, HD), lambda i: (0, i, 0)),
        ],
        out_specs=[pl.BlockSpec((256, 384), lambda i: (i, 0)), pl.BlockSpec((2, 1, 256), lambda i: (0, 0, i))],
        out_shape=[jax.ShapeDtypeStruct((2048, 384), BF), jax.ShapeDtypeStruct((2, 1, 2048), F32)],
        scratch_shapes=[pltpu.VMEM((1, 384), F32)],
        compiler_params=params(),
        cost_estimate=short(2 * 2048 * 2048 * 384, 12 << 20),
    )(normed, gp, w)


def scatter(values, axes):
    return lax.psum_scatter(values, axes, scatter_dimension=0, tiled=True).astype(F32)


def pick(values, index, axis):
    return lax.dynamic_index_in_dim(values, index, axis, False)


def after(values, *others):
    return lax.optimization_barrier((values, *others))[0]


def add(left, right):
    return (left.astype(F32) + right.astype(F32)).astype(BF)


def over_x(own, partner, x_hi, axis):
    size = own.shape[axis] // 2
    own = add(own, x_partner(partner))

    def part(at):
        return lax.dynamic_slice_in_dim(own, at * size, size, axis)

    return part(x_hi).astype(F32) + x_far(part(1 - x_hi)).astype(F32)


def exchange(values, axes):
    return jnp.sum(lax.all_to_all(values, axes, 0, 0).astype(F32), axis=0)


def sum_of_all(values):
    for axes, count in ((("z", "core"), 8), (("x_hi", "y", "x_lo"), 16)):
        values = exchange(jnp.broadcast_to(values[None], (count, *values.shape)), axes)
    return values


def body(
    tokens,
    ln1_gain,
    ln1_shift,
    qkv_weight,
    out_weight,
    ln2_gain,
    ln2_shift,
    up_weight,
    down_weight,
    lengths,
    cotangent,
):
    x_hi, y, x_lo, z, core = (lax.axis_index(axis) for axis in AXES)
    tensor = x_lo * 8 + z * 2 + core
    length = lengths[0]

    place = jnp.stack([core, z, x_lo, y % 2])

    out_own = lax.all_gather(out_weight, ("z", "core"), axis=0, tiled=True)
    live_rows = (tensor * 128 + jnp.arange(128, dtype=jnp.int32) < length).astype(F32)[:, None]
    incoming_rows = cotangent.astype(F32) * live_rows
    sent_rows = incoming_rows.astype(BF)
    along_z = [z_down(sent_rows), z_far(sent_rows), z_up(sent_rows)]
    up_partner, down_partner = x_partner(up_weight), x_partner(down_weight)

    normed_first, projected, weights = project(tokens, ln1_gain, ln1_shift, qkv_weight)
    attended, totals = attend(projected, lengths)
    heads = lax.all_to_all(attended, ("z", "core"), 0, 0)
    branch_mine, branch_other = branch(place[2:], after(heads, *along_z, up_partner), out_own)
    branch_other = after(x_pair(branch_other), down_partner)
    token_rows = lax.dynamic_slice_in_dim(tokens, tensor * 128, 128, 0).astype(F32)
    middle_rows = token_rows + (branch_mine + branch_other.astype(F32))
    unit_second, inverse_second = norm_stats(middle_rows)
    normed_rows = (unit_second * ln2_gain + ln2_shift).astype(BF)
    out_partner = x_partner(after(out_own, branch_other))
    along_z = stack(after(sent_rows, normed_rows), *along_z)
    from_core = core_swap(along_z)

    normed_second = lax.all_gather(normed_rows, ("z", "core"), axis=0, tiled=True)
    activated, grad_hidden, grad_normed_part, incoming = front(
        place,
        normed_second.reshape(4, 2, 128, 2048),
        along_z,
        from_core,
        up_weight,
        up_partner,
        down_weight,
        down_partner,
    )
    incoming = incoming.reshape(1024, 2048)
    grad_normed_second = scatter(grad_normed_part.reshape(1024, 2048), ("z", "core"))
    down_kept, down_sent, up_kept, up_sent = weight_grads(
        place[3:], normed_second, incoming, activated, after(grad_hidden, out_partner)
    )
    down_got, up_got = x_partner(down_sent), y_pair(up_sent)

    grad_middle = incoming_rows + norm_back(grad_normed_second, ln2_gain, unit_second, inverse_second)
    gain_second = jnp.sum(grad_normed_second * unit_second, axis=0)
    shift_second = jnp.sum(grad_normed_second, axis=0)
    grad_branch = grad_middle.astype(BF)
    branch_back = lax.all_gather(grad_branch, ("z", "core"), axis=0, tiled=True)

    branch_sent = after(grad_branch, down_got, up_got)
    by_head = jnp.stack(
        [dot(branch_sent, w, (1, 1)).astype(BF).reshape(128, 8, HD).transpose(1, 0, 2) for w in (out_own, out_partner)]
    )
    by_head = jnp.where(x_lo == 0, by_head, by_head[::-1]).reshape(16, 128, HD)
    grad_attended = lax.all_to_all(by_head, TENSOR, 0, 0).reshape(2048, HD)
    down_sums = add(down_kept, after(down_got, by_head)).reshape(512, 2, 1024)
    up_sums = add(up_kept, after(up_got, by_head))
    mixed_mine, mixed_other = mix(place, after(activated, by_head), down_weight, down_partner)
    partner_heads = x_pair(pick(attended, 1 - x_lo, 1).reshape(1024, HD))

    grad_projected = attend_back(projected, after(grad_attended, down_sums, up_sums, mixed_mine), totals, lengths)
    grad_first_part = dot(grad_projected, weights, (1, 1)).astype(BF)
    mixed = add(mixed_mine, after(core_swap(mixed_other), grad_first_part)).reshape(2, 2, 128, 2048)
    down_got = x_far(pick(down_sums, 1 - x_hi, 1))
    up_got = y_far(pick(up_sums, 1 - y // 2, 1))
    grad_normed_first = scatter(after(grad_first_part, down_got, up_got), TENSOR)

    down_sums = pick(down_sums, x_hi, 1).astype(F32) + after(down_got, grad_first_part).astype(F32)
    up_sums = add(pick(up_sums, y // 2, 1), after(up_got, grad_first_part)).reshape(512, 1024)
    grad_up = over_x(up_sums[:, :512], up_sums[:, 512:], x_hi, 0)
    grad_down = exchange(down_sums.astype(BF).reshape(512, 4, 256).transpose(1, 0, 2), "y")
    out_blocks = out_grads(
        x_lo[None], after(pick(attended, x_lo, 1).reshape(1024, HD), grad_first_part), partner_heads, branch_back
    )
    grad_out = exchange(out_blocks.reshape(16, HD, 256), ("x_hi", "y", "x_lo"))
    grad_qkv, first_sums = qkv_grads(normed_first, after(grad_projected, out_blocks), qkv_weight)
    shift_first = first_sums[1, 0]
    gain_first = (first_sums[0, 0] - ln1_shift * shift_first) / ln1_gain
    sums = sum_of_all(jnp.stack([gain_first, gain_second, shift_first, shift_second]))
    grad_qkv = exchange(grad_qkv.reshape(8, 256, 384), BATCH)
    grad_qkv = grad_qkv.reshape(256, 3, HD).transpose(1, 0, 2)
    mixed = add(pick(mixed, z % 2, 1), z_pair(pick(mixed, 1 - z % 2, 1)))
    output = (
        middle_rows + pick(mixed, z // 2, 0).astype(F32) + z_far(pick(mixed, 1 - z // 2, 0)).astype(F32)
    ).astype(BF)

    unit_rows, inverse_rows = norm_stats(token_rows)
    grad_tokens = (grad_middle + norm_back(grad_normed_first, ln1_gain, unit_rows, inverse_rows)).astype(BF)
    return (output, grad_tokens, grad_qkv, grad_out, grad_up, grad_down, sums[:2], sums[2:])


def solution(mesh):
    return jax.shard_map(
        body,
        mesh=Mesh(mesh.devices.reshape(2, 4, 2, 4, 2), AXES),
        in_specs=(
            P(BATCH, None),
            P(),
            P(),
            P(None, None, TENSOR),
            P(TENSOR, None),
            P(),
            P(),
            P(None, TENSOR),
            P(TENSOR, None),
            P(BATCH),
            P(AXES, None),
        ),
        out_specs=(
            P(AXES, None),
            P(AXES, None),
            P(None, BATCH, TENSOR),
            P(TENSOR, BATCH),
            P(BATCH, TENSOR),
            P(TENSOR, BATCH),
            P(),
            P(),
        ),
        check_vma=False,
    )
```

```python
import functools

import jax
import jax.numpy as jnp
from jax import lax
from jax.experimental import pallas as pl
from jax.experimental.pallas import tpu as pltpu
from jax.sharding import Mesh
from jax.sharding import PartitionSpec as P

HD = 128
EPS = 1e-05
MASKED_SCORE = -1e30
BF = jnp.bfloat16
F32 = jnp.float32

AXES = ("x_hi", "y", "x_lo", "z", "core")
BATCH, TENSOR = AXES[:2], AXES[2:]


def core_swap(values):
    return lax.ppermute(values, "core", [(0, 1), (1, 0)])


def x_pair(values):
    return lax.ppermute(values, "x_lo", [(0, 1), (1, 0)])


def x_partner(values):
    pairs = [(r * 2 + c, ((r + (1, -1)[c]) % 4) * 2 + c) for r in range(4) for c in range(2)]
    return lax.ppermute(values, ("x_hi", "x_lo", "core"), pairs)


def neighbours(axis):
    pairs = [(i * 2 + c, ((i ^ 1) if c == 0 else 3 - i) * 2 + c) for i in range(4) for c in range(2)]
    return lambda values: lax.ppermute(values, (axis, "core"), pairs)


y_pair, z_pair = neighbours("y"), neighbours("z")


def shift(axes, sizes, step):
    return lambda values: lax.ppermute(values, axes, [(i, (i + step) % sizes) for i in range(sizes)])


z_up, z_down, z_far = (shift("z", 4, step) for step in (1, -1, 2))
y_up, y_far = (shift("y", 4, step) for step in (1, 2))
x_up, x_far = (shift(("x_hi", "x_lo"), 4, step) for step in (1, 2))


def norm_stats(values):
    centre = jnp.mean(values, axis=-1, keepdims=True)
    offsets = values - centre
    variance = jnp.mean(offsets * offsets, axis=-1, keepdims=True)
    inverse = lax.rsqrt(variance + EPS)
    return (offsets * inverse, inverse)


def norm_back(grad_normed, gain, unit_rows, inverse):
    scaled = grad_normed * gain
    return inverse * (
        scaled
        - jnp.mean(scaled, axis=-1, keepdims=True)
        - unit_rows * jnp.mean(scaled * unit_rows, axis=-1, keepdims=True)
    )


def dot(left, right, dims):
    return lax.dot_general(left, right, ((dims[:1], dims[1:]), ((), ())), preferred_element_type=F32)


def short(flops, moved):
    return pl.CostEstimate(flops=flops // 64, bytes_accessed=moved // 64, transcendentals=0)


def add(left, right):
    return (left.astype(F32) + right.astype(F32)).astype(BF)


def params(limit=60, **kw):
    return pltpu.CompilerParams(vmem_limit_bytes=limit * 2**20, **kw)


def qkv_kernel(x_ref, gain_ref, shift_ref, w_ref, normed_ref, out_ref, weights):
    @pl.when(pl.program_id(0) == 0)
    def _():
        for c in range(3):
            weights[:, c * HD : (c + 1) * HD] = w_ref[c]

    x = x_ref[...].astype(F32)
    offsets = x - jnp.mean(x, axis=-1, keepdims=True)
    inverse = lax.rsqrt(jnp.mean(offsets * offsets, axis=-1, keepdims=True) + EPS)
    normed = (offsets * inverse * gain_ref[...] + shift_ref[...]).astype(BF)
    normed_ref[...] = normed
    out_ref[...] = dot(normed, weights[...], (1, 0)).astype(BF)

def project(tokens, gain, shift, weight):
    rows = 256
    return pl.pallas_call(
        qkv_kernel,
        grid=(2048 // rows,),
        in_specs=[
            pl.BlockSpec((rows, 2048), lambda i: (i, 0)),
            pl.BlockSpec((1, 2048), lambda i: (0, 0)),
            pl.BlockSpec((1, 2048), lambda i: (0, 0)),
            pl.BlockSpec((3, 2048, HD), lambda i: (0, 0, 0)),
        ],
        out_specs=[
            pl.BlockSpec((rows, 2048), lambda i: (i, 0)),
            pl.BlockSpec((rows, 3 * HD), lambda i: (i, 0)),
            pl.BlockSpec((2048, 3 * HD), lambda i: (0, 0)),
        ],
        out_shape=[jax.ShapeDtypeStruct((2048, 2048), BF)] + [jax.ShapeDtypeStruct((2048, 3 * HD), BF)] * 2,
        compiler_params=params(),
        cost_estimate=short(2 * 2048 * 2048 * 384, 20 << 20),
    )(tokens, gain[None], shift[None], weight)


QB = 512
SCALE = HD ** -0.5

def masked(scores, first_query, first_key, length):
    query = first_query + lax.broadcasted_iota(jnp.int32, scores.shape, 0)
    key = first_key + lax.broadcasted_iota(jnp.int32, scores.shape, 1)
    return jnp.where((key <= query) & (key < length), scores, MASKED_SCORE)

def forward_kernel(length_ref, qkv_ref, out_ref, total_ref):
    length = length_ref[0]
    for i in range(2048 // QB):
        q = qkv_ref[i * QB : (i + 1) * QB, :HD]
        parts = []
        for j in range(i + 1):
            k = qkv_ref[j * QB : (j + 1) * QB, HD : 2 * HD]
            parts.append(masked(dot(q, k, (1, 1)) * SCALE, i * QB, j * QB, length))
        peak = functools.reduce(jnp.maximum, [jnp.max(p, axis=-1, keepdims=True) for p in parts])
        total = jnp.zeros((QB, 1), F32)
        acc = jnp.zeros((QB, HD), F32)
        for j in range(i + 1):
            e = jnp.exp(parts[j] - peak)
            total += jnp.sum(e, axis=-1, keepdims=True)
            acc += dot(e.astype(BF), qkv_ref[j * QB : (j + 1) * QB, 2 * HD :], (1, 0))
        out = (acc / total).astype(BF)
        for b in range(QB // HD):
            block = i * (QB // HD) + b
            out_ref[block % 8, block // 8] = out[b * HD : (b + 1) * HD]
        total_ref[i * QB : (i + 1) * QB] = peak + jnp.log(total)

def attend(qkv, lengths):
    return pl.pallas_call(
        forward_kernel,
        in_specs=[pl.BlockSpec(memory_space=pltpu.SMEM), pl.BlockSpec(memory_space=pltpu.VMEM)],
        out_specs=[pl.BlockSpec(memory_space=pltpu.VMEM)] * 2,
        out_shape=[jax.ShapeDtypeStruct((8, 2, 128, HD), BF), jax.ShapeDtypeStruct((2048, 1), F32)],
        compiler_params=params(),
        cost_estimate=short(2 * 2 * 2048 * 2048 * 128, 3 << 20),
    )(lengths, qkv)

def backward_kernel(length_ref, qkv_ref, grad_ref, total_ref, out_ref, gk, gv, probs, gprobs):
    length = length_ref[0]
    n = 2048 // QB
    gk[...] = jnp.zeros_like(gk)
    gv[...] = jnp.zeros_like(gv)
    for i in range(n):
        rows = slice(i * QB, (i + 1) * QB)
        q = qkv_ref[rows, :HD]
        g = grad_ref[rows]
        total = total_ref[rows]
        centre = jnp.zeros((QB, 1), F32)
        for j in range(i + 1):
            keys = slice(j * QB, (j + 1) * QB)
            s = masked(dot(q, qkv_ref[keys, HD : 2 * HD], (1, 1)) * SCALE, i * QB, j * QB, length)
            p = jnp.exp(s - total)
            gp = dot(g, qkv_ref[keys, 2 * HD :], (1, 1))
            centre += jnp.sum(p * gp, axis=-1, keepdims=True)
            probs[:, keys] = p
            gprobs[:, keys] = gp
        gq = jnp.zeros((QB, HD), F32)
        for j in range(i + 1):
            keys = slice(j * QB, (j + 1) * QB)
            p = probs[:, keys]
            gs = (p * (gprobs[:, keys] - centre)).astype(BF)
            gq += dot(gs, qkv_ref[keys, HD : 2 * HD], (1, 0))
            gk[keys] += dot(gs, q, (0, 0))
            gv[keys] += dot(p.astype(BF), g, (0, 0))
        out_ref[rows, :HD] = (gq * SCALE).astype(BF)
    out_ref[:, HD : 2 * HD] = (gk[...] * SCALE).astype(BF)
    out_ref[:, 2 * HD :] = gv[...].astype(BF)

def attend_back(qkv, grad, totals, lengths):
    return pl.pallas_call(
        backward_kernel,
        in_specs=[pl.BlockSpec(memory_space=pltpu.SMEM)] + [pl.BlockSpec(memory_space=pltpu.VMEM)] * 3,
        out_specs=pl.BlockSpec(memory_space=pltpu.VMEM),
        out_shape=jax.ShapeDtypeStruct((2048, 3 * HD), BF),
        scratch_shapes=[pltpu.VMEM((2048, HD), F32), pltpu.VMEM((2048, HD), F32), pltpu.VMEM((QB, 2048), F32), pltpu.VMEM((QB, 2048), F32)],
        compiler_params=params(),
        cost_estimate=short(5 * 2 * 2048 * 1280 * 128, 4 << 20),
    )(lengths, qkv, grad, totals)


GELU_A = 0.7978845608028654
GELU_B = 0.044715

def front_kernel(place_ref, n_ref, mine_ref, other_ref, uo, up, do, dp, act_ref, gh_ref, part_ref, inc_ref):
    core = place_ref[0]
    inc_ref[0, core] = mine_ref[0]
    inc_ref[0, 1 - core] = other_ref[0]
    n = n_ref[0].reshape(256, 2048)
    inc = inc_ref[0].reshape(256, 2048)
    part = jnp.zeros((256, 2048), F32)
    for h, (u, d) in enumerate(((uo, do), (up, dp))):
        cols = slice(h * 512, (h + 1) * 512)
        hidden = dot(n, u[...], (1, 0))
        square = hidden * hidden
        t = jnp.tanh(GELU_A * (hidden + GELU_B * hidden * square))
        act_ref[:, cols] = (0.5 * hidden * (1 + t)).astype(BF)
        slope = 0.5 * (1 + t) + 0.5 * hidden * (1 - t * t) * (GELU_A * (1 + 3 * GELU_B * square))
        gh = (dot(inc, d[...], (1, 1)) * slope).astype(BF)
        gh_ref[:, cols] = gh
        part += dot(gh, u[...], (1, 1))
    part_ref[0] = part.astype(BF).reshape(2, 128, 2048)

def front(place, normed, mine, other, uo, up, do, dp):
    whole = lambda a: pl.BlockSpec(a.shape, lambda i, p: (0,) * a.ndim)
    blk = pl.BlockSpec((1, 2, 128, 2048), lambda i, p: (i, 0, 0, 0))
    one = pl.BlockSpec((1, 128, 2048), lambda i, p: ((i + 4 - p[1]) % 4, 0, 0))
    col = pl.BlockSpec((256, 1024), lambda i, p: (i, 0))
    return pl.pallas_call(
        front_kernel,
        grid_spec=pltpu.PrefetchScalarGridSpec(
            num_scalar_prefetch=1, grid=(4,),
            in_specs=[blk, one, one, whole(uo), whole(up), whole(do), whole(dp)],
            out_specs=[col, col, blk, blk],
        ),
        out_shape=[jax.ShapeDtypeStruct((1024, 1024), BF)] * 2 + [jax.ShapeDtypeStruct((4, 2, 128, 2048), BF)] * 2,
        compiler_params=params(),
        cost_estimate=short(6 * 1024 * 1024 * 2048, 28 << 20),
    )(place, normed, mine, other, uo, up, do, dp)


def mixed_kernel(place_ref, act_ref, do, dp, mine_ref, other_ref, rows):
    a = act_ref[...]
    rows[...] = (dot(a[:, :512], do[...], (1, 0)) + dot(a[:, 512:], dp[...], (1, 0))).astype(BF).reshape(2, 128, 2048)
    mine_ref[0] = rows[place_ref[0]]
    other_ref[0] = rows[1 - place_ref[0]]

def mix(place, act, do, dp):
    whole = lambda a: pl.BlockSpec(a.shape, lambda i, p: (0,) * a.ndim)
    return pl.pallas_call(
        mixed_kernel,
        grid_spec=pltpu.PrefetchScalarGridSpec(
            num_scalar_prefetch=1, grid=(4,),
            in_specs=[pl.BlockSpec((256, 1024), lambda i, p: (i, 0)), whole(do), whole(dp)],
            out_specs=[pl.BlockSpec((1, 128, 2048), lambda i, p: (i, 0, 0))] * 2,
            scratch_shapes=[pltpu.VMEM((2, 128, 2048), BF)],
        ),
        out_shape=[jax.ShapeDtypeStruct((4, 128, 2048), BF)] * 2,
        compiler_params=params(),
        cost_estimate=short(2 * 1024 * 1024 * 2048, 10 << 20),
    )(place, act, do, dp)

def branch_kernel(place_ref, heads_ref, w_ref, mine_ref, other_ref, left, out):
    @pl.when(pl.program_id(0) == 0)
    def _():
        for h in range(8):
            left[:, h * HD : (h + 1) * HD] = heads_ref[h].reshape(256, HD)

    out[...] = dot(left[...], w_ref[...], (1, 0)).reshape(2, 128, 512)
    mine_ref[...] = out[place_ref[0]]
    other_ref[...] = out[1 - place_ref[0]].astype(BF)

def branch(place, heads, w):
    col = pl.BlockSpec((128, 512), lambda i, p: (0, i))
    return pl.pallas_call(
        branch_kernel,
        grid_spec=pltpu.PrefetchScalarGridSpec(
            num_scalar_prefetch=1, grid=(4,),
            in_specs=[pl.BlockSpec((8, 2, 128, HD), lambda i, p: (0, 0, 0, 0)), pl.BlockSpec((1024, 512), lambda i, p: (0, i))],
            out_specs=[col, col],
            scratch_shapes=[pltpu.VMEM((256, 1024), BF), pltpu.VMEM((2, 128, 512), F32)],
        ),
        out_shape=[jax.ShapeDtypeStruct((128, 2048), F32), jax.ShapeDtypeStruct((128, 2048), BF)],
        compiler_params=params(),
        cost_estimate=short(2 * 256 * 1024 * 2048, 6 << 20),
    )(place, heads, w)

def grads_kernel(place_ref, n_ref, inc_ref, act_ref, gh_ref, mine_ref, partner_ref, keep_ref, send_ref, up):
    def down(ref):
        ref[...] = dot(act_ref[...], inc_ref[...], (0, 0)).astype(BF)

    @pl.when(pl.program_id(0) < 2)
    def _():
        down(mine_ref)

    @pl.when(pl.program_id(0) >= 2)
    def _():
        down(partner_ref)

    up[...] = dot(n_ref[...], gh_ref[...], (0, 0)).astype(BF).reshape(2, 2, 2, 256, 256)
    keep_ref[...] = up[:, :, place_ref[0]]
    send_ref[...] = up[:, :, 1 - place_ref[0]]

def weight_grads(place, n, inc, act, gh):
    rows = pl.BlockSpec((1024, 2048), lambda j, p: (0, 0))
    cols = pl.BlockSpec((1024, 256), lambda j, p: (0, j))
    part = pl.BlockSpec((2, 2, 256, 256), lambda j, p: (0, 0, 0, j))
    return pl.pallas_call(
        grads_kernel,
        grid_spec=pltpu.PrefetchScalarGridSpec(
            num_scalar_prefetch=1, grid=(4,),
            in_specs=[rows, rows, cols, cols],
            out_specs=[
                pl.BlockSpec((256, 2048), lambda j, p: (jnp.minimum(j, 1), 0)),
                pl.BlockSpec((256, 2048), lambda j, p: (jnp.maximum(j - 2, 0), 0)),
                part, part,
            ],
            scratch_shapes=[pltpu.VMEM((2, 2, 2, 256, 256), BF)],
        ),
        out_shape=[jax.ShapeDtypeStruct((512, 2048), BF)] * 2 + [jax.ShapeDtypeStruct((2, 2, 256, 1024), BF)] * 2,
        compiler_params=params(),
        cost_estimate=short(4 * 1024 * 1024 * 2048, 20 << 20),
    )(place, n, inc, act, gh)

def cut_kernel(place_ref, down_ref, down_got_ref, up_ref, up_got_ref, down_keep, down_send, up_keep, up_send, up):
    down = add(down_ref[...], down_got_ref[...])

    @pl.when(place_ref[0] == 0)
    def _():
        down_keep[...] = down[:, :1024]
        down_send[...] = down[:, 1024:]

    @pl.when(place_ref[0] == 1)
    def _():
        down_keep[...] = down[:, 1024:]
        down_send[...] = down[:, :1024]

    up[...] = add(up_ref[...], up_got_ref[...])
    up_keep[...] = up[:, place_ref[1]]
    up_send[...] = up[:, 1 - place_ref[1]]

def cut(place, down, down_got, up, up_got):
    wide = pl.BlockSpec((128, 2048), lambda i, p: (i, 0))
    half = pl.BlockSpec((128, 1024), lambda i, p: (i, 0))
    four = pl.BlockSpec((2, 2, 64, 1024), lambda i, p: (0, 0, i, 0))
    two = pl.BlockSpec((2, 64, 1024), lambda i, p: (0, i, 0))
    return pl.pallas_call(
        cut_kernel,
        grid_spec=pltpu.PrefetchScalarGridSpec(
            num_scalar_prefetch=1, grid=(4,),
            in_specs=[wide, wide, four, four],
            out_specs=[half, half, two, two],
            scratch_shapes=[pltpu.VMEM((2, 2, 64, 1024), BF)],
        ),
        out_shape=[jax.ShapeDtypeStruct((512, 1024), BF)] * 2 + [jax.ShapeDtypeStruct((2, 256, 1024), BF)] * 2,
        compiler_params=params(),
    )(place, down, down_got, up, up_got)


def heads_kernel(place_ref, grad_ref, own_ref, partner_ref, last_ref, out_ref):
    step_at = pl.program_id(0)

    def step(w_ref):
        part = dot(grad_ref[...], w_ref[...], (1, 1)).astype(BF)
        out_ref[0, 0] = part[:, :HD]
        out_ref[0, 1] = part[:, HD:]

    @pl.when(step_at < 4)
    def _():
        step(own_ref)

    @pl.when((step_at >= 4) & (step_at < 7))
    def _():
        step(partner_ref)

    @pl.when(step_at == 7)
    def _():
        step(last_ref)

def to_heads(place, grad, own, partner, last):
    return pl.pallas_call(
        heads_kernel,
        grid_spec=pltpu.PrefetchScalarGridSpec(
            num_scalar_prefetch=1, grid=(8,),
            in_specs=[
                pl.BlockSpec((128, 2048), lambda i, p: (0, 0)),
                pl.BlockSpec((256, 2048), lambda i, p: (jnp.minimum(i, 3), 0)),
                pl.BlockSpec((256, 2048), lambda i, p: (jnp.clip(i - 4, 0, 2), 0)),
                pl.BlockSpec((256, 2048), lambda i, p: (0, 0)),
            ],
            out_specs=pl.BlockSpec((1, 2, 128, HD), lambda i, p: ((p[0] + i // 4) % 2, i % 4, 0, 0)),
        ),
        out_shape=jax.ShapeDtypeStruct((2, 8, 128, HD), BF),
        compiler_params=params(),
    )(place, grad, own, partner, last)


def stack_kernel(*refs):
    for i, ref in enumerate(refs[:-1]):
        refs[-1][i] = ref[...]

def stack(*arrays):
    return pl.pallas_call(
        stack_kernel,
        in_specs=[pl.BlockSpec(memory_space=pltpu.VMEM)] * len(arrays),
        out_specs=pl.BlockSpec(memory_space=pltpu.VMEM),
        out_shape=jax.ShapeDtypeStruct((len(arrays), *arrays[0].shape), arrays[0].dtype),
        compiler_params=params(),
    )(*arrays)

def out_kernel(place_ref, mine_ref, partner_ref, grad_ref, out_ref):
    grad = grad_ref[...]
    out_ref[0, place_ref[0]] = dot(mine_ref[...], grad, (0, 0)).astype(BF)
    out_ref[0, 1 - place_ref[0]] = dot(partner_ref[...], grad, (0, 0)).astype(BF)

def out_grads(place, mine, partner, grad):
    heads = pl.BlockSpec((1024, HD), lambda i, p: (0, 0))
    return pl.pallas_call(
        out_kernel,
        grid_spec=pltpu.PrefetchScalarGridSpec(
            num_scalar_prefetch=1, grid=(8,),
            in_specs=[heads, heads, pl.BlockSpec((1024, 256), lambda i, p: (0, i))],
            out_specs=pl.BlockSpec((1, 2, HD, 256), lambda i, p: (i, 0, 0, 0)),
        ),
        out_shape=jax.ShapeDtypeStruct((8, 2, HD, 256), BF),
        compiler_params=params(),
        cost_estimate=short(2 * 1024 * 256 * 2048, 6 << 20),
    )(place, mine, partner, grad)


def qkv_grads_kernel(n_ref, gp_ref, w_ref, out_ref, sums_ref, columns):
    @pl.when(pl.program_id(0) == 0)
    def _():
        columns[...] = jnp.sum(gp_ref[...].astype(F32), axis=0, keepdims=True)

    grad = dot(n_ref[...], gp_ref[...], (0, 0))
    out_ref[...] = grad.astype(BF)
    ones = jnp.ones((8, HD), F32)
    gain = jnp.zeros((8, 256), F32)
    shift = jnp.zeros((8, 256), F32)
    for c in range(3):
        cols = slice(c * HD, (c + 1) * HD)
        w = w_ref[c].astype(F32)
        total = lambda v: lax.dot_general(ones, v, (((1,), (1,)), ((), ())), precision=lax.Precision.HIGHEST, preferred_element_type=F32)
        gain += total(w * grad[:, cols])
        shift += total(w * columns[:, cols])
    sums_ref[0] = gain[0:1]
    sums_ref[1] = shift[0:1]

def qkv_grads(normed, gp, w):
    return pl.pallas_call(
        qkv_grads_kernel, grid=(8,),
        in_specs=[
            pl.BlockSpec((2048, 256), lambda i: (0, i)),
            pl.BlockSpec((2048, 384), lambda i: (0, 0)),
            pl.BlockSpec((3, 256, HD), lambda i: (0, i, 0)),
        ],
        out_specs=[pl.BlockSpec((256, 384), lambda i: (i, 0)), pl.BlockSpec((2, 1, 256), lambda i: (0, 0, i))],
        out_shape=[jax.ShapeDtypeStruct((2048, 384), BF), jax.ShapeDtypeStruct((2, 1, 2048), F32)],
        scratch_shapes=[pltpu.VMEM((1, 384), F32)],
        compiler_params=params(),
        cost_estimate=short(2 * 2048 * 2048 * 384, 12 << 20),
    )(normed, gp, w)


def scatter(values, axes):
    return lax.psum_scatter(values, axes, scatter_dimension=0, tiled=True).astype(F32)


def pick(values, index, axis):
    return lax.dynamic_index_in_dim(values, index, axis, False)


def after(values, *others):
    return lax.optimization_barrier((values, *others))[0]


def over_x(own, partner, x_hi, axis):
    size = own.shape[axis] // 2
    own = add(own, x_partner(partner))

    def part(at):
        return lax.dynamic_slice_in_dim(own, at * size, size, axis)

    return part(x_hi).astype(F32) + x_far(part(1 - x_hi)).astype(F32)


def exchange(values, axes):
    return jnp.sum(lax.all_to_all(values, axes, 0, 0).astype(F32), axis=0)


def sum_of_all(values):
    for axes, count in ((("z", "core"), 8), (("x_hi", "y", "x_lo"), 16)):
        values = exchange(jnp.broadcast_to(values[None], (count, *values.shape)), axes)
    return values


def body(
    tokens,
    ln1_gain,
    ln1_shift,
    qkv_weight,
    out_weight,
    ln2_gain,
    ln2_shift,
    up_weight,
    down_weight,
    lengths,
    cotangent,
):
    x_hi, y, x_lo, z, core = (lax.axis_index(axis) for axis in AXES)
    tensor = x_lo * 8 + z * 2 + core
    length = lengths[0]

    place = jnp.stack([core, z, x_lo, y % 2])

    out_own = lax.all_gather(out_weight, ("z", "core"), axis=0, tiled=True)
    live_rows = (tensor * 128 + jnp.arange(128, dtype=jnp.int32) < length).astype(F32)[:, None]
    incoming_rows = cotangent.astype(F32) * live_rows
    sent_rows = incoming_rows.astype(BF)
    later_rows = after(sent_rows, out_own)
    along_z = [z_down(later_rows), z_far(sent_rows), z_up(later_rows)]
    up_partner, down_partner = x_partner(up_weight), x_partner(down_weight)

    normed_first, projected, weights = project(tokens, ln1_gain, ln1_shift, qkv_weight)
    attended, totals = attend(projected, lengths)
    heads = lax.all_to_all(attended, ("z", "core"), 0, 0)
    branch_mine, branch_other = branch(place[2:], after(heads, up_partner, along_z[1]), out_own)
    branch_other = after(x_pair(branch_other), down_partner, along_z[0], along_z[2])
    token_rows = lax.dynamic_slice_in_dim(tokens, tensor * 128, 128, 0).astype(F32)
    middle_rows = token_rows + (branch_mine + branch_other.astype(F32))
    unit_second, inverse_second = norm_stats(middle_rows)
    normed_rows = (unit_second * ln2_gain + ln2_shift).astype(BF)
    out_later = after(out_own, branch_other)
    out_partner = [x_partner(out_later[:768]), x_partner(out_later[768:])]
    along_z = stack(after(sent_rows, normed_rows), *along_z)
    from_core = core_swap(along_z)

    normed_second = lax.all_gather(normed_rows, ("z", "core"), axis=0, tiled=True)
    activated, grad_hidden, grad_normed_part, incoming = front(
        place,
        after(normed_second, out_partner[0]).reshape(4, 2, 128, 2048),
        along_z,
        from_core,
        up_weight,
        up_partner,
        down_weight,
        down_partner,
    )
    incoming = incoming.reshape(1024, 2048)
    grad_normed_second = scatter(grad_normed_part.reshape(1024, 2048), ("z", "core"))
    down_kept, down_sent, up_kept, up_sent = weight_grads(
        place[3:], normed_second, incoming, activated, grad_hidden
    )
    down_got, up_got = x_partner(down_sent), y_pair(up_sent)
    grad_normed_second = after(grad_normed_second, down_got, up_got, out_partner[1])

    grad_middle = incoming_rows + norm_back(grad_normed_second, ln2_gain, unit_second, inverse_second)
    gain_second = jnp.sum(grad_normed_second * unit_second, axis=0)
    shift_second = jnp.sum(grad_normed_second, axis=0)
    grad_branch = grad_middle.astype(BF)
    branch_back = lax.all_gather(grad_branch, ("z", "core"), axis=0, tiled=True)

    by_head = to_heads(x_lo[None], grad_branch, out_own, *out_partner).reshape(16, 128, HD)
    grad_attended = lax.all_to_all(by_head, TENSOR, 0, 0).reshape(2048, HD)
    down_kept, down_sent, up_kept, up_sent = cut(
        jnp.stack([x_hi, y // 2]), down_kept, after(down_got, by_head), up_kept, up_got
    )
    down_got, up_got = x_far(down_sent), y_far(up_sent)
    mixed_mine, mixed_other = mix(place, after(activated, by_head), down_weight, down_partner)
    partner_heads = x_pair(pick(attended, 1 - x_lo, 1).reshape(1024, HD))

    grad_projected = attend_back(projected, after(grad_attended, down_sent, mixed_mine), totals, lengths)
    grad_first_part = dot(grad_projected, weights, (1, 1)).astype(BF)
    grad_normed_first = scatter(after(grad_first_part, down_got, up_got), TENSOR)

    down_sums = add(down_kept, after(down_got, grad_first_part))
    grad_down = exchange(down_sums.reshape(512, 4, 256).transpose(1, 0, 2), "y")
    out_blocks = out_grads(
        x_lo[None], after(pick(attended, x_lo, 1).reshape(1024, HD), down_sums), partner_heads, branch_back
    )
    grad_out = exchange(out_blocks.reshape(16, HD, 256), ("x_hi", "y", "x_lo"))
    grad_qkv, first_sums = qkv_grads(normed_first, after(grad_projected, out_blocks, grad_down), qkv_weight)
    shift_first = first_sums[1, 0]
    gain_first = (first_sums[0, 0] - ln1_shift * shift_first) / ln1_gain
    grad_qkv = exchange(after(grad_qkv, grad_out).reshape(8, 256, 384), BATCH)
    sums = jnp.stack([gain_first, gain_second, shift_first, shift_second])
    sums = sum_of_all(after(sums, grad_qkv))
    grad_qkv = grad_qkv.reshape(256, 3, HD).transpose(1, 0, 2)

    up_sums = add(up_kept, after(up_got, grad_first_part)).reshape(512, 1024)
    grad_up = over_x(up_sums[:, :512], up_sums[:, 512:], x_hi, 0)
    mixed = add(mixed_mine, after(core_swap(mixed_other), grad_first_part)).reshape(2, 2, 128, 2048)
    mixed = add(pick(mixed, z % 2, 1), z_pair(pick(mixed, 1 - z % 2, 1)))
    output = (
        middle_rows + pick(mixed, z // 2, 0).astype(F32) + z_far(pick(mixed, 1 - z // 2, 0)).astype(F32)
    ).astype(BF)

    unit_rows, inverse_rows = norm_stats(token_rows)
    grad_tokens = (grad_middle + norm_back(grad_normed_first, ln1_gain, unit_rows, inverse_rows)).astype(BF)
    return (output, grad_tokens, grad_qkv, grad_out, grad_up, grad_down, sums[:2], sums[2:])


def solution(mesh):
    return jax.shard_map(
        body,
        mesh=Mesh(mesh.devices.reshape(2, 4, 2, 4, 2), AXES),
        in_specs=(
            P(BATCH, None),
            P(),
            P(),
            P(None, None, TENSOR),
            P(TENSOR, None),
            P(),
            P(),
            P(None, TENSOR),
            P(TENSOR, None),
            P(BATCH),
            P(AXES, None),
        ),
        out_specs=(
            P(AXES, None),
            P(AXES, None),
            P(None, BATCH, TENSOR),
            P(TENSOR, BATCH),
            P(BATCH, TENSOR),
            P(TENSOR, BATCH),
            P(),
            P(),
        ),
        check_vma=False,
    )
```

```python
import functools

import jax
import jax.numpy as jnp
from jax import lax
from jax.experimental import pallas as pl
from jax.experimental.pallas import tpu as pltpu
from jax.sharding import Mesh
from jax.sharding import PartitionSpec as P

HD = 128
EPS = 1e-05
MASKED_SCORE = -1e30
BF = jnp.bfloat16
F32 = jnp.float32

AXES = ("x_hi", "y", "x_lo", "z", "core")
BATCH, TENSOR = AXES[:2], AXES[2:]


def core_swap(values):
    return lax.ppermute(values, "core", [(0, 1), (1, 0)])


def x_pair(values):
    return lax.ppermute(values, "x_lo", [(0, 1), (1, 0)])


def x_partner(values):
    pairs = [(r * 2 + c, ((r + (1, -1)[c]) % 4) * 2 + c) for r in range(4) for c in range(2)]
    return lax.ppermute(values, ("x_hi", "x_lo", "core"), pairs)


def neighbours(axis):
    pairs = [(i * 2 + c, ((i ^ 1) if c == 0 else 3 - i) * 2 + c) for i in range(4) for c in range(2)]
    return lambda values: lax.ppermute(values, (axis, "core"), pairs)


y_pair, z_pair = neighbours("y"), neighbours("z")


def shift(axes, sizes, step):
    return lambda values: lax.ppermute(values, axes, [(i, (i + step) % sizes) for i in range(sizes)])


z_up, z_down, z_far = (shift("z", 4, step) for step in (1, -1, 2))
y_up, y_far = (shift("y", 4, step) for step in (1, 2))
x_up, x_far = (shift(("x_hi", "x_lo"), 4, step) for step in (1, 2))


def norm_stats(values):
    centre = jnp.mean(values, axis=-1, keepdims=True)
    offsets = values - centre
    variance = jnp.mean(offsets * offsets, axis=-1, keepdims=True)
    inverse = lax.rsqrt(variance + EPS)
    return (offsets * inverse, inverse)


def norm_back(grad_normed, gain, unit_rows, inverse):
    scaled = grad_normed * gain
    return inverse * (
        scaled
        - jnp.mean(scaled, axis=-1, keepdims=True)
        - unit_rows * jnp.mean(scaled * unit_rows, axis=-1, keepdims=True)
    )


def dot(left, right, dims):
    return lax.dot_general(left, right, ((dims[:1], dims[1:]), ((), ())), preferred_element_type=F32)


def short(flops, moved, by=64):
    return pl.CostEstimate(flops=flops // by, bytes_accessed=moved // by, transcendentals=0)


def add(left, right):
    return (left.astype(F32) + right.astype(F32)).astype(BF)


def params(limit=60, **kw):
    return pltpu.CompilerParams(vmem_limit_bytes=limit * 2**20, **kw)


def qkv_kernel(x_ref, gain_ref, shift_ref, w_ref, normed_ref, out_ref, weights):
    @pl.when(pl.program_id(0) == 0)
    def _():
        for c in range(3):
            weights[:, c * HD : (c + 1) * HD] = w_ref[c]

    x = x_ref[...].astype(F32)
    offsets = x - jnp.mean(x, axis=-1, keepdims=True)
    inverse = lax.rsqrt(jnp.mean(offsets * offsets, axis=-1, keepdims=True) + EPS)
    normed = (offsets * inverse * gain_ref[...] + shift_ref[...]).astype(BF)
    normed_ref[...] = normed
    out_ref[...] = dot(normed, weights[...], (1, 0)).astype(BF)

def project(tokens, gain, shift, weight):
    rows = 256
    return pl.pallas_call(
        qkv_kernel,
        grid=(2048 // rows,),
        in_specs=[
            pl.BlockSpec((rows, 2048), lambda i: (i, 0)),
            pl.BlockSpec((1, 2048), lambda i: (0, 0)),
            pl.BlockSpec((1, 2048), lambda i: (0, 0)),
            pl.BlockSpec((3, 2048, HD), lambda i: (0, 0, 0)),
        ],
        out_specs=[
            pl.BlockSpec((rows, 2048), lambda i: (i, 0)),
            pl.BlockSpec((rows, 3 * HD), lambda i: (i, 0)),
        ],
        out_shape=[jax.ShapeDtypeStruct((2048, 2048), BF), jax.ShapeDtypeStruct((2048, 3 * HD), BF)],
        scratch_shapes=[pltpu.VMEM((2048, 3 * HD), BF)],
        compiler_params=params(),
        cost_estimate=short(2 * 2048 * 2048 * 384, 20 << 20),
    )(tokens, gain[None], shift[None], weight)


QB = 512
SCALE = HD ** -0.5

def masked(scores, first_query, first_key, length):
    query = first_query + lax.broadcasted_iota(jnp.int32, scores.shape, 0)
    key = first_key + lax.broadcasted_iota(jnp.int32, scores.shape, 1)
    return jnp.where((key <= query) & (key < length), scores, MASKED_SCORE)

def forward_kernel(length_ref, qkv_ref, out_ref, total_ref):
    length = length_ref[0]
    for i in range(2048 // QB):
        q = qkv_ref[i * QB : (i + 1) * QB, :HD]
        parts = []
        for j in range(i + 1):
            k = qkv_ref[j * QB : (j + 1) * QB, HD : 2 * HD]
            parts.append(masked(dot(q, k, (1, 1)) * SCALE, i * QB, j * QB, length))
        peak = functools.reduce(jnp.maximum, [jnp.max(p, axis=-1, keepdims=True) for p in parts])
        total = jnp.zeros((QB, 1), F32)
        acc = jnp.zeros((QB, HD), F32)
        for j in range(i + 1):
            e = jnp.exp(parts[j] - peak)
            total += jnp.sum(e, axis=-1, keepdims=True)
            acc += dot(e.astype(BF), qkv_ref[j * QB : (j + 1) * QB, 2 * HD :], (1, 0))
        out = (acc / total).astype(BF)
        for b in range(QB // HD):
            block = i * (QB // HD) + b
            out_ref[block % 8, block // 8] = out[b * HD : (b + 1) * HD]
        total_ref[i * QB : (i + 1) * QB] = peak + jnp.log(total)

def attend(qkv, lengths):
    return pl.pallas_call(
        forward_kernel,
        in_specs=[pl.BlockSpec(memory_space=pltpu.SMEM), pl.BlockSpec(memory_space=pltpu.VMEM)],
        out_specs=[pl.BlockSpec(memory_space=pltpu.VMEM)] * 2,
        out_shape=[jax.ShapeDtypeStruct((8, 2, 128, HD), BF), jax.ShapeDtypeStruct((2048, 1), F32)],
        compiler_params=params(),
        cost_estimate=short(2 * 2 * 2048 * 2048 * 128, 3 << 20),
    )(lengths, qkv)

def backward_kernel(length_ref, qkv_ref, grad_ref, total_ref, out_ref, sent_ref, gk, gv, probs, gprobs):
    length = length_ref[0]
    n = 2048 // QB
    gk[...] = jnp.zeros_like(gk)
    gv[...] = jnp.zeros_like(gv)
    for i in range(n):
        rows = slice(i * QB, (i + 1) * QB)
        q = qkv_ref[rows, :HD]
        blocks = [i * (QB // HD) + b for b in range(QB // HD)]
        g = jnp.concatenate([grad_ref[b % 8, b // 8] for b in blocks], axis=0)
        total = total_ref[rows]
        centre = jnp.zeros((QB, 1), F32)
        for j in range(i + 1):
            keys = slice(j * QB, (j + 1) * QB)
            s = masked(dot(q, qkv_ref[keys, HD : 2 * HD], (1, 1)) * SCALE, i * QB, j * QB, length)
            p = jnp.exp(s - total)
            gp = dot(g, qkv_ref[keys, 2 * HD :], (1, 1))
            centre += jnp.sum(p * gp, axis=-1, keepdims=True)
            probs[:, keys] = p
            gprobs[:, keys] = gp
        gq = jnp.zeros((QB, HD), F32)
        for j in range(i + 1):
            keys = slice(j * QB, (j + 1) * QB)
            p = probs[:, keys]
            gs = (p * (gprobs[:, keys] - centre)).astype(BF)
            gq += dot(gs, qkv_ref[keys, HD : 2 * HD], (1, 0))
            gk[keys] += dot(gs, q, (0, 0))
            gv[keys] += dot(p.astype(BF), g, (0, 0))
        out_ref[rows, :HD] = (gq * SCALE).astype(BF)
    out_ref[:, HD : 2 * HD] = (gk[...] * SCALE).astype(BF)
    out_ref[:, 2 * HD :] = gv[...].astype(BF)

    @pl.when(length_ref[1] == 0)
    def _():
        sent_ref[...] = out_ref[1024:]

    @pl.when(length_ref[1] == 1)
    def _():
        sent_ref[...] = out_ref[:1024]

def attend_back(qkv, grad, totals, lengths):
    return pl.pallas_call(
        backward_kernel,
        in_specs=[pl.BlockSpec(memory_space=pltpu.SMEM)] + [pl.BlockSpec(memory_space=pltpu.VMEM)] * 3,
        out_specs=[pl.BlockSpec(memory_space=pltpu.VMEM)] * 2,
        out_shape=[jax.ShapeDtypeStruct((2048, 3 * HD), BF), jax.ShapeDtypeStruct((1024, 3 * HD), BF)],
        scratch_shapes=[pltpu.VMEM((2048, HD), F32), pltpu.VMEM((2048, HD), F32), pltpu.VMEM((QB, 2048), F32), pltpu.VMEM((QB, 2048), F32)],
        compiler_params=params(),
        cost_estimate=short(5 * 2 * 2048 * 1280 * 128, 4 << 20),
    )(lengths, qkv, grad, totals)


GELU_A = 0.7978845608028654
GELU_B = 0.044715

def front_kernel(place_ref, n_ref, mine_ref, other_ref, uo, up, do, dp, act_ref, gh_ref, part_ref, inc_ref):
    core = place_ref[0]
    inc_ref[0, core] = mine_ref[0]
    inc_ref[0, 1 - core] = other_ref[0]
    n = n_ref[0].reshape(256, 2048)
    inc = inc_ref[0].reshape(256, 2048)
    part = jnp.zeros((256, 2048), F32)
    for h, (u, d) in enumerate(((uo, do), (up, dp))):
        cols = slice(h * 512, (h + 1) * 512)
        hidden = dot(n, u[...], (1, 0))
        square = hidden * hidden
        t = jnp.tanh(GELU_A * (hidden + GELU_B * hidden * square))
        act_ref[:, cols] = (0.5 * hidden * (1 + t)).astype(BF)
        slope = 0.5 * (1 + t) + 0.5 * hidden * (1 - t * t) * (GELU_A * (1 + 3 * GELU_B * square))
        gh = (dot(inc, d[...], (1, 1)) * slope).astype(BF)
        gh_ref[:, cols] = gh
        part += dot(gh, u[...], (1, 1))
    part_ref[0] = part.astype(BF).reshape(2, 128, 2048)

def front(place, normed, mine, other, uo, up, do, dp):
    whole = lambda a: pl.BlockSpec(a.shape, lambda i, p: (0,) * a.ndim)
    blk = pl.BlockSpec((1, 2, 128, 2048), lambda i, p: (i, 0, 0, 0))
    one = pl.BlockSpec((1, 128, 2048), lambda i, p: ((i + 4 - p[1]) % 4, 0, 0))
    col = pl.BlockSpec((256, 1024), lambda i, p: (i, 0))
    return pl.pallas_call(
        front_kernel,
        grid_spec=pltpu.PrefetchScalarGridSpec(
            num_scalar_prefetch=1, grid=(4,),
            in_specs=[blk, one, one, whole(uo), whole(up), whole(do), whole(dp)],
            out_specs=[col, col, blk, blk],
        ),
        out_shape=[jax.ShapeDtypeStruct((1024, 1024), BF)] * 2 + [jax.ShapeDtypeStruct((4, 2, 128, 2048), BF)] * 2,
        compiler_params=params(),
        cost_estimate=short(6 * 1024 * 1024 * 2048, 28 << 20),
    )(place, normed, mine, other, uo, up, do, dp)


def mixed_kernel(place_ref, act_ref, do, dp, mine_ref, other_ref, rows):
    a = act_ref[...]
    rows[...] = (dot(a[:, :512], do[...], (1, 0)) + dot(a[:, 512:], dp[...], (1, 0))).astype(BF).reshape(2, 128, 2048)
    mine_ref[0] = rows[place_ref[0]]
    other_ref[0] = rows[1 - place_ref[0]]

def mix(place, act, do, dp):
    whole = lambda a: pl.BlockSpec(a.shape, lambda i, p: (0,) * a.ndim)
    return pl.pallas_call(
        mixed_kernel,
        grid_spec=pltpu.PrefetchScalarGridSpec(
            num_scalar_prefetch=1, grid=(4,),
            in_specs=[pl.BlockSpec((256, 1024), lambda i, p: (i, 0)), whole(do), whole(dp)],
            out_specs=[pl.BlockSpec((1, 128, 2048), lambda i, p: (i, 0, 0))] * 2,
            scratch_shapes=[pltpu.VMEM((2, 128, 2048), BF)],
        ),
        out_shape=[jax.ShapeDtypeStruct((4, 128, 2048), BF)] * 2,
        compiler_params=params(),
        cost_estimate=short(2 * 1024 * 1024 * 2048, 10 << 20),
    )(place, act, do, dp)

def branch_kernel(place_ref, heads_ref, w_ref, mine_ref, other_ref, left, out):
    @pl.when(pl.program_id(0) == 0)
    def _():
        for h in range(8):
            left[:, h * HD : (h + 1) * HD] = heads_ref[h].reshape(256, HD)

    out[...] = dot(left[...], w_ref[...], (1, 0)).reshape(2, 128, 512)
    mine_ref[...] = out[place_ref[0]]
    other_ref[...] = out[1 - place_ref[0]].astype(BF)

def branch(place, heads, w):
    col = pl.BlockSpec((128, 512), lambda i, p: (0, i))
    return pl.pallas_call(
        branch_kernel,
        grid_spec=pltpu.PrefetchScalarGridSpec(
            num_scalar_prefetch=1, grid=(4,),
            in_specs=[pl.BlockSpec((8, 2, 128, HD), lambda i, p: (0, 0, 0, 0)), pl.BlockSpec((1024, 512), lambda i, p: (0, i))],
            out_specs=[col, col],
            scratch_shapes=[pltpu.VMEM((256, 1024), BF), pltpu.VMEM((2, 128, 512), F32)],
        ),
        out_shape=[jax.ShapeDtypeStruct((128, 2048), F32), jax.ShapeDtypeStruct((128, 2048), BF)],
        compiler_params=params(),
        cost_estimate=short(2 * 256 * 1024 * 2048, 6 << 20),
    )(place, heads, w)

def grads_kernel(place_ref, n_ref, inc_ref, act_ref, gh_ref, mine_ref, partner_ref, keep_ref, send_ref):
    def down(ref):
        ref[...] = dot(act_ref[...], inc_ref[...], (0, 0)).astype(BF)

    @pl.when(pl.program_id(0) < 2)
    def _():
        down(mine_ref)

    @pl.when(pl.program_id(0) >= 2)
    def _():
        down(partner_ref)

    up = dot(gh_ref[...], n_ref[...], (0, 0)).astype(BF)
    even, odd = (
        jnp.concatenate([up[:, (2 * i + low) * 256 : (2 * i + low + 1) * 256] for i in range(4)], axis=1)
        for low in range(2)
    )

    @pl.when(place_ref[0] == 0)
    def _():
        keep_ref[...] = even
        send_ref[...] = odd

    @pl.when(place_ref[0] == 1)
    def _():
        keep_ref[...] = odd
        send_ref[...] = even

def weight_grads(place, n, inc, act, gh):
    rows = pl.BlockSpec((1024, 2048), lambda j, p: (0, 0))
    cols = pl.BlockSpec((1024, 256), lambda j, p: (0, j))
    part = pl.BlockSpec((256, 1024), lambda j, p: (j, 0))
    return pl.pallas_call(
        grads_kernel,
        grid_spec=pltpu.PrefetchScalarGridSpec(
            num_scalar_prefetch=1, grid=(4,),
            in_specs=[rows, rows, cols, cols],
            out_specs=[
                pl.BlockSpec((256, 2048), lambda j, p: (jnp.minimum(j, 1), 0)),
                pl.BlockSpec((256, 2048), lambda j, p: (jnp.maximum(j - 2, 0), 0)),
                part, part,
            ],
        ),
        out_shape=[jax.ShapeDtypeStruct((512, 2048), BF)] * 2 + [jax.ShapeDtypeStruct((1024, 1024), BF)] * 2,
        compiler_params=params(),
        cost_estimate=short(4 * 1024 * 1024 * 2048, 20 << 20),
    )(place, n, inc, act, gh)


def cut_kernel(place_ref, down_ref, down_got_ref, up_ref, up_got_ref, down_keep, down_send, up_keep, up_send):
    down = add(down_ref[...], down_got_ref[...])
    up = add(up_ref[...], up_got_ref[...])
    low = jnp.concatenate([up[:, :256], up[:, 512:768]], axis=1)
    high = jnp.concatenate([up[:, 256:512], up[:, 768:]], axis=1)

    @pl.when(place_ref[0] == 0)
    def _():
        down_keep[...] = down[:, :1024]
        down_send[...] = down[:, 1024:]

    @pl.when(place_ref[0] == 1)
    def _():
        down_keep[...] = down[:, 1024:]
        down_send[...] = down[:, :1024]

    @pl.when(place_ref[1] == 0)
    def _():
        up_keep[...] = low
        up_send[...] = high

    @pl.when(place_ref[1] == 1)
    def _():
        up_keep[...] = high
        up_send[...] = low

def cut(place, down, down_got, up, up_got):
    wide = pl.BlockSpec((128, 2048), lambda i, p: (i, 0))
    half = pl.BlockSpec((128, 1024), lambda i, p: (i, 0))
    four = pl.BlockSpec((256, 1024), lambda i, p: (i, 0))
    two = pl.BlockSpec((256, 512), lambda i, p: (i, 0))
    return pl.pallas_call(
        cut_kernel,
        grid_spec=pltpu.PrefetchScalarGridSpec(
            num_scalar_prefetch=1, grid=(4,),
            in_specs=[wide, wide, four, four],
            out_specs=[half, half, two, two],
        ),
        out_shape=[jax.ShapeDtypeStruct((512, 1024), BF)] * 2 + [jax.ShapeDtypeStruct((1024, 512), BF)] * 2,
        compiler_params=params(),
    )(place, down, down_got, up, up_got)


def heads_kernel(place_ref, mine_ref, other_ref, w_ref, out_ref, left):
    @pl.when(pl.program_id(0) == 0)
    def _():
        left[place_ref[0]] = mine_ref[...]
        left[1 - place_ref[0]] = other_ref[...]

    part = dot(left[...].reshape(256, 2048), w_ref[...], (1, 1)).astype(BF)
    for h in range(4):
        out_ref[h] = part[:, h * HD : (h + 1) * HD].reshape(2, 128, HD)

def to_heads(place, mine, other, w):
    rows = pl.BlockSpec((128, 2048), lambda i, p: (0, 0))
    return pl.pallas_call(
        heads_kernel,
        grid_spec=pltpu.PrefetchScalarGridSpec(
            num_scalar_prefetch=1, grid=(2,),
            in_specs=[rows, rows, pl.BlockSpec((512, 2048), lambda i, p: (i, 0))],
            out_specs=pl.BlockSpec((4, 2, 128, HD), lambda i, p: (i, 0, 0, 0)),
            scratch_shapes=[pltpu.VMEM((2, 128, 2048), BF)],
        ),
        out_shape=jax.ShapeDtypeStruct((8, 2, 128, HD), BF),
        compiler_params=params(),
    )(place, mine, other, w)


def first_kernel(place_ref, mine_ref, got_ref, own_ref, partner_ref, out_ref, left, right):
    @pl.when(pl.program_id(0) == 0)
    def _():
        for c in range(3):
            right[:, c * HD : (c + 1) * HD] = own_ref[c]
            right[:, (c + 3) * HD : (c + 4) * HD] = partner_ref[c]

    left[:, : 3 * HD] = mine_ref[...]
    left[:, 3 * HD :] = got_ref[...]
    out_ref[...] = dot(left[...], right[...], (1, 1)).astype(BF)

def first_back(place, mine, got, own, partner):
    whole = pl.BlockSpec((3, 2048, HD), lambda i, p: (0, 0, 0))
    return pl.pallas_call(
        first_kernel,
        grid_spec=pltpu.PrefetchScalarGridSpec(
            num_scalar_prefetch=1, grid=(4,),
            in_specs=[
                pl.BlockSpec((256, 3 * HD), lambda i, p: (p[0] * 4 + i, 0)),
                pl.BlockSpec((256, 3 * HD), lambda i, p: (i, 0)),
                whole, whole,
            ],
            out_specs=pl.BlockSpec((256, 2048), lambda i, p: (i, 0)),
            scratch_shapes=[pltpu.VMEM((256, 6 * HD), BF), pltpu.VMEM((2048, 6 * HD), BF)],
        ),
        out_shape=jax.ShapeDtypeStruct((1024, 2048), BF),
        compiler_params=params(),
    )(place, mine, got, own, partner)


def stack_kernel(*refs):
    for i, ref in enumerate(refs[:-1]):
        refs[-1][i] = ref[...]

def stack(*arrays):
    return pl.pallas_call(
        stack_kernel,
        in_specs=[pl.BlockSpec(memory_space=pltpu.VMEM)] * len(arrays),
        out_specs=pl.BlockSpec(memory_space=pltpu.VMEM),
        out_shape=jax.ShapeDtypeStruct((len(arrays), *arrays[0].shape), arrays[0].dtype),
        compiler_params=params(),
    )(*arrays)

def out_kernel(place_ref, mine_ref, partner_ref, grad_ref, out_ref):
    grad = grad_ref[...]
    out_ref[0, place_ref[0]] = dot(mine_ref[...], grad, (0, 0)).astype(BF)
    out_ref[0, 1 - place_ref[0]] = dot(partner_ref[...], grad, (0, 0)).astype(BF)

def out_grads(place, mine, partner, grad):
    heads = pl.BlockSpec((1024, HD), lambda i, p: (0, 0))
    return pl.pallas_call(
        out_kernel,
        grid_spec=pltpu.PrefetchScalarGridSpec(
            num_scalar_prefetch=1, grid=(8,),
            in_specs=[heads, heads, pl.BlockSpec((1024, 256), lambda i, p: (0, i))],
            out_specs=pl.BlockSpec((1, 2, HD, 256), lambda i, p: (i, 0, 0, 0)),
        ),
        out_shape=jax.ShapeDtypeStruct((8, 2, HD, 256), BF),
        compiler_params=params(),
        cost_estimate=short(2 * 1024 * 256 * 2048, 6 << 20, 1),
    )(place, mine, partner, grad)


def qkv_grads_kernel(n_ref, gp_ref, w_ref, out_ref, sums_ref, columns):
    @pl.when(pl.program_id(0) == 0)
    def _():
        columns[...] = jnp.sum(gp_ref[...].astype(F32), axis=0, keepdims=True)

    grad = dot(n_ref[...], gp_ref[...], (0, 0))
    out_ref[...] = grad.astype(BF)
    ones = jnp.ones((8, HD), F32)
    gain = jnp.zeros((8, 256), F32)
    shift = jnp.zeros((8, 256), F32)
    for c in range(3):
        cols = slice(c * HD, (c + 1) * HD)
        w = w_ref[c].astype(F32)
        total = lambda v: lax.dot_general(ones, v, (((1,), (1,)), ((), ())), precision=lax.Precision.HIGHEST, preferred_element_type=F32)
        gain += total(w * grad[:, cols])
        shift += total(w * columns[:, cols])
    sums_ref[0] = gain[0:1]
    sums_ref[1] = shift[0:1]

def qkv_grads(normed, gp, w):
    return pl.pallas_call(
        qkv_grads_kernel, grid=(8,),
        in_specs=[
            pl.BlockSpec((2048, 256), lambda i: (0, i)),
            pl.BlockSpec((2048, 384), lambda i: (0, 0)),
            pl.BlockSpec((3, 256, HD), lambda i: (0, i, 0)),
        ],
        out_specs=[pl.BlockSpec((256, 384), lambda i: (i, 0)), pl.BlockSpec((2, 1, 256), lambda i: (0, 0, i))],
        out_shape=[jax.ShapeDtypeStruct((2048, 384), BF), jax.ShapeDtypeStruct((2, 1, 2048), F32)],
        scratch_shapes=[pltpu.VMEM((1, 384), F32)],
        compiler_params=params(),
        cost_estimate=short(2 * 2048 * 2048 * 384, 12 << 20, 1),
    )(normed, gp, w)


def scatter(values, axes):
    return lax.psum_scatter(values, axes, scatter_dimension=0, tiled=True).astype(F32)


def pick(values, index, axis):
    return lax.dynamic_index_in_dim(values, index, axis, False)


def after(values, *others):
    return lax.optimization_barrier((values, *others))[0]


def over_x(own, partner, x_hi, axis):
    size = own.shape[axis] // 2
    own = add(own, x_partner(partner))

    def part(at):
        return lax.dynamic_slice_in_dim(own, at * size, size, axis)

    return part(x_hi).astype(F32) + x_far(part(1 - x_hi)).astype(F32)


def exchange(values, axes):
    return jnp.sum(lax.all_to_all(values, axes, 0, 0).astype(F32), axis=0)


def sum_of_all(values):
    for axes, count in ((("z", "core"), 8), (("x_hi", "y", "x_lo"), 16)):
        values = exchange(jnp.broadcast_to(values[None], (count, *values.shape)), axes)
    return values


def body(
    tokens,
    ln1_gain,
    ln1_shift,
    qkv_weight,
    out_weight,
    ln2_gain,
    ln2_shift,
    up_weight,
    down_weight,
    lengths,
    cotangent,
):
    x_hi, y, x_lo, z, core = (lax.axis_index(axis) for axis in AXES)
    tensor = x_lo * 8 + z * 2 + core
    length = lengths[0]

    place = jnp.stack([core, z, x_lo, y % 2])

    out_own = lax.all_gather(out_weight, ("z", "core"), axis=0, tiled=True)
    live_rows = (tensor * 128 + jnp.arange(128, dtype=jnp.int32) < length).astype(F32)[:, None]
    incoming_rows = cotangent.astype(F32) * live_rows
    sent_rows = incoming_rows.astype(BF)
    later_rows = after(sent_rows, out_own)
    along_z = [z_down(later_rows), z_far(sent_rows), z_up(later_rows)]
    up_partner, down_partner, qkv_partner = x_partner(up_weight), x_partner(down_weight), x_partner(qkv_weight)

    normed_first, projected = project(tokens, ln1_gain, ln1_shift, qkv_weight)
    attended, totals = attend(projected, lengths)
    heads = lax.all_to_all(attended, ("z", "core"), 0, 0)
    branch_mine, branch_other = branch(place[2:], after(heads, up_partner, along_z[1]), out_own)
    branch_other = after(x_pair(branch_other), down_partner, along_z[0], along_z[2])
    token_rows = lax.dynamic_slice_in_dim(tokens, tensor * 128, 128, 0).astype(F32)
    middle_rows = token_rows + (branch_mine + branch_other.astype(F32))
    unit_second, inverse_second = norm_stats(middle_rows)
    normed_rows = (unit_second * ln2_gain + ln2_shift).astype(BF)
    along_z = stack(after(sent_rows, normed_rows), *along_z)
    from_core = core_swap(along_z)

    normed_second = lax.all_gather(normed_rows, ("z", "core"), axis=0, tiled=True)
    activated, grad_hidden, grad_normed_part, incoming = front(
        place,
        after(normed_second, qkv_partner).reshape(4, 2, 128, 2048),
        along_z,
        from_core,
        up_weight,
        up_partner,
        down_weight,
        down_partner,
    )
    incoming = incoming.reshape(1024, 2048)
    grad_normed_second = scatter(grad_normed_part.reshape(1024, 2048), ("z", "core"))
    down_kept, down_sent, up_kept, up_sent = weight_grads(
        place[3:], normed_second, incoming, activated, grad_hidden
    )
    down_got, up_got = x_partner(down_sent), y_pair(up_sent)
    grad_normed_second = after(grad_normed_second, down_got, up_got)

    grad_middle = incoming_rows + norm_back(grad_normed_second, ln2_gain, unit_second, inverse_second)
    gain_second = jnp.sum(grad_normed_second * unit_second, axis=0)
    shift_second = jnp.sum(grad_normed_second, axis=0)
    grad_branch = grad_middle.astype(BF)
    branch_back = lax.all_gather(grad_branch, ("z", "core"), axis=0, tiled=True)

    branch_got = x_pair(grad_branch)
    mixed_mine, mixed_other = mix(place, after(activated, grad_branch), down_weight, down_partner)
    by_head = to_heads(place[2:], grad_branch, after(branch_got, mixed_mine), out_own)
    grad_attended = lax.all_to_all(by_head, ("z", "core"), 0, 0)
    down_kept, down_sent, up_kept, up_sent = cut(
        jnp.stack([x_hi, y // 2]), down_kept, after(down_got, by_head), up_kept, up_got
    )
    down_got, up_got = x_far(down_sent), y_far(up_sent)
    partner_heads = x_pair(pick(attended, 1 - x_lo, 1).reshape(1024, HD))

    grad_projected, projected_sent = attend_back(
        projected, after(grad_attended, down_sent, partner_heads), totals, jnp.stack([length, x_lo])
    )
    projected_got = x_pair(projected_sent)
    out_blocks = out_grads(
        x_lo[None], after(pick(attended, x_lo, 1).reshape(1024, HD), projected_sent), partner_heads, branch_back
    )
    grad_qkv, first_sums = qkv_grads(normed_first, after(grad_projected, out_blocks), qkv_weight)
    projected_got = after(projected_got, grad_qkv, down_got, up_got)
    grad_first_part = first_back(place[2:], grad_projected, projected_got, qkv_weight, qkv_partner)
    grad_normed_first = scatter(grad_first_part, ("z", "core"))

    down_sums = add(down_kept, after(down_got, out_blocks))
    grad_down = exchange(down_sums.reshape(512, 4, 256).transpose(1, 0, 2), "y")
    grad_out = exchange(after(out_blocks, grad_down).reshape(16, HD, 256), ("x_hi", "y", "x_lo"))
    shift_first = first_sums[1, 0]
    gain_first = (first_sums[0, 0] - ln1_shift * shift_first) / ln1_gain
    sums = jnp.stack([gain_first, gain_second, shift_first, shift_second])
    sums = sum_of_all(after(sums, grad_out))
    grad_qkv = exchange(grad_qkv.reshape(8, 256, 384), BATCH)
    grad_qkv = grad_qkv.reshape(256, 3, HD).transpose(1, 0, 2)

    up_sums = add(up_kept, after(up_got, grad_first_part))
    grad_up = over_x(up_sums[:512], up_sums[512:], x_hi, 1).T
    mixed = add(mixed_mine, after(core_swap(mixed_other), grad_first_part)).reshape(2, 2, 128, 2048)
    mixed = add(pick(mixed, z % 2, 1), z_pair(pick(mixed, 1 - z % 2, 1)))
    output = (
        middle_rows + pick(mixed, z // 2, 0).astype(F32) + z_far(pick(mixed, 1 - z // 2, 0)).astype(F32)
    ).astype(BF)

    unit_rows, inverse_rows = norm_stats(token_rows)
    grad_tokens = (grad_middle + norm_back(grad_normed_first, ln1_gain, unit_rows, inverse_rows)).astype(BF)
    return (output, grad_tokens, grad_qkv, grad_out, grad_up, grad_down, sums[:2], sums[2:])


def solution(mesh):
    return jax.shard_map(
        body,
        mesh=Mesh(mesh.devices.reshape(2, 4, 2, 4, 2), AXES),
        in_specs=(
            P(BATCH, None),
            P(),
            P(),
            P(None, None, TENSOR),
            P(TENSOR, None),
            P(),
            P(),
            P(None, TENSOR),
            P(TENSOR, None),
            P(BATCH),
            P(AXES, None),
        ),
        out_specs=(
            P(AXES, None),
            P(AXES, None),
            P(None, BATCH, TENSOR),
            P(TENSOR, BATCH),
            P(BATCH, TENSOR),
            P(TENSOR, BATCH),
            P(),
            P(),
        ),
        check_vma=False,
    )
```

```python
import functools

import jax
import jax.numpy as jnp
from jax import lax
from jax.experimental import pallas as pl
from jax.experimental.pallas import tpu as pltpu
from jax.sharding import Mesh
from jax.sharding import PartitionSpec as P

HD = 128
EPS = 1e-05
MASKED_SCORE = -1e30
BF = jnp.bfloat16
F32 = jnp.float32

AXES = ("x_hi", "y", "x_lo", "z", "core")
BATCH, TENSOR = AXES[:2], AXES[2:]


def core_swap(values):
    return lax.ppermute(values, "core", [(0, 1), (1, 0)])


def x_pair(values):
    return lax.ppermute(values, "x_lo", [(0, 1), (1, 0)])


def y_near(values):
    return lax.ppermute(values, "y", [(i, i ^ 1) for i in range(4)])


def x_partner(values):
    pairs = [(r * 2 + c, ((r + (1, -1)[c]) % 4) * 2 + c) for r in range(4) for c in range(2)]
    return lax.ppermute(values, ("x_hi", "x_lo", "core"), pairs)


def neighbours(axis):
    pairs = [(i * 2 + c, ((i ^ 1) if c == 0 else 3 - i) * 2 + c) for i in range(4) for c in range(2)]
    return lambda values: lax.ppermute(values, (axis, "core"), pairs)


y_pair, z_pair = neighbours("y"), neighbours("z")


def shift(axes, sizes, step):
    return lambda values: lax.ppermute(values, axes, [(i, (i + step) % sizes) for i in range(sizes)])


z_up, z_down, z_far = (shift("z", 4, step) for step in (1, -1, 2))
y_up, y_down, y_far = (shift("y", 4, step) for step in (1, -1, 2))
x_up, x_down, x_far = (shift(("x_hi", "x_lo"), 4, step) for step in (1, -1, 2))


def norm_stats(values):
    centre = jnp.mean(values, axis=-1, keepdims=True)
    offsets = values - centre
    variance = jnp.mean(offsets * offsets, axis=-1, keepdims=True)
    inverse = lax.rsqrt(variance + EPS)
    return (offsets * inverse, inverse)


def norm_back(grad_normed, gain, unit_rows, inverse):
    scaled = grad_normed * gain
    return inverse * (
        scaled
        - jnp.mean(scaled, axis=-1, keepdims=True)
        - unit_rows * jnp.mean(scaled * unit_rows, axis=-1, keepdims=True)
    )


def dot(left, right, dims):
    return lax.dot_general(left, right, ((dims[:1], dims[1:]), ((), ())), preferred_element_type=F32)


def short(flops, moved, by=64):
    return pl.CostEstimate(flops=flops // by, bytes_accessed=moved // by, transcendentals=0)


def add(left, right):
    return (left.astype(F32) + right.astype(F32)).astype(BF)


def params(limit=60, **kw):
    return pltpu.CompilerParams(vmem_limit_bytes=limit * 2**20, **kw)


def qkv_kernel(x_ref, gain_ref, shift_ref, w_ref, normed_ref, out_ref, weights):
    @pl.when(pl.program_id(0) == 0)
    def _():
        for c in range(3):
            weights[:, c * HD : (c + 1) * HD] = w_ref[c]

    x = x_ref[...].astype(F32)
    offsets = x - jnp.mean(x, axis=-1, keepdims=True)
    inverse = lax.rsqrt(jnp.mean(offsets * offsets, axis=-1, keepdims=True) + EPS)
    normed = (offsets * inverse * gain_ref[...] + shift_ref[...]).astype(BF)
    normed_ref[...] = normed
    out_ref[...] = dot(normed, weights[...], (1, 0)).astype(BF)

def project(tokens, gain, shift, weight):
    rows = 256
    return pl.pallas_call(
        qkv_kernel,
        grid=(2048 // rows,),
        in_specs=[
            pl.BlockSpec((rows, 2048), lambda i: (i, 0)),
            pl.BlockSpec((1, 2048), lambda i: (0, 0)),
            pl.BlockSpec((1, 2048), lambda i: (0, 0)),
            pl.BlockSpec((3, 2048, HD), lambda i: (0, 0, 0)),
        ],
        out_specs=[
            pl.BlockSpec((rows, 2048), lambda i: (i, 0)),
            pl.BlockSpec((rows, 3 * HD), lambda i: (i, 0)),
        ],
        out_shape=[jax.ShapeDtypeStruct((2048, 2048), BF), jax.ShapeDtypeStruct((2048, 3 * HD), BF)],
        scratch_shapes=[pltpu.VMEM((2048, 3 * HD), BF)],
        compiler_params=params(),
        cost_estimate=short(2 * 2048 * 2048 * 384, 20 << 20),
    )(tokens, gain[None], shift[None], weight)


QB = 512
SCALE = HD ** -0.5

def masked(scores, first_query, first_key, length):
    query = first_query + lax.broadcasted_iota(jnp.int32, scores.shape, 0)
    key = first_key + lax.broadcasted_iota(jnp.int32, scores.shape, 1)
    return jnp.where((key <= query) & (key < length), scores, MASKED_SCORE)

def forward_kernel(length_ref, qkv_ref, out_ref, total_ref):
    length = length_ref[0]
    for i in range(2048 // QB):
        q = qkv_ref[i * QB : (i + 1) * QB, :HD]
        parts = []
        for j in range(i + 1):
            k = qkv_ref[j * QB : (j + 1) * QB, HD : 2 * HD]
            parts.append(masked(dot(q, k, (1, 1)) * SCALE, i * QB, j * QB, length))
        peak = functools.reduce(jnp.maximum, [jnp.max(p, axis=-1, keepdims=True) for p in parts])
        total = jnp.zeros((QB, 1), F32)
        acc = jnp.zeros((QB, HD), F32)
        for j in range(i + 1):
            e = jnp.exp(parts[j] - peak)
            total += jnp.sum(e, axis=-1, keepdims=True)
            acc += dot(e.astype(BF), qkv_ref[j * QB : (j + 1) * QB, 2 * HD :], (1, 0))
        out = (acc / total).astype(BF)
        for b in range(QB // HD):
            block = i * (QB // HD) + b
            out_ref[block % 8, block // 8] = out[b * HD : (b + 1) * HD]
        total_ref[i * QB : (i + 1) * QB] = peak + jnp.log(total)

def attend(qkv, lengths):
    return pl.pallas_call(
        forward_kernel,
        in_specs=[pl.BlockSpec(memory_space=pltpu.SMEM), pl.BlockSpec(memory_space=pltpu.VMEM)],
        out_specs=[pl.BlockSpec(memory_space=pltpu.VMEM)] * 2,
        out_shape=[jax.ShapeDtypeStruct((8, 2, 128, HD), BF), jax.ShapeDtypeStruct((2048, 1), F32)],
        compiler_params=params(),
        cost_estimate=short(2 * 2 * 2048 * 2048 * 128, 3 << 20),
    )(lengths, qkv)

def backward_kernel(length_ref, qkv_ref, grad_ref, total_ref, out_ref, sent_ref, gk, gv, probs, gprobs):
    length = length_ref[0]
    n = 2048 // QB
    gk[...] = jnp.zeros_like(gk)
    gv[...] = jnp.zeros_like(gv)
    for i in range(n):
        rows = slice(i * QB, (i + 1) * QB)
        q = qkv_ref[rows, :HD]
        blocks = [i * (QB // HD) + b for b in range(QB // HD)]
        g = jnp.concatenate([grad_ref[b % 8, b // 8] for b in blocks], axis=0)
        total = total_ref[rows]
        centre = jnp.zeros((QB, 1), F32)
        for j in range(i + 1):
            keys = slice(j * QB, (j + 1) * QB)
            s = masked(dot(q, qkv_ref[keys, HD : 2 * HD], (1, 1)) * SCALE, i * QB, j * QB, length)
            p = jnp.exp(s - total)
            gp = dot(g, qkv_ref[keys, 2 * HD :], (1, 1))
            centre += jnp.sum(p * gp, axis=-1, keepdims=True)
            probs[:, keys] = p
            gprobs[:, keys] = gp
        gq = jnp.zeros((QB, HD), F32)
        for j in range(i + 1):
            keys = slice(j * QB, (j + 1) * QB)
            p = probs[:, keys]
            gs = (p * (gprobs[:, keys] - centre)).astype(BF)
            gq += dot(gs, qkv_ref[keys, HD : 2 * HD], (1, 0))
            gk[keys] += dot(gs, q, (0, 0))
            gv[keys] += dot(p.astype(BF), g, (0, 0))
        out_ref[rows, :HD] = (gq * SCALE).astype(BF)
    out_ref[:, HD : 2 * HD] = (gk[...] * SCALE).astype(BF)
    out_ref[:, 2 * HD :] = gv[...].astype(BF)

    @pl.when(length_ref[1] == 0)
    def _():
        sent_ref[...] = out_ref[1024:]

    @pl.when(length_ref[1] == 1)
    def _():
        sent_ref[...] = out_ref[:1024]

def attend_back(qkv, grad, totals, lengths):
    return pl.pallas_call(
        backward_kernel,
        in_specs=[pl.BlockSpec(memory_space=pltpu.SMEM)] + [pl.BlockSpec(memory_space=pltpu.VMEM)] * 3,
        out_specs=[pl.BlockSpec(memory_space=pltpu.VMEM)] * 2,
        out_shape=[jax.ShapeDtypeStruct((2048, 3 * HD), BF), jax.ShapeDtypeStruct((1024, 3 * HD), BF)],
        scratch_shapes=[pltpu.VMEM((2048, HD), F32), pltpu.VMEM((2048, HD), F32), pltpu.VMEM((QB, 2048), F32), pltpu.VMEM((QB, 2048), F32)],
        compiler_params=params(),
        cost_estimate=short(5 * 2 * 2048 * 1280 * 128, 4 << 20),
    )(lengths, qkv, grad, totals)


GELU_A = 0.7978845608028654
GELU_B = 0.044715

def front_kernel(place_ref, n_ref, mine_ref, other_ref, uo, up, do, dp, act_ref, gh_ref, part_ref, inc_ref):
    core = place_ref[0]
    inc_ref[0, core] = mine_ref[0]
    inc_ref[0, 1 - core] = other_ref[0]
    n = n_ref[0].reshape(256, 2048)
    inc = inc_ref[0].reshape(256, 2048)
    part = jnp.zeros((256, 2048), F32)
    for h, (u, d) in enumerate(((uo, do), (up, dp))):
        cols = slice(h * 512, (h + 1) * 512)
        hidden = dot(n, u[...], (1, 0))
        square = hidden * hidden
        t = jnp.tanh(GELU_A * (hidden + GELU_B * hidden * square))
        act_ref[:, cols] = (0.5 * hidden * (1 + t)).astype(BF)
        slope = 0.5 * (1 + t) + 0.5 * hidden * (1 - t * t) * (GELU_A * (1 + 3 * GELU_B * square))
        gh = (dot(inc, d[...], (1, 1)) * slope).astype(BF)
        gh_ref[:, cols] = gh
        part += dot(gh, u[...], (1, 1))
    part_ref[0] = part.astype(BF).reshape(2, 128, 2048)

def front(place, normed, mine, other, uo, up, do, dp):
    whole = lambda a: pl.BlockSpec(a.shape, lambda i, p: (0,) * a.ndim)
    blk = pl.BlockSpec((1, 2, 128, 2048), lambda i, p: (i, 0, 0, 0))
    one = pl.BlockSpec((1, 128, 2048), lambda i, p: ((i + 4 - p[1]) % 4, 0, 0))
    col = pl.BlockSpec((256, 1024), lambda i, p: (i, 0))
    return pl.pallas_call(
        front_kernel,
        grid_spec=pltpu.PrefetchScalarGridSpec(
            num_scalar_prefetch=1, grid=(4,),
            in_specs=[blk, one, one, whole(uo), whole(up), whole(do), whole(dp)],
            out_specs=[col, col, blk, blk],
        ),
        out_shape=[jax.ShapeDtypeStruct((1024, 1024), BF)] * 2 + [jax.ShapeDtypeStruct((4, 2, 128, 2048), BF)] * 2,
        compiler_params=params(),
        cost_estimate=short(6 * 1024 * 1024 * 2048, 28 << 20),
    )(place, normed, mine, other, uo, up, do, dp)


def mixed_kernel(place_ref, act_ref, do, dp, mine_ref, other_ref, rows):
    a = act_ref[...]
    rows[...] = (dot(a[:, :512], do[...], (1, 0)) + dot(a[:, 512:], dp[...], (1, 0))).astype(BF).reshape(2, 128, 2048)
    mine_ref[0] = rows[place_ref[0]]
    other_ref[0] = rows[1 - place_ref[0]]

def mix(place, act, do, dp):
    whole = lambda a: pl.BlockSpec(a.shape, lambda i, p: (0,) * a.ndim)
    return pl.pallas_call(
        mixed_kernel,
        grid_spec=pltpu.PrefetchScalarGridSpec(
            num_scalar_prefetch=1, grid=(4,),
            in_specs=[pl.BlockSpec((256, 1024), lambda i, p: (i, 0)), whole(do), whole(dp)],
            out_specs=[pl.BlockSpec((1, 128, 2048), lambda i, p: (i, 0, 0))] * 2,
            scratch_shapes=[pltpu.VMEM((2, 128, 2048), BF)],
        ),
        out_shape=[jax.ShapeDtypeStruct((4, 128, 2048), BF)] * 2,
        compiler_params=params(),
        cost_estimate=short(2 * 1024 * 1024 * 2048, 10 << 20),
    )(place, act, do, dp)

def branch_kernel(place_ref, heads_ref, w_ref, mine_ref, other_ref, left, out):
    @pl.when(pl.program_id(0) == 0)
    def _():
        for h in range(8):
            left[:, h * HD : (h + 1) * HD] = heads_ref[h].reshape(256, HD)

    out[...] = dot(left[...], w_ref[...], (1, 0)).reshape(2, 128, 512)
    mine_ref[...] = out[place_ref[0]]
    other_ref[...] = out[1 - place_ref[0]].astype(BF)

def branch(place, heads, w):
    col = pl.BlockSpec((128, 512), lambda i, p: (0, i))
    return pl.pallas_call(
        branch_kernel,
        grid_spec=pltpu.PrefetchScalarGridSpec(
            num_scalar_prefetch=1, grid=(4,),
            in_specs=[pl.BlockSpec((8, 2, 128, HD), lambda i, p: (0, 0, 0, 0)), pl.BlockSpec((1024, 512), lambda i, p: (0, i))],
            out_specs=[col, col],
            scratch_shapes=[pltpu.VMEM((256, 1024), BF), pltpu.VMEM((2, 128, 512), F32)],
        ),
        out_shape=[jax.ShapeDtypeStruct((128, 2048), F32), jax.ShapeDtypeStruct((128, 2048), BF)],
        compiler_params=params(),
        cost_estimate=short(2 * 256 * 1024 * 2048, 6 << 20),
    )(place, heads, w)

def grads_kernel(place_ref, n_ref, inc_ref, act_ref, gh_ref, mine_ref, partner_ref, keep_ref, send_ref):
    def down(ref):
        ref[...] = dot(act_ref[...], inc_ref[...], (0, 0)).astype(BF)

    @pl.when(pl.program_id(0) < 2)
    def _():
        down(mine_ref)

    @pl.when(pl.program_id(0) >= 2)
    def _():
        down(partner_ref)

    up = dot(gh_ref[...], n_ref[...], (0, 0)).astype(BF)
    even, odd = (
        jnp.concatenate([up[:, (2 * i + low) * 256 : (2 * i + low + 1) * 256] for i in range(4)], axis=1)
        for low in range(2)
    )

    @pl.when(place_ref[0] == 0)
    def _():
        keep_ref[...] = even
        send_ref[...] = odd

    @pl.when(place_ref[0] == 1)
    def _():
        keep_ref[...] = odd
        send_ref[...] = even

def weight_grads(place, n, inc, act, gh):
    rows = pl.BlockSpec((1024, 2048), lambda j, p: (0, 0))
    cols = pl.BlockSpec((1024, 256), lambda j, p: (0, j))
    part = pl.BlockSpec((256, 1024), lambda j, p: (j, 0))
    return pl.pallas_call(
        grads_kernel,
        grid_spec=pltpu.PrefetchScalarGridSpec(
            num_scalar_prefetch=1, grid=(4,),
            in_specs=[rows, rows, cols, cols],
            out_specs=[
                pl.BlockSpec((256, 2048), lambda j, p: (jnp.minimum(j, 1), 0)),
                pl.BlockSpec((256, 2048), lambda j, p: (jnp.maximum(j - 2, 0), 0)),
                part, part,
            ],
        ),
        out_shape=[jax.ShapeDtypeStruct((512, 2048), BF)] * 2 + [jax.ShapeDtypeStruct((1024, 1024), BF)] * 2,
        compiler_params=params(),
        cost_estimate=short(4 * 1024 * 1024 * 2048, 20 << 20),
    )(place, n, inc, act, gh)


def cut_kernel(place_ref, down_ref, down_got_ref, up_ref, up_got_ref, down_keep, down_send, up_keep, up_send):
    down = add(down_ref[...], down_got_ref[...])
    up = add(up_ref[...], up_got_ref[...])
    low = jnp.concatenate([up[:, :256], up[:, 512:768]], axis=1)
    high = jnp.concatenate([up[:, 256:512], up[:, 768:]], axis=1)

    @pl.when(place_ref[0] == 0)
    def _():
        down_keep[...] = down[:, :1024]
        down_send[...] = down[:, 1024:]

    @pl.when(place_ref[0] == 1)
    def _():
        down_keep[...] = down[:, 1024:]
        down_send[...] = down[:, :1024]

    @pl.when(place_ref[1] == 0)
    def _():
        up_keep[...] = low
        up_send[...] = high

    @pl.when(place_ref[1] == 1)
    def _():
        up_keep[...] = high
        up_send[...] = low

def cut(place, down, down_got, up, up_got):
    wide = pl.BlockSpec((128, 2048), lambda i, p: (i, 0))
    half = pl.BlockSpec((128, 1024), lambda i, p: (i, 0))
    four = pl.BlockSpec((256, 1024), lambda i, p: (i, 0))
    two = pl.BlockSpec((256, 512), lambda i, p: (i, 0))
    return pl.pallas_call(
        cut_kernel,
        grid_spec=pltpu.PrefetchScalarGridSpec(
            num_scalar_prefetch=1, grid=(4,),
            in_specs=[wide, wide, four, four],
            out_specs=[half, half, two, two],
        ),
        out_shape=[jax.ShapeDtypeStruct((512, 1024), BF)] * 2 + [jax.ShapeDtypeStruct((1024, 512), BF)] * 2,
        compiler_params=params(),
    )(place, down, down_got, up, up_got)


def heads_kernel(place_ref, mine_ref, other_ref, w_ref, out_ref, left):
    @pl.when(pl.program_id(0) == 0)
    def _():
        left[place_ref[0]] = mine_ref[...]
        left[1 - place_ref[0]] = other_ref[...]

    part = dot(left[...].reshape(256, 2048), w_ref[...], (1, 1)).astype(BF)
    for h in range(4):
        out_ref[h] = part[:, h * HD : (h + 1) * HD].reshape(2, 128, HD)

def to_heads(place, mine, other, w):
    rows = pl.BlockSpec((128, 2048), lambda i, p: (0, 0))
    return pl.pallas_call(
        heads_kernel,
        grid_spec=pltpu.PrefetchScalarGridSpec(
            num_scalar_prefetch=1, grid=(2,),
            in_specs=[rows, rows, pl.BlockSpec((512, 2048), lambda i, p: (i, 0))],
            out_specs=pl.BlockSpec((4, 2, 128, HD), lambda i, p: (i, 0, 0, 0)),
            scratch_shapes=[pltpu.VMEM((2, 128, 2048), BF)],
        ),
        out_shape=jax.ShapeDtypeStruct((8, 2, 128, HD), BF),
        compiler_params=params(),
    )(place, mine, other, w)


def both_kernel(own_ref, partner_ref, out_ref):
    for c in range(3):
        out_ref[c * HD : (c + 1) * HD] = own_ref[c].T
        out_ref[(c + 3) * HD : (c + 4) * HD] = partner_ref[c].T

def both_weights(own, partner):
    part = pl.BlockSpec((3, 256, HD), lambda i: (0, i, 0))
    return pl.pallas_call(
        both_kernel, grid=(8,),
        in_specs=[part, part],
        out_specs=pl.BlockSpec((6 * HD, 256), lambda i: (0, i)),
        out_shape=jax.ShapeDtypeStruct((6 * HD, 2048), BF),
        compiler_params=params(),
    )(own, partner)


def first_kernel(place_ref, mine_ref, got_ref, w_ref, out_ref, left):
    left[:, : 3 * HD] = mine_ref[...]
    left[:, 3 * HD :] = got_ref[...]
    out_ref[...] = dot(left[...], w_ref[...], (1, 0)).astype(BF)

def first_back(place, mine, got, weights):
    return pl.pallas_call(
        first_kernel,
        grid_spec=pltpu.PrefetchScalarGridSpec(
            num_scalar_prefetch=1, grid=(2,),
            in_specs=[
                pl.BlockSpec((512, 3 * HD), lambda i, p: (p[0] * 2 + i, 0)),
                pl.BlockSpec((512, 3 * HD), lambda i, p: (i, 0)),
                pl.BlockSpec((6 * HD, 2048), lambda i, p: (0, 0)),
            ],
            out_specs=pl.BlockSpec((512, 2048), lambda i, p: (i, 0)),
            scratch_shapes=[pltpu.VMEM((512, 6 * HD), BF)],
        ),
        out_shape=jax.ShapeDtypeStruct((1024, 2048), BF),
        compiler_params=params(),
        cost_estimate=short(2 * 1024 * 2048 * 768, 8 << 20, 1),
    )(place, mine, got, weights)


def stack_kernel(*refs):
    for i, ref in enumerate(refs[:-1]):
        refs[-1][i] = ref[...]

def stack(*arrays):
    return pl.pallas_call(
        stack_kernel,
        in_specs=[pl.BlockSpec(memory_space=pltpu.VMEM)] * len(arrays),
        out_specs=pl.BlockSpec(memory_space=pltpu.VMEM),
        out_shape=jax.ShapeDtypeStruct((len(arrays), *arrays[0].shape), arrays[0].dtype),
        compiler_params=params(),
    )(*arrays)

def out_kernel(place_ref, mine_ref, partner_ref, grad_ref, out_ref):
    grad = grad_ref[...]
    out_ref[0, place_ref[0]] = dot(mine_ref[...], grad, (0, 0)).astype(BF)
    out_ref[0, 1 - place_ref[0]] = dot(partner_ref[...], grad, (0, 0)).astype(BF)

def out_grads(place, mine, partner, grad):
    heads = pl.BlockSpec((1024, HD), lambda i, p: (0, 0))
    return pl.pallas_call(
        out_kernel,
        grid_spec=pltpu.PrefetchScalarGridSpec(
            num_scalar_prefetch=1, grid=(8,),
            in_specs=[heads, heads, pl.BlockSpec((1024, 256), lambda i, p: (0, i))],
            out_specs=pl.BlockSpec((1, 2, HD, 256), lambda i, p: (i, 0, 0, 0)),
        ),
        out_shape=jax.ShapeDtypeStruct((8, 2, HD, 256), BF),
        compiler_params=params(),
        cost_estimate=short(2 * 1024 * 256 * 2048, 6 << 20, 1),
    )(place, mine, partner, grad)


def qkv_grads_kernel(n_ref, gp_ref, w_ref, out_ref, sums_ref, left, columns):
    @pl.when(pl.program_id(0) == 0)
    def _():
        left[...] = gp_ref[...].T
        columns[...] = jnp.sum(left[...].astype(F32), axis=1, keepdims=True)

    grad = dot(left[...], n_ref[...], (1, 0))
    out_ref[0] = grad.astype(BF)
    w = jnp.concatenate([w_ref[c].T for c in range(3)], axis=0).astype(F32)
    sums_ref[0] = jnp.sum(w * grad, axis=0, keepdims=True)
    sums_ref[1] = jnp.sum(w * columns[...], axis=0, keepdims=True)

def qkv_grads(normed, gp, w):
    return pl.pallas_call(
        qkv_grads_kernel, grid=(8,),
        in_specs=[
            pl.BlockSpec((2048, 256), lambda i: (0, i)),
            pl.BlockSpec((2048, 384), lambda i: (0, 0)),
            pl.BlockSpec((3, 256, HD), lambda i: (0, i, 0)),
        ],
        out_specs=[pl.BlockSpec((1, 384, 256), lambda i: (i, 0, 0)), pl.BlockSpec((2, 1, 256), lambda i: (0, 0, i))],
        out_shape=[jax.ShapeDtypeStruct((8, 384, 256), BF), jax.ShapeDtypeStruct((2, 1, 2048), F32)],
        scratch_shapes=[pltpu.VMEM((384, 2048), BF), pltpu.VMEM((384, 1), F32)],
        compiler_params=params(),
        cost_estimate=short(2 * 2048 * 2048 * 384, 12 << 20, 1),
    )(normed, gp, w)


def scatter(values, axes):
    return lax.psum_scatter(values, axes, scatter_dimension=0, tiled=True).astype(F32)


def pick(values, index, axis):
    return lax.dynamic_index_in_dim(values, index, axis, False)


def after(values, *others):
    return lax.optimization_barrier((values, *others))[0]


def columns(values, at):
    size = values.shape[1] // 2
    return lax.dynamic_slice_in_dim(values, at * size, size, 1)


def over_x(own, partner, x_hi, axis):
    size = own.shape[axis] // 2
    own = add(own, x_partner(partner))

    def part(at):
        return lax.dynamic_slice_in_dim(own, at * size, size, axis)

    return part(x_hi).astype(F32) + x_far(part(1 - x_hi)).astype(F32)


def sum_of_all(values, last_gate):
    values = values + core_swap(values)
    for up, down, far in ((z_up, z_down, z_far), (x_up, x_down, x_far), (y_up, y_down, y_far)):
        if up is y_up:
            values = after(values, last_gate)
        values = (values + far(values)) + (up(values) + down(values))
    return values


def body(
    tokens,
    ln1_gain,
    ln1_shift,
    qkv_weight,
    out_weight,
    ln2_gain,
    ln2_shift,
    up_weight,
    down_weight,
    lengths,
    cotangent,
):
    x_hi, y, x_lo, z, core = (lax.axis_index(axis) for axis in AXES)
    tensor = x_lo * 8 + z * 2 + core
    length = lengths[0]

    place = jnp.stack([core, z, x_lo, y % 2])

    out_own = lax.all_gather(out_weight, ("z", "core"), axis=0, tiled=True)
    live_rows = (tensor * 128 + jnp.arange(128, dtype=jnp.int32) < length).astype(F32)[:, None]
    incoming_rows = cotangent.astype(F32) * live_rows
    sent_rows = incoming_rows.astype(BF)
    later_rows = after(sent_rows, out_own)
    along_z = [z_down(later_rows), z_far(sent_rows), z_up(later_rows)]
    up_partner, down_partner, qkv_partner = x_partner(up_weight), x_partner(down_weight), x_partner(qkv_weight)

    normed_first, projected = project(tokens, ln1_gain, ln1_shift, qkv_weight)
    attended, totals = attend(projected, lengths)
    heads = lax.all_to_all(attended, ("z", "core"), 0, 0)
    branch_mine, branch_other = branch(place[2:], after(heads, up_partner, along_z[1]), out_own)
    branch_other = after(x_pair(branch_other), down_partner, along_z[0], along_z[2])
    token_rows = lax.dynamic_slice_in_dim(tokens, tensor * 128, 128, 0).astype(F32)
    middle_rows = token_rows + (branch_mine + branch_other.astype(F32))
    unit_second, inverse_second = norm_stats(middle_rows)
    normed_rows = (unit_second * ln2_gain + ln2_shift).astype(BF)
    along_z = stack(after(sent_rows, normed_rows), *along_z)
    from_core = core_swap(along_z)
    qkv_both = both_weights(qkv_weight, after(qkv_partner, normed_rows))

    normed_second = lax.all_gather(normed_rows, ("z", "core"), axis=0, tiled=True)
    activated, grad_hidden, grad_normed_part, incoming = front(
        place,
        after(normed_second, qkv_both).reshape(4, 2, 128, 2048),
        along_z,
        from_core,
        up_weight,
        up_partner,
        down_weight,
        down_partner,
    )
    incoming = incoming.reshape(1024, 2048)
    grad_normed_second = scatter(grad_normed_part.reshape(1024, 2048), ("z", "core"))
    down_kept, down_sent, up_kept, up_sent = weight_grads(
        place[3:], normed_second, incoming, activated, grad_hidden
    )
    down_got, up_got = x_partner(down_sent), y_pair(up_sent)
    grad_normed_second = after(grad_normed_second, down_got, up_got)

    grad_middle = incoming_rows + norm_back(grad_normed_second, ln2_gain, unit_second, inverse_second)
    gain_second = jnp.sum(grad_normed_second * unit_second, axis=0)
    shift_second = jnp.sum(grad_normed_second, axis=0)
    grad_branch = grad_middle.astype(BF)
    branch_back = lax.all_gather(grad_branch, ("z", "core"), axis=0, tiled=True)

    branch_got = x_pair(grad_branch)
    mixed_mine, mixed_other = mix(place, after(activated, grad_branch), down_weight, down_partner)
    by_head = to_heads(place[2:], grad_branch, after(branch_got, mixed_mine), out_own)
    grad_attended = lax.all_to_all(by_head, ("z", "core"), 0, 0)
    down_kept, down_sent, up_kept, up_sent = cut(
        jnp.stack([x_hi, y // 2]), down_kept, after(down_got, by_head), up_kept, up_got
    )
    down_got, up_got = x_far(down_sent), y_far(up_sent)
    mixed_got = core_swap(after(mixed_other, by_head))
    partner_heads = x_pair(pick(attended, 1 - x_lo, 1).reshape(1024, HD))

    grad_projected, projected_sent = attend_back(
        projected, after(grad_attended, down_sent, partner_heads, mixed_got), totals, jnp.stack([length, x_lo])
    )
    projected_got = x_pair(projected_sent)
    out_blocks = out_grads(
        x_lo[None], after(pick(attended, x_lo, 1).reshape(1024, HD), projected_sent), partner_heads, branch_back
    )
    out_got = lax.all_to_all(out_blocks.reshape(16, HD, 256), ("x_hi", "y", "x_lo"), 0, 0)
    mixed = add(mixed_mine, mixed_got).reshape(2, 2, 128, 2048)
    projected_got = after(projected_got, out_blocks, mixed, down_got, up_got)
    grad_first_part = first_back(place[2:], grad_projected, projected_got, qkv_both)
    grad_normed_first = scatter(after(grad_first_part, out_got), ("z", "core"))

    down_sums = add(down_kept, after(down_got, grad_first_part))
    grad_out = jnp.sum(out_got.astype(F32), axis=0)
    grad_qkv, first_sums = qkv_grads(normed_first, after(grad_projected, grad_first_part), qkv_weight)
    down_sums = add(columns(down_sums, y // 2), y_far(columns(down_sums, 1 - y // 2)))
    grad_down = columns(down_sums, y % 2).astype(F32) + y_near(columns(down_sums, 1 - y % 2)).astype(F32)
    shift_first = first_sums[1, 0]
    gain_first = (first_sums[0, 0] - ln1_shift * shift_first) / ln1_gain
    grad_qkv = lax.all_to_all(grad_qkv, BATCH, 0, 0)
    sums = sum_of_all(jnp.stack([gain_first, gain_second, shift_first, shift_second]), grad_qkv)
    grad_qkv = jnp.sum(grad_qkv.astype(F32), axis=0).reshape(3, HD, 256).transpose(0, 2, 1)

    up_sums = add(up_kept, after(up_got, grad_first_part))
    grad_up = over_x(up_sums[:512], up_sums[512:], x_hi, 1).T
    mixed = after(mixed, grad_first_part)
    mixed = add(pick(mixed, z % 2, 1), z_pair(pick(mixed, 1 - z % 2, 1)))
    output = (
        middle_rows + pick(mixed, z // 2, 0).astype(F32) + z_far(pick(mixed, 1 - z // 2, 0)).astype(F32)
    ).astype(BF)

    unit_rows, inverse_rows = norm_stats(token_rows)
    grad_tokens = (grad_middle + norm_back(grad_normed_first, ln1_gain, unit_rows, inverse_rows)).astype(BF)
    return (output, grad_tokens, grad_qkv, grad_out, grad_up, grad_down, sums[:2], sums[2:])


def solution(mesh):
    return jax.shard_map(
        body,
        mesh=Mesh(mesh.devices.reshape(2, 4, 2, 4, 2), AXES),
        in_specs=(
            P(BATCH, None),
            P(),
            P(),
            P(None, None, TENSOR),
            P(TENSOR, None),
            P(),
            P(),
            P(None, TENSOR),
            P(TENSOR, None),
            P(BATCH),
            P(AXES, None),
        ),
        out_specs=(
            P(AXES, None),
            P(AXES, None),
            P(None, BATCH, TENSOR),
            P(TENSOR, BATCH),
            P(BATCH, TENSOR),
            P(TENSOR, BATCH),
            P(),
            P(),
        ),
        check_vma=False,
    )
```

```python
import functools

import jax
import jax.numpy as jnp
from jax import lax
from jax.experimental import pallas as pl
from jax.experimental.pallas import tpu as pltpu
from jax.sharding import Mesh
from jax.sharding import PartitionSpec as P

HD = 128
EPS = 1e-05
MASKED_SCORE = -1e30
BF = jnp.bfloat16
F32 = jnp.float32

AXES = ("x_hi", "y", "x_lo", "z", "core")
BATCH, TENSOR = AXES[:2], AXES[2:]


def core_swap(values):
    return lax.ppermute(values, "core", [(0, 1), (1, 0)])


def x_pair(values):
    return lax.ppermute(values, "x_lo", [(0, 1), (1, 0)])


def y_near(values):
    return lax.ppermute(values, "y", [(i, i ^ 1) for i in range(4)])


def x_partner(values):
    pairs = [(r * 2 + c, ((r + (1, -1)[c]) % 4) * 2 + c) for r in range(4) for c in range(2)]
    return lax.ppermute(values, ("x_hi", "x_lo", "core"), pairs)


def neighbours(axis):
    pairs = [(i * 2 + c, ((i ^ 1) if c == 0 else 3 - i) * 2 + c) for i in range(4) for c in range(2)]
    return lambda values: lax.ppermute(values, (axis, "core"), pairs)


y_pair, z_pair = neighbours("y"), neighbours("z")


def shift(axes, sizes, step):
    return lambda values: lax.ppermute(values, axes, [(i, (i + step) % sizes) for i in range(sizes)])


z_up, z_down, z_far = (shift("z", 4, step) for step in (1, -1, 2))
y_far, x_far = shift("y", 4, 2), shift(("x_hi", "x_lo"), 4, 2)


def norm_stats(values):
    centre = jnp.mean(values, axis=-1, keepdims=True)
    offsets = values - centre
    variance = jnp.mean(offsets * offsets, axis=-1, keepdims=True)
    inverse = lax.rsqrt(variance + EPS)
    return (offsets * inverse, inverse)


def norm_back(grad_normed, gain, unit_rows, inverse):
    scaled = grad_normed * gain
    return inverse * (
        scaled
        - jnp.mean(scaled, axis=-1, keepdims=True)
        - unit_rows * jnp.mean(scaled * unit_rows, axis=-1, keepdims=True)
    )


def dot(left, right, dims):
    return lax.dot_general(left, right, ((dims[:1], dims[1:]), ((), ())), preferred_element_type=F32)


def short(flops, moved, by=64):
    return pl.CostEstimate(flops=flops // by, bytes_accessed=moved // by, transcendentals=0)


def add(left, right):
    return (left.astype(F32) + right.astype(F32)).astype(BF)


def params(limit=60, **kw):
    return pltpu.CompilerParams(vmem_limit_bytes=limit * 2**20, **kw)


def qkv_kernel(x_ref, gain_ref, shift_ref, w_ref, normed_ref, out_ref, weights):
    @pl.when(pl.program_id(0) == 0)
    def _():
        for c in range(3):
            weights[:, c * HD : (c + 1) * HD] = w_ref[c]

    x = x_ref[...].astype(F32)
    offsets = x - jnp.mean(x, axis=-1, keepdims=True)
    inverse = lax.rsqrt(jnp.mean(offsets * offsets, axis=-1, keepdims=True) + EPS)
    normed = (offsets * inverse * gain_ref[...] + shift_ref[...]).astype(BF)
    normed_ref[...] = normed
    out_ref[...] = dot(normed, weights[...], (1, 0)).astype(BF)

def project(tokens, gain, shift, weight):
    rows = 256
    return pl.pallas_call(
        qkv_kernel,
        grid=(2048 // rows,),
        in_specs=[
            pl.BlockSpec((rows, 2048), lambda i: (i, 0)),
            pl.BlockSpec((1, 2048), lambda i: (0, 0)),
            pl.BlockSpec((1, 2048), lambda i: (0, 0)),
            pl.BlockSpec((3, 2048, HD), lambda i: (0, 0, 0)),
        ],
        out_specs=[
            pl.BlockSpec((rows, 2048), lambda i: (i, 0)),
            pl.BlockSpec((rows, 3 * HD), lambda i: (i, 0)),
        ],
        out_shape=[jax.ShapeDtypeStruct((2048, 2048), BF), jax.ShapeDtypeStruct((2048, 3 * HD), BF)],
        scratch_shapes=[pltpu.VMEM((2048, 3 * HD), BF)],
        compiler_params=params(),
        cost_estimate=short(2 * 2048 * 2048 * 384, 20 << 20),
    )(tokens, gain[None], shift[None], weight)


QB = 512
SCALE = HD ** -0.5

def masked(scores, first_query, first_key, length):
    query = first_query + lax.broadcasted_iota(jnp.int32, scores.shape, 0)
    key = first_key + lax.broadcasted_iota(jnp.int32, scores.shape, 1)
    return jnp.where((key <= query) & (key < length), scores, MASKED_SCORE)

def forward_kernel(length_ref, qkv_ref, out_ref, total_ref):
    length = length_ref[0]
    for i in range(2048 // QB):
        q = qkv_ref[i * QB : (i + 1) * QB, :HD]
        parts = []
        for j in range(i + 1):
            k = qkv_ref[j * QB : (j + 1) * QB, HD : 2 * HD]
            parts.append(masked(dot(q, k, (1, 1)) * SCALE, i * QB, j * QB, length))
        peak = functools.reduce(jnp.maximum, [jnp.max(p, axis=-1, keepdims=True) for p in parts])
        total = jnp.zeros((QB, 1), F32)
        acc = jnp.zeros((QB, HD), F32)
        for j in range(i + 1):
            e = jnp.exp(parts[j] - peak)
            total += jnp.sum(e, axis=-1, keepdims=True)
            acc += dot(e.astype(BF), qkv_ref[j * QB : (j + 1) * QB, 2 * HD :], (1, 0))
        out = (acc / total).astype(BF)
        for b in range(QB // HD):
            block = i * (QB // HD) + b
            out_ref[block % 8, block // 8] = out[b * HD : (b + 1) * HD]
        total_ref[i * QB : (i + 1) * QB] = peak + jnp.log(total)

def attend(qkv, lengths):
    return pl.pallas_call(
        forward_kernel,
        in_specs=[pl.BlockSpec(memory_space=pltpu.SMEM), pl.BlockSpec(memory_space=pltpu.VMEM)],
        out_specs=[pl.BlockSpec(memory_space=pltpu.VMEM)] * 2,
        out_shape=[jax.ShapeDtypeStruct((8, 2, 128, HD), BF), jax.ShapeDtypeStruct((2048, 1), F32)],
        compiler_params=params(),
        cost_estimate=short(2 * 2 * 2048 * 2048 * 128, 3 << 20),
    )(lengths, qkv)

def backward_kernel(length_ref, qkv_ref, grad_ref, total_ref, out_ref, sent_ref, gk, gv, probs, gprobs):
    length = length_ref[0]
    n = 2048 // QB
    gk[...] = jnp.zeros_like(gk)
    gv[...] = jnp.zeros_like(gv)
    for i in range(n):
        rows = slice(i * QB, (i + 1) * QB)
        q = qkv_ref[rows, :HD]
        blocks = [i * (QB // HD) + b for b in range(QB // HD)]
        g = jnp.concatenate([grad_ref[b % 8, b // 8] for b in blocks], axis=0)
        total = total_ref[rows]
        centre = jnp.zeros((QB, 1), F32)
        for j in range(i + 1):
            keys = slice(j * QB, (j + 1) * QB)
            s = masked(dot(q, qkv_ref[keys, HD : 2 * HD], (1, 1)) * SCALE, i * QB, j * QB, length)
            p = jnp.exp(s - total)
            gp = dot(g, qkv_ref[keys, 2 * HD :], (1, 1))
            centre += jnp.sum(p * gp, axis=-1, keepdims=True)
            probs[:, keys] = p
            gprobs[:, keys] = gp
        gq = jnp.zeros((QB, HD), F32)
        for j in range(i + 1):
            keys = slice(j * QB, (j + 1) * QB)
            p = probs[:, keys]
            gs = (p * (gprobs[:, keys] - centre)).astype(BF)
            gq += dot(gs, qkv_ref[keys, HD : 2 * HD], (1, 0))
            gk[keys] += dot(gs, q, (0, 0))
            gv[keys] += dot(p.astype(BF), g, (0, 0))
        out_ref[rows, :HD] = (gq * SCALE).astype(BF)
    out_ref[:, HD : 2 * HD] = (gk[...] * SCALE).astype(BF)
    out_ref[:, 2 * HD :] = gv[...].astype(BF)

    @pl.when(length_ref[1] == 0)
    def _():
        sent_ref[...] = out_ref[1024:]

    @pl.when(length_ref[1] == 1)
    def _():
        sent_ref[...] = out_ref[:1024]

def attend_back(qkv, grad, totals, lengths):
    return pl.pallas_call(
        backward_kernel,
        in_specs=[pl.BlockSpec(memory_space=pltpu.SMEM)] + [pl.BlockSpec(memory_space=pltpu.VMEM)] * 3,
        out_specs=[pl.BlockSpec(memory_space=pltpu.VMEM)] * 2,
        out_shape=[jax.ShapeDtypeStruct((2048, 3 * HD), BF), jax.ShapeDtypeStruct((1024, 3 * HD), BF)],
        scratch_shapes=[pltpu.VMEM((2048, HD), F32), pltpu.VMEM((2048, HD), F32), pltpu.VMEM((QB, 2048), F32), pltpu.VMEM((QB, 2048), F32)],
        compiler_params=params(),
        cost_estimate=short(5 * 2 * 2048 * 1280 * 128, 4 << 20),
    )(lengths, qkv, grad, totals)


GELU_A = 0.7978845608028654
GELU_B = 0.044715

def front_kernel(place_ref, n_ref, mine_ref, other_ref, uo, up, do, dp, act_ref, gh_ref, part_ref, inc_ref):
    core = place_ref[0]
    inc_ref[0, core] = mine_ref[0]
    inc_ref[0, 1 - core] = other_ref[0]
    n = n_ref[0].reshape(256, 2048)
    inc = inc_ref[0].reshape(256, 2048)
    part = jnp.zeros((256, 2048), F32)
    for h, (u, d) in enumerate(((uo, do), (up, dp))):
        cols = slice(h * 512, (h + 1) * 512)
        hidden = dot(n, u[...], (1, 0))
        square = hidden * hidden
        t = jnp.tanh(GELU_A * (hidden + GELU_B * hidden * square))
        act_ref[:, cols] = (0.5 * hidden * (1 + t)).astype(BF)
        slope = 0.5 * (1 + t) + 0.5 * hidden * (1 - t * t) * (GELU_A * (1 + 3 * GELU_B * square))
        gh = (dot(inc, d[...], (1, 1)) * slope).astype(BF)
        gh_ref[:, cols] = gh
        part += dot(gh, u[...], (1, 1))
    part_ref[0] = part.astype(BF).reshape(2, 128, 2048)

def front(place, normed, mine, other, uo, up, do, dp):
    whole = lambda a: pl.BlockSpec(a.shape, lambda i, p: (0,) * a.ndim)
    blk = pl.BlockSpec((1, 2, 128, 2048), lambda i, p: (i, 0, 0, 0))
    one = pl.BlockSpec((1, 128, 2048), lambda i, p: ((i + 4 - p[1]) % 4, 0, 0))
    col = pl.BlockSpec((256, 1024), lambda i, p: (i, 0))
    return pl.pallas_call(
        front_kernel,
        grid_spec=pltpu.PrefetchScalarGridSpec(
            num_scalar_prefetch=1, grid=(4,),
            in_specs=[blk, one, one, whole(uo), whole(up), whole(do), whole(dp)],
            out_specs=[col, col, blk, blk],
        ),
        out_shape=[jax.ShapeDtypeStruct((1024, 1024), BF)] * 2 + [jax.ShapeDtypeStruct((4, 2, 128, 2048), BF)] * 2,
        compiler_params=params(),
        cost_estimate=short(6 * 1024 * 1024 * 2048, 28 << 20),
    )(place, normed, mine, other, uo, up, do, dp)


def mixed_kernel(place_ref, act_ref, do, dp, mine_ref, other_ref, rows):
    a = act_ref[...]
    rows[...] = (dot(a[:, :512], do[...], (1, 0)) + dot(a[:, 512:], dp[...], (1, 0))).astype(BF).reshape(2, 128, 2048)
    mine_ref[0] = rows[place_ref[0]]
    other_ref[0] = rows[1 - place_ref[0]]

def mix(place, act, do, dp):
    whole = lambda a: pl.BlockSpec(a.shape, lambda i, p: (0,) * a.ndim)
    return pl.pallas_call(
        mixed_kernel,
        grid_spec=pltpu.PrefetchScalarGridSpec(
            num_scalar_prefetch=1, grid=(4,),
            in_specs=[pl.BlockSpec((256, 1024), lambda i, p: (i, 0)), whole(do), whole(dp)],
            out_specs=[pl.BlockSpec((1, 128, 2048), lambda i, p: (i, 0, 0))] * 2,
            scratch_shapes=[pltpu.VMEM((2, 128, 2048), BF)],
        ),
        out_shape=[jax.ShapeDtypeStruct((4, 128, 2048), BF)] * 2,
        compiler_params=params(),
        cost_estimate=short(2 * 1024 * 1024 * 2048, 10 << 20, 1),
    )(place, act, do, dp)

def branch_kernel(place_ref, heads_ref, w_ref, mine_ref, other_ref, left, out):
    @pl.when(pl.program_id(0) == 0)
    def _():
        for h in range(8):
            left[:, h * HD : (h + 1) * HD] = heads_ref[h].reshape(256, HD)

    out[...] = dot(left[...], w_ref[...], (1, 0)).reshape(2, 128, 512)
    mine_ref[...] = out[place_ref[0]]
    other_ref[...] = out[1 - place_ref[0]].astype(BF)

def branch(place, heads, w):
    col = pl.BlockSpec((128, 512), lambda i, p: (0, i))
    return pl.pallas_call(
        branch_kernel,
        grid_spec=pltpu.PrefetchScalarGridSpec(
            num_scalar_prefetch=1, grid=(4,),
            in_specs=[pl.BlockSpec((8, 2, 128, HD), lambda i, p: (0, 0, 0, 0)), pl.BlockSpec((1024, 512), lambda i, p: (0, i))],
            out_specs=[col, col],
            scratch_shapes=[pltpu.VMEM((256, 1024), BF), pltpu.VMEM((2, 128, 512), F32)],
        ),
        out_shape=[jax.ShapeDtypeStruct((128, 2048), F32), jax.ShapeDtypeStruct((128, 2048), BF)],
        compiler_params=params(),
        cost_estimate=short(2 * 256 * 1024 * 2048, 6 << 20),
    )(place, heads, w)

def grads_kernel(place_ref, n_ref, inc_ref, act_ref, gh_ref, mine_ref, partner_ref, keep_ref, send_ref):
    def down(ref):
        ref[...] = dot(act_ref[...], inc_ref[...], (0, 0)).astype(BF)

    @pl.when(pl.program_id(0) < 2)
    def _():
        down(mine_ref)

    @pl.when(pl.program_id(0) >= 2)
    def _():
        down(partner_ref)

    up = dot(gh_ref[...], n_ref[...], (0, 0)).astype(BF)
    even, odd = (
        jnp.concatenate([up[:, (2 * i + low) * 256 : (2 * i + low + 1) * 256] for i in range(4)], axis=1)
        for low in range(2)
    )

    @pl.when(place_ref[0] == 0)
    def _():
        keep_ref[...] = even
        send_ref[...] = odd

    @pl.when(place_ref[0] == 1)
    def _():
        keep_ref[...] = odd
        send_ref[...] = even

def weight_grads(place, n, inc, act, gh):
    rows = pl.BlockSpec((1024, 2048), lambda j, p: (0, 0))
    cols = pl.BlockSpec((1024, 256), lambda j, p: (0, j))
    part = pl.BlockSpec((256, 1024), lambda j, p: (j, 0))
    return pl.pallas_call(
        grads_kernel,
        grid_spec=pltpu.PrefetchScalarGridSpec(
            num_scalar_prefetch=1, grid=(4,),
            in_specs=[rows, rows, cols, cols],
            out_specs=[
                pl.BlockSpec((256, 2048), lambda j, p: (jnp.minimum(j, 1), 0)),
                pl.BlockSpec((256, 2048), lambda j, p: (jnp.maximum(j - 2, 0), 0)),
                part, part,
            ],
        ),
        out_shape=[jax.ShapeDtypeStruct((512, 2048), BF)] * 2 + [jax.ShapeDtypeStruct((1024, 1024), BF)] * 2,
        compiler_params=params(),
        cost_estimate=short(4 * 1024 * 1024 * 2048, 20 << 20),
    )(place, n, inc, act, gh)


def cut_kernel(place_ref, down_ref, down_got_ref, up_ref, up_got_ref, down_keep, down_send, up_keep, up_send):
    down = add(down_ref[...], down_got_ref[...])
    up = add(up_ref[...], up_got_ref[...])
    low = jnp.concatenate([up[:, :256], up[:, 512:768]], axis=1)
    high = jnp.concatenate([up[:, 256:512], up[:, 768:]], axis=1)

    @pl.when(place_ref[0] == 0)
    def _():
        down_keep[...] = down[:, :1024]
        down_send[...] = down[:, 1024:]

    @pl.when(place_ref[0] == 1)
    def _():
        down_keep[...] = down[:, 1024:]
        down_send[...] = down[:, :1024]

    @pl.when(place_ref[1] == 0)
    def _():
        up_keep[...] = low
        up_send[...] = high

    @pl.when(place_ref[1] == 1)
    def _():
        up_keep[...] = high
        up_send[...] = low

def cut(place, down, down_got, up, up_got):
    wide = pl.BlockSpec((128, 2048), lambda i, p: (i, 0))
    half = pl.BlockSpec((128, 1024), lambda i, p: (i, 0))
    four = pl.BlockSpec((256, 1024), lambda i, p: (i, 0))
    two = pl.BlockSpec((256, 512), lambda i, p: (i, 0))
    return pl.pallas_call(
        cut_kernel,
        grid_spec=pltpu.PrefetchScalarGridSpec(
            num_scalar_prefetch=1, grid=(4,),
            in_specs=[wide, wide, four, four],
            out_specs=[half, half, two, two],
        ),
        out_shape=[jax.ShapeDtypeStruct((512, 1024), BF)] * 2 + [jax.ShapeDtypeStruct((1024, 512), BF)] * 2,
        compiler_params=params(),
    )(place, down, down_got, up, up_got)


def heads_kernel(place_ref, mine_ref, other_ref, w_ref, out_ref, left):
    @pl.when(pl.program_id(0) == 0)
    def _():
        left[place_ref[0]] = mine_ref[...]
        left[1 - place_ref[0]] = other_ref[...]

    part = dot(left[...].reshape(256, 2048), w_ref[...], (1, 1)).astype(BF)
    for h in range(4):
        out_ref[h] = part[:, h * HD : (h + 1) * HD].reshape(2, 128, HD)

def to_heads(place, mine, other, w):
    rows = pl.BlockSpec((128, 2048), lambda i, p: (0, 0))
    return pl.pallas_call(
        heads_kernel,
        grid_spec=pltpu.PrefetchScalarGridSpec(
            num_scalar_prefetch=1, grid=(2,),
            in_specs=[rows, rows, pl.BlockSpec((512, 2048), lambda i, p: (i, 0))],
            out_specs=pl.BlockSpec((4, 2, 128, HD), lambda i, p: (i, 0, 0, 0)),
            scratch_shapes=[pltpu.VMEM((2, 128, 2048), BF)],
        ),
        out_shape=jax.ShapeDtypeStruct((8, 2, 128, HD), BF),
        compiler_params=params(),
    )(place, mine, other, w)


def both_kernel(own_ref, partner_ref, out_ref):
    for c in range(3):
        out_ref[c * HD : (c + 1) * HD] = own_ref[c].T
        out_ref[(c + 3) * HD : (c + 4) * HD] = partner_ref[c].T

def both_weights(own, partner):
    part = pl.BlockSpec((3, 256, HD), lambda i: (0, i, 0))
    return pl.pallas_call(
        both_kernel, grid=(8,),
        in_specs=[part, part],
        out_specs=pl.BlockSpec((6 * HD, 256), lambda i: (0, i)),
        out_shape=jax.ShapeDtypeStruct((6 * HD, 2048), BF),
        compiler_params=params(),
    )(own, partner)


def first_kernel(place_ref, mine_ref, got_ref, w_ref, out_ref, left):
    left[:, : 3 * HD] = mine_ref[...]
    left[:, 3 * HD :] = got_ref[...]
    out_ref[...] = dot(left[...], w_ref[...], (1, 0)).astype(BF)

def first_back(place, mine, got, weights):
    return pl.pallas_call(
        first_kernel,
        grid_spec=pltpu.PrefetchScalarGridSpec(
            num_scalar_prefetch=1, grid=(2,),
            in_specs=[
                pl.BlockSpec((512, 3 * HD), lambda i, p: (p[0] * 2 + i, 0)),
                pl.BlockSpec((512, 3 * HD), lambda i, p: (i, 0)),
                pl.BlockSpec((6 * HD, 2048), lambda i, p: (0, 0)),
            ],
            out_specs=pl.BlockSpec((512, 2048), lambda i, p: (i, 0)),
            scratch_shapes=[pltpu.VMEM((512, 6 * HD), BF)],
        ),
        out_shape=jax.ShapeDtypeStruct((1024, 2048), BF),
        compiler_params=params(),
        cost_estimate=short(2 * 1024 * 2048 * 768, 8 << 20, 1),
    )(place, mine, got, weights)


def stack_kernel(*refs):
    for i, ref in enumerate(refs[:-1]):
        refs[-1][i] = ref[...]

def stack(*arrays):
    return pl.pallas_call(
        stack_kernel,
        in_specs=[pl.BlockSpec(memory_space=pltpu.VMEM)] * len(arrays),
        out_specs=pl.BlockSpec(memory_space=pltpu.VMEM),
        out_shape=jax.ShapeDtypeStruct((len(arrays), *arrays[0].shape), arrays[0].dtype),
        compiler_params=params(),
    )(*arrays)

def out_kernel(place_ref, mine_ref, partner_ref, grad_ref, out_ref):
    grad = grad_ref[...]
    out_ref[0, place_ref[0]] = dot(mine_ref[...], grad, (0, 0)).astype(BF)
    out_ref[0, 1 - place_ref[0]] = dot(partner_ref[...], grad, (0, 0)).astype(BF)

def out_grads(place, mine, partner, grad):
    heads = pl.BlockSpec((1024, HD), lambda i, p: (0, 0))
    return pl.pallas_call(
        out_kernel,
        grid_spec=pltpu.PrefetchScalarGridSpec(
            num_scalar_prefetch=1, grid=(8,),
            in_specs=[heads, heads, pl.BlockSpec((1024, 256), lambda i, p: (0, i))],
            out_specs=pl.BlockSpec((1, 2, HD, 256), lambda i, p: (i, 0, 0, 0)),
        ),
        out_shape=jax.ShapeDtypeStruct((8, 2, HD, 256), BF),
        compiler_params=params(),
        cost_estimate=short(2 * 1024 * 256 * 2048, 6 << 20, 1),
    )(place, mine, partner, grad)


def qkv_grads_kernel(n_ref, gp_ref, w_ref, gain_ref, shift_ref, second_ref, out_ref, left, columns, sums):
    at = pl.program_id(0)

    @pl.when(at == 0)
    def _():
        left[...] = gp_ref[...].T
        columns[...] = jnp.sum(left[...].astype(F32), axis=1, keepdims=True)

    grad = dot(left[...], n_ref[...], (1, 0))
    out_ref[at, : 3 * HD] = grad.astype(BF)
    w = jnp.concatenate([w_ref[c].T for c in range(3)], axis=0).astype(F32)
    shift = jnp.sum(w * columns[...], axis=0, keepdims=True)
    gain = (jnp.sum(w * grad, axis=0, keepdims=True) - shift_ref[...] * shift) / gain_ref[...]
    for i, row in enumerate((gain, second_ref[0], shift, second_ref[1])):
        sums[pl.ds(8 * i + at, 1)] = row

    @pl.when(at == 7)
    def _():
        for i in range(8):
            out_ref[i, 3 * HD :] = sums[...].astype(BF)

def qkv_grads(normed, gp, w, gain, shift, second):
    row = pl.BlockSpec((1, 256), lambda i: (0, i))
    return pl.pallas_call(
        qkv_grads_kernel, grid=(8,),
        in_specs=[
            pl.BlockSpec((2048, 256), lambda i: (0, i)),
            pl.BlockSpec((2048, 384), lambda i: (0, 0)),
            pl.BlockSpec((3, 256, HD), lambda i: (0, i, 0)),
            row, row,
            pl.BlockSpec((2, 1, 256), lambda i: (0, 0, i)),
        ],
        out_specs=pl.BlockSpec((8, 3 * HD + 32, 256), lambda i: (0, 0, 0)),
        out_shape=jax.ShapeDtypeStruct((8, 3 * HD + 32, 256), BF),
        scratch_shapes=[pltpu.VMEM((384, 2048), BF), pltpu.VMEM((384, 1), F32), pltpu.VMEM((32, 256), F32)],
        compiler_params=params(),
        cost_estimate=short(2 * 2048 * 2048 * 384, 12 << 20, 1),
    )(normed, gp, w, gain[None], shift[None], second)


def scatter(values, axes):
    return lax.psum_scatter(values, axes, scatter_dimension=0, tiled=True).astype(F32)


def pick(values, index, axis):
    return lax.dynamic_index_in_dim(values, index, axis, False)


def after(values, *others):
    return lax.optimization_barrier((values, *others))[0]


def columns(values, at):
    size = values.shape[1] // 2
    return lax.dynamic_slice_in_dim(values, at * size, size, 1)


def over_x(own, partner, x_hi, axis):
    size = own.shape[axis] // 2
    own = add(own, x_partner(partner))

    def part(at):
        return lax.dynamic_slice_in_dim(own, at * size, size, axis)

    return part(x_hi).astype(F32) + x_far(part(1 - x_hi)).astype(F32)


def sum_over_tensor(values):
    values = values + core_swap(values)
    values = (values + z_far(values)) + (z_up(values) + z_down(values))
    return values + x_pair(values)


def body(
    tokens,
    ln1_gain,
    ln1_shift,
    qkv_weight,
    out_weight,
    ln2_gain,
    ln2_shift,
    up_weight,
    down_weight,
    lengths,
    cotangent,
):
    x_hi, y, x_lo, z, core = (lax.axis_index(axis) for axis in AXES)
    tensor = x_lo * 8 + z * 2 + core
    length = lengths[0]

    place = jnp.stack([core, z, x_lo, y % 2])

    out_own = lax.all_gather(out_weight, ("z", "core"), axis=0, tiled=True)
    live_rows = (tensor * 128 + jnp.arange(128, dtype=jnp.int32) < length).astype(F32)[:, None]
    incoming_rows = cotangent.astype(F32) * live_rows
    sent_rows = incoming_rows.astype(BF)
    later_rows = after(sent_rows, out_own)
    along_z = [z_down(later_rows), z_far(sent_rows), z_up(later_rows)]
    up_partner, down_partner, qkv_partner = x_partner(up_weight), x_partner(down_weight), x_partner(qkv_weight)

    normed_first, projected = project(tokens, ln1_gain, ln1_shift, qkv_weight)
    attended, totals = attend(projected, lengths)
    heads = lax.all_to_all(attended, ("z", "core"), 0, 0)
    branch_mine, branch_other = branch(place[2:], after(heads, up_partner, along_z[1]), out_own)
    branch_other = after(x_pair(branch_other), down_partner, along_z[0], along_z[2])
    token_rows = lax.dynamic_slice_in_dim(tokens, tensor * 128, 128, 0).astype(F32)
    middle_rows = token_rows + (branch_mine + branch_other.astype(F32))
    unit_second, inverse_second = norm_stats(middle_rows)
    normed_rows = (unit_second * ln2_gain + ln2_shift).astype(BF)
    along_z = stack(after(sent_rows, normed_rows), *along_z)
    from_core = core_swap(along_z)
    qkv_both = both_weights(qkv_weight, after(qkv_partner, normed_rows))

    normed_second = lax.all_gather(normed_rows, ("z", "core"), axis=0, tiled=True)
    activated, grad_hidden, grad_normed_part, incoming = front(
        place,
        after(normed_second, qkv_both).reshape(4, 2, 128, 2048),
        along_z,
        from_core,
        up_weight,
        up_partner,
        down_weight,
        down_partner,
    )
    incoming = incoming.reshape(1024, 2048)
    grad_normed_second = scatter(grad_normed_part.reshape(1024, 2048), ("z", "core"))
    down_kept, down_sent, up_kept, up_sent = weight_grads(
        place[3:], normed_second, incoming, activated, grad_hidden
    )
    down_got, up_got = x_partner(down_sent), y_pair(up_sent)
    mixed_mine, mixed_other = mix(place, after(activated, down_sent), down_weight, down_partner)
    grad_normed_second = after(grad_normed_second, down_got, up_got, mixed_mine)

    grad_middle = incoming_rows + norm_back(grad_normed_second, ln2_gain, unit_second, inverse_second)
    gain_second = jnp.sum(grad_normed_second * unit_second, axis=0)
    shift_second = jnp.sum(grad_normed_second, axis=0)
    grad_branch = grad_middle.astype(BF)
    branch_back = lax.all_gather(grad_branch, ("z", "core"), axis=0, tiled=True)

    branch_got = x_pair(grad_branch)
    down_kept, down_sent, up_kept, up_sent = cut(
        jnp.stack([x_hi, y // 2]), down_kept, after(down_got, grad_branch), up_kept, up_got
    )
    down_got, up_got = x_far(down_sent), y_far(up_sent)
    mixed_got = core_swap(after(mixed_other, grad_branch))
    by_head = to_heads(place[2:], grad_branch, after(branch_got, down_sent), out_own)
    grad_attended = lax.all_to_all(by_head, ("z", "core"), 0, 0)
    mixed = add(mixed_mine, after(mixed_got, by_head)).reshape(2, 2, 128, 2048)
    mixed_got = z_pair(pick(mixed, 1 - z % 2, 1))
    partner_heads = x_pair(pick(attended, 1 - x_lo, 1).reshape(1024, HD))

    grad_projected, projected_sent = attend_back(
        projected, after(grad_attended, mixed, partner_heads), totals, jnp.stack([length, x_lo])
    )
    projected_got = x_pair(projected_sent)
    second = jnp.stack([gain_second, shift_second])[:, None]
    qkv_sent = qkv_grads(normed_first, grad_projected, qkv_weight, ln1_gain, ln1_shift, second)
    qkv_got = lax.all_to_all(qkv_sent, BATCH, 0, 0)
    down_sums = add(down_kept, after(down_got, qkv_sent))
    up_sums = add(up_kept, after(up_got, qkv_sent))
    projected_got = after(projected_got, qkv_sent, down_sums, up_sums, mixed_got)
    grad_first_part = first_back(place[2:], grad_projected, projected_got, qkv_both)
    grad_normed_first = scatter(grad_first_part, ("z", "core"))

    grad_up = over_x(up_sums[:512], up_sums[512:], x_hi, 1).T
    down_sums = add(columns(down_sums, y // 2), y_far(columns(down_sums, 1 - y // 2)))
    grad_down = columns(down_sums, y % 2).astype(F32) + y_near(columns(down_sums, 1 - y % 2)).astype(F32)
    out_sent = out_grads(
        x_lo[None], after(pick(attended, x_lo, 1).reshape(1024, HD), grad_first_part), partner_heads, branch_back
    )
    out_got = lax.all_to_all(after(out_sent, qkv_got).reshape(16, HD, 256), ("x_hi", "y", "x_lo"), 0, 0)
    qkv_sums = jnp.sum(after(qkv_got, out_sent).astype(F32), axis=0)
    sums = sum_over_tensor(qkv_sums[3 * HD :].reshape(4, 2048))
    grad_qkv = qkv_sums[: 3 * HD].reshape(3, HD, 256).transpose(0, 2, 1)
    mixed = add(pick(mixed, z % 2, 1), mixed_got)
    output = (
        middle_rows + pick(mixed, z // 2, 0).astype(F32) + z_far(pick(mixed, 1 - z // 2, 0)).astype(F32)
    ).astype(BF)
    grad_out = jnp.sum(out_got.astype(F32), axis=0)

    unit_rows, inverse_rows = norm_stats(token_rows)
    grad_tokens = (grad_middle + norm_back(grad_normed_first, ln1_gain, unit_rows, inverse_rows)).astype(BF)
    return (output, grad_tokens, grad_qkv, grad_out, grad_up, grad_down, sums[:2], sums[2:])


def solution(mesh):
    return jax.shard_map(
        body,
        mesh=Mesh(mesh.devices.reshape(2, 4, 2, 4, 2), AXES),
        in_specs=(
            P(BATCH, None),
            P(),
            P(),
            P(None, None, TENSOR),
            P(TENSOR, None),
            P(),
            P(),
            P(None, TENSOR),
            P(TENSOR, None),
            P(BATCH),
            P(AXES, None),
        ),
        out_specs=(
            P(AXES, None),
            P(AXES, None),
            P(None, BATCH, TENSOR),
            P(TENSOR, BATCH),
            P(BATCH, TENSOR),
            P(TENSOR, BATCH),
            P(),
            P(),
        ),
        check_vma=False,
    )
```

```python
import functools

import jax
import jax.numpy as jnp
from jax import lax
from jax.experimental import pallas as pl
from jax.experimental.pallas import tpu as pltpu
from jax.sharding import Mesh
from jax.sharding import PartitionSpec as P

HD = 128
EPS = 1e-05
MASKED_SCORE = -1e30
BF = jnp.bfloat16
F32 = jnp.float32

AXES = ("x_hi", "y", "x_lo", "z", "core")
BATCH, TENSOR = AXES[:2], AXES[2:]


def core_swap(values):
    return lax.ppermute(values, "core", [(0, 1), (1, 0)])


def x_pair(values):
    return lax.ppermute(values, "x_lo", [(0, 1), (1, 0)])


def y_near(values):
    return lax.ppermute(values, "y", [(i, i ^ 1) for i in range(4)])


def x_partner(values):
    pairs = [(r * 2 + c, ((r + (1, -1)[c]) % 4) * 2 + c) for r in range(4) for c in range(2)]
    return lax.ppermute(values, ("x_hi", "x_lo", "core"), pairs)


def neighbours(axis):
    pairs = [(i * 2 + c, ((i ^ 1) if c == 0 else 3 - i) * 2 + c) for i in range(4) for c in range(2)]
    return lambda values: lax.ppermute(values, (axis, "core"), pairs)


y_pair, z_pair = neighbours("y"), neighbours("z")


def shift(axes, sizes, step):
    return lambda values: lax.ppermute(values, axes, [(i, (i + step) % sizes) for i in range(sizes)])


z_up, z_down, z_far = (shift("z", 4, step) for step in (1, -1, 2))
y_far, x_far = shift("y", 4, 2), shift(("x_hi", "x_lo"), 4, 2)


def norm_stats(values):
    centre = jnp.mean(values, axis=-1, keepdims=True)
    offsets = values - centre
    variance = jnp.mean(offsets * offsets, axis=-1, keepdims=True)
    inverse = lax.rsqrt(variance + EPS)
    return (offsets * inverse, inverse)


def norm_back(grad_normed, gain, unit_rows, inverse):
    scaled = grad_normed * gain
    return inverse * (
        scaled
        - jnp.mean(scaled, axis=-1, keepdims=True)
        - unit_rows * jnp.mean(scaled * unit_rows, axis=-1, keepdims=True)
    )


def dot(left, right, dims):
    return lax.dot_general(left, right, ((dims[:1], dims[1:]), ((), ())), preferred_element_type=F32)


def short(flops, moved, by=64):
    return pl.CostEstimate(flops=flops // by, bytes_accessed=moved // by, transcendentals=0)


def add(left, right):
    return (left.astype(F32) + right.astype(F32)).astype(BF)


def params(limit=60, **kw):
    return pltpu.CompilerParams(vmem_limit_bytes=limit * 2**20, **kw)


def qkv_kernel(x_ref, gain_ref, shift_ref, w_ref, normed_ref, out_ref, weights):
    @pl.when(pl.program_id(0) == 0)
    def _():
        for c in range(3):
            weights[:, c * HD : (c + 1) * HD] = w_ref[c]

    x = x_ref[...].astype(F32)
    offsets = x - jnp.mean(x, axis=-1, keepdims=True)
    inverse = lax.rsqrt(jnp.mean(offsets * offsets, axis=-1, keepdims=True) + EPS)
    normed = (offsets * inverse * gain_ref[...] + shift_ref[...]).astype(BF)
    normed_ref[...] = normed
    out_ref[...] = dot(normed, weights[...], (1, 0)).astype(BF)

def project(tokens, gain, shift, weight):
    rows = 256
    return pl.pallas_call(
        qkv_kernel,
        grid=(2048 // rows,),
        in_specs=[
            pl.BlockSpec((rows, 2048), lambda i: (i, 0)),
            pl.BlockSpec((1, 2048), lambda i: (0, 0)),
            pl.BlockSpec((1, 2048), lambda i: (0, 0)),
            pl.BlockSpec((3, 2048, HD), lambda i: (0, 0, 0)),
        ],
        out_specs=[
            pl.BlockSpec((rows, 2048), lambda i: (i, 0)),
            pl.BlockSpec((rows, 3 * HD), lambda i: (i, 0)),
        ],
        out_shape=[jax.ShapeDtypeStruct((2048, 2048), BF), jax.ShapeDtypeStruct((2048, 3 * HD), BF)],
        scratch_shapes=[pltpu.VMEM((2048, 3 * HD), BF)],
        compiler_params=params(),
        cost_estimate=short(2 * 2048 * 2048 * 384, 20 << 20),
    )(tokens, gain[None], shift[None], weight)


QB = 512
SCALE = HD ** -0.5

def masked(scores, first_query, first_key, length):
    query = first_query + lax.broadcasted_iota(jnp.int32, scores.shape, 0)
    key = first_key + lax.broadcasted_iota(jnp.int32, scores.shape, 1)
    return jnp.where((key <= query) & (key < length), scores, MASKED_SCORE)

def forward_kernel(length_ref, qkv_ref, out_ref, total_ref):
    length = length_ref[0]
    for i in range(2048 // QB):
        q = qkv_ref[i * QB : (i + 1) * QB, :HD]
        parts = []
        for j in range(i + 1):
            k = qkv_ref[j * QB : (j + 1) * QB, HD : 2 * HD]
            parts.append(masked(dot(q, k, (1, 1)) * SCALE, i * QB, j * QB, length))
        peak = functools.reduce(jnp.maximum, [jnp.max(p, axis=-1, keepdims=True) for p in parts])
        total = jnp.zeros((QB, 1), F32)
        acc = jnp.zeros((QB, HD), F32)
        for j in range(i + 1):
            e = jnp.exp(parts[j] - peak)
            total += jnp.sum(e, axis=-1, keepdims=True)
            acc += dot(e.astype(BF), qkv_ref[j * QB : (j + 1) * QB, 2 * HD :], (1, 0))
        out = (acc / total).astype(BF)
        for b in range(QB // HD):
            block = i * (QB // HD) + b
            out_ref[block % 8, block // 8] = out[b * HD : (b + 1) * HD]
        total_ref[i * QB : (i + 1) * QB] = peak + jnp.log(total)

def attend(qkv, lengths):
    return pl.pallas_call(
        forward_kernel,
        in_specs=[pl.BlockSpec(memory_space=pltpu.SMEM), pl.BlockSpec(memory_space=pltpu.VMEM)],
        out_specs=[pl.BlockSpec(memory_space=pltpu.VMEM)] * 2,
        out_shape=[jax.ShapeDtypeStruct((8, 2, 128, HD), BF), jax.ShapeDtypeStruct((2048, 1), F32)],
        compiler_params=params(),
        cost_estimate=short(2 * 2 * 2048 * 2048 * 128, 3 << 20),
    )(lengths, qkv)

def backward_kernel(length_ref, qkv_ref, grad_ref, total_ref, out_ref, sent_ref, gk, gv, probs, gprobs):
    length = length_ref[0]
    n = 2048 // QB
    gk[...] = jnp.zeros_like(gk)
    gv[...] = jnp.zeros_like(gv)
    for i in range(n):
        rows = slice(i * QB, (i + 1) * QB)
        q = qkv_ref[rows, :HD]
        blocks = [i * (QB // HD) + b for b in range(QB // HD)]
        g = jnp.concatenate([grad_ref[b % 8, b // 8] for b in blocks], axis=0)
        total = total_ref[rows]
        centre = jnp.zeros((QB, 1), F32)
        for j in range(i + 1):
            keys = slice(j * QB, (j + 1) * QB)
            s = masked(dot(q, qkv_ref[keys, HD : 2 * HD], (1, 1)) * SCALE, i * QB, j * QB, length)
            p = jnp.exp(s - total)
            gp = dot(g, qkv_ref[keys, 2 * HD :], (1, 1))
            centre += jnp.sum(p * gp, axis=-1, keepdims=True)
            probs[:, keys] = p
            gprobs[:, keys] = gp
        gq = jnp.zeros((QB, HD), F32)
        for j in range(i + 1):
            keys = slice(j * QB, (j + 1) * QB)
            p = probs[:, keys]
            gs = (p * (gprobs[:, keys] - centre)).astype(BF)
            gq += dot(gs, qkv_ref[keys, HD : 2 * HD], (1, 0))
            gk[keys] += dot(gs, q, (0, 0))
            gv[keys] += dot(p.astype(BF), g, (0, 0))
        out_ref[rows, :HD] = (gq * SCALE).astype(BF)
    out_ref[:, HD : 2 * HD] = (gk[...] * SCALE).astype(BF)
    out_ref[:, 2 * HD :] = gv[...].astype(BF)

    @pl.when(length_ref[1] == 0)
    def _():
        sent_ref[...] = out_ref[1024:]

    @pl.when(length_ref[1] == 1)
    def _():
        sent_ref[...] = out_ref[:1024]

def attend_back(qkv, grad, totals, lengths):
    return pl.pallas_call(
        backward_kernel,
        in_specs=[pl.BlockSpec(memory_space=pltpu.SMEM)] + [pl.BlockSpec(memory_space=pltpu.VMEM)] * 3,
        out_specs=[pl.BlockSpec(memory_space=pltpu.VMEM)] * 2,
        out_shape=[jax.ShapeDtypeStruct((2048, 3 * HD), BF), jax.ShapeDtypeStruct((1024, 3 * HD), BF)],
        scratch_shapes=[pltpu.VMEM((2048, HD), F32), pltpu.VMEM((2048, HD), F32), pltpu.VMEM((QB, 2048), F32), pltpu.VMEM((QB, 2048), F32)],
        compiler_params=params(),
        cost_estimate=short(5 * 2 * 2048 * 1280 * 128, 4 << 20),
    )(lengths, qkv, grad, totals)


GELU_A = 0.7978845608028654
GELU_B = 0.044715

def front_kernel(place_ref, n_ref, mine_ref, other_ref, uo, up, do, dp, act_ref, gh_ref, part_ref, inc_ref):
    core = place_ref[0]
    inc_ref[0, core] = mine_ref[0]
    inc_ref[0, 1 - core] = other_ref[0]
    n = n_ref[0].reshape(256, 2048)
    inc = inc_ref[0].reshape(256, 2048)
    part = jnp.zeros((256, 2048), F32)
    for h, (u, d) in enumerate(((uo, do), (up, dp))):
        cols = slice(h * 512, (h + 1) * 512)
        hidden = dot(n, u[...], (1, 0))
        square = hidden * hidden
        t = jnp.tanh(GELU_A * (hidden + GELU_B * hidden * square))
        act_ref[:, cols] = (0.5 * hidden * (1 + t)).astype(BF)
        slope = 0.5 * (1 + t) + 0.5 * hidden * (1 - t * t) * (GELU_A * (1 + 3 * GELU_B * square))
        gh = (dot(inc, d[...], (1, 1)) * slope).astype(BF)
        gh_ref[:, cols] = gh
        part += dot(gh, u[...], (1, 1))
    part_ref[0] = part.astype(BF).reshape(2, 128, 2048)

def front(place, normed, mine, other, uo, up, do, dp):
    whole = lambda a: pl.BlockSpec(a.shape, lambda i, p: (0,) * a.ndim)
    blk = pl.BlockSpec((1, 2, 128, 2048), lambda i, p: (i, 0, 0, 0))
    one = pl.BlockSpec((1, 128, 2048), lambda i, p: ((i + 4 - p[1]) % 4, 0, 0))
    col = pl.BlockSpec((256, 1024), lambda i, p: (i, 0))
    return pl.pallas_call(
        front_kernel,
        grid_spec=pltpu.PrefetchScalarGridSpec(
            num_scalar_prefetch=1, grid=(4,),
            in_specs=[blk, one, one, whole(uo), whole(up), whole(do), whole(dp)],
            out_specs=[col, col, blk, blk],
        ),
        out_shape=[jax.ShapeDtypeStruct((1024, 1024), BF)] * 2 + [jax.ShapeDtypeStruct((4, 2, 128, 2048), BF)] * 2,
        compiler_params=params(),
        cost_estimate=short(6 * 1024 * 1024 * 2048, 28 << 20),
    )(place, normed, mine, other, uo, up, do, dp)


def mixed_kernel(place_ref, act_ref, do, dp, mine_ref, other_ref, rows):
    a = act_ref[...]
    rows[...] = (dot(a[:, :512], do[...], (1, 0)) + dot(a[:, 512:], dp[...], (1, 0))).astype(BF).reshape(2, 128, 2048)
    mine_ref[0] = rows[place_ref[0]]
    other_ref[0] = rows[1 - place_ref[0]]

def mix(place, act, do, dp):
    whole = lambda a: pl.BlockSpec(a.shape, lambda i, p: (0,) * a.ndim)
    return pl.pallas_call(
        mixed_kernel,
        grid_spec=pltpu.PrefetchScalarGridSpec(
            num_scalar_prefetch=1, grid=(4,),
            in_specs=[pl.BlockSpec((256, 1024), lambda i, p: (i, 0)), whole(do), whole(dp)],
            out_specs=[pl.BlockSpec((1, 128, 2048), lambda i, p: (i, 0, 0))] * 2,
            scratch_shapes=[pltpu.VMEM((2, 128, 2048), BF)],
        ),
        out_shape=[jax.ShapeDtypeStruct((4, 128, 2048), BF)] * 2,
        compiler_params=params(),
        cost_estimate=short(2 * 1024 * 1024 * 2048, 10 << 20, 1),
    )(place, act, do, dp)

def branch_kernel(place_ref, heads_ref, w_ref, mine_ref, other_ref, left, out):
    @pl.when(pl.program_id(0) == 0)
    def _():
        for h in range(8):
            left[:, h * HD : (h + 1) * HD] = heads_ref[h].reshape(256, HD)

    out[...] = dot(left[...], w_ref[...], (1, 0)).reshape(2, 128, 512)
    mine_ref[...] = out[place_ref[0]]
    other_ref[...] = out[1 - place_ref[0]].astype(BF)

def branch(place, heads, w):
    col = pl.BlockSpec((128, 512), lambda i, p: (0, i))
    return pl.pallas_call(
        branch_kernel,
        grid_spec=pltpu.PrefetchScalarGridSpec(
            num_scalar_prefetch=1, grid=(4,),
            in_specs=[pl.BlockSpec((8, 2, 128, HD), lambda i, p: (0, 0, 0, 0)), pl.BlockSpec((1024, 512), lambda i, p: (0, i))],
            out_specs=[col, col],
            scratch_shapes=[pltpu.VMEM((256, 1024), BF), pltpu.VMEM((2, 128, 512), F32)],
        ),
        out_shape=[jax.ShapeDtypeStruct((128, 2048), F32), jax.ShapeDtypeStruct((128, 2048), BF)],
        compiler_params=params(),
        cost_estimate=short(2 * 256 * 1024 * 2048, 6 << 20),
    )(place, heads, w)

def grads_kernel(place_ref, n_ref, inc_ref, act_ref, gh_ref, mine_ref, partner_ref, keep_ref, send_ref):
    def down(ref):
        ref[...] = dot(act_ref[...], inc_ref[...], (0, 0)).astype(BF)

    @pl.when(pl.program_id(0) < 2)
    def _():
        down(mine_ref)

    @pl.when(pl.program_id(0) >= 2)
    def _():
        down(partner_ref)

    up = dot(gh_ref[...], n_ref[...], (0, 0)).astype(BF)
    even, odd = (
        jnp.concatenate([up[:, (2 * i + low) * 256 : (2 * i + low + 1) * 256] for i in range(4)], axis=1)
        for low in range(2)
    )

    @pl.when(place_ref[0] == 0)
    def _():
        keep_ref[...] = even
        send_ref[...] = odd

    @pl.when(place_ref[0] == 1)
    def _():
        keep_ref[...] = odd
        send_ref[...] = even

def weight_grads(place, n, inc, act, gh):
    rows = pl.BlockSpec((1024, 2048), lambda j, p: (0, 0))
    cols = pl.BlockSpec((1024, 256), lambda j, p: (0, j))
    part = pl.BlockSpec((256, 1024), lambda j, p: (j, 0))
    return pl.pallas_call(
        grads_kernel,
        grid_spec=pltpu.PrefetchScalarGridSpec(
            num_scalar_prefetch=1, grid=(4,),
            in_specs=[rows, rows, cols, cols],
            out_specs=[
                pl.BlockSpec((256, 2048), lambda j, p: (jnp.minimum(j, 1), 0)),
                pl.BlockSpec((256, 2048), lambda j, p: (jnp.maximum(j - 2, 0), 0)),
                part, part,
            ],
        ),
        out_shape=[jax.ShapeDtypeStruct((512, 2048), BF)] * 2 + [jax.ShapeDtypeStruct((1024, 1024), BF)] * 2,
        compiler_params=params(),
        cost_estimate=short(4 * 1024 * 1024 * 2048, 20 << 20),
    )(place, n, inc, act, gh)


def cut_kernel(place_ref, down_ref, down_got_ref, up_ref, up_got_ref, down_keep, down_send, up_keep, up_send):
    down = add(down_ref[...], down_got_ref[...])
    up = add(up_ref[...], up_got_ref[...])
    low = jnp.concatenate([up[:, :256], up[:, 512:768]], axis=1)
    high = jnp.concatenate([up[:, 256:512], up[:, 768:]], axis=1)

    @pl.when(place_ref[0] == 0)
    def _():
        down_keep[...] = down[:, :1024]
        down_send[...] = down[:, 1024:]

    @pl.when(place_ref[0] == 1)
    def _():
        down_keep[...] = down[:, 1024:]
        down_send[...] = down[:, :1024]

    @pl.when(place_ref[1] == 0)
    def _():
        up_keep[...] = low
        up_send[...] = high

    @pl.when(place_ref[1] == 1)
    def _():
        up_keep[...] = high
        up_send[...] = low

def cut(place, down, down_got, up, up_got):
    wide = pl.BlockSpec((128, 2048), lambda i, p: (i, 0))
    half = pl.BlockSpec((128, 1024), lambda i, p: (i, 0))
    four = pl.BlockSpec((256, 1024), lambda i, p: (i, 0))
    two = pl.BlockSpec((256, 512), lambda i, p: (i, 0))
    return pl.pallas_call(
        cut_kernel,
        grid_spec=pltpu.PrefetchScalarGridSpec(
            num_scalar_prefetch=1, grid=(4,),
            in_specs=[wide, wide, four, four],
            out_specs=[half, half, two, two],
        ),
        out_shape=[jax.ShapeDtypeStruct((512, 1024), BF)] * 2 + [jax.ShapeDtypeStruct((1024, 512), BF)] * 2,
        compiler_params=params(),
    )(place, down, down_got, up, up_got)


def cut_again_kernel(place_ref, down_ref, down_got_ref, up_ref, up_got_ref, down_keep, down_send, up_keep, up_send):
    down = add(down_ref[...], down_got_ref[...])
    up = add(up_ref[...], up_got_ref[...])
    half = down.shape[1] // 2

    def put(values, at, keep, send):
        @pl.when(at == 0)
        def _():
            keep[...] = values[:, :half]
            send[...] = values[:, half:]

        @pl.when(at == 1)
        def _():
            keep[...] = values[:, half:]
            send[...] = values[:, :half]

    put(down, place_ref[0], down_keep, down_send)
    if up.shape[0] == 1024:
        up_keep[...] = up[:512]
        up_send[...] = up[512:]
    else:
        put(up, place_ref[1], up_keep, up_send)

def cut_again(place, down, down_got, up, up_got):
    size = down.shape[1] // 2
    vmem = pl.BlockSpec(memory_space=pltpu.VMEM)
    return pl.pallas_call(
        cut_again_kernel,
        in_specs=[pl.BlockSpec(memory_space=pltpu.SMEM)] + [vmem] * 4,
        out_specs=[vmem] * 4,
        out_shape=[jax.ShapeDtypeStruct((512, size), BF)] * 4,
        compiler_params=params(),
    )(place, down, down_got, up, up_got)

def finish_kernel(down_ref, down_got_ref, up_ref, up_got_ref, down_out, up_out):
    down_out[...] = down_ref[...].astype(F32) + down_got_ref[...].astype(F32)
    up_out[...] = (up_ref[...].astype(F32) + up_got_ref[...].astype(F32)).T

def finish(*arrays):
    vmem = pl.BlockSpec(memory_space=pltpu.VMEM)
    return pl.pallas_call(
        finish_kernel,
        in_specs=[vmem] * 4,
        out_specs=[vmem] * 2,
        out_shape=[jax.ShapeDtypeStruct((512, 256), F32), jax.ShapeDtypeStruct((256, 512), F32)],
        compiler_params=params(),
    )(*arrays)


def heads_kernel(place_ref, mine_ref, other_ref, w_ref, out_ref, left):
    @pl.when(pl.program_id(0) == 0)
    def _():
        left[place_ref[0]] = mine_ref[...]
        left[1 - place_ref[0]] = other_ref[...]

    part = dot(left[...].reshape(256, 2048), w_ref[...], (1, 1)).astype(BF)
    for h in range(4):
        out_ref[h] = part[:, h * HD : (h + 1) * HD].reshape(2, 128, HD)

def to_heads(place, mine, other, w):
    rows = pl.BlockSpec((128, 2048), lambda i, p: (0, 0))
    return pl.pallas_call(
        heads_kernel,
        grid_spec=pltpu.PrefetchScalarGridSpec(
            num_scalar_prefetch=1, grid=(2,),
            in_specs=[rows, rows, pl.BlockSpec((512, 2048), lambda i, p: (i, 0))],
            out_specs=pl.BlockSpec((4, 2, 128, HD), lambda i, p: (i, 0, 0, 0)),
            scratch_shapes=[pltpu.VMEM((2, 128, 2048), BF)],
        ),
        out_shape=jax.ShapeDtypeStruct((8, 2, 128, HD), BF),
        compiler_params=params(),
    )(place, mine, other, w)


def both_kernel(own_ref, partner_ref, out_ref):
    for c in range(3):
        out_ref[c * HD : (c + 1) * HD] = own_ref[c].T
        out_ref[(c + 3) * HD : (c + 4) * HD] = partner_ref[c].T

def both_weights(own, partner):
    part = pl.BlockSpec((3, 256, HD), lambda i: (0, i, 0))
    return pl.pallas_call(
        both_kernel, grid=(8,),
        in_specs=[part, part],
        out_specs=pl.BlockSpec((6 * HD, 256), lambda i: (0, i)),
        out_shape=jax.ShapeDtypeStruct((6 * HD, 2048), BF),
        compiler_params=params(),
    )(own, partner)


def first_kernel(place_ref, mine_ref, got_ref, w_ref, out_ref, left):
    left[:, : 3 * HD] = mine_ref[...]
    left[:, 3 * HD :] = got_ref[...]
    out_ref[...] = dot(left[...], w_ref[...], (1, 0)).astype(BF)

def first_back(place, mine, got, weights):
    return pl.pallas_call(
        first_kernel,
        grid_spec=pltpu.PrefetchScalarGridSpec(
            num_scalar_prefetch=1, grid=(2,),
            in_specs=[
                pl.BlockSpec((512, 3 * HD), lambda i, p: (p[0] * 2 + i, 0)),
                pl.BlockSpec((512, 3 * HD), lambda i, p: (i, 0)),
                pl.BlockSpec((6 * HD, 2048), lambda i, p: (0, 0)),
            ],
            out_specs=pl.BlockSpec((512, 2048), lambda i, p: (i, 0)),
            scratch_shapes=[pltpu.VMEM((512, 6 * HD), BF)],
        ),
        out_shape=jax.ShapeDtypeStruct((1024, 2048), BF),
        compiler_params=params(),
        cost_estimate=short(2 * 1024 * 2048 * 768, 8 << 20),
    )(place, mine, got, weights)


def stack_kernel(*refs):
    for i, ref in enumerate(refs[:-1]):
        refs[-1][i] = ref[...]

def stack(*arrays):
    return pl.pallas_call(
        stack_kernel,
        in_specs=[pl.BlockSpec(memory_space=pltpu.VMEM)] * len(arrays),
        out_specs=pl.BlockSpec(memory_space=pltpu.VMEM),
        out_shape=jax.ShapeDtypeStruct((len(arrays), *arrays[0].shape), arrays[0].dtype),
        compiler_params=params(),
    )(*arrays)

def out_kernel(place_ref, mine_ref, partner_ref, grad_ref, out_ref):
    grad = grad_ref[...]
    out_ref[0, place_ref[0]] = dot(mine_ref[...], grad, (0, 0)).astype(BF)
    out_ref[0, 1 - place_ref[0]] = dot(partner_ref[...], grad, (0, 0)).astype(BF)

def out_grads(place, mine, partner, grad):
    heads = pl.BlockSpec((1024, HD), lambda i, p: (0, 0))
    return pl.pallas_call(
        out_kernel,
        grid_spec=pltpu.PrefetchScalarGridSpec(
            num_scalar_prefetch=1, grid=(8,),
            in_specs=[heads, heads, pl.BlockSpec((1024, 256), lambda i, p: (0, i))],
            out_specs=pl.BlockSpec((1, 2, HD, 256), lambda i, p: (i, 0, 0, 0)),
        ),
        out_shape=jax.ShapeDtypeStruct((8, 2, HD, 256), BF),
        compiler_params=params(),
        cost_estimate=short(2 * 1024 * 256 * 2048, 6 << 20),
    )(place, mine, partner, grad)


def qkv_grads_kernel(n_ref, gp_ref, w_ref, gain_ref, shift_ref, second_ref, out_ref, left, columns, sums):
    at = pl.program_id(0)

    @pl.when(at == 0)
    def _():
        left[...] = gp_ref[...].T
        columns[...] = jnp.sum(left[...].astype(F32), axis=1, keepdims=True)

    grad = dot(left[...], n_ref[...], (1, 0))
    out_ref[at, : 3 * HD] = grad.astype(BF)
    w = jnp.concatenate([w_ref[c].T for c in range(3)], axis=0).astype(F32)
    shift = jnp.sum(w * columns[...], axis=0, keepdims=True)
    gain = (jnp.sum(w * grad, axis=0, keepdims=True) - shift_ref[...] * shift) / gain_ref[...]
    for i, row in enumerate((gain, second_ref[0], shift, second_ref[1])):
        sums[pl.ds(8 * i + at, 1)] = row

    @pl.when(at == 7)
    def _():
        for i in range(8):
            out_ref[i, 3 * HD :] = sums[...].astype(BF)

def qkv_grads(normed, gp, w, gain, shift, second):
    row = pl.BlockSpec((1, 256), lambda i: (0, i))
    return pl.pallas_call(
        qkv_grads_kernel, grid=(8,),
        in_specs=[
            pl.BlockSpec((2048, 256), lambda i: (0, i)),
            pl.BlockSpec((2048, 384), lambda i: (0, 0)),
            pl.BlockSpec((3, 256, HD), lambda i: (0, i, 0)),
            row, row,
            pl.BlockSpec((2, 1, 256), lambda i: (0, 0, i)),
        ],
        out_specs=pl.BlockSpec((8, 3 * HD + 32, 256), lambda i: (0, 0, 0)),
        out_shape=jax.ShapeDtypeStruct((8, 3 * HD + 32, 256), BF),
        scratch_shapes=[pltpu.VMEM((384, 2048), BF), pltpu.VMEM((384, 1), F32), pltpu.VMEM((32, 256), F32)],
        compiler_params=params(),
        cost_estimate=short(2 * 2048 * 2048 * 384, 12 << 20, 1),
    )(normed, gp, w, gain[None], shift[None], second)


def scatter(values, axes):
    return lax.psum_scatter(values, axes, scatter_dimension=0, tiled=True).astype(F32)


def pick(values, index, axis):
    return lax.dynamic_index_in_dim(values, index, axis, False)


def after(values, *others):
    return lax.optimization_barrier((values, *others))[0]


def sum_over_tensor(values, last_gate):
    values = values + core_swap(values)
    values = (values + z_far(values)) + (z_up(values) + z_down(values))
    values = after(values, last_gate)
    return values + x_pair(values)


def body(
    tokens,
    ln1_gain,
    ln1_shift,
    qkv_weight,
    out_weight,
    ln2_gain,
    ln2_shift,
    up_weight,
    down_weight,
    lengths,
    cotangent,
):
    x_hi, y, x_lo, z, core = (lax.axis_index(axis) for axis in AXES)
    tensor = x_lo * 8 + z * 2 + core
    length = lengths[0]

    place = jnp.stack([core, z, x_lo, y % 2])

    out_own = lax.all_gather(out_weight, ("z", "core"), axis=0, tiled=True)
    live_rows = (tensor * 128 + jnp.arange(128, dtype=jnp.int32) < length).astype(F32)[:, None]
    incoming_rows = cotangent.astype(F32) * live_rows
    sent_rows = incoming_rows.astype(BF)
    later_rows = after(sent_rows, out_own)
    along_z = [z_down(later_rows), z_far(sent_rows), z_up(later_rows)]
    up_partner, down_partner, qkv_partner = x_partner(up_weight), x_partner(down_weight), x_partner(qkv_weight)

    normed_first, projected = project(tokens, ln1_gain, ln1_shift, qkv_weight)
    attended, totals = attend(projected, lengths)
    heads = lax.all_to_all(attended, ("z", "core"), 0, 0)
    branch_mine, branch_other = branch(place[2:], after(heads, up_partner, along_z[1]), out_own)
    branch_other = after(x_pair(branch_other), down_partner, along_z[0], along_z[2])
    token_rows = lax.dynamic_slice_in_dim(tokens, tensor * 128, 128, 0).astype(F32)
    middle_rows = token_rows + (branch_mine + branch_other.astype(F32))
    unit_second, inverse_second = norm_stats(middle_rows)
    normed_rows = (unit_second * ln2_gain + ln2_shift).astype(BF)
    along_z = stack(after(sent_rows, normed_rows), *along_z)
    from_core = core_swap(along_z)
    qkv_both = both_weights(qkv_weight, after(qkv_partner, normed_rows))

    normed_second = lax.all_gather(normed_rows, ("z", "core"), axis=0, tiled=True)
    activated, grad_hidden, grad_normed_part, incoming = front(
        place,
        after(normed_second, qkv_both).reshape(4, 2, 128, 2048),
        along_z,
        from_core,
        up_weight,
        up_partner,
        down_weight,
        down_partner,
    )
    incoming = incoming.reshape(1024, 2048)
    grad_normed_second = scatter(grad_normed_part.reshape(1024, 2048), ("z", "core"))
    down_kept, down_sent, up_kept, up_sent = weight_grads(
        place[3:], normed_second, incoming, activated, grad_hidden
    )
    down_got, up_got = x_partner(down_sent), y_pair(up_sent)
    mixed_mine, mixed_other = mix(place, after(activated, down_sent), down_weight, down_partner)
    grad_normed_second = after(grad_normed_second, down_got, up_got, mixed_mine)

    grad_middle = incoming_rows + norm_back(grad_normed_second, ln2_gain, unit_second, inverse_second)
    gain_second = jnp.sum(grad_normed_second * unit_second, axis=0)
    shift_second = jnp.sum(grad_normed_second, axis=0)
    grad_branch = grad_middle.astype(BF)
    branch_back = lax.all_gather(grad_branch, ("z", "core"), axis=0, tiled=True)

    branch_got = x_pair(grad_branch)
    down_kept, down_sent, up_kept, up_sent = cut(
        jnp.stack([x_hi, y // 2]), down_kept, after(down_got, grad_branch), up_kept, up_got
    )
    down_got, up_got = x_far(down_sent), y_far(up_sent)
    mixed_got = core_swap(after(mixed_other, grad_branch))
    by_head = to_heads(place[2:], grad_branch, after(branch_got, down_sent), out_own)
    grad_attended = lax.all_to_all(by_head, ("z", "core"), 0, 0)
    mixed = add(mixed_mine, after(mixed_got, by_head)).reshape(2, 2, 128, 2048)
    mixed_got = z_pair(pick(mixed, 1 - z % 2, 1))
    partner_heads = x_pair(pick(attended, 1 - x_lo, 1).reshape(1024, HD))

    grad_projected, projected_sent = attend_back(
        projected, after(grad_attended, mixed, partner_heads), totals, jnp.stack([length, x_lo])
    )
    projected_got = x_pair(projected_sent)
    second = jnp.stack([gain_second, shift_second])[:, None]
    qkv_sent = qkv_grads(normed_first, grad_projected, qkv_weight, ln1_gain, ln1_shift, second)
    qkv_got = lax.all_to_all(qkv_sent, BATCH, 0, 0)
    projected_got = after(projected_got, qkv_sent, down_got, up_got, mixed_got)
    grad_first_part = first_back(place[2:], grad_projected, projected_got, qkv_both)
    grad_normed_first = scatter(grad_first_part, ("z", "core"))

    down_kept, down_sent, up_kept, up_sent = cut_again(
        jnp.stack([y // 2, x_hi]), down_kept, after(down_got, grad_first_part), up_kept, up_got
    )
    down_got, up_got = y_far(down_sent), x_partner(up_sent)
    out_sent = out_grads(
        x_lo[None], after(pick(attended, x_lo, 1).reshape(1024, HD), down_sent), partner_heads, branch_back
    )
    qkv_got = after(qkv_got, down_sent, out_sent)
    down_kept, down_sent, up_kept, up_sent = cut_again(
        jnp.stack([y % 2, x_hi]), down_kept, down_got, up_kept, up_got
    )
    grad_down, grad_up = finish(down_kept, y_near(down_sent), up_kept, x_far(up_sent))
    out_got = lax.all_to_all(after(out_sent, qkv_got).reshape(16, HD, 256), ("x_hi", "y", "x_lo"), 0, 0)
    qkv_sums = jnp.sum(after(qkv_got, out_sent).astype(F32), axis=0)
    sums = sum_over_tensor(qkv_sums[3 * HD :].reshape(4, 2048), down_sent)
    grad_qkv = qkv_sums[: 3 * HD].reshape(3, HD, 256).transpose(0, 2, 1)
    mixed = add(pick(mixed, z % 2, 1), mixed_got)
    output = (
        middle_rows + pick(mixed, z // 2, 0).astype(F32) + z_far(pick(mixed, 1 - z // 2, 0)).astype(F32)
    ).astype(BF)
    grad_out = jnp.sum(out_got.astype(F32), axis=0)

    unit_rows, inverse_rows = norm_stats(token_rows)
    grad_tokens = (grad_middle + norm_back(grad_normed_first, ln1_gain, unit_rows, inverse_rows)).astype(BF)
    return (output, grad_tokens, grad_qkv, grad_out, grad_up, grad_down, sums[:2], sums[2:])


def solution(mesh):
    return jax.shard_map(
        body,
        mesh=Mesh(mesh.devices.reshape(2, 4, 2, 4, 2), AXES),
        in_specs=(
            P(BATCH, None),
            P(),
            P(),
            P(None, None, TENSOR),
            P(TENSOR, None),
            P(),
            P(),
            P(None, TENSOR),
            P(TENSOR, None),
            P(BATCH),
            P(AXES, None),
        ),
        out_specs=(
            P(AXES, None),
            P(AXES, None),
            P(None, BATCH, TENSOR),
            P(TENSOR, BATCH),
            P(BATCH, TENSOR),
            P(TENSOR, BATCH),
            P(),
            P(),
        ),
        check_vma=False,
    )
```

```python
import functools

import jax
import jax.numpy as jnp
from jax import lax
from jax.experimental import pallas as pl
from jax.experimental.pallas import tpu as pltpu
from jax.sharding import Mesh
from jax.sharding import PartitionSpec as P

HD = 128
EPS = 1e-05
MASKED_SCORE = -1e30
BF = jnp.bfloat16
F32 = jnp.float32

AXES = ("x_hi", "y", "x_lo", "z", "core")
BATCH, TENSOR = AXES[:2], AXES[2:]


def core_swap(values):
    return lax.ppermute(values, "core", [(0, 1), (1, 0)])


def x_pair(values):
    return lax.ppermute(values, "x_lo", [(0, 1), (1, 0)])


def y_near(values):
    return lax.ppermute(values, "y", [(i, i ^ 1) for i in range(4)])


def x_partner(values):
    pairs = [(r * 2 + c, ((r + (1, -1)[c]) % 4) * 2 + c) for r in range(4) for c in range(2)]
    return lax.ppermute(values, ("x_hi", "x_lo", "core"), pairs)


def neighbours(axis):
    pairs = [(i * 2 + c, ((i ^ 1) if c == 0 else 3 - i) * 2 + c) for i in range(4) for c in range(2)]
    return lambda values: lax.ppermute(values, (axis, "core"), pairs)


y_pair, z_pair = neighbours("y"), neighbours("z")


def shift(axes, sizes, step):
    return lambda values: lax.ppermute(values, axes, [(i, (i + step) % sizes) for i in range(sizes)])


z_up, z_down, z_far = (shift("z", 4, step) for step in (1, -1, 2))
y_far, x_far = shift("y", 4, 2), shift(("x_hi", "x_lo"), 4, 2)


def norm_stats(values):
    centre = jnp.mean(values, axis=-1, keepdims=True)
    offsets = values - centre
    variance = jnp.mean(offsets * offsets, axis=-1, keepdims=True)
    inverse = lax.rsqrt(variance + EPS)
    return (offsets * inverse, inverse)


def norm_back(grad_normed, gain, unit_rows, inverse):
    scaled = grad_normed * gain
    return inverse * (
        scaled
        - jnp.mean(scaled, axis=-1, keepdims=True)
        - unit_rows * jnp.mean(scaled * unit_rows, axis=-1, keepdims=True)
    )


def dot(left, right, dims):
    return lax.dot_general(left, right, ((dims[:1], dims[1:]), ((), ())), preferred_element_type=F32)


def short(flops, moved, by=64):
    return pl.CostEstimate(flops=flops // by, bytes_accessed=moved // by, transcendentals=0)


def add(left, right):
    return (left.astype(F32) + right.astype(F32)).astype(BF)


def params(limit=60, **kw):
    return pltpu.CompilerParams(vmem_limit_bytes=limit * 2**20, **kw)


def qkv_kernel(x_ref, gain_ref, shift_ref, w_ref, normed_ref, out_ref, weights):
    @pl.when(pl.program_id(0) == 0)
    def _():
        for c in range(3):
            weights[:, c * HD : (c + 1) * HD] = w_ref[c]

    x = x_ref[...].astype(F32)
    offsets = x - jnp.mean(x, axis=-1, keepdims=True)
    inverse = lax.rsqrt(jnp.mean(offsets * offsets, axis=-1, keepdims=True) + EPS)
    normed = (offsets * inverse * gain_ref[...] + shift_ref[...]).astype(BF)
    normed_ref[...] = normed
    out_ref[...] = dot(normed, weights[...], (1, 0)).astype(BF)

def project(tokens, gain, shift, weight):
    rows = 256
    return pl.pallas_call(
        qkv_kernel,
        grid=(2048 // rows,),
        in_specs=[
            pl.BlockSpec((rows, 2048), lambda i: (i, 0)),
            pl.BlockSpec((1, 2048), lambda i: (0, 0)),
            pl.BlockSpec((1, 2048), lambda i: (0, 0)),
            pl.BlockSpec((3, 2048, HD), lambda i: (0, 0, 0)),
        ],
        out_specs=[
            pl.BlockSpec((rows, 2048), lambda i: (i, 0)),
            pl.BlockSpec((rows, 3 * HD), lambda i: (i, 0)),
        ],
        out_shape=[jax.ShapeDtypeStruct((2048, 2048), BF), jax.ShapeDtypeStruct((2048, 3 * HD), BF)],
        scratch_shapes=[pltpu.VMEM((2048, 3 * HD), BF)],
        compiler_params=params(),
        cost_estimate=short(2 * 2048 * 2048 * 384, 20 << 20),
    )(tokens, gain[None], shift[None], weight)


QB = 512
SCALE = HD ** -0.5

def masked(scores, first_query, first_key, length):
    query = first_query + lax.broadcasted_iota(jnp.int32, scores.shape, 0)
    key = first_key + lax.broadcasted_iota(jnp.int32, scores.shape, 1)
    return jnp.where((key <= query) & (key < length), scores, MASKED_SCORE)

def forward_kernel(length_ref, qkv_ref, out_ref, total_ref):
    length = length_ref[0]
    for i in range(2048 // QB):
        q = qkv_ref[i * QB : (i + 1) * QB, :HD]
        parts = []
        for j in range(i + 1):
            k = qkv_ref[j * QB : (j + 1) * QB, HD : 2 * HD]
            parts.append(masked(dot(q, k, (1, 1)) * SCALE, i * QB, j * QB, length))
        peak = functools.reduce(jnp.maximum, [jnp.max(p, axis=-1, keepdims=True) for p in parts])
        total = jnp.zeros((QB, 1), F32)
        acc = jnp.zeros((QB, HD), F32)
        for j in range(i + 1):
            e = jnp.exp(parts[j] - peak)
            total += jnp.sum(e, axis=-1, keepdims=True)
            acc += dot(e.astype(BF), qkv_ref[j * QB : (j + 1) * QB, 2 * HD :], (1, 0))
        out = (acc / total).astype(BF)
        for b in range(QB // HD):
            block = i * (QB // HD) + b
            out_ref[block % 8, block // 8] = out[b * HD : (b + 1) * HD]
        total_ref[i * QB : (i + 1) * QB] = peak + jnp.log(total)

def attend(qkv, lengths):
    return pl.pallas_call(
        forward_kernel,
        in_specs=[pl.BlockSpec(memory_space=pltpu.SMEM), pl.BlockSpec(memory_space=pltpu.VMEM)],
        out_specs=[pl.BlockSpec(memory_space=pltpu.VMEM)] * 2,
        out_shape=[jax.ShapeDtypeStruct((8, 2, 128, HD), BF), jax.ShapeDtypeStruct((2048, 1), F32)],
        compiler_params=params(),
        cost_estimate=short(2 * 2 * 2048 * 2048 * 128, 3 << 20),
    )(lengths, qkv)

def backward_kernel(length_ref, qkv_ref, grad_ref, total_ref, out_ref, sent_ref, gk, gv, probs, gprobs):
    length = length_ref[0]
    n = 2048 // QB
    gk[...] = jnp.zeros_like(gk)
    gv[...] = jnp.zeros_like(gv)
    for i in range(n):
        rows = slice(i * QB, (i + 1) * QB)
        q = qkv_ref[rows, :HD]
        blocks = [i * (QB // HD) + b for b in range(QB // HD)]
        g = jnp.concatenate([grad_ref[b % 8, b // 8] for b in blocks], axis=0)
        total = total_ref[rows]
        centre = jnp.zeros((QB, 1), F32)
        for j in range(i + 1):
            keys = slice(j * QB, (j + 1) * QB)
            s = masked(dot(q, qkv_ref[keys, HD : 2 * HD], (1, 1)) * SCALE, i * QB, j * QB, length)
            p = jnp.exp(s - total)
            gp = dot(g, qkv_ref[keys, 2 * HD :], (1, 1))
            centre += jnp.sum(p * gp, axis=-1, keepdims=True)
            probs[:, keys] = p
            gprobs[:, keys] = gp
        gq = jnp.zeros((QB, HD), F32)
        for j in range(i + 1):
            keys = slice(j * QB, (j + 1) * QB)
            p = probs[:, keys]
            gs = (p * (gprobs[:, keys] - centre)).astype(BF)
            gq += dot(gs, qkv_ref[keys, HD : 2 * HD], (1, 0))
            gk[keys] += dot(gs, q, (0, 0))
            gv[keys] += dot(p.astype(BF), g, (0, 0))
        out_ref[rows, :HD] = (gq * SCALE).astype(BF)
    out_ref[:, HD : 2 * HD] = (gk[...] * SCALE).astype(BF)
    out_ref[:, 2 * HD :] = gv[...].astype(BF)

    @pl.when(length_ref[1] == 0)
    def _():
        sent_ref[...] = out_ref[1024:]

    @pl.when(length_ref[1] == 1)
    def _():
        sent_ref[...] = out_ref[:1024]

def attend_back(qkv, grad, totals, lengths):
    return pl.pallas_call(
        backward_kernel,
        in_specs=[pl.BlockSpec(memory_space=pltpu.SMEM)] + [pl.BlockSpec(memory_space=pltpu.VMEM)] * 3,
        out_specs=[pl.BlockSpec(memory_space=pltpu.VMEM)] * 2,
        out_shape=[jax.ShapeDtypeStruct((2048, 3 * HD), BF), jax.ShapeDtypeStruct((1024, 3 * HD), BF)],
        scratch_shapes=[pltpu.VMEM((2048, HD), F32), pltpu.VMEM((2048, HD), F32), pltpu.VMEM((QB, 2048), F32), pltpu.VMEM((QB, 2048), F32)],
        compiler_params=params(),
        cost_estimate=short(5 * 2 * 2048 * 1280 * 128, 4 << 20),
    )(lengths, qkv, grad, totals)


GELU_A = 0.7978845608028654
GELU_B = 0.044715

def front_kernel(place_ref, n_ref, mine_ref, other_ref, uo, up, do, dp, act_ref, gh_ref, part_ref, inc_ref):
    core = place_ref[0]
    inc_ref[0, core] = mine_ref[0]
    inc_ref[0, 1 - core] = other_ref[0]
    n = n_ref[0].reshape(256, 2048)
    inc = inc_ref[0].reshape(256, 2048)
    part = jnp.zeros((256, 2048), F32)
    for h, (u, d) in enumerate(((uo, do), (up, dp))):
        cols = slice(h * 512, (h + 1) * 512)
        hidden = dot(n, u[...], (1, 0))
        square = hidden * hidden
        t = jnp.tanh(GELU_A * (hidden + GELU_B * hidden * square))
        act_ref[:, cols] = (0.5 * hidden * (1 + t)).astype(BF)
        slope = 0.5 * (1 + t) + 0.5 * hidden * (1 - t * t) * (GELU_A * (1 + 3 * GELU_B * square))
        gh = (dot(inc, d[...], (1, 1)) * slope).astype(BF)
        gh_ref[:, cols] = gh
        part += dot(gh, u[...], (1, 1))
    part_ref[0] = part.astype(BF).reshape(2, 128, 2048)

def front(place, normed, mine, other, uo, up, do, dp):
    whole = lambda a: pl.BlockSpec(a.shape, lambda i, p: (0,) * a.ndim)
    blk = pl.BlockSpec((1, 2, 128, 2048), lambda i, p: (i, 0, 0, 0))
    one = pl.BlockSpec((1, 128, 2048), lambda i, p: ((i + 4 - p[1]) % 4, 0, 0))
    col = pl.BlockSpec((256, 1024), lambda i, p: (i, 0))
    return pl.pallas_call(
        front_kernel,
        grid_spec=pltpu.PrefetchScalarGridSpec(
            num_scalar_prefetch=1, grid=(4,),
            in_specs=[blk, one, one, whole(uo), whole(up), whole(do), whole(dp)],
            out_specs=[col, col, blk, blk],
        ),
        out_shape=[jax.ShapeDtypeStruct((1024, 1024), BF)] * 2 + [jax.ShapeDtypeStruct((4, 2, 128, 2048), BF)] * 2,
        compiler_params=params(),
        cost_estimate=short(6 * 1024 * 1024 * 2048, 28 << 20),
    )(place, normed, mine, other, uo, up, do, dp)


def mixed_kernel(place_ref, act_ref, do, dp, mine_ref, other_ref, rows):
    a = act_ref[...]
    rows[...] = (dot(a[:, :512], do[...], (1, 0)) + dot(a[:, 512:], dp[...], (1, 0))).astype(BF).reshape(2, 128, 2048)
    mine_ref[0] = rows[place_ref[0]]
    other_ref[0] = rows[1 - place_ref[0]]

def mix(place, act, do, dp):
    whole = lambda a: pl.BlockSpec(a.shape, lambda i, p: (0,) * a.ndim)
    return pl.pallas_call(
        mixed_kernel,
        grid_spec=pltpu.PrefetchScalarGridSpec(
            num_scalar_prefetch=1, grid=(4,),
            in_specs=[pl.BlockSpec((256, 1024), lambda i, p: (i, 0)), whole(do), whole(dp)],
            out_specs=[pl.BlockSpec((1, 128, 2048), lambda i, p: (i, 0, 0))] * 2,
            scratch_shapes=[pltpu.VMEM((2, 128, 2048), BF)],
        ),
        out_shape=[jax.ShapeDtypeStruct((4, 128, 2048), BF)] * 2,
        compiler_params=params(),
        cost_estimate=short(2 * 1024 * 1024 * 2048, 10 << 20, 1),
    )(place, act, do, dp)

def branch_kernel(place_ref, heads_ref, w_ref, mine_ref, other_ref, left, out):
    @pl.when(pl.program_id(0) == 0)
    def _():
        for h in range(8):
            left[:, h * HD : (h + 1) * HD] = heads_ref[h].reshape(256, HD)

    out[...] = dot(left[...], w_ref[...], (1, 0)).reshape(2, 128, 512)
    mine_ref[...] = out[place_ref[0]]
    other_ref[...] = out[1 - place_ref[0]].astype(BF)

def branch(place, heads, w):
    col = pl.BlockSpec((128, 512), lambda i, p: (0, i))
    return pl.pallas_call(
        branch_kernel,
        grid_spec=pltpu.PrefetchScalarGridSpec(
            num_scalar_prefetch=1, grid=(4,),
            in_specs=[pl.BlockSpec((8, 2, 128, HD), lambda i, p: (0, 0, 0, 0)), pl.BlockSpec((1024, 512), lambda i, p: (0, i))],
            out_specs=[col, col],
            scratch_shapes=[pltpu.VMEM((256, 1024), BF), pltpu.VMEM((2, 128, 512), F32)],
        ),
        out_shape=[jax.ShapeDtypeStruct((128, 2048), F32), jax.ShapeDtypeStruct((128, 2048), BF)],
        compiler_params=params(),
        cost_estimate=short(2 * 256 * 1024 * 2048, 6 << 20),
    )(place, heads, w)

def grads_kernel(place_ref, n_ref, inc_ref, act_ref, gh_ref, mine_ref, partner_ref, keep_ref, send_ref):
    def down(ref):
        ref[...] = dot(act_ref[...], inc_ref[...], (0, 0)).astype(BF)

    @pl.when(pl.program_id(0) < 2)
    def _():
        down(mine_ref)

    @pl.when(pl.program_id(0) >= 2)
    def _():
        down(partner_ref)

    up = dot(gh_ref[...], n_ref[...], (0, 0)).astype(BF)
    even, odd = (
        jnp.concatenate([up[:, (2 * i + low) * 256 : (2 * i + low + 1) * 256] for i in range(4)], axis=1)
        for low in range(2)
    )

    @pl.when(place_ref[0] == 0)
    def _():
        keep_ref[...] = even
        send_ref[...] = odd

    @pl.when(place_ref[0] == 1)
    def _():
        keep_ref[...] = odd
        send_ref[...] = even

def weight_grads(place, n, inc, act, gh):
    rows = pl.BlockSpec((1024, 2048), lambda j, p: (0, 0))
    cols = pl.BlockSpec((1024, 256), lambda j, p: (0, j))
    part = pl.BlockSpec((256, 1024), lambda j, p: (j, 0))
    return pl.pallas_call(
        grads_kernel,
        grid_spec=pltpu.PrefetchScalarGridSpec(
            num_scalar_prefetch=1, grid=(4,),
            in_specs=[rows, rows, cols, cols],
            out_specs=[
                pl.BlockSpec((256, 2048), lambda j, p: (jnp.minimum(j, 1), 0)),
                pl.BlockSpec((256, 2048), lambda j, p: (jnp.maximum(j - 2, 0), 0)),
                part, part,
            ],
        ),
        out_shape=[jax.ShapeDtypeStruct((512, 2048), BF)] * 2 + [jax.ShapeDtypeStruct((1024, 1024), BF)] * 2,
        compiler_params=params(),
        cost_estimate=short(4 * 1024 * 1024 * 2048, 20 << 20),
    )(place, n, inc, act, gh)


def cut_kernel(place_ref, down_ref, down_got_ref, up_ref, up_got_ref, down_keep, down_send, up_keep, up_send):
    down = add(down_ref[...], down_got_ref[...])
    up = add(up_ref[...], up_got_ref[...])
    low = jnp.concatenate([up[:, :256], up[:, 512:768]], axis=1)
    high = jnp.concatenate([up[:, 256:512], up[:, 768:]], axis=1)

    @pl.when(place_ref[0] == 0)
    def _():
        down_keep[...] = down[:, :1024]
        down_send[...] = down[:, 1024:]

    @pl.when(place_ref[0] == 1)
    def _():
        down_keep[...] = down[:, 1024:]
        down_send[...] = down[:, :1024]

    @pl.when(place_ref[1] == 0)
    def _():
        up_keep[...] = low
        up_send[...] = high

    @pl.when(place_ref[1] == 1)
    def _():
        up_keep[...] = high
        up_send[...] = low

def cut(place, down, down_got, up, up_got):
    wide = pl.BlockSpec((128, 2048), lambda i, p: (i, 0))
    half = pl.BlockSpec((128, 1024), lambda i, p: (i, 0))
    four = pl.BlockSpec((256, 1024), lambda i, p: (i, 0))
    two = pl.BlockSpec((256, 512), lambda i, p: (i, 0))
    return pl.pallas_call(
        cut_kernel,
        grid_spec=pltpu.PrefetchScalarGridSpec(
            num_scalar_prefetch=1, grid=(4,),
            in_specs=[wide, wide, four, four],
            out_specs=[half, half, two, two],
        ),
        out_shape=[jax.ShapeDtypeStruct((512, 1024), BF)] * 2 + [jax.ShapeDtypeStruct((1024, 512), BF)] * 2,
        compiler_params=params(),
    )(place, down, down_got, up, up_got)


def cut_again_kernel(place_ref, down_ref, down_got_ref, up_ref, up_got_ref, down_keep, down_send, up_keep, up_send):
    down = add(down_ref[...], down_got_ref[...])
    up = add(up_ref[...], up_got_ref[...])
    half = down.shape[1] // 2

    def put(values, at, keep, send):
        @pl.when(at == 0)
        def _():
            keep[...] = values[:, :half]
            send[...] = values[:, half:]

        @pl.when(at == 1)
        def _():
            keep[...] = values[:, half:]
            send[...] = values[:, :half]

    put(down, place_ref[0], down_keep, down_send)
    if up.shape[0] == 1024:
        up_keep[...] = up[:512]
        up_send[...] = up[512:]
    else:
        put(up, place_ref[1], up_keep, up_send)

def cut_again(place, down, down_got, up, up_got):
    size = down.shape[1] // 2
    vmem = pl.BlockSpec(memory_space=pltpu.VMEM)
    return pl.pallas_call(
        cut_again_kernel,
        in_specs=[pl.BlockSpec(memory_space=pltpu.SMEM)] + [vmem] * 4,
        out_specs=[vmem] * 4,
        out_shape=[jax.ShapeDtypeStruct((512, size), BF)] * 4,
        compiler_params=params(),
    )(place, down, down_got, up, up_got)

def finish_kernel(down_ref, down_got_ref, up_ref, up_got_ref, down_out, up_out):
    down_out[...] = down_ref[...].astype(F32) + down_got_ref[...].astype(F32)
    up_out[...] = (up_ref[...].astype(F32) + up_got_ref[...].astype(F32)).T

def finish(*arrays):
    vmem = pl.BlockSpec(memory_space=pltpu.VMEM)
    return pl.pallas_call(
        finish_kernel,
        in_specs=[vmem] * 4,
        out_specs=[vmem] * 2,
        out_shape=[jax.ShapeDtypeStruct((512, 256), F32), jax.ShapeDtypeStruct((256, 512), F32)],
        compiler_params=params(),
    )(*arrays)


def heads_kernel(place_ref, mine_ref, other_ref, w_ref, out_ref, left):
    @pl.when(pl.program_id(0) == 0)
    def _():
        left[place_ref[0]] = mine_ref[...]
        left[1 - place_ref[0]] = other_ref[...]

    part = dot(left[...].reshape(256, 2048), w_ref[...], (1, 1)).astype(BF)
    for h in range(4):
        out_ref[h] = part[:, h * HD : (h + 1) * HD].reshape(2, 128, HD)

def to_heads(place, mine, other, w):
    rows = pl.BlockSpec((128, 2048), lambda i, p: (0, 0))
    return pl.pallas_call(
        heads_kernel,
        grid_spec=pltpu.PrefetchScalarGridSpec(
            num_scalar_prefetch=1, grid=(2,),
            in_specs=[rows, rows, pl.BlockSpec((512, 2048), lambda i, p: (i, 0))],
            out_specs=pl.BlockSpec((4, 2, 128, HD), lambda i, p: (i, 0, 0, 0)),
            scratch_shapes=[pltpu.VMEM((2, 128, 2048), BF)],
        ),
        out_shape=jax.ShapeDtypeStruct((8, 2, 128, HD), BF),
        compiler_params=params(),
    )(place, mine, other, w)


def both_kernel(own_ref, partner_ref, out_ref):
    for c in range(3):
        out_ref[c * HD : (c + 1) * HD] = own_ref[c].T
        out_ref[(c + 3) * HD : (c + 4) * HD] = partner_ref[c].T

def both_weights(own, partner):
    part = pl.BlockSpec((3, 256, HD), lambda i: (0, i, 0))
    return pl.pallas_call(
        both_kernel, grid=(8,),
        in_specs=[part, part],
        out_specs=pl.BlockSpec((6 * HD, 256), lambda i: (0, i)),
        out_shape=jax.ShapeDtypeStruct((6 * HD, 2048), BF),
        compiler_params=params(),
    )(own, partner)


def first_kernel(place_ref, mine_ref, got_ref, w_ref, out_ref, left):
    left[:, : 3 * HD] = mine_ref[...]
    left[:, 3 * HD :] = got_ref[...]
    out_ref[...] = dot(left[...], w_ref[...], (1, 0)).astype(BF)

def first_back(place, mine, got, weights):
    return pl.pallas_call(
        first_kernel,
        grid_spec=pltpu.PrefetchScalarGridSpec(
            num_scalar_prefetch=1, grid=(2,),
            in_specs=[
                pl.BlockSpec((512, 3 * HD), lambda i, p: (p[0] * 2 + i, 0)),
                pl.BlockSpec((512, 3 * HD), lambda i, p: (i, 0)),
                pl.BlockSpec((6 * HD, 2048), lambda i, p: (0, 0)),
            ],
            out_specs=pl.BlockSpec((512, 2048), lambda i, p: (i, 0)),
            scratch_shapes=[pltpu.VMEM((512, 6 * HD), BF)],
        ),
        out_shape=jax.ShapeDtypeStruct((1024, 2048), BF),
        compiler_params=params(),
        cost_estimate=short(2 * 1024 * 2048 * 768, 8 << 20),
    )(place, mine, got, weights)


def stack_kernel(*refs):
    for i, ref in enumerate(refs[:-1]):
        refs[-1][i] = ref[...]

def stack(*arrays):
    return pl.pallas_call(
        stack_kernel,
        in_specs=[pl.BlockSpec(memory_space=pltpu.VMEM)] * len(arrays),
        out_specs=pl.BlockSpec(memory_space=pltpu.VMEM),
        out_shape=jax.ShapeDtypeStruct((len(arrays), *arrays[0].shape), arrays[0].dtype),
        compiler_params=params(),
    )(*arrays)

def out_kernel(place_ref, mine_ref, partner_ref, grad_ref, out_ref):
    grad = grad_ref[...]
    out_ref[0, place_ref[0]] = dot(mine_ref[...], grad, (0, 0)).astype(BF)
    out_ref[0, 1 - place_ref[0]] = dot(partner_ref[...], grad, (0, 0)).astype(BF)

def out_grads(place, mine, partner, grad):
    heads = pl.BlockSpec((1024, HD), lambda i, p: (0, 0))
    return pl.pallas_call(
        out_kernel,
        grid_spec=pltpu.PrefetchScalarGridSpec(
            num_scalar_prefetch=1, grid=(8,),
            in_specs=[heads, heads, pl.BlockSpec((1024, 256), lambda i, p: (0, i))],
            out_specs=pl.BlockSpec((1, 2, HD, 256), lambda i, p: (i, 0, 0, 0)),
        ),
        out_shape=jax.ShapeDtypeStruct((8, 2, HD, 256), BF),
        compiler_params=params(),
        cost_estimate=short(2 * 1024 * 256 * 2048, 6 << 20),
    )(place, mine, partner, grad)


def qkv_grads_kernel(n_ref, gp_ref, w_ref, gain_ref, shift_ref, second_ref, out_ref, left, columns, sums):
    at = pl.program_id(0)

    @pl.when(at == 0)
    def _():
        left[...] = gp_ref[...].T
        columns[...] = jnp.sum(left[...].astype(F32), axis=1, keepdims=True)

    grad = dot(left[...], n_ref[...], (1, 0))
    out_ref[at, : 3 * HD] = grad.astype(BF)
    w = jnp.concatenate([w_ref[c].T for c in range(3)], axis=0).astype(F32)
    shift = jnp.sum(w * columns[...], axis=0, keepdims=True)
    gain = (jnp.sum(w * grad, axis=0, keepdims=True) - shift_ref[...] * shift) / gain_ref[...]
    for i, row in enumerate((gain, second_ref[0], shift, second_ref[1])):
        sums[pl.ds(8 * i + at, 1)] = row

    @pl.when(at == 7)
    def _():
        for i in range(8):
            out_ref[i, 3 * HD :] = sums[...].astype(BF)

def qkv_grads(normed, gp, w, gain, shift, second):
    row = pl.BlockSpec((1, 256), lambda i: (0, i))
    return pl.pallas_call(
        qkv_grads_kernel, grid=(8,),
        in_specs=[
            pl.BlockSpec((2048, 256), lambda i: (0, i)),
            pl.BlockSpec((2048, 384), lambda i: (0, 0)),
            pl.BlockSpec((3, 256, HD), lambda i: (0, i, 0)),
            row, row,
            pl.BlockSpec((2, 1, 256), lambda i: (0, 0, i)),
        ],
        out_specs=pl.BlockSpec((8, 3 * HD + 32, 256), lambda i: (0, 0, 0)),
        out_shape=jax.ShapeDtypeStruct((8, 3 * HD + 32, 256), BF),
        scratch_shapes=[pltpu.VMEM((384, 2048), BF), pltpu.VMEM((384, 1), F32), pltpu.VMEM((32, 256), F32)],
        compiler_params=params(),
        cost_estimate=short(2 * 2048 * 2048 * 384, 12 << 20, 1),
    )(normed, gp, w, gain[None], shift[None], second)


def scatter(values, axes):
    return lax.psum_scatter(values, axes, scatter_dimension=0, tiled=True).astype(F32)


def pick(values, index, axis):
    return lax.dynamic_index_in_dim(values, index, axis, False)


def after(values, *others):
    return lax.optimization_barrier((values, *others))[0]


def sum_over_tensor(values, gate, last_gate):
    values = after(values + core_swap(values), *gate)
    values = (values + z_far(values)) + (z_up(values) + z_down(values))
    values = after(values, last_gate)
    return values + x_pair(values)


def body(
    tokens,
    ln1_gain,
    ln1_shift,
    qkv_weight,
    out_weight,
    ln2_gain,
    ln2_shift,
    up_weight,
    down_weight,
    lengths,
    cotangent,
):
    x_hi, y, x_lo, z, core = (lax.axis_index(axis) for axis in AXES)
    tensor = x_lo * 8 + z * 2 + core
    length = lengths[0]

    place = jnp.stack([core, z, x_lo, y % 2])

    out_own = lax.all_gather(out_weight, ("z", "core"), axis=0, tiled=True)
    live_rows = (tensor * 128 + jnp.arange(128, dtype=jnp.int32) < length).astype(F32)[:, None]
    incoming_rows = cotangent.astype(F32) * live_rows
    sent_rows = incoming_rows.astype(BF)
    later_rows = after(sent_rows, out_own)
    along_z = [z_down(later_rows), z_far(sent_rows), z_up(later_rows)]
    up_partner, down_partner, qkv_partner = x_partner(up_weight), x_partner(down_weight), x_partner(qkv_weight)

    normed_first, projected = project(tokens, ln1_gain, ln1_shift, qkv_weight)
    attended, totals = attend(projected, lengths)
    heads = lax.all_to_all(attended, ("z", "core"), 0, 0)
    branch_mine, branch_other = branch(place[2:], after(heads, up_partner, along_z[1]), out_own)
    branch_other = after(x_pair(branch_other), down_partner, along_z[0], along_z[2])
    token_rows = lax.dynamic_slice_in_dim(tokens, tensor * 128, 128, 0).astype(F32)
    middle_rows = token_rows + (branch_mine + branch_other.astype(F32))
    unit_second, inverse_second = norm_stats(middle_rows)
    normed_rows = (unit_second * ln2_gain + ln2_shift).astype(BF)
    along_z = stack(after(sent_rows, normed_rows), *along_z)
    from_core = core_swap(along_z)

    normed_second = lax.all_gather(normed_rows, ("z", "core"), axis=0, tiled=True)
    activated, grad_hidden, grad_normed_part, incoming = front(
        place,
        after(normed_second, qkv_partner).reshape(4, 2, 128, 2048),
        along_z,
        from_core,
        up_weight,
        up_partner,
        down_weight,
        down_partner,
    )
    incoming = incoming.reshape(1024, 2048)
    grad_normed_second = scatter(grad_normed_part.reshape(1024, 2048), ("z", "core"))
    down_kept, down_sent, up_kept, up_sent = weight_grads(
        place[3:], normed_second, incoming, activated, grad_hidden
    )
    down_got, up_got = x_partner(down_sent), y_pair(up_sent)
    mixed_mine, mixed_other = mix(place, after(activated, down_sent), down_weight, down_partner)
    qkv_both = both_weights(qkv_weight, after(qkv_partner, mixed_mine))
    grad_normed_second = after(grad_normed_second, down_got, up_got, mixed_mine, qkv_both)

    grad_middle = incoming_rows + norm_back(grad_normed_second, ln2_gain, unit_second, inverse_second)
    gain_second = jnp.sum(grad_normed_second * unit_second, axis=0)
    shift_second = jnp.sum(grad_normed_second, axis=0)
    grad_branch = grad_middle.astype(BF)
    branch_back = lax.all_gather(grad_branch, ("z", "core"), axis=0, tiled=True)

    branch_got = x_pair(grad_branch)
    down_kept, down_sent, up_kept, up_sent = cut(
        jnp.stack([x_hi, y // 2]), down_kept, after(down_got, grad_branch), up_kept, up_got
    )
    down_got, up_got = x_far(down_sent), y_far(up_sent)
    mixed_got = core_swap(after(mixed_other, grad_branch))
    by_head = to_heads(place[2:], grad_branch, after(branch_got, down_sent), out_own)
    grad_attended = lax.all_to_all(by_head, ("z", "core"), 0, 0)
    mixed = add(mixed_mine, after(mixed_got, by_head)).reshape(2, 2, 128, 2048)
    mixed_got = z_pair(pick(mixed, 1 - z % 2, 1))
    partner_heads = x_pair(pick(attended, 1 - x_lo, 1).reshape(1024, HD))

    grad_projected, projected_sent = attend_back(
        projected, after(grad_attended, mixed, partner_heads), totals, jnp.stack([length, x_lo])
    )
    projected_got = x_pair(projected_sent)
    second = jnp.stack([gain_second, shift_second])[:, None]
    qkv_sent = qkv_grads(normed_first, grad_projected, qkv_weight, ln1_gain, ln1_shift, second)
    qkv_got = lax.all_to_all(qkv_sent, BATCH, 0, 0)
    down_kept, down_sent, up_kept, up_sent = cut_again(
        jnp.stack([y // 2, x_hi]), down_kept, after(down_got, qkv_sent), up_kept, up_got
    )
    down_got, up_got = y_far(down_sent), x_partner(up_sent)
    projected_got = after(projected_got, down_sent, mixed_got)
    grad_first_part = first_back(place[2:], grad_projected, projected_got, qkv_both)
    grad_normed_first = scatter(grad_first_part, ("z", "core"))

    out_sent = out_grads(
        x_lo[None], after(pick(attended, x_lo, 1).reshape(1024, HD), grad_first_part), partner_heads, branch_back
    )
    down_kept, down_sent, up_kept, up_sent = cut_again(
        jnp.stack([y % 2, x_hi]), down_kept, after(down_got, out_sent), up_kept, up_got
    )
    qkv_got = after(qkv_got, down_sent)
    down_got, up_got = y_near(down_sent), x_far(up_sent)
    grad_down, grad_up = finish(down_kept, down_got, up_kept, up_got)
    out_got = lax.all_to_all(after(out_sent, qkv_got).reshape(16, HD, 256), ("x_hi", "y", "x_lo"), 0, 0)
    qkv_sums = jnp.sum(after(qkv_got, out_sent).astype(F32), axis=0)
    sums = sum_over_tensor(qkv_sums[3 * HD :].reshape(4, 2048), (down_got, up_got), out_got)
    grad_qkv = qkv_sums[: 3 * HD].reshape(3, HD, 256).transpose(0, 2, 1)
    mixed = add(pick(mixed, z % 2, 1), mixed_got)
    output = (
        middle_rows + pick(mixed, z // 2, 0).astype(F32) + z_far(pick(mixed, 1 - z // 2, 0)).astype(F32)
    ).astype(BF)
    grad_out = jnp.sum(out_got.astype(F32), axis=0)

    unit_rows, inverse_rows = norm_stats(token_rows)
    grad_tokens = (grad_middle + norm_back(grad_normed_first, ln1_gain, unit_rows, inverse_rows)).astype(BF)
    return (output, grad_tokens, grad_qkv, grad_out, grad_up, grad_down, sums[:2], sums[2:])


def solution(mesh):
    return jax.shard_map(
        body,
        mesh=Mesh(mesh.devices.reshape(2, 4, 2, 4, 2), AXES),
        in_specs=(
            P(BATCH, None),
            P(),
            P(),
            P(None, None, TENSOR),
            P(TENSOR, None),
            P(),
            P(),
            P(None, TENSOR),
            P(TENSOR, None),
            P(BATCH),
            P(AXES, None),
        ),
        out_specs=(
            P(AXES, None),
            P(AXES, None),
            P(None, BATCH, TENSOR),
            P(TENSOR, BATCH),
            P(BATCH, TENSOR),
            P(TENSOR, BATCH),
            P(),
            P(),
        ),
        check_vma=False,
    )
```

```python
import functools

import jax
import jax.numpy as jnp
from jax import lax
from jax.experimental import pallas as pl
from jax.experimental.pallas import tpu as pltpu
from jax.sharding import Mesh
from jax.sharding import PartitionSpec as P

HD = 128
EPS = 1e-05
MASKED_SCORE = -1e30
BF = jnp.bfloat16
F32 = jnp.float32

AXES = ("x_hi", "y", "x_lo", "z", "core")
BATCH, TENSOR = AXES[:2], AXES[2:]


def core_swap(values):
    return lax.ppermute(values, "core", [(0, 1), (1, 0)])


def x_pair(values):
    return lax.ppermute(values, "x_lo", [(0, 1), (1, 0)])


def x_partner(values):
    pairs = [(r * 2 + c, ((r + (1, -1)[c]) % 4) * 2 + c) for r in range(4) for c in range(2)]
    return lax.ppermute(values, ("x_hi", "x_lo", "core"), pairs)


def neighbours(axis):
    pairs = [(i * 2 + c, ((i ^ 1) if c == 0 else 3 - i) * 2 + c) for i in range(4) for c in range(2)]
    return lambda values: lax.ppermute(values, (axis, "core"), pairs)


y_pair = neighbours("y")


def shift(axes, sizes, step):
    return lambda values: lax.ppermute(values, axes, [(i, (i + step) % sizes) for i in range(sizes)])


z_up, z_down, z_far = (shift("z", 4, step) for step in (1, -1, 2))
y_far, x_far = shift("y", 4, 2), shift(("x_hi", "x_lo"), 4, 2)


def norm_stats(values):
    centre = jnp.mean(values, axis=-1, keepdims=True)
    offsets = values - centre
    variance = jnp.mean(offsets * offsets, axis=-1, keepdims=True)
    inverse = lax.rsqrt(variance + EPS)
    return (offsets * inverse, inverse)


def norm_back(grad_normed, gain, unit_rows, inverse):
    scaled = grad_normed * gain
    return inverse * (
        scaled
        - jnp.mean(scaled, axis=-1, keepdims=True)
        - unit_rows * jnp.mean(scaled * unit_rows, axis=-1, keepdims=True)
    )


def dot(left, right, dims):
    return lax.dot_general(left, right, ((dims[:1], dims[1:]), ((), ())), preferred_element_type=F32)


def short(flops, moved, by=64):
    return pl.CostEstimate(flops=flops // by, bytes_accessed=moved // by, transcendentals=0)


def add(left, right):
    return (left.astype(F32) + right.astype(F32)).astype(BF)


def params(limit=60, **kw):
    return pltpu.CompilerParams(vmem_limit_bytes=limit * 2**20, **kw)


def qkv_kernel(x_ref, gain_ref, shift_ref, w_ref, normed_ref, out_ref, weights):
    @pl.when(pl.program_id(0) == 0)
    def _():
        for c in range(3):
            weights[:, c * HD : (c + 1) * HD] = w_ref[c]

    x = x_ref[...].astype(F32)
    offsets = x - jnp.mean(x, axis=-1, keepdims=True)
    inverse = lax.rsqrt(jnp.mean(offsets * offsets, axis=-1, keepdims=True) + EPS)
    normed = (offsets * inverse * gain_ref[...] + shift_ref[...]).astype(BF)
    normed_ref[...] = normed
    out_ref[...] = dot(normed, weights[...], (1, 0)).astype(BF)

def project(tokens, gain, shift, weight):
    rows = 256
    return pl.pallas_call(
        qkv_kernel,
        grid=(2048 // rows,),
        in_specs=[
            pl.BlockSpec((rows, 2048), lambda i: (i, 0)),
            pl.BlockSpec((1, 2048), lambda i: (0, 0)),
            pl.BlockSpec((1, 2048), lambda i: (0, 0)),
            pl.BlockSpec((3, 2048, HD), lambda i: (0, 0, 0)),
        ],
        out_specs=[
            pl.BlockSpec((rows, 2048), lambda i: (i, 0)),
            pl.BlockSpec((rows, 3 * HD), lambda i: (i, 0)),
        ],
        out_shape=[jax.ShapeDtypeStruct((2048, 2048), BF), jax.ShapeDtypeStruct((2048, 3 * HD), BF)],
        scratch_shapes=[pltpu.VMEM((2048, 3 * HD), BF)],
        compiler_params=params(),
        cost_estimate=short(2 * 2048 * 2048 * 384, 20 << 20),
    )(tokens, gain[None], shift[None], weight)


QB = 512
SCALE = HD ** -0.5

def masked(scores, first_query, first_key, length):
    query = first_query + lax.broadcasted_iota(jnp.int32, scores.shape, 0)
    key = first_key + lax.broadcasted_iota(jnp.int32, scores.shape, 1)
    return jnp.where((key <= query) & (key < length), scores, MASKED_SCORE)

def forward_kernel(length_ref, qkv_ref, out_ref, total_ref):
    length = length_ref[0]
    for i in range(2048 // QB):
        q = qkv_ref[i * QB : (i + 1) * QB, :HD]
        parts = []
        for j in range(i + 1):
            k = qkv_ref[j * QB : (j + 1) * QB, HD : 2 * HD]
            parts.append(masked(dot(q, k, (1, 1)) * SCALE, i * QB, j * QB, length))
        peak = functools.reduce(jnp.maximum, [jnp.max(p, axis=-1, keepdims=True) for p in parts])
        total = jnp.zeros((QB, 1), F32)
        acc = jnp.zeros((QB, HD), F32)
        for j in range(i + 1):
            e = jnp.exp(parts[j] - peak)
            total += jnp.sum(e, axis=-1, keepdims=True)
            acc += dot(e.astype(BF), qkv_ref[j * QB : (j + 1) * QB, 2 * HD :], (1, 0))
        out = (acc / total).astype(BF)
        for b in range(QB // HD):
            block = i * (QB // HD) + b
            out_ref[block % 8, block // 8] = out[b * HD : (b + 1) * HD]
        total_ref[i * QB : (i + 1) * QB] = peak + jnp.log(total)

def attend(qkv, lengths):
    return pl.pallas_call(
        forward_kernel,
        in_specs=[pl.BlockSpec(memory_space=pltpu.SMEM), pl.BlockSpec(memory_space=pltpu.VMEM)],
        out_specs=[pl.BlockSpec(memory_space=pltpu.VMEM)] * 2,
        out_shape=[jax.ShapeDtypeStruct((8, 2, 128, HD), BF), jax.ShapeDtypeStruct((2048, 1), F32)],
        compiler_params=params(),
        cost_estimate=short(2 * 2 * 2048 * 2048 * 128, 3 << 20),
    )(lengths, qkv)

def backward_kernel(length_ref, qkv_ref, grad_ref, total_ref, out_ref, sent_ref, gk, gv, probs, gprobs):
    length = length_ref[0]
    n = 2048 // QB
    gk[...] = jnp.zeros_like(gk)
    gv[...] = jnp.zeros_like(gv)
    for i in range(n):
        rows = slice(i * QB, (i + 1) * QB)
        q = qkv_ref[rows, :HD]
        blocks = [i * (QB // HD) + b for b in range(QB // HD)]
        g = jnp.concatenate([grad_ref[b % 8, b // 8] for b in blocks], axis=0)
        total = total_ref[rows]
        centre = jnp.zeros((QB, 1), F32)
        for j in range(i + 1):
            keys = slice(j * QB, (j + 1) * QB)
            s = masked(dot(q, qkv_ref[keys, HD : 2 * HD], (1, 1)) * SCALE, i * QB, j * QB, length)
            p = jnp.exp(s - total)
            gp = dot(g, qkv_ref[keys, 2 * HD :], (1, 1))
            centre += jnp.sum(p * gp, axis=-1, keepdims=True)
            probs[:, keys] = p
            gprobs[:, keys] = gp
        gq = jnp.zeros((QB, HD), F32)
        for j in range(i + 1):
            keys = slice(j * QB, (j + 1) * QB)
            p = probs[:, keys]
            gs = (p * (gprobs[:, keys] - centre)).astype(BF)
            gq += dot(gs, qkv_ref[keys, HD : 2 * HD], (1, 0))
            gk[keys] += dot(gs, q, (0, 0))
            gv[keys] += dot(p.astype(BF), g, (0, 0))
        out_ref[rows, :HD] = (gq * SCALE).astype(BF)
    out_ref[:, HD : 2 * HD] = (gk[...] * SCALE).astype(BF)
    out_ref[:, 2 * HD :] = gv[...].astype(BF)

    @pl.when(length_ref[1] == 0)
    def _():
        sent_ref[...] = out_ref[1024:]

    @pl.when(length_ref[1] == 1)
    def _():
        sent_ref[...] = out_ref[:1024]

def attend_back(qkv, grad, totals, lengths):
    return pl.pallas_call(
        backward_kernel,
        in_specs=[pl.BlockSpec(memory_space=pltpu.SMEM)] + [pl.BlockSpec(memory_space=pltpu.VMEM)] * 3,
        out_specs=[pl.BlockSpec(memory_space=pltpu.VMEM)] * 2,
        out_shape=[jax.ShapeDtypeStruct((2048, 3 * HD), BF), jax.ShapeDtypeStruct((1024, 3 * HD), BF)],
        scratch_shapes=[pltpu.VMEM((2048, HD), F32), pltpu.VMEM((2048, HD), F32), pltpu.VMEM((QB, 2048), F32), pltpu.VMEM((QB, 2048), F32)],
        compiler_params=params(),
        cost_estimate=short(5 * 2 * 2048 * 1280 * 128, 4 << 20),
    )(lengths, qkv, grad, totals)


GELU_A = 0.7978845608028654
GELU_B = 0.044715

def front_kernel(place_ref, n_ref, mine_ref, other_ref, uo, up, do, dp, act_ref, gh_ref, part_ref, inc_ref):
    core = place_ref[0]
    inc_ref[0, core] = mine_ref[0]
    inc_ref[0, 1 - core] = other_ref[0]
    n = n_ref[0].reshape(256, 2048)
    inc = inc_ref[0].reshape(256, 2048)
    part = jnp.zeros((256, 2048), F32)
    for h, (u, d) in enumerate(((uo, do), (up, dp))):
        cols = slice(h * 512, (h + 1) * 512)
        hidden = dot(n, u[...], (1, 0))
        square = hidden * hidden
        t = jnp.tanh(GELU_A * (hidden + GELU_B * hidden * square))
        act_ref[:, cols] = (0.5 * hidden * (1 + t)).astype(BF)
        slope = 0.5 * (1 + t) + 0.5 * hidden * (1 - t * t) * (GELU_A * (1 + 3 * GELU_B * square))
        gh = (dot(inc, d[...], (1, 1)) * slope).astype(BF)
        gh_ref[:, cols] = gh
        part += dot(gh, u[...], (1, 1))
    part_ref[0] = part.astype(BF).reshape(2, 128, 2048)

def front(place, normed, mine, other, uo, up, do, dp):
    whole = lambda a: pl.BlockSpec(a.shape, lambda i, p: (0,) * a.ndim)
    blk = pl.BlockSpec((1, 2, 128, 2048), lambda i, p: (i, 0, 0, 0))
    one = pl.BlockSpec((1, 128, 2048), lambda i, p: ((i + 4 - p[1]) % 4, 0, 0))
    col = pl.BlockSpec((256, 1024), lambda i, p: (i, 0))
    return pl.pallas_call(
        front_kernel,
        grid_spec=pltpu.PrefetchScalarGridSpec(
            num_scalar_prefetch=1, grid=(4,),
            in_specs=[blk, one, one, whole(uo), whole(up), whole(do), whole(dp)],
            out_specs=[col, col, blk, blk],
        ),
        out_shape=[jax.ShapeDtypeStruct((1024, 1024), BF)] * 2 + [jax.ShapeDtypeStruct((4, 2, 128, 2048), BF)] * 2,
        compiler_params=params(),
        cost_estimate=short(6 * 1024 * 1024 * 2048, 28 << 20),
    )(place, normed, mine, other, uo, up, do, dp)


def mixed_kernel(act_ref, do, dp, out_ref):
    a = act_ref[...]
    out_ref[...] = (dot(a[:, :512], do[...], (1, 0)) + dot(a[:, 512:], dp[...], (1, 0))).astype(BF)

def mix(act, do, dp):
    whole = lambda a: pl.BlockSpec(a.shape, lambda i: (0,) * a.ndim)
    return pl.pallas_call(
        mixed_kernel, grid=(4,),
        in_specs=[pl.BlockSpec((256, 1024), lambda i: (i, 0)), whole(do), whole(dp)],
        out_specs=pl.BlockSpec((256, 2048), lambda i: (i, 0)),
        out_shape=jax.ShapeDtypeStruct((1024, 2048), BF),
        compiler_params=params(),
        cost_estimate=short(2 * 1024 * 1024 * 2048, 10 << 20, 1),
    )(act, do, dp)


def branch_kernel(place_ref, heads_ref, w_ref, mine_ref, other_ref, left, out):
    @pl.when(pl.program_id(0) == 0)
    def _():
        for h in range(8):
            left[:, h * HD : (h + 1) * HD] = heads_ref[h].reshape(256, HD)

    out[...] = dot(left[...], w_ref[...], (1, 0)).reshape(2, 128, 512)
    mine_ref[...] = out[place_ref[0]]
    other_ref[...] = out[1 - place_ref[0]].astype(BF)

def branch(place, heads, w):
    col = pl.BlockSpec((128, 512), lambda i, p: (0, i))
    return pl.pallas_call(
        branch_kernel,
        grid_spec=pltpu.PrefetchScalarGridSpec(
            num_scalar_prefetch=1, grid=(4,),
            in_specs=[pl.BlockSpec((8, 2, 128, HD), lambda i, p: (0, 0, 0, 0)), pl.BlockSpec((1024, 512), lambda i, p: (0, i))],
            out_specs=[col, col],
            scratch_shapes=[pltpu.VMEM((256, 1024), BF), pltpu.VMEM((2, 128, 512), F32)],
        ),
        out_shape=[jax.ShapeDtypeStruct((128, 2048), F32), jax.ShapeDtypeStruct((128, 2048), BF)],
        compiler_params=params(),
        cost_estimate=short(2 * 256 * 1024 * 2048, 6 << 20),
    )(place, heads, w)

def grads_kernel(place_ref, n_ref, inc_ref, act_ref, gh_ref, mine_ref, partner_ref, keep_ref, send_ref):
    def down(ref):
        ref[...] = dot(act_ref[...], inc_ref[...], (0, 0)).astype(BF)

    @pl.when(pl.program_id(0) < 2)
    def _():
        down(mine_ref)

    @pl.when(pl.program_id(0) >= 2)
    def _():
        down(partner_ref)

    up = dot(gh_ref[...], n_ref[...], (0, 0)).astype(BF)
    even, odd = (
        jnp.concatenate([up[:, (2 * i + low) * 256 : (2 * i + low + 1) * 256] for i in range(4)], axis=1)
        for low in range(2)
    )

    @pl.when(place_ref[0] == 0)
    def _():
        keep_ref[...] = even
        send_ref[...] = odd

    @pl.when(place_ref[0] == 1)
    def _():
        keep_ref[...] = odd
        send_ref[...] = even

def weight_grads(place, n, inc, act, gh):
    rows = pl.BlockSpec((1024, 2048), lambda j, p: (0, 0))
    cols = pl.BlockSpec((1024, 256), lambda j, p: (0, j))
    part = pl.BlockSpec((256, 1024), lambda j, p: (j, 0))
    return pl.pallas_call(
        grads_kernel,
        grid_spec=pltpu.PrefetchScalarGridSpec(
            num_scalar_prefetch=1, grid=(4,),
            in_specs=[rows, rows, cols, cols],
            out_specs=[
                pl.BlockSpec((256, 2048), lambda j, p: (jnp.minimum(j, 1), 0)),
                pl.BlockSpec((256, 2048), lambda j, p: (jnp.maximum(j - 2, 0), 0)),
                part, part,
            ],
        ),
        out_shape=[jax.ShapeDtypeStruct((512, 2048), BF)] * 2 + [jax.ShapeDtypeStruct((1024, 1024), BF)] * 2,
        compiler_params=params(),
        cost_estimate=short(4 * 1024 * 1024 * 2048, 20 << 20),
    )(place, n, inc, act, gh)


def cut_kernel(place_ref, down_ref, down_got_ref, up_ref, up_got_ref, down_keep, down_send, up_keep, up_send):
    down = add(down_ref[...], down_got_ref[...])
    up = add(up_ref[...], up_got_ref[...])
    low = jnp.concatenate([up[:, :256], up[:, 512:768]], axis=1)
    high = jnp.concatenate([up[:, 256:512], up[:, 768:]], axis=1)

    @pl.when(place_ref[0] == 0)
    def _():
        down_keep[...] = down[:, :1024]
        down_send[...] = down[:, 1024:]

    @pl.when(place_ref[0] == 1)
    def _():
        down_keep[...] = down[:, 1024:]
        down_send[...] = down[:, :1024]

    @pl.when(place_ref[1] == 0)
    def _():
        up_keep[...] = low
        up_send[...] = high

    @pl.when(place_ref[1] == 1)
    def _():
        up_keep[...] = high
        up_send[...] = low

def cut(place, down, down_got, up, up_got):
    wide = pl.BlockSpec((128, 2048), lambda i, p: (i, 0))
    half = pl.BlockSpec((128, 1024), lambda i, p: (i, 0))
    four = pl.BlockSpec((256, 1024), lambda i, p: (i, 0))
    two = pl.BlockSpec((256, 512), lambda i, p: (i, 0))
    return pl.pallas_call(
        cut_kernel,
        grid_spec=pltpu.PrefetchScalarGridSpec(
            num_scalar_prefetch=1, grid=(4,),
            in_specs=[wide, wide, four, four],
            out_specs=[half, half, two, two],
        ),
        out_shape=[jax.ShapeDtypeStruct((512, 1024), BF)] * 2 + [jax.ShapeDtypeStruct((1024, 512), BF)] * 2,
        compiler_params=params(),
    )(place, down, down_got, up, up_got)


def cut_again_kernel(place_ref, down_ref, down_got_ref, up_ref, up_got_ref, down_keep, down_send, up_keep, up_send):
    down = add(down_ref[...], down_got_ref[...])
    up = add(up_ref[...], up_got_ref[...])

    def put(halves, at, keep, send):
        @pl.when(at == 0)
        def _():
            keep[...] = halves[0]
            send[...] = halves[1]

        @pl.when(at == 1)
        def _():
            keep[...] = halves[1]
            send[...] = halves[0]

    if up.shape[0] == 1024:
        quarters = [down[:, i * 256 : (i + 1) * 256] for i in range(4)]
        put([jnp.concatenate(quarters[i::2], axis=1) for i in range(2)], place_ref[0], down_keep, down_send)
        up_keep[...] = up[:512]
        up_send[...] = up[512:]
    else:
        put([down[:, :256], down[:, 256:]], place_ref[0], down_keep, down_send)
        put([up[:, :256], up[:, 256:]], place_ref[1], up_keep, up_send)

def cut_again(place, down, down_got, up, up_got):
    size = down.shape[1] // 2
    vmem = pl.BlockSpec(memory_space=pltpu.VMEM)
    return pl.pallas_call(
        cut_again_kernel,
        in_specs=[pl.BlockSpec(memory_space=pltpu.SMEM)] + [vmem] * 4,
        out_specs=[vmem] * 4,
        out_shape=[jax.ShapeDtypeStruct((512, size), BF)] * 4,
        compiler_params=params(),
    )(place, down, down_got, up, up_got)

def finish_kernel(down_ref, down_got_ref, up_ref, up_got_ref, down_out, up_out):
    down_out[...] = down_ref[...].astype(F32) + down_got_ref[...].astype(F32)
    up_out[...] = (up_ref[...].astype(F32) + up_got_ref[...].astype(F32)).T

def finish(*arrays):
    vmem = pl.BlockSpec(memory_space=pltpu.VMEM)
    return pl.pallas_call(
        finish_kernel,
        in_specs=[vmem] * 4,
        out_specs=[vmem] * 2,
        out_shape=[jax.ShapeDtypeStruct((512, 256), F32), jax.ShapeDtypeStruct((256, 512), F32)],
        compiler_params=params(),
    )(*arrays)


def heads_kernel(place_ref, mine_ref, other_ref, w_ref, out_ref, left):
    @pl.when(pl.program_id(0) == 0)
    def _():
        left[place_ref[0]] = mine_ref[...]
        left[1 - place_ref[0]] = other_ref[...]

    part = dot(left[...].reshape(256, 2048), w_ref[...], (1, 1)).astype(BF)
    for h in range(4):
        out_ref[h] = part[:, h * HD : (h + 1) * HD].reshape(2, 128, HD)

def to_heads(place, mine, other, w):
    rows = pl.BlockSpec((128, 2048), lambda i, p: (0, 0))
    return pl.pallas_call(
        heads_kernel,
        grid_spec=pltpu.PrefetchScalarGridSpec(
            num_scalar_prefetch=1, grid=(2,),
            in_specs=[rows, rows, pl.BlockSpec((512, 2048), lambda i, p: (i, 0))],
            out_specs=pl.BlockSpec((4, 2, 128, HD), lambda i, p: (i, 0, 0, 0)),
            scratch_shapes=[pltpu.VMEM((2, 128, 2048), BF)],
        ),
        out_shape=jax.ShapeDtypeStruct((8, 2, 128, HD), BF),
        compiler_params=params(),
    )(place, mine, other, w)


def both_kernel(own_ref, partner_ref, out_ref):
    for c in range(3):
        out_ref[c * HD : (c + 1) * HD] = own_ref[c].T
        out_ref[(c + 3) * HD : (c + 4) * HD] = partner_ref[c].T

def both_weights(own, partner):
    part = pl.BlockSpec((3, 256, HD), lambda i: (0, i, 0))
    return pl.pallas_call(
        both_kernel, grid=(8,),
        in_specs=[part, part],
        out_specs=pl.BlockSpec((6 * HD, 256), lambda i: (0, i)),
        out_shape=jax.ShapeDtypeStruct((6 * HD, 2048), BF),
        compiler_params=params(),
    )(own, partner)


def first_kernel(place_ref, mine_ref, got_ref, w_ref, out_ref, left):
    left[:, : 3 * HD] = mine_ref[...]
    left[:, 3 * HD :] = got_ref[...]
    out_ref[...] = dot(left[...], w_ref[...], (1, 0)).astype(BF)

def first_back(place, mine, got, weights):
    return pl.pallas_call(
        first_kernel,
        grid_spec=pltpu.PrefetchScalarGridSpec(
            num_scalar_prefetch=1, grid=(2,),
            in_specs=[
                pl.BlockSpec((512, 3 * HD), lambda i, p: (p[0] * 2 + i, 0)),
                pl.BlockSpec((512, 3 * HD), lambda i, p: (i, 0)),
                pl.BlockSpec((6 * HD, 2048), lambda i, p: (0, 0)),
            ],
            out_specs=pl.BlockSpec((512, 2048), lambda i, p: (i, 0)),
            scratch_shapes=[pltpu.VMEM((512, 6 * HD), BF)],
        ),
        out_shape=jax.ShapeDtypeStruct((1024, 2048), BF),
        compiler_params=params(),
        cost_estimate=short(2 * 1024 * 2048 * 768, 8 << 20),
    )(place, mine, got, weights)


def stack_kernel(*refs):
    for i, ref in enumerate(refs[:-1]):
        refs[-1][i] = ref[...]

def stack(*arrays):
    return pl.pallas_call(
        stack_kernel,
        in_specs=[pl.BlockSpec(memory_space=pltpu.VMEM)] * len(arrays),
        out_specs=pl.BlockSpec(memory_space=pltpu.VMEM),
        out_shape=jax.ShapeDtypeStruct((len(arrays), *arrays[0].shape), arrays[0].dtype),
        compiler_params=params(),
    )(*arrays)

def out_kernel(place_ref, mine_ref, partner_ref, grad_ref, out_ref):
    grad = grad_ref[...]
    out_ref[0, place_ref[0]] = dot(mine_ref[...], grad, (0, 0)).astype(BF)
    out_ref[0, 1 - place_ref[0]] = dot(partner_ref[...], grad, (0, 0)).astype(BF)

def out_grads(place, mine, partner, grad):
    heads = pl.BlockSpec((1024, HD), lambda i, p: (0, 0))
    return pl.pallas_call(
        out_kernel,
        grid_spec=pltpu.PrefetchScalarGridSpec(
            num_scalar_prefetch=1, grid=(8,),
            in_specs=[heads, heads, pl.BlockSpec((1024, 256), lambda i, p: (0, i))],
            out_specs=pl.BlockSpec((1, 2, HD, 256), lambda i, p: (i, 0, 0, 0)),
        ),
        out_shape=jax.ShapeDtypeStruct((8, 2, HD, 256), BF),
        compiler_params=params(),
        cost_estimate=short(2 * 1024 * 256 * 2048, 6 << 20),
    )(place, mine, partner, grad)


def qkv_grads_kernel(n_ref, gp_ref, w_ref, gain_ref, shift_ref, second_ref, out_ref, left, columns, sums):
    at = pl.program_id(0)

    @pl.when(at == 0)
    def _():
        left[...] = gp_ref[...].T
        columns[...] = jnp.sum(left[...].astype(F32), axis=1, keepdims=True)

    grad = dot(left[...], n_ref[...], (1, 0))
    out_ref[at, : 3 * HD] = grad.astype(BF)
    w = jnp.concatenate([w_ref[c].T for c in range(3)], axis=0).astype(F32)
    shift = jnp.sum(w * columns[...], axis=0, keepdims=True)
    gain = (jnp.sum(w * grad, axis=0, keepdims=True) - shift_ref[...] * shift) / gain_ref[...]
    for i, row in enumerate((gain, second_ref[0], shift, second_ref[1])):
        sums[pl.ds(8 * i + at, 1)] = row

    @pl.when(at == 7)
    def _():
        for i in range(8):
            out_ref[i, 3 * HD :] = sums[...].astype(BF)

def qkv_grads(normed, gp, w, gain, shift, second):
    row = pl.BlockSpec((1, 256), lambda i: (0, i))
    return pl.pallas_call(
        qkv_grads_kernel, grid=(8,),
        in_specs=[
            pl.BlockSpec((2048, 256), lambda i: (0, i)),
            pl.BlockSpec((2048, 384), lambda i: (0, 0)),
            pl.BlockSpec((3, 256, HD), lambda i: (0, i, 0)),
            row, row,
            pl.BlockSpec((2, 1, 256), lambda i: (0, 0, i)),
        ],
        out_specs=pl.BlockSpec((8, 3 * HD + 32, 256), lambda i: (0, 0, 0)),
        out_shape=jax.ShapeDtypeStruct((8, 3 * HD + 32, 256), BF),
        scratch_shapes=[pltpu.VMEM((384, 2048), BF), pltpu.VMEM((384, 1), F32), pltpu.VMEM((32, 256), F32)],
        compiler_params=params(),
        cost_estimate=short(2 * 2048 * 2048 * 384, 12 << 20, 1),
    )(normed, gp, w, gain[None], shift[None], second)


def scatter(values, axes):
    return lax.psum_scatter(values, axes, scatter_dimension=0, tiled=True).astype(F32)


def pick(values, index, axis):
    return lax.dynamic_index_in_dim(values, index, axis, False)


def after(values, *others):
    return lax.optimization_barrier((values, *others))[0]


def sum_over_tensor(values, gate, last_gate):
    values = after(values + core_swap(values), *gate)
    values = (values + z_far(values)) + (z_up(values) + z_down(values))
    values = after(values, last_gate)
    return values + x_pair(values)


def body(
    tokens,
    ln1_gain,
    ln1_shift,
    qkv_weight,
    out_weight,
    ln2_gain,
    ln2_shift,
    up_weight,
    down_weight,
    lengths,
    cotangent,
):
    x_hi, y, x_lo, z, core = (lax.axis_index(axis) for axis in AXES)
    tensor = x_lo * 8 + z * 2 + core
    length = lengths[0]

    place = jnp.stack([core, z, x_lo, y % 2])

    out_own = lax.all_gather(out_weight, ("z", "core"), axis=0, tiled=True)
    live_rows = (tensor * 128 + jnp.arange(128, dtype=jnp.int32) < length).astype(F32)[:, None]
    incoming_rows = cotangent.astype(F32) * live_rows
    sent_rows = incoming_rows.astype(BF)
    later_rows = after(sent_rows, out_own)
    along_z = [z_down(later_rows), z_far(sent_rows), z_up(later_rows)]
    up_partner, down_partner, qkv_partner = x_partner(up_weight), x_partner(down_weight), x_partner(qkv_weight)

    normed_first, projected = project(tokens, ln1_gain, ln1_shift, qkv_weight)
    attended, totals = attend(projected, lengths)
    heads = lax.all_to_all(attended, ("z", "core"), 0, 0)
    branch_mine, branch_other = branch(place[2:], after(heads, up_partner, along_z[1]), out_own)
    branch_other = after(x_pair(branch_other), down_partner, along_z[0], along_z[2])
    token_rows = lax.dynamic_slice_in_dim(tokens, tensor * 128, 128, 0).astype(F32)
    middle_rows = token_rows + (branch_mine + branch_other.astype(F32))
    unit_second, inverse_second = norm_stats(middle_rows)
    normed_rows = (unit_second * ln2_gain + ln2_shift).astype(BF)
    along_z = stack(after(sent_rows, normed_rows), *along_z)
    from_core = core_swap(along_z)

    normed_second = lax.all_gather(normed_rows, ("z", "core"), axis=0, tiled=True)
    activated, grad_hidden, grad_normed_part, incoming = front(
        place,
        after(normed_second, qkv_partner).reshape(4, 2, 128, 2048),
        along_z,
        from_core,
        up_weight,
        up_partner,
        down_weight,
        down_partner,
    )
    incoming = incoming.reshape(1024, 2048)
    grad_normed_second = scatter(grad_normed_part.reshape(1024, 2048), ("z", "core"))
    down_kept, down_sent, up_kept, up_sent = weight_grads(
        place[3:], normed_second, incoming, activated, grad_hidden
    )
    down_got, up_got = x_partner(down_sent), y_pair(up_sent)
    mixed_part = mix(after(activated, down_sent), down_weight, down_partner)
    qkv_both = both_weights(qkv_weight, after(qkv_partner, mixed_part))
    grad_normed_second = after(grad_normed_second, down_got, up_got, mixed_part, qkv_both)

    grad_middle = incoming_rows + norm_back(grad_normed_second, ln2_gain, unit_second, inverse_second)
    gain_second = jnp.sum(grad_normed_second * unit_second, axis=0)
    shift_second = jnp.sum(grad_normed_second, axis=0)
    grad_branch = grad_middle.astype(BF)
    branch_back = lax.all_gather(grad_branch, ("z", "core"), axis=0, tiled=True)

    branch_got = x_pair(grad_branch)
    down_kept, down_sent, up_kept, up_sent = cut(
        jnp.stack([x_hi, y // 2]), down_kept, after(down_got, grad_branch), up_kept, up_got
    )
    down_got, up_got = x_far(down_sent), y_far(up_sent)
    by_head = to_heads(place[2:], grad_branch, after(branch_got, down_sent), out_own)
    grad_attended = lax.all_to_all(by_head, ("z", "core"), 0, 0)
    mixed_rows = scatter(after(mixed_part, by_head), ("z", "core"))
    partner_heads = x_pair(pick(attended, 1 - x_lo, 1).reshape(1024, HD))

    grad_projected, projected_sent = attend_back(
        projected, after(grad_attended, partner_heads), totals, jnp.stack([length, x_lo])
    )
    projected_got = x_pair(projected_sent)
    second = jnp.stack([gain_second, shift_second])[:, None]
    qkv_sent = qkv_grads(normed_first, grad_projected, qkv_weight, ln1_gain, ln1_shift, second)
    qkv_got = lax.all_to_all(qkv_sent, BATCH, 0, 0)
    down_kept, down_sent, up_kept, up_sent = cut_again(
        jnp.stack([y % 2, x_hi]), down_kept, after(down_got, qkv_sent), up_kept, up_got
    )
    down_got, up_got = y_pair(down_sent), x_partner(up_sent)
    projected_got = after(projected_got, down_sent, mixed_rows)
    grad_first_part = first_back(place[2:], grad_projected, projected_got, qkv_both)
    grad_normed_first = scatter(grad_first_part, ("z", "core"))

    out_sent = out_grads(
        x_lo[None], after(pick(attended, x_lo, 1).reshape(1024, HD), grad_first_part), partner_heads, branch_back
    )
    down_kept, down_sent, up_kept, up_sent = cut_again(
        jnp.stack([y // 2, x_hi]), down_kept, after(down_got, out_sent), up_kept, up_got
    )
    qkv_got = after(qkv_got, down_sent)
    down_got, up_got = y_far(down_sent), x_far(up_sent)
    grad_down, grad_up = finish(down_kept, down_got, up_kept, up_got)
    out_got = lax.all_to_all(after(out_sent, qkv_got).reshape(16, HD, 256), ("x_hi", "y", "x_lo"), 0, 0)
    qkv_sums = jnp.sum(after(qkv_got, out_sent).astype(F32), axis=0)
    sums = sum_over_tensor(qkv_sums[3 * HD :].reshape(4, 2048), (down_got, up_got), out_got)
    grad_qkv = qkv_sums[: 3 * HD].reshape(3, HD, 256).transpose(0, 2, 1)
    output = (middle_rows + mixed_rows).astype(BF)
    grad_out = jnp.sum(out_got.astype(F32), axis=0)

    unit_rows, inverse_rows = norm_stats(token_rows)
    grad_tokens = (grad_middle + norm_back(grad_normed_first, ln1_gain, unit_rows, inverse_rows)).astype(BF)
    return (output, grad_tokens, grad_qkv, grad_out, grad_up, grad_down, sums[:2], sums[2:])


def solution(mesh):
    return jax.shard_map(
        body,
        mesh=Mesh(mesh.devices.reshape(2, 4, 2, 4, 2), AXES),
        in_specs=(
            P(BATCH, None),
            P(),
            P(),
            P(None, None, TENSOR),
            P(TENSOR, None),
            P(),
            P(),
            P(None, TENSOR),
            P(TENSOR, None),
            P(BATCH),
            P(AXES, None),
        ),
        out_specs=(
            P(AXES, None),
            P(AXES, None),
            P(None, BATCH, TENSOR),
            P(TENSOR, BATCH),
            P(BATCH, TENSOR),
            P(TENSOR, BATCH),
            P(),
            P(),
        ),
        check_vma=False,
    )
```

```python
import functools

import jax
import jax.numpy as jnp
from jax import lax
from jax.experimental import pallas as pl
from jax.experimental.pallas import tpu as pltpu
from jax.sharding import Mesh
from jax.sharding import PartitionSpec as P

HD = 128
EPS = 1e-05
MASKED_SCORE = -1e30
BF = jnp.bfloat16
F32 = jnp.float32

AXES = ("x_hi", "y", "x_lo", "z", "core")
BATCH, TENSOR = AXES[:2], AXES[2:]


def core_swap(values):
    return lax.ppermute(values, "core", [(0, 1), (1, 0)])


def x_pair(values):
    return lax.ppermute(values, "x_lo", [(0, 1), (1, 0)])


def x_partner(values):
    pairs = [(r * 2 + c, ((r + (1, -1)[c]) % 4) * 2 + c) for r in range(4) for c in range(2)]
    return lax.ppermute(values, ("x_hi", "x_lo", "core"), pairs)


def neighbours(axis):
    pairs = [(i * 2 + c, ((i ^ 1) if c == 0 else 3 - i) * 2 + c) for i in range(4) for c in range(2)]
    return lambda values: lax.ppermute(values, (axis, "core"), pairs)


y_pair = neighbours("y")


def shift(axes, sizes, step):
    return lambda values: lax.ppermute(values, axes, [(i, (i + step) % sizes) for i in range(sizes)])


z_up, z_down, z_far = (shift("z", 4, step) for step in (1, -1, 2))
y_far, x_far = shift("y", 4, 2), shift(("x_hi", "x_lo"), 4, 2)


def norm_stats(values):
    centre = jnp.mean(values, axis=-1, keepdims=True)
    offsets = values - centre
    variance = jnp.mean(offsets * offsets, axis=-1, keepdims=True)
    inverse = lax.rsqrt(variance + EPS)
    return (offsets * inverse, inverse)


def norm_back(grad_normed, gain, unit_rows, inverse):
    scaled = grad_normed * gain
    return inverse * (
        scaled
        - jnp.mean(scaled, axis=-1, keepdims=True)
        - unit_rows * jnp.mean(scaled * unit_rows, axis=-1, keepdims=True)
    )


def dot(left, right, dims):
    return lax.dot_general(left, right, ((dims[:1], dims[1:]), ((), ())), preferred_element_type=F32)


def short(flops, moved, by=64):
    return pl.CostEstimate(flops=flops // by, bytes_accessed=moved // by, transcendentals=0)


def add(left, right):
    return (left.astype(F32) + right.astype(F32)).astype(BF)


def params(limit=60, **kw):
    return pltpu.CompilerParams(vmem_limit_bytes=limit * 2**20, **kw)


def qkv_kernel(x_ref, gain_ref, shift_ref, w_ref, normed_ref, out_ref, weights):
    @pl.when(pl.program_id(0) == 0)
    def _():
        for c in range(3):
            weights[:, c * HD : (c + 1) * HD] = w_ref[c]

    x = x_ref[...].astype(F32)
    offsets = x - jnp.mean(x, axis=-1, keepdims=True)
    inverse = lax.rsqrt(jnp.mean(offsets * offsets, axis=-1, keepdims=True) + EPS)
    normed = (offsets * inverse * gain_ref[...] + shift_ref[...]).astype(BF)
    normed_ref[...] = normed
    out_ref[...] = dot(normed, weights[...], (1, 0)).astype(BF)

def project(tokens, gain, shift, weight):
    rows = 256
    return pl.pallas_call(
        qkv_kernel,
        grid=(2048 // rows,),
        in_specs=[
            pl.BlockSpec((rows, 2048), lambda i: (i, 0)),
            pl.BlockSpec((1, 2048), lambda i: (0, 0)),
            pl.BlockSpec((1, 2048), lambda i: (0, 0)),
            pl.BlockSpec((3, 2048, HD), lambda i: (0, 0, 0)),
        ],
        out_specs=[
            pl.BlockSpec((rows, 2048), lambda i: (i, 0)),
            pl.BlockSpec((rows, 3 * HD), lambda i: (i, 0)),
        ],
        out_shape=[jax.ShapeDtypeStruct((2048, 2048), BF), jax.ShapeDtypeStruct((2048, 3 * HD), BF)],
        scratch_shapes=[pltpu.VMEM((2048, 3 * HD), BF)],
        compiler_params=params(),
        cost_estimate=short(2 * 2048 * 2048 * 384, 20 << 20),
    )(tokens, gain[None], shift[None], weight)


QB = 512
SCALE = HD ** -0.5

def masked(scores, first_query, first_key, length):
    query = first_query + lax.broadcasted_iota(jnp.int32, scores.shape, 0)
    key = first_key + lax.broadcasted_iota(jnp.int32, scores.shape, 1)
    return jnp.where((key <= query) & (key < length), scores, MASKED_SCORE)

def forward_kernel(length_ref, qkv_ref, out_ref, total_ref):
    length = length_ref[0]
    for i in range(2048 // QB):
        q = qkv_ref[i * QB : (i + 1) * QB, :HD]
        parts = []
        for j in range(i + 1):
            k = qkv_ref[j * QB : (j + 1) * QB, HD : 2 * HD]
            parts.append(masked(dot(q, k, (1, 1)) * SCALE, i * QB, j * QB, length))
        peak = functools.reduce(jnp.maximum, [jnp.max(p, axis=-1, keepdims=True) for p in parts])
        total = jnp.zeros((QB, 1), F32)
        acc = jnp.zeros((QB, HD), F32)
        for j in range(i + 1):
            e = jnp.exp(parts[j] - peak)
            total += jnp.sum(e, axis=-1, keepdims=True)
            acc += dot(e.astype(BF), qkv_ref[j * QB : (j + 1) * QB, 2 * HD :], (1, 0))
        out = (acc / total).astype(BF)
        for b in range(QB // HD):
            block = i * (QB // HD) + b
            out_ref[block % 8, block // 8] = out[b * HD : (b + 1) * HD]
        total_ref[i * QB : (i + 1) * QB] = peak + jnp.log(total)

def attend(qkv, lengths):
    return pl.pallas_call(
        forward_kernel,
        in_specs=[pl.BlockSpec(memory_space=pltpu.SMEM), pl.BlockSpec(memory_space=pltpu.VMEM)],
        out_specs=[pl.BlockSpec(memory_space=pltpu.VMEM)] * 2,
        out_shape=[jax.ShapeDtypeStruct((8, 2, 128, HD), BF), jax.ShapeDtypeStruct((2048, 1), F32)],
        compiler_params=params(),
        cost_estimate=short(2 * 2 * 2048 * 2048 * 128, 3 << 20),
    )(lengths, qkv)

def backward_kernel(length_ref, qkv_ref, grad_ref, total_ref, out_ref, sent_ref, gk, gv, probs, gprobs):
    length = length_ref[0]
    n = 2048 // QB
    gk[...] = jnp.zeros_like(gk)
    gv[...] = jnp.zeros_like(gv)
    for i in range(n):
        rows = slice(i * QB, (i + 1) * QB)
        q = qkv_ref[rows, :HD]
        blocks = [i * (QB // HD) + b for b in range(QB // HD)]
        g = jnp.concatenate([grad_ref[b % 8, b // 8] for b in blocks], axis=0)
        total = total_ref[rows]
        centre = jnp.zeros((QB, 1), F32)
        for j in range(i + 1):
            keys = slice(j * QB, (j + 1) * QB)
            s = masked(dot(q, qkv_ref[keys, HD : 2 * HD], (1, 1)) * SCALE, i * QB, j * QB, length)
            p = jnp.exp(s - total)
            gp = dot(g, qkv_ref[keys, 2 * HD :], (1, 1))
            centre += jnp.sum(p * gp, axis=-1, keepdims=True)
            probs[:, keys] = p
            gprobs[:, keys] = gp
        gq = jnp.zeros((QB, HD), F32)
        for j in range(i + 1):
            keys = slice(j * QB, (j + 1) * QB)
            p = probs[:, keys]
            gs = (p * (gprobs[:, keys] - centre)).astype(BF)
            gq += dot(gs, qkv_ref[keys, HD : 2 * HD], (1, 0))
            gk[keys] += dot(gs, q, (0, 0))
            gv[keys] += dot(p.astype(BF), g, (0, 0))
        out_ref[rows, :HD] = (gq * SCALE).astype(BF)
    out_ref[:, HD : 2 * HD] = (gk[...] * SCALE).astype(BF)
    out_ref[:, 2 * HD :] = gv[...].astype(BF)

    @pl.when(length_ref[1] == 0)
    def _():
        sent_ref[...] = out_ref[1024:]

    @pl.when(length_ref[1] == 1)
    def _():
        sent_ref[...] = out_ref[:1024]

def attend_back(qkv, grad, totals, lengths):
    return pl.pallas_call(
        backward_kernel,
        in_specs=[pl.BlockSpec(memory_space=pltpu.SMEM)] + [pl.BlockSpec(memory_space=pltpu.VMEM)] * 3,
        out_specs=[pl.BlockSpec(memory_space=pltpu.VMEM)] * 2,
        out_shape=[jax.ShapeDtypeStruct((2048, 3 * HD), BF), jax.ShapeDtypeStruct((1024, 3 * HD), BF)],
        scratch_shapes=[pltpu.VMEM((2048, HD), F32), pltpu.VMEM((2048, HD), F32), pltpu.VMEM((QB, 2048), F32), pltpu.VMEM((QB, 2048), F32)],
        compiler_params=params(),
        cost_estimate=short(5 * 2 * 2048 * 1280 * 128, 4 << 20),
    )(lengths, qkv, grad, totals)


GELU_A = 0.7978845608028654
GELU_B = 0.044715

def front_kernel(place_ref, n_ref, mine_ref, other_ref, uo, up, do, dp, act_ref, gh_ref, part_ref, inc_ref):
    core = place_ref[0]
    inc_ref[0, core] = mine_ref[0]
    inc_ref[0, 1 - core] = other_ref[0]
    n = n_ref[0].reshape(256, 2048)
    inc = inc_ref[0].reshape(256, 2048)
    part = jnp.zeros((256, 2048), F32)
    for h, (u, d) in enumerate(((uo, do), (up, dp))):
        cols = slice(h * 512, (h + 1) * 512)
        hidden = dot(n, u[...], (1, 0))
        square = hidden * hidden
        t = jnp.tanh(GELU_A * (hidden + GELU_B * hidden * square))
        act_ref[:, cols] = (0.5 * hidden * (1 + t)).astype(BF)
        slope = 0.5 * (1 + t) + 0.5 * hidden * (1 - t * t) * (GELU_A * (1 + 3 * GELU_B * square))
        gh = (dot(inc, d[...], (1, 1)) * slope).astype(BF)
        gh_ref[:, cols] = gh
        part += dot(gh, u[...], (1, 1))
    part_ref[0] = part.astype(BF).reshape(2, 128, 2048)

def front(place, normed, mine, other, uo, up, do, dp):
    whole = lambda a: pl.BlockSpec(a.shape, lambda i, p: (0,) * a.ndim)
    blk = pl.BlockSpec((1, 2, 128, 2048), lambda i, p: (i, 0, 0, 0))
    one = pl.BlockSpec((1, 128, 2048), lambda i, p: ((i + 4 - p[1]) % 4, 0, 0))
    col = pl.BlockSpec((256, 1024), lambda i, p: (i, 0))
    return pl.pallas_call(
        front_kernel,
        grid_spec=pltpu.PrefetchScalarGridSpec(
            num_scalar_prefetch=1, grid=(4,),
            in_specs=[blk, one, one, whole(uo), whole(up), whole(do), whole(dp)],
            out_specs=[col, col, blk, blk],
        ),
        out_shape=[jax.ShapeDtypeStruct((1024, 1024), BF)] * 2 + [jax.ShapeDtypeStruct((4, 2, 128, 2048), BF)] * 2,
        compiler_params=params(),
        cost_estimate=short(6 * 1024 * 1024 * 2048, 28 << 20),
    )(place, normed, mine, other, uo, up, do, dp)


def mixed_kernel(act_ref, do, dp, out_ref):
    a = act_ref[...]
    out_ref[...] = (dot(a[:, :512], do[...], (1, 0)) + dot(a[:, 512:], dp[...], (1, 0))).astype(BF)

def mix(act, do, dp):
    whole = lambda a: pl.BlockSpec(a.shape, lambda i: (0,) * a.ndim)
    return pl.pallas_call(
        mixed_kernel, grid=(4,),
        in_specs=[pl.BlockSpec((256, 1024), lambda i: (i, 0)), whole(do), whole(dp)],
        out_specs=pl.BlockSpec((256, 2048), lambda i: (i, 0)),
        out_shape=jax.ShapeDtypeStruct((1024, 2048), BF),
        compiler_params=params(),
        cost_estimate=short(2 * 1024 * 1024 * 2048, 10 << 20, 1),
    )(act, do, dp)


def branch_kernel(place_ref, heads_ref, w_ref, mine_ref, other_ref, left, out):
    @pl.when(pl.program_id(0) == 0)
    def _():
        for h in range(8):
            left[:, h * HD : (h + 1) * HD] = heads_ref[h].reshape(256, HD)

    out[...] = dot(left[...], w_ref[...], (1, 0)).reshape(2, 128, 512)
    mine_ref[...] = out[place_ref[0]]
    other_ref[...] = out[1 - place_ref[0]].astype(BF)

def branch(place, heads, w):
    col = pl.BlockSpec((128, 512), lambda i, p: (0, i))
    return pl.pallas_call(
        branch_kernel,
        grid_spec=pltpu.PrefetchScalarGridSpec(
            num_scalar_prefetch=1, grid=(4,),
            in_specs=[pl.BlockSpec((8, 2, 128, HD), lambda i, p: (0, 0, 0, 0)), pl.BlockSpec((1024, 512), lambda i, p: (0, i))],
            out_specs=[col, col],
            scratch_shapes=[pltpu.VMEM((256, 1024), BF), pltpu.VMEM((2, 128, 512), F32)],
        ),
        out_shape=[jax.ShapeDtypeStruct((128, 2048), F32), jax.ShapeDtypeStruct((128, 2048), BF)],
        compiler_params=params(),
        cost_estimate=short(2 * 256 * 1024 * 2048, 6 << 20),
    )(place, heads, w)

def grads_kernel(place_ref, n_ref, inc_ref, act_ref, gh_ref, mine_ref, partner_ref, keep_ref, send_ref):
    def down(ref):
        ref[...] = dot(act_ref[...], inc_ref[...], (0, 0)).astype(BF)

    @pl.when(pl.program_id(0) < 2)
    def _():
        down(mine_ref)

    @pl.when(pl.program_id(0) >= 2)
    def _():
        down(partner_ref)

    up = dot(gh_ref[...], n_ref[...], (0, 0)).astype(BF)
    even, odd = (
        jnp.concatenate([up[:, (2 * i + low) * 256 : (2 * i + low + 1) * 256] for i in range(4)], axis=1)
        for low in range(2)
    )

    @pl.when(place_ref[0] == 0)
    def _():
        keep_ref[...] = even
        send_ref[...] = odd

    @pl.when(place_ref[0] == 1)
    def _():
        keep_ref[...] = odd
        send_ref[...] = even

def weight_grads(place, n, inc, act, gh):
    rows = pl.BlockSpec((1024, 2048), lambda j, p: (0, 0))
    cols = pl.BlockSpec((1024, 256), lambda j, p: (0, j))
    part = pl.BlockSpec((256, 1024), lambda j, p: (j, 0))
    return pl.pallas_call(
        grads_kernel,
        grid_spec=pltpu.PrefetchScalarGridSpec(
            num_scalar_prefetch=1, grid=(4,),
            in_specs=[rows, rows, cols, cols],
            out_specs=[
                pl.BlockSpec((256, 2048), lambda j, p: (jnp.minimum(j, 1), 0)),
                pl.BlockSpec((256, 2048), lambda j, p: (jnp.maximum(j - 2, 0), 0)),
                part, part,
            ],
        ),
        out_shape=[jax.ShapeDtypeStruct((512, 2048), BF)] * 2 + [jax.ShapeDtypeStruct((1024, 1024), BF)] * 2,
        compiler_params=params(),
        cost_estimate=short(4 * 1024 * 1024 * 2048, 20 << 20),
    )(place, n, inc, act, gh)


def cut_kernel(place_ref, down_ref, down_got_ref, up_ref, up_got_ref, down_keep, down_send, up_keep, up_send):
    down = add(down_ref[...], down_got_ref[...])
    up = add(up_ref[...], up_got_ref[...])
    low = jnp.concatenate([up[:, :256], up[:, 512:768]], axis=1)
    high = jnp.concatenate([up[:, 256:512], up[:, 768:]], axis=1)

    @pl.when(place_ref[0] == 0)
    def _():
        down_keep[...] = down[:, :1024]
        down_send[...] = down[:, 1024:]

    @pl.when(place_ref[0] == 1)
    def _():
        down_keep[...] = down[:, 1024:]
        down_send[...] = down[:, :1024]

    @pl.when(place_ref[1] == 0)
    def _():
        up_keep[...] = low
        up_send[...] = high

    @pl.when(place_ref[1] == 1)
    def _():
        up_keep[...] = high
        up_send[...] = low

def cut(place, down, down_got, up, up_got):
    wide = pl.BlockSpec((128, 2048), lambda i, p: (i, 0))
    half = pl.BlockSpec((128, 1024), lambda i, p: (i, 0))
    four = pl.BlockSpec((256, 1024), lambda i, p: (i, 0))
    two = pl.BlockSpec((256, 512), lambda i, p: (i, 0))
    return pl.pallas_call(
        cut_kernel,
        grid_spec=pltpu.PrefetchScalarGridSpec(
            num_scalar_prefetch=1, grid=(4,),
            in_specs=[wide, wide, four, four],
            out_specs=[half, half, two, two],
        ),
        out_shape=[jax.ShapeDtypeStruct((512, 1024), BF)] * 2 + [jax.ShapeDtypeStruct((1024, 512), BF)] * 2,
        compiler_params=params(),
    )(place, down, down_got, up, up_got)


def cut_again_kernel(place_ref, down_ref, down_got_ref, up_ref, up_got_ref, down_keep, down_send, up_keep, up_send):
    down = add(down_ref[...], down_got_ref[...])
    up = add(up_ref[...], up_got_ref[...])

    def put(halves, at, keep, send):
        @pl.when(at == 0)
        def _():
            keep[...] = halves[0]
            send[...] = halves[1]

        @pl.when(at == 1)
        def _():
            keep[...] = halves[1]
            send[...] = halves[0]

    if up.shape[0] == 1024:
        quarters = [down[:, i * 256 : (i + 1) * 256] for i in range(4)]
        put([jnp.concatenate(quarters[i::2], axis=1) for i in range(2)], place_ref[0], down_keep, down_send)
        up_keep[...] = up[:512]
        up_send[...] = up[512:]
    else:
        put([down[:, :256], down[:, 256:]], place_ref[0], down_keep, down_send)
        put([up[:, :256], up[:, 256:]], place_ref[1], up_keep, up_send)

def cut_again(place, down, down_got, up, up_got):
    size = down.shape[1] // 2
    vmem = pl.BlockSpec(memory_space=pltpu.VMEM)
    return pl.pallas_call(
        cut_again_kernel,
        in_specs=[pl.BlockSpec(memory_space=pltpu.SMEM)] + [vmem] * 4,
        out_specs=[vmem] * 4,
        out_shape=[jax.ShapeDtypeStruct((512, size), BF)] * 4,
        compiler_params=params(),
    )(place, down, down_got, up, up_got)

def finish_kernel(down_ref, down_got_ref, up_ref, up_got_ref, down_out, up_out):
    down_out[...] = down_ref[...].astype(F32) + down_got_ref[...].astype(F32)
    up_out[...] = (up_ref[...].astype(F32) + up_got_ref[...].astype(F32)).T

def finish(*arrays):
    vmem = pl.BlockSpec(memory_space=pltpu.VMEM)
    return pl.pallas_call(
        finish_kernel,
        in_specs=[vmem] * 4,
        out_specs=[vmem] * 2,
        out_shape=[jax.ShapeDtypeStruct((512, 256), F32), jax.ShapeDtypeStruct((256, 512), F32)],
        compiler_params=params(),
    )(*arrays)


def heads_kernel(place_ref, mine_ref, other_ref, w_ref, out_ref, left):
    @pl.when(pl.program_id(0) == 0)
    def _():
        left[place_ref[0]] = mine_ref[...]
        left[1 - place_ref[0]] = other_ref[...]

    part = dot(left[...].reshape(256, 2048), w_ref[...], (1, 1)).astype(BF)
    for h in range(4):
        out_ref[h] = part[:, h * HD : (h + 1) * HD].reshape(2, 128, HD)

def to_heads(place, mine, other, w):
    rows = pl.BlockSpec((128, 2048), lambda i, p: (0, 0))
    return pl.pallas_call(
        heads_kernel,
        grid_spec=pltpu.PrefetchScalarGridSpec(
            num_scalar_prefetch=1, grid=(2,),
            in_specs=[rows, rows, pl.BlockSpec((512, 2048), lambda i, p: (i, 0))],
            out_specs=pl.BlockSpec((4, 2, 128, HD), lambda i, p: (i, 0, 0, 0)),
            scratch_shapes=[pltpu.VMEM((2, 128, 2048), BF)],
        ),
        out_shape=jax.ShapeDtypeStruct((8, 2, 128, HD), BF),
        compiler_params=params(),
    )(place, mine, other, w)


def both_kernel(own_ref, partner_ref, out_ref):
    for c in range(3):
        out_ref[c * HD : (c + 1) * HD] = own_ref[c].T
        out_ref[(c + 3) * HD : (c + 4) * HD] = partner_ref[c].T

def both_weights(own, partner):
    part = pl.BlockSpec((3, 256, HD), lambda i: (0, i, 0))
    return pl.pallas_call(
        both_kernel, grid=(8,),
        in_specs=[part, part],
        out_specs=pl.BlockSpec((6 * HD, 256), lambda i: (0, i)),
        out_shape=jax.ShapeDtypeStruct((6 * HD, 2048), BF),
        compiler_params=params(),
    )(own, partner)


def first_kernel(place_ref, mine_ref, got_ref, w_ref, out_ref, left):
    left[:, : 3 * HD] = mine_ref[...]
    left[:, 3 * HD :] = got_ref[...]
    out_ref[...] = dot(left[...], w_ref[...], (1, 0)).astype(BF)

def first_back(place, mine, got, weights):
    return pl.pallas_call(
        first_kernel,
        grid_spec=pltpu.PrefetchScalarGridSpec(
            num_scalar_prefetch=1, grid=(2,),
            in_specs=[
                pl.BlockSpec((512, 3 * HD), lambda i, p: (p[0] * 2 + i, 0)),
                pl.BlockSpec((512, 3 * HD), lambda i, p: (i, 0)),
                pl.BlockSpec((6 * HD, 2048), lambda i, p: (0, 0)),
            ],
            out_specs=pl.BlockSpec((512, 2048), lambda i, p: (i, 0)),
            scratch_shapes=[pltpu.VMEM((512, 6 * HD), BF)],
        ),
        out_shape=jax.ShapeDtypeStruct((1024, 2048), BF),
        compiler_params=params(),
        cost_estimate=short(2 * 1024 * 2048 * 768, 8 << 20),
    )(place, mine, got, weights)


def stack_kernel(*refs):
    for i, ref in enumerate(refs[:-1]):
        refs[-1][i] = ref[...]

def stack(*arrays):
    return pl.pallas_call(
        stack_kernel,
        in_specs=[pl.BlockSpec(memory_space=pltpu.VMEM)] * len(arrays),
        out_specs=pl.BlockSpec(memory_space=pltpu.VMEM),
        out_shape=jax.ShapeDtypeStruct((len(arrays), *arrays[0].shape), arrays[0].dtype),
        compiler_params=params(),
    )(*arrays)

def out_kernel(place_ref, mine_ref, partner_ref, grad_ref, out_ref):
    grad = grad_ref[...]
    out_ref[0, place_ref[0]] = dot(mine_ref[...], grad, (0, 0)).astype(BF)
    out_ref[0, 1 - place_ref[0]] = dot(partner_ref[...], grad, (0, 0)).astype(BF)

def out_grads(place, mine, partner, grad):
    heads = pl.BlockSpec((1024, HD), lambda i, p: (0, 0))
    return pl.pallas_call(
        out_kernel,
        grid_spec=pltpu.PrefetchScalarGridSpec(
            num_scalar_prefetch=1, grid=(8,),
            in_specs=[heads, heads, pl.BlockSpec((1024, 256), lambda i, p: (0, i))],
            out_specs=pl.BlockSpec((1, 2, HD, 256), lambda i, p: (i, 0, 0, 0)),
        ),
        out_shape=jax.ShapeDtypeStruct((8, 2, HD, 256), BF),
        compiler_params=params(),
        cost_estimate=short(2 * 1024 * 256 * 2048, 6 << 20),
    )(place, mine, partner, grad)


def qkv_grads_kernel(n_ref, gp_ref, w_ref, gain_ref, shift_ref, second_ref, out_ref, left, columns, sums):
    at = pl.program_id(0)

    @pl.when(at == 0)
    def _():
        left[...] = gp_ref[...].T
        columns[...] = jnp.sum(left[...].astype(F32), axis=1, keepdims=True)

    grad = dot(left[...], n_ref[...], (1, 0))
    out_ref[at, : 3 * HD] = grad.astype(BF)
    w = jnp.concatenate([w_ref[c].T for c in range(3)], axis=0).astype(F32)
    shift = jnp.sum(w * columns[...], axis=0, keepdims=True)
    gain = (jnp.sum(w * grad, axis=0, keepdims=True) - shift_ref[...] * shift) / gain_ref[...]
    for i, row in enumerate((gain, second_ref[0], shift, second_ref[1])):
        sums[pl.ds(8 * i + at, 1)] = row

    @pl.when(at == 7)
    def _():
        for i in range(8):
            out_ref[i, 3 * HD :] = sums[...].astype(BF)

def qkv_grads(normed, gp, w, gain, shift, second):
    row = pl.BlockSpec((1, 256), lambda i: (0, i))
    return pl.pallas_call(
        qkv_grads_kernel, grid=(8,),
        in_specs=[
            pl.BlockSpec((2048, 256), lambda i: (0, i)),
            pl.BlockSpec((2048, 384), lambda i: (0, 0)),
            pl.BlockSpec((3, 256, HD), lambda i: (0, i, 0)),
            row, row,
            pl.BlockSpec((2, 1, 256), lambda i: (0, 0, i)),
        ],
        out_specs=pl.BlockSpec((8, 3 * HD + 32, 256), lambda i: (0, 0, 0)),
        out_shape=jax.ShapeDtypeStruct((8, 3 * HD + 32, 256), BF),
        scratch_shapes=[pltpu.VMEM((384, 2048), BF), pltpu.VMEM((384, 1), F32), pltpu.VMEM((32, 256), F32)],
        compiler_params=params(),
        cost_estimate=short(2 * 2048 * 2048 * 384, 12 << 20, 1),
    )(normed, gp, w, gain[None], shift[None], second)


def scatter(values, axes):
    return lax.psum_scatter(values, axes, scatter_dimension=0, tiled=True).astype(F32)


def pick(values, index, axis):
    return lax.dynamic_index_in_dim(values, index, axis, False)


def after(values, *others):
    return lax.optimization_barrier((values, *others))[0]


def sum_over_tensor(values, last_gate):
    values = values + core_swap(values)
    values = (values + z_far(values)) + (z_up(values) + z_down(values))
    values = after(values, last_gate)
    return values + x_pair(values)


def body(
    tokens,
    ln1_gain,
    ln1_shift,
    qkv_weight,
    out_weight,
    ln2_gain,
    ln2_shift,
    up_weight,
    down_weight,
    lengths,
    cotangent,
):
    x_hi, y, x_lo, z, core = (lax.axis_index(axis) for axis in AXES)
    tensor = x_lo * 8 + z * 2 + core
    length = lengths[0]

    place = jnp.stack([core, z, x_lo, y % 2])

    out_own = lax.all_gather(out_weight, ("z", "core"), axis=0, tiled=True)
    live_rows = (tensor * 128 + jnp.arange(128, dtype=jnp.int32) < length).astype(F32)[:, None]
    incoming_rows = cotangent.astype(F32) * live_rows
    sent_rows = incoming_rows.astype(BF)
    later_rows = after(sent_rows, out_own)
    along_z = [z_down(later_rows), z_far(sent_rows), z_up(later_rows)]
    up_partner, down_partner, qkv_partner = x_partner(up_weight), x_partner(down_weight), x_partner(qkv_weight)

    normed_first, projected = project(tokens, ln1_gain, ln1_shift, qkv_weight)
    attended, totals = attend(projected, lengths)
    heads = lax.all_to_all(attended, ("z", "core"), 0, 0)
    branch_mine, branch_other = branch(place[2:], after(heads, up_partner, along_z[1]), out_own)
    branch_other = after(x_pair(branch_other), down_partner, along_z[0], along_z[2])
    token_rows = lax.dynamic_slice_in_dim(tokens, tensor * 128, 128, 0).astype(F32)
    middle_rows = token_rows + (branch_mine + branch_other.astype(F32))
    unit_second, inverse_second = norm_stats(middle_rows)
    normed_rows = (unit_second * ln2_gain + ln2_shift).astype(BF)
    along_z = stack(after(sent_rows, normed_rows), *along_z)
    from_core = core_swap(along_z)

    normed_second = lax.all_gather(normed_rows, ("z", "core"), axis=0, tiled=True)
    activated, grad_hidden, grad_normed_part, incoming = front(
        place,
        after(normed_second, qkv_partner).reshape(4, 2, 128, 2048),
        along_z,
        from_core,
        up_weight,
        up_partner,
        down_weight,
        down_partner,
    )
    incoming = incoming.reshape(1024, 2048)
    grad_normed_second = scatter(grad_normed_part.reshape(1024, 2048), ("z", "core"))
    down_kept, down_sent, up_kept, up_sent = weight_grads(
        place[3:], normed_second, incoming, activated, grad_hidden
    )
    down_got, up_got = x_partner(down_sent), y_pair(up_sent)
    mixed_part = mix(after(activated, down_sent), down_weight, down_partner)
    qkv_both = both_weights(qkv_weight, after(qkv_partner, mixed_part))
    grad_normed_second = after(grad_normed_second, down_got, up_got, mixed_part, qkv_both)

    grad_middle = incoming_rows + norm_back(grad_normed_second, ln2_gain, unit_second, inverse_second)
    gain_second = jnp.sum(grad_normed_second * unit_second, axis=0)
    shift_second = jnp.sum(grad_normed_second, axis=0)
    grad_branch = grad_middle.astype(BF)
    branch_back = lax.all_gather(grad_branch, ("z", "core"), axis=0, tiled=True)

    branch_got = x_pair(grad_branch)
    down_kept, down_sent, up_kept, up_sent = cut(
        jnp.stack([x_hi, y // 2]), down_kept, after(down_got, grad_branch), up_kept, up_got
    )
    down_got, up_got = x_far(down_sent), y_far(up_sent)
    by_head = to_heads(place[2:], grad_branch, after(branch_got, down_sent), out_own)
    grad_attended = lax.all_to_all(by_head, ("z", "core"), 0, 0)
    mixed_rows = scatter(after(mixed_part, by_head), ("z", "core"))
    partner_heads = x_pair(pick(attended, 1 - x_lo, 1).reshape(1024, HD))

    grad_projected, projected_sent = attend_back(
        projected, after(grad_attended, partner_heads), totals, jnp.stack([length, x_lo])
    )
    projected_got = x_pair(projected_sent)
    second = jnp.stack([gain_second, shift_second])[:, None]
    qkv_sent = qkv_grads(normed_first, grad_projected, qkv_weight, ln1_gain, ln1_shift, second)
    qkv_got = lax.all_to_all(qkv_sent, BATCH, 0, 0)
    down_kept, down_sent, up_kept, up_sent = cut_again(
        jnp.stack([y % 2, x_hi]), down_kept, after(down_got, qkv_sent), up_kept, up_got
    )
    down_got, up_got = y_pair(down_sent), x_partner(up_sent)
    projected_got = after(projected_got, down_sent, mixed_rows)
    grad_first_part = first_back(place[2:], grad_projected, projected_got, qkv_both)
    grad_normed_first = scatter(after(grad_first_part, down_got, up_got), ("z", "core"))

    down_kept, down_sent, up_kept, up_sent = cut_again(
        jnp.stack([y // 2, x_hi]), down_kept, after(down_got, grad_first_part), up_kept, up_got
    )
    out_sent = out_grads(
        x_lo[None], after(pick(attended, x_lo, 1).reshape(1024, HD), down_sent), partner_heads, branch_back
    )
    down_got, up_got = y_far(down_sent), x_far(up_sent)
    grad_down, grad_up = finish(down_kept, down_got, up_kept, up_got)
    out_got = lax.all_to_all(after(out_sent, qkv_got).reshape(16, HD, 256), ("x_hi", "y", "x_lo"), 0, 0)
    qkv_sums = jnp.sum(after(qkv_got, out_sent, down_got, up_got).astype(F32), axis=0)
    sums = sum_over_tensor(qkv_sums[3 * HD :].reshape(4, 2048), out_got)
    grad_qkv = qkv_sums[: 3 * HD].reshape(3, HD, 256).transpose(0, 2, 1)
    output = (middle_rows + mixed_rows).astype(BF)
    grad_out = jnp.sum(out_got.astype(F32), axis=0)

    unit_rows, inverse_rows = norm_stats(token_rows)
    grad_tokens = (grad_middle + norm_back(grad_normed_first, ln1_gain, unit_rows, inverse_rows)).astype(BF)
    return (output, grad_tokens, grad_qkv, grad_out, grad_up, grad_down, sums[:2], sums[2:])


def solution(mesh):
    return jax.shard_map(
        body,
        mesh=Mesh(mesh.devices.reshape(2, 4, 2, 4, 2), AXES),
        in_specs=(
            P(BATCH, None),
            P(),
            P(),
            P(None, None, TENSOR),
            P(TENSOR, None),
            P(),
            P(),
            P(None, TENSOR),
            P(TENSOR, None),
            P(BATCH),
            P(AXES, None),
        ),
        out_specs=(
            P(AXES, None),
            P(AXES, None),
            P(None, BATCH, TENSOR),
            P(TENSOR, BATCH),
            P(BATCH, TENSOR),
            P(TENSOR, BATCH),
            P(),
            P(),
        ),
        check_vma=False,
    )
```

```python
import functools

import jax
import jax.numpy as jnp
from jax import lax
from jax.experimental import pallas as pl
from jax.experimental.pallas import tpu as pltpu
from jax.sharding import Mesh
from jax.sharding import PartitionSpec as P

HD = 128
EPS = 1e-05
MASKED_SCORE = -1e30
BF = jnp.bfloat16
F32 = jnp.float32

AXES = ("x_hi", "y", "x_lo", "z", "core")
BATCH, TENSOR = AXES[:2], AXES[2:]


def core_swap(values):
    return lax.ppermute(values, "core", [(0, 1), (1, 0)])


def x_pair(values):
    return lax.ppermute(values, "x_lo", [(0, 1), (1, 0)])


def x_partner(values):
    pairs = [(r * 2 + c, ((r + (1, -1)[c]) % 4) * 2 + c) for r in range(4) for c in range(2)]
    return lax.ppermute(values, ("x_hi", "x_lo", "core"), pairs)


def neighbours(axis):
    pairs = [(i * 2 + c, ((i ^ 1) if c == 0 else 3 - i) * 2 + c) for i in range(4) for c in range(2)]
    return lambda values: lax.ppermute(values, (axis, "core"), pairs)


y_pair = neighbours("y")


def shift(axes, sizes, step):
    return lambda values: lax.ppermute(values, axes, [(i, (i + step) % sizes) for i in range(sizes)])


z_up, z_down, z_far = (shift("z", 4, step) for step in (1, -1, 2))
y_far, x_far = shift("y", 4, 2), shift(("x_hi", "x_lo"), 4, 2)


def norm_stats(values):
    centre = jnp.mean(values, axis=-1, keepdims=True)
    offsets = values - centre
    variance = jnp.mean(offsets * offsets, axis=-1, keepdims=True)
    inverse = lax.rsqrt(variance + EPS)
    return (offsets * inverse, inverse)


def norm_back(grad_normed, gain, unit_rows, inverse):
    scaled = grad_normed * gain
    return inverse * (
        scaled
        - jnp.mean(scaled, axis=-1, keepdims=True)
        - unit_rows * jnp.mean(scaled * unit_rows, axis=-1, keepdims=True)
    )


def dot(left, right, dims):
    return lax.dot_general(left, right, ((dims[:1], dims[1:]), ((), ())), preferred_element_type=F32)


def short(flops, moved, by=64):
    return pl.CostEstimate(flops=flops // by, bytes_accessed=moved // by, transcendentals=0)


def add(left, right):
    return (left.astype(F32) + right.astype(F32)).astype(BF)


def params(limit=60, **kw):
    return pltpu.CompilerParams(vmem_limit_bytes=limit * 2**20, **kw)


def qkv_kernel(x_ref, gain_ref, shift_ref, w_ref, normed_ref, out_ref, weights):
    @pl.when(pl.program_id(0) == 0)
    def _():
        for c in range(3):
            weights[:, c * HD : (c + 1) * HD] = w_ref[c]

    x = x_ref[...].astype(F32)
    offsets = x - jnp.mean(x, axis=-1, keepdims=True)
    inverse = lax.rsqrt(jnp.mean(offsets * offsets, axis=-1, keepdims=True) + EPS)
    normed = (offsets * inverse * gain_ref[...] + shift_ref[...]).astype(BF)
    normed_ref[...] = normed
    out_ref[...] = dot(normed, weights[...], (1, 0)).astype(BF)

def project(tokens, gain, shift, weight):
    rows = 256
    return pl.pallas_call(
        qkv_kernel,
        grid=(2048 // rows,),
        in_specs=[
            pl.BlockSpec((rows, 2048), lambda i: (i, 0)),
            pl.BlockSpec((1, 2048), lambda i: (0, 0)),
            pl.BlockSpec((1, 2048), lambda i: (0, 0)),
            pl.BlockSpec((3, 2048, HD), lambda i: (0, 0, 0)),
        ],
        out_specs=[
            pl.BlockSpec((rows, 2048), lambda i: (i, 0)),
            pl.BlockSpec((rows, 3 * HD), lambda i: (i, 0)),
        ],
        out_shape=[jax.ShapeDtypeStruct((2048, 2048), BF), jax.ShapeDtypeStruct((2048, 3 * HD), BF)],
        scratch_shapes=[pltpu.VMEM((2048, 3 * HD), BF)],
        compiler_params=params(),
        cost_estimate=short(2 * 2048 * 2048 * 384, 20 << 20),
    )(tokens, gain[None], shift[None], weight)


QB = 512
SCALE = HD ** -0.5

def masked(scores, first_query, first_key, length):
    query = first_query + lax.broadcasted_iota(jnp.int32, scores.shape, 0)
    key = first_key + lax.broadcasted_iota(jnp.int32, scores.shape, 1)
    return jnp.where((key <= query) & (key < length), scores, MASKED_SCORE)

def forward_kernel(length_ref, qkv_ref, out_ref, total_ref):
    length = length_ref[0]
    for i in range(2048 // QB):
        q = qkv_ref[i * QB : (i + 1) * QB, :HD]
        parts = []
        for j in range(i + 1):
            k = qkv_ref[j * QB : (j + 1) * QB, HD : 2 * HD]
            parts.append(masked(dot(q, k, (1, 1)) * SCALE, i * QB, j * QB, length))
        peak = functools.reduce(jnp.maximum, [jnp.max(p, axis=-1, keepdims=True) for p in parts])
        total = jnp.zeros((QB, 1), F32)
        acc = jnp.zeros((QB, HD), F32)
        for j in range(i + 1):
            e = jnp.exp(parts[j] - peak)
            total += jnp.sum(e, axis=-1, keepdims=True)
            acc += dot(e.astype(BF), qkv_ref[j * QB : (j + 1) * QB, 2 * HD :], (1, 0))
        out = (acc / total).astype(BF)
        for b in range(QB // HD):
            block = i * (QB // HD) + b
            out_ref[block % 8, block // 8] = out[b * HD : (b + 1) * HD]
        total_ref[i * QB : (i + 1) * QB] = peak + jnp.log(total)

def attend(qkv, lengths):
    return pl.pallas_call(
        forward_kernel,
        in_specs=[pl.BlockSpec(memory_space=pltpu.SMEM), pl.BlockSpec(memory_space=pltpu.VMEM)],
        out_specs=[pl.BlockSpec(memory_space=pltpu.VMEM)] * 2,
        out_shape=[jax.ShapeDtypeStruct((8, 2, 128, HD), BF), jax.ShapeDtypeStruct((2048, 1), F32)],
        compiler_params=params(),
        cost_estimate=short(2 * 2 * 2048 * 2048 * 128, 3 << 20),
    )(lengths, qkv)

def backward_kernel(length_ref, qkv_ref, grad_ref, total_ref, out_ref, sent_ref, gk, gv, probs, gprobs):
    length = length_ref[0]
    n = 2048 // QB
    gk[...] = jnp.zeros_like(gk)
    gv[...] = jnp.zeros_like(gv)
    for i in range(n):
        rows = slice(i * QB, (i + 1) * QB)
        q = qkv_ref[rows, :HD]
        blocks = [i * (QB // HD) + b for b in range(QB // HD)]
        g = jnp.concatenate([grad_ref[b % 8, b // 8] for b in blocks], axis=0)
        total = total_ref[rows]
        centre = jnp.zeros((QB, 1), F32)
        for j in range(i + 1):
            keys = slice(j * QB, (j + 1) * QB)
            s = masked(dot(q, qkv_ref[keys, HD : 2 * HD], (1, 1)) * SCALE, i * QB, j * QB, length)
            p = jnp.exp(s - total)
            gp = dot(g, qkv_ref[keys, 2 * HD :], (1, 1))
            centre += jnp.sum(p * gp, axis=-1, keepdims=True)
            probs[:, keys] = p
            gprobs[:, keys] = gp
        gq = jnp.zeros((QB, HD), F32)
        for j in range(i + 1):
            keys = slice(j * QB, (j + 1) * QB)
            p = probs[:, keys]
            gs = (p * (gprobs[:, keys] - centre)).astype(BF)
            gq += dot(gs, qkv_ref[keys, HD : 2 * HD], (1, 0))
            gk[keys] += dot(gs, q, (0, 0))
            gv[keys] += dot(p.astype(BF), g, (0, 0))
        out_ref[rows, :HD] = (gq * SCALE).astype(BF)
    out_ref[:, HD : 2 * HD] = (gk[...] * SCALE).astype(BF)
    out_ref[:, 2 * HD :] = gv[...].astype(BF)

    @pl.when(length_ref[1] == 0)
    def _():
        sent_ref[...] = out_ref[1024:]

    @pl.when(length_ref[1] == 1)
    def _():
        sent_ref[...] = out_ref[:1024]

def attend_back(qkv, grad, totals, lengths):
    return pl.pallas_call(
        backward_kernel,
        in_specs=[pl.BlockSpec(memory_space=pltpu.SMEM)] + [pl.BlockSpec(memory_space=pltpu.VMEM)] * 3,
        out_specs=[pl.BlockSpec(memory_space=pltpu.VMEM)] * 2,
        out_shape=[jax.ShapeDtypeStruct((2048, 3 * HD), BF), jax.ShapeDtypeStruct((1024, 3 * HD), BF)],
        scratch_shapes=[pltpu.VMEM((2048, HD), F32), pltpu.VMEM((2048, HD), F32), pltpu.VMEM((QB, 2048), F32), pltpu.VMEM((QB, 2048), F32)],
        compiler_params=params(),
        cost_estimate=short(5 * 2 * 2048 * 1280 * 128, 4 << 20),
    )(lengths, qkv, grad, totals)


GELU_A = 0.7978845608028654
GELU_B = 0.044715

def front_kernel(place_ref, n_ref, mine_ref, other_ref, uo, up, do, dp, act_ref, gh_ref, part_ref, inc_ref):
    core = place_ref[0]
    inc_ref[0, core] = mine_ref[0]
    inc_ref[0, 1 - core] = other_ref[0]
    n = n_ref[0].reshape(256, 2048)
    inc = inc_ref[0].reshape(256, 2048)
    part = jnp.zeros((256, 2048), F32)
    for h, (u, d) in enumerate(((uo, do), (up, dp))):
        cols = slice(h * 512, (h + 1) * 512)
        hidden = dot(n, u[...], (1, 0))
        square = hidden * hidden
        t = jnp.tanh(GELU_A * (hidden + GELU_B * hidden * square))
        act_ref[:, cols] = (0.5 * hidden * (1 + t)).astype(BF)
        slope = 0.5 * (1 + t) + 0.5 * hidden * (1 - t * t) * (GELU_A * (1 + 3 * GELU_B * square))
        gh = (dot(inc, d[...], (1, 1)) * slope).astype(BF)
        gh_ref[:, cols] = gh
        part += dot(gh, u[...], (1, 1))
    part_ref[0] = part.astype(BF).reshape(2, 128, 2048)

def front(place, normed, mine, other, uo, up, do, dp):
    whole = lambda a: pl.BlockSpec(a.shape, lambda i, p: (0,) * a.ndim)
    blk = pl.BlockSpec((1, 2, 128, 2048), lambda i, p: (i, 0, 0, 0))
    one = pl.BlockSpec((1, 128, 2048), lambda i, p: ((i + 4 - p[1]) % 4, 0, 0))
    col = pl.BlockSpec((256, 1024), lambda i, p: (i, 0))
    return pl.pallas_call(
        front_kernel,
        grid_spec=pltpu.PrefetchScalarGridSpec(
            num_scalar_prefetch=1, grid=(4,),
            in_specs=[blk, one, one, whole(uo), whole(up), whole(do), whole(dp)],
            out_specs=[col, col, blk, blk],
        ),
        out_shape=[jax.ShapeDtypeStruct((1024, 1024), BF)] * 2 + [jax.ShapeDtypeStruct((4, 2, 128, 2048), BF)] * 2,
        compiler_params=params(),
        cost_estimate=short(6 * 1024 * 1024 * 2048, 28 << 20),
    )(place, normed, mine, other, uo, up, do, dp)


def mixed_kernel(act_ref, do, dp, out_ref):
    a = act_ref[...]
    out_ref[...] = (dot(a[:, :512], do[...], (1, 0)) + dot(a[:, 512:], dp[...], (1, 0))).astype(BF)

def mix(act, do, dp):
    whole = lambda a: pl.BlockSpec(a.shape, lambda i: (0,) * a.ndim)
    return pl.pallas_call(
        mixed_kernel, grid=(4,),
        in_specs=[pl.BlockSpec((256, 1024), lambda i: (i, 0)), whole(do), whole(dp)],
        out_specs=pl.BlockSpec((256, 2048), lambda i: (i, 0)),
        out_shape=jax.ShapeDtypeStruct((1024, 2048), BF),
        compiler_params=params(),
        cost_estimate=short(2 * 1024 * 1024 * 2048, 10 << 20, 1),
    )(act, do, dp)


def branch_kernel(place_ref, heads_ref, w_ref, mine_ref, other_ref, left, out):
    @pl.when(pl.program_id(0) == 0)
    def _():
        for h in range(8):
            left[:, h * HD : (h + 1) * HD] = heads_ref[h].reshape(256, HD)

    out[...] = dot(left[...], w_ref[...], (1, 0)).reshape(2, 128, 512)
    mine_ref[...] = out[place_ref[0]]
    other_ref[...] = out[1 - place_ref[0]].astype(BF)

def branch(place, heads, w):
    col = pl.BlockSpec((128, 512), lambda i, p: (0, i))
    return pl.pallas_call(
        branch_kernel,
        grid_spec=pltpu.PrefetchScalarGridSpec(
            num_scalar_prefetch=1, grid=(4,),
            in_specs=[pl.BlockSpec((8, 2, 128, HD), lambda i, p: (0, 0, 0, 0)), pl.BlockSpec((1024, 512), lambda i, p: (0, i))],
            out_specs=[col, col],
            scratch_shapes=[pltpu.VMEM((256, 1024), BF), pltpu.VMEM((2, 128, 512), F32)],
        ),
        out_shape=[jax.ShapeDtypeStruct((128, 2048), F32), jax.ShapeDtypeStruct((128, 2048), BF)],
        compiler_params=params(),
        cost_estimate=short(2 * 256 * 1024 * 2048, 6 << 20),
    )(place, heads, w)

def grads_kernel(place_ref, n_ref, inc_ref, act_ref, gh_ref, mine_ref, partner_ref, keep_ref, send_ref):
    def down(ref):
        ref[...] = dot(act_ref[...], inc_ref[...], (0, 0)).astype(BF)

    @pl.when(pl.program_id(0) < 2)
    def _():
        down(mine_ref)

    @pl.when(pl.program_id(0) >= 2)
    def _():
        down(partner_ref)

    up = dot(gh_ref[...], n_ref[...], (0, 0)).astype(BF)
    even, odd = (
        jnp.concatenate([up[:, (2 * i + low) * 256 : (2 * i + low + 1) * 256] for i in range(4)], axis=1)
        for low in range(2)
    )

    @pl.when(place_ref[0] == 0)
    def _():
        keep_ref[...] = even
        send_ref[...] = odd

    @pl.when(place_ref[0] == 1)
    def _():
        keep_ref[...] = odd
        send_ref[...] = even

def weight_grads(place, n, inc, act, gh):
    rows = pl.BlockSpec((1024, 2048), lambda j, p: (0, 0))
    cols = pl.BlockSpec((1024, 256), lambda j, p: (0, j))
    part = pl.BlockSpec((256, 1024), lambda j, p: (j, 0))
    return pl.pallas_call(
        grads_kernel,
        grid_spec=pltpu.PrefetchScalarGridSpec(
            num_scalar_prefetch=1, grid=(4,),
            in_specs=[rows, rows, cols, cols],
            out_specs=[
                pl.BlockSpec((256, 2048), lambda j, p: (jnp.minimum(j, 1), 0)),
                pl.BlockSpec((256, 2048), lambda j, p: (jnp.maximum(j - 2, 0), 0)),
                part, part,
            ],
        ),
        out_shape=[jax.ShapeDtypeStruct((512, 2048), BF)] * 2 + [jax.ShapeDtypeStruct((1024, 1024), BF)] * 2,
        compiler_params=params(),
        cost_estimate=short(4 * 1024 * 1024 * 2048, 20 << 20),
    )(place, n, inc, act, gh)


def cut_kernel(place_ref, down_ref, down_got_ref, up_ref, up_got_ref, down_keep, down_send, up_keep, up_send):
    down = add(down_ref[...], down_got_ref[...])
    up = add(up_ref[...], up_got_ref[...])
    low = jnp.concatenate([up[:, :256], up[:, 512:768]], axis=1)
    high = jnp.concatenate([up[:, 256:512], up[:, 768:]], axis=1)

    @pl.when(place_ref[0] == 0)
    def _():
        down_keep[...] = down[:, :1024]
        down_send[...] = down[:, 1024:]

    @pl.when(place_ref[0] == 1)
    def _():
        down_keep[...] = down[:, 1024:]
        down_send[...] = down[:, :1024]

    @pl.when(place_ref[1] == 0)
    def _():
        up_keep[...] = low
        up_send[...] = high

    @pl.when(place_ref[1] == 1)
    def _():
        up_keep[...] = high
        up_send[...] = low

def cut(place, down, down_got, up, up_got):
    wide = pl.BlockSpec((128, 2048), lambda i, p: (i, 0))
    half = pl.BlockSpec((128, 1024), lambda i, p: (i, 0))
    four = pl.BlockSpec((256, 1024), lambda i, p: (i, 0))
    two = pl.BlockSpec((256, 512), lambda i, p: (i, 0))
    return pl.pallas_call(
        cut_kernel,
        grid_spec=pltpu.PrefetchScalarGridSpec(
            num_scalar_prefetch=1, grid=(4,),
            in_specs=[wide, wide, four, four],
            out_specs=[half, half, two, two],
        ),
        out_shape=[jax.ShapeDtypeStruct((512, 1024), BF)] * 2 + [jax.ShapeDtypeStruct((1024, 512), BF)] * 2,
        compiler_params=params(),
    )(place, down, down_got, up, up_got)


def cut_again_kernel(place_ref, down_ref, down_got_ref, up_ref, up_got_ref, down_keep, down_send, up_keep, up_send):
    down = add(down_ref[...], down_got_ref[...])
    up = add(up_ref[...], up_got_ref[...])

    def put(halves, at, keep, send):
        @pl.when(at == 0)
        def _():
            keep[...] = halves[0]
            send[...] = halves[1]

        @pl.when(at == 1)
        def _():
            keep[...] = halves[1]
            send[...] = halves[0]

    if up.shape[0] == 1024:
        quarters = [down[:, i * 256 : (i + 1) * 256] for i in range(4)]
        put([jnp.concatenate(quarters[i::2], axis=1) for i in range(2)], place_ref[0], down_keep, down_send)
        up_keep[...] = up[:512]
        up_send[...] = up[512:]
    else:
        put([down[:, :256], down[:, 256:]], place_ref[0], down_keep, down_send)
        put([up[:, :256], up[:, 256:]], place_ref[1], up_keep, up_send)

def cut_again(place, down, down_got, up, up_got):
    size = down.shape[1] // 2
    vmem = pl.BlockSpec(memory_space=pltpu.VMEM)
    return pl.pallas_call(
        cut_again_kernel,
        in_specs=[pl.BlockSpec(memory_space=pltpu.SMEM)] + [vmem] * 4,
        out_specs=[vmem] * 4,
        out_shape=[jax.ShapeDtypeStruct((512, size), BF)] * 4,
        compiler_params=params(),
    )(place, down, down_got, up, up_got)

def finish_kernel(down_ref, down_got_ref, up_ref, up_got_ref, down_out, up_out):
    down_out[...] = down_ref[...].astype(F32) + down_got_ref[...].astype(F32)
    up_out[...] = (up_ref[...].astype(F32) + up_got_ref[...].astype(F32)).T

def finish(*arrays):
    vmem = pl.BlockSpec(memory_space=pltpu.VMEM)
    return pl.pallas_call(
        finish_kernel,
        in_specs=[vmem] * 4,
        out_specs=[vmem] * 2,
        out_shape=[jax.ShapeDtypeStruct((512, 256), F32), jax.ShapeDtypeStruct((256, 512), F32)],
        compiler_params=params(),
    )(*arrays)


def heads_kernel(place_ref, mine_ref, other_ref, w_ref, out_ref, left):
    @pl.when(pl.program_id(0) == 0)
    def _():
        left[place_ref[0]] = mine_ref[...]
        left[1 - place_ref[0]] = other_ref[...]

    part = dot(left[...].reshape(256, 2048), w_ref[...], (1, 1)).astype(BF)
    for h in range(4):
        out_ref[h] = part[:, h * HD : (h + 1) * HD].reshape(2, 128, HD)

def to_heads(place, mine, other, w):
    rows = pl.BlockSpec((128, 2048), lambda i, p: (0, 0))
    return pl.pallas_call(
        heads_kernel,
        grid_spec=pltpu.PrefetchScalarGridSpec(
            num_scalar_prefetch=1, grid=(2,),
            in_specs=[rows, rows, pl.BlockSpec((512, 2048), lambda i, p: (i, 0))],
            out_specs=pl.BlockSpec((4, 2, 128, HD), lambda i, p: (i, 0, 0, 0)),
            scratch_shapes=[pltpu.VMEM((2, 128, 2048), BF)],
        ),
        out_shape=jax.ShapeDtypeStruct((8, 2, 128, HD), BF),
        compiler_params=params(),
    )(place, mine, other, w)


def both_kernel(own_ref, partner_ref, out_ref):
    for c in range(3):
        out_ref[c * HD : (c + 1) * HD] = own_ref[c].T
        out_ref[(c + 3) * HD : (c + 4) * HD] = partner_ref[c].T

def both_weights(own, partner):
    part = pl.BlockSpec((3, 256, HD), lambda i: (0, i, 0))
    return pl.pallas_call(
        both_kernel, grid=(8,),
        in_specs=[part, part],
        out_specs=pl.BlockSpec((6 * HD, 256), lambda i: (0, i)),
        out_shape=jax.ShapeDtypeStruct((6 * HD, 2048), BF),
        compiler_params=params(),
    )(own, partner)


def first_kernel(place_ref, mine_ref, got_ref, w_ref, out_ref, left):
    left[:, : 3 * HD] = mine_ref[...]
    left[:, 3 * HD :] = got_ref[...]
    out_ref[...] = dot(left[...], w_ref[...], (1, 0)).astype(BF)

def first_back(place, mine, got, weights):
    return pl.pallas_call(
        first_kernel,
        grid_spec=pltpu.PrefetchScalarGridSpec(
            num_scalar_prefetch=1, grid=(2,),
            in_specs=[
                pl.BlockSpec((512, 3 * HD), lambda i, p: (p[0] * 2 + i, 0)),
                pl.BlockSpec((512, 3 * HD), lambda i, p: (i, 0)),
                pl.BlockSpec((6 * HD, 2048), lambda i, p: (0, 0)),
            ],
            out_specs=pl.BlockSpec((512, 2048), lambda i, p: (i, 0)),
            scratch_shapes=[pltpu.VMEM((512, 6 * HD), BF)],
        ),
        out_shape=jax.ShapeDtypeStruct((1024, 2048), BF),
        compiler_params=params(),
        cost_estimate=short(2 * 1024 * 2048 * 768, 8 << 20),
    )(place, mine, got, weights)


def stack_kernel(*refs):
    for i, ref in enumerate(refs[:-1]):
        refs[-1][i] = ref[...]

def stack(*arrays):
    return pl.pallas_call(
        stack_kernel,
        in_specs=[pl.BlockSpec(memory_space=pltpu.VMEM)] * len(arrays),
        out_specs=pl.BlockSpec(memory_space=pltpu.VMEM),
        out_shape=jax.ShapeDtypeStruct((len(arrays), *arrays[0].shape), arrays[0].dtype),
        compiler_params=params(),
    )(*arrays)

def out_kernel(place_ref, mine_ref, partner_ref, grad_ref, out_ref):
    grad = grad_ref[...]
    out_ref[0, place_ref[0]] = dot(mine_ref[...], grad, (0, 0)).astype(BF)
    out_ref[0, 1 - place_ref[0]] = dot(partner_ref[...], grad, (0, 0)).astype(BF)

def out_grads(place, mine, partner, grad):
    heads = pl.BlockSpec((1024, HD), lambda i, p: (0, 0))
    return pl.pallas_call(
        out_kernel,
        grid_spec=pltpu.PrefetchScalarGridSpec(
            num_scalar_prefetch=1, grid=(8,),
            in_specs=[heads, heads, pl.BlockSpec((1024, 256), lambda i, p: (0, i))],
            out_specs=pl.BlockSpec((1, 2, HD, 256), lambda i, p: (i, 0, 0, 0)),
        ),
        out_shape=jax.ShapeDtypeStruct((8, 2, HD, 256), BF),
        compiler_params=params(),
        cost_estimate=short(2 * 1024 * 256 * 2048, 6 << 20),
    )(place, mine, partner, grad)


def qkv_grads_kernel(n_ref, gp_ref, w_ref, gain_ref, shift_ref, second_ref, out_ref, left, columns, sums):
    at = pl.program_id(0)

    @pl.when(at == 0)
    def _():
        left[...] = gp_ref[...].T
        columns[...] = jnp.sum(left[...].astype(F32), axis=1, keepdims=True)

    grad = dot(left[...], n_ref[...], (1, 0))
    out_ref[at, : 3 * HD] = grad.astype(BF)
    w = jnp.concatenate([w_ref[c].T for c in range(3)], axis=0).astype(F32)
    shift = jnp.sum(w * columns[...], axis=0, keepdims=True)
    gain = (jnp.sum(w * grad, axis=0, keepdims=True) - shift_ref[...] * shift) / gain_ref[...]
    for i, row in enumerate((gain, second_ref[0], shift, second_ref[1])):
        sums[pl.ds(8 * i + at, 1)] = row

    @pl.when(at == 7)
    def _():
        for i in range(8):
            out_ref[i, 3 * HD :] = sums[...].astype(BF)

def qkv_grads(normed, gp, w, gain, shift, second):
    row = pl.BlockSpec((1, 256), lambda i: (0, i))
    return pl.pallas_call(
        qkv_grads_kernel, grid=(8,),
        in_specs=[
            pl.BlockSpec((2048, 256), lambda i: (0, i)),
            pl.BlockSpec((2048, 384), lambda i: (0, 0)),
            pl.BlockSpec((3, 256, HD), lambda i: (0, i, 0)),
            row, row,
            pl.BlockSpec((2, 1, 256), lambda i: (0, 0, i)),
        ],
        out_specs=pl.BlockSpec((8, 3 * HD + 32, 256), lambda i: (0, 0, 0)),
        out_shape=jax.ShapeDtypeStruct((8, 3 * HD + 32, 256), BF),
        scratch_shapes=[pltpu.VMEM((384, 2048), BF), pltpu.VMEM((384, 1), F32), pltpu.VMEM((32, 256), F32)],
        compiler_params=params(),
        cost_estimate=short(2 * 2048 * 2048 * 384, 12 << 20, 1),
    )(normed, gp, w, gain[None], shift[None], second)


def scatter(values, axes):
    return lax.psum_scatter(values, axes, scatter_dimension=0, tiled=True).astype(F32)


def pick(values, index, axis):
    return lax.dynamic_index_in_dim(values, index, axis, False)


def after(values, *others):
    return lax.optimization_barrier((values, *others))[0]


def sum_over_tensor(values, last_gate):
    values = values + core_swap(values)
    values = (values + z_far(values)) + (z_up(values) + z_down(values))
    return values + after(x_pair(values), last_gate)


def body(
    tokens,
    ln1_gain,
    ln1_shift,
    qkv_weight,
    out_weight,
    ln2_gain,
    ln2_shift,
    up_weight,
    down_weight,
    lengths,
    cotangent,
):
    x_hi, y, x_lo, z, core = (lax.axis_index(axis) for axis in AXES)
    tensor = x_lo * 8 + z * 2 + core
    length = lengths[0]

    place = jnp.stack([core, z, x_lo, y % 2])

    out_own = lax.all_gather(out_weight, ("z", "core"), axis=0, tiled=True)
    live_rows = (tensor * 128 + jnp.arange(128, dtype=jnp.int32) < length).astype(F32)[:, None]
    incoming_rows = cotangent.astype(F32) * live_rows
    sent_rows = incoming_rows.astype(BF)
    later_rows = after(sent_rows, out_own)
    along_z = [z_down(later_rows), z_far(sent_rows), z_up(later_rows)]
    up_partner, down_partner, qkv_partner = x_partner(up_weight), x_partner(down_weight), x_partner(qkv_weight)

    normed_first, projected = project(tokens, ln1_gain, ln1_shift, qkv_weight)
    attended, totals = attend(projected, lengths)
    heads = lax.all_to_all(attended, ("z", "core"), 0, 0)
    branch_mine, branch_other = branch(place[2:], after(heads, up_partner, along_z[1]), out_own)
    branch_other = after(x_pair(branch_other), down_partner, along_z[0], along_z[2])
    token_rows = lax.dynamic_slice_in_dim(tokens, tensor * 128, 128, 0).astype(F32)
    middle_rows = token_rows + (branch_mine + branch_other.astype(F32))
    unit_second, inverse_second = norm_stats(middle_rows)
    normed_rows = (unit_second * ln2_gain + ln2_shift).astype(BF)
    partner_heads = x_pair(pick(after(attended, normed_rows), 1 - x_lo, 1).reshape(1024, HD))
    along_z = stack(after(sent_rows, normed_rows), *along_z)
    from_core = core_swap(along_z)

    normed_second = lax.all_gather(normed_rows, ("z", "core"), axis=0, tiled=True)
    activated, grad_hidden, grad_normed_part, incoming = front(
        place,
        after(normed_second, qkv_partner, partner_heads).reshape(4, 2, 128, 2048),
        along_z,
        from_core,
        up_weight,
        up_partner,
        down_weight,
        down_partner,
    )
    incoming = incoming.reshape(1024, 2048)
    grad_normed_second = scatter(grad_normed_part.reshape(1024, 2048), ("z", "core"))
    down_kept, down_sent, up_kept, up_sent = weight_grads(
        place[3:], normed_second, incoming, activated, grad_hidden
    )
    down_got, up_got = x_partner(down_sent), y_pair(up_sent)
    mixed_part = mix(after(activated, down_sent), down_weight, down_partner)
    qkv_both = both_weights(qkv_weight, after(qkv_partner, mixed_part))
    grad_normed_second = after(grad_normed_second, down_got, up_got, mixed_part, qkv_both)

    grad_middle = incoming_rows + norm_back(grad_normed_second, ln2_gain, unit_second, inverse_second)
    gain_second = jnp.sum(grad_normed_second * unit_second, axis=0)
    shift_second = jnp.sum(grad_normed_second, axis=0)
    grad_branch = grad_middle.astype(BF)
    branch_back = lax.all_gather(grad_branch, ("z", "core"), axis=0, tiled=True)

    branch_got = x_pair(grad_branch)
    down_kept, down_sent, up_kept, up_sent = cut(
        jnp.stack([x_hi, y // 2]), down_kept, after(down_got, grad_branch), up_kept, up_got
    )
    down_got, up_got = x_far(down_sent), y_far(up_sent)
    by_head = to_heads(place[2:], grad_branch, after(branch_got, down_sent), out_own)
    grad_attended = lax.all_to_all(by_head, ("z", "core"), 0, 0)
    mixed_rows = scatter(after(mixed_part, by_head), ("z", "core"))

    grad_projected, projected_sent = attend_back(
        projected, grad_attended, totals, jnp.stack([length, x_lo])
    )
    projected_got = x_pair(projected_sent)
    second = jnp.stack([gain_second, shift_second])[:, None]
    qkv_sent = qkv_grads(normed_first, grad_projected, qkv_weight, ln1_gain, ln1_shift, second)
    qkv_got = lax.all_to_all(qkv_sent, BATCH, 0, 0)
    down_kept, down_sent, up_kept, up_sent = cut_again(
        jnp.stack([y % 2, x_hi]), down_kept, after(down_got, qkv_sent), up_kept, up_got
    )
    down_got, up_got = y_pair(down_sent), x_partner(up_sent)
    projected_got = after(projected_got, down_sent, mixed_rows)
    grad_first_part = first_back(place[2:], grad_projected, projected_got, qkv_both)
    grad_normed_first = scatter(after(grad_first_part, down_got, up_got), ("z", "core"))

    down_kept, down_sent, up_kept, up_sent = cut_again(
        jnp.stack([y // 2, x_hi]), down_kept, after(down_got, grad_first_part), up_kept, up_got
    )
    out_sent = out_grads(
        x_lo[None], after(pick(attended, x_lo, 1).reshape(1024, HD), down_sent), partner_heads, branch_back
    )
    down_got, up_got = y_far(down_sent), x_far(up_sent)
    grad_down, grad_up = finish(down_kept, down_got, up_kept, up_got)
    out_got = lax.all_to_all(after(out_sent, qkv_got).reshape(16, HD, 256), ("x_hi", "y", "x_lo"), 0, 0)
    qkv_sums = jnp.sum(after(qkv_got, out_sent, down_got, up_got).astype(F32), axis=0)
    sums = sum_over_tensor(qkv_sums[3 * HD :].reshape(4, 2048), out_got)
    grad_qkv = qkv_sums[: 3 * HD].reshape(3, HD, 256).transpose(0, 2, 1)
    output = (middle_rows + mixed_rows).astype(BF)
    grad_out = jnp.sum(out_got.astype(F32), axis=0)

    unit_rows, inverse_rows = norm_stats(token_rows)
    grad_tokens = (grad_middle + norm_back(grad_normed_first, ln1_gain, unit_rows, inverse_rows)).astype(BF)
    return (output, grad_tokens, grad_qkv, grad_out, grad_up, grad_down, sums[:2], sums[2:])


def solution(mesh):
    return jax.shard_map(
        body,
        mesh=Mesh(mesh.devices.reshape(2, 4, 2, 4, 2), AXES),
        in_specs=(
            P(BATCH, None),
            P(),
            P(),
            P(None, None, TENSOR),
            P(TENSOR, None),
            P(),
            P(),
            P(None, TENSOR),
            P(TENSOR, None),
            P(BATCH),
            P(AXES, None),
        ),
        out_specs=(
            P(AXES, None),
            P(AXES, None),
            P(None, BATCH, TENSOR),
            P(TENSOR, BATCH),
            P(BATCH, TENSOR),
            P(TENSOR, BATCH),
            P(),
            P(),
        ),
        check_vma=False,
    )
```

```python
import functools

import jax
import jax.numpy as jnp
from jax import lax
from jax.experimental import pallas as pl
from jax.experimental.pallas import tpu as pltpu
from jax.sharding import Mesh
from jax.sharding import PartitionSpec as P

HD = 128
EPS = 1e-05
MASKED_SCORE = -1e30
BF = jnp.bfloat16
F32 = jnp.float32

AXES = ("x_hi", "y", "x_lo", "z", "core")
BATCH, TENSOR = AXES[:2], AXES[2:]


def core_swap(values):
    return lax.ppermute(values, "core", [(0, 1), (1, 0)])


def x_pair(values):
    return lax.ppermute(values, "x_lo", [(0, 1), (1, 0)])


def x_partner(values):
    pairs = [(r * 2 + c, ((r + (1, -1)[c]) % 4) * 2 + c) for r in range(4) for c in range(2)]
    return lax.ppermute(values, ("x_hi", "x_lo", "core"), pairs)


def neighbours(axis):
    pairs = [(i * 2 + c, ((i ^ 1) if c == 0 else 3 - i) * 2 + c) for i in range(4) for c in range(2)]
    return lambda values: lax.ppermute(values, (axis, "core"), pairs)


y_pair = neighbours("y")


def shift(axes, sizes, step):
    return lambda values: lax.ppermute(values, axes, [(i, (i + step) % sizes) for i in range(sizes)])


z_up, z_down, z_far = (shift("z", 4, step) for step in (1, -1, 2))
y_far, x_far = shift("y", 4, 2), shift(("x_hi", "x_lo"), 4, 2)


def norm_stats(values):
    centre = jnp.mean(values, axis=-1, keepdims=True)
    offsets = values - centre
    variance = jnp.mean(offsets * offsets, axis=-1, keepdims=True)
    inverse = lax.rsqrt(variance + EPS)
    return (offsets * inverse, inverse)


def norm_back(grad_normed, gain, unit_rows, inverse):
    scaled = grad_normed * gain
    return inverse * (
        scaled
        - jnp.mean(scaled, axis=-1, keepdims=True)
        - unit_rows * jnp.mean(scaled * unit_rows, axis=-1, keepdims=True)
    )


def dot(left, right, dims):
    return lax.dot_general(left, right, ((dims[:1], dims[1:]), ((), ())), preferred_element_type=F32)


def short(flops, moved, by=64):
    return pl.CostEstimate(flops=flops // by, bytes_accessed=moved // by, transcendentals=0)


def add(left, right):
    return (left.astype(F32) + right.astype(F32)).astype(BF)


def params(limit=60, **kw):
    return pltpu.CompilerParams(vmem_limit_bytes=limit * 2**20, **kw)


def qkv_kernel(x_ref, gain_ref, shift_ref, w_ref, normed_ref, out_ref, weights):
    @pl.when(pl.program_id(0) == 0)
    def _():
        for c in range(3):
            weights[:, c * HD : (c + 1) * HD] = w_ref[c]

    x = x_ref[...].astype(F32)
    offsets = x - jnp.mean(x, axis=-1, keepdims=True)
    inverse = lax.rsqrt(jnp.mean(offsets * offsets, axis=-1, keepdims=True) + EPS)
    normed = (offsets * inverse * gain_ref[...] + shift_ref[...]).astype(BF)
    normed_ref[...] = normed
    out_ref[...] = dot(normed, weights[...], (1, 0)).astype(BF)

def project(tokens, gain, shift, weight):
    rows = 256
    return pl.pallas_call(
        qkv_kernel,
        grid=(2048 // rows,),
        in_specs=[
            pl.BlockSpec((rows, 2048), lambda i: (i, 0)),
            pl.BlockSpec((1, 2048), lambda i: (0, 0)),
            pl.BlockSpec((1, 2048), lambda i: (0, 0)),
            pl.BlockSpec((3, 2048, HD), lambda i: (0, 0, 0)),
        ],
        out_specs=[
            pl.BlockSpec((rows, 2048), lambda i: (i, 0)),
            pl.BlockSpec((rows, 3 * HD), lambda i: (i, 0)),
        ],
        out_shape=[jax.ShapeDtypeStruct((2048, 2048), BF), jax.ShapeDtypeStruct((2048, 3 * HD), BF)],
        scratch_shapes=[pltpu.VMEM((2048, 3 * HD), BF)],
        compiler_params=params(),
        cost_estimate=short(2 * 2048 * 2048 * 384, 20 << 20),
    )(tokens, gain[None], shift[None], weight)


QB = 512
SCALE = HD ** -0.5

def masked(scores, first_query, first_key, length):
    query = first_query + lax.broadcasted_iota(jnp.int32, scores.shape, 0)
    key = first_key + lax.broadcasted_iota(jnp.int32, scores.shape, 1)
    return jnp.where((key <= query) & (key < length), scores, MASKED_SCORE)

def forward_kernel(length_ref, qkv_ref, out_ref, total_ref):
    length = length_ref[0]
    for i in range(2048 // QB):
        q = qkv_ref[i * QB : (i + 1) * QB, :HD]
        parts = []
        for j in range(i + 1):
            k = qkv_ref[j * QB : (j + 1) * QB, HD : 2 * HD]
            parts.append(masked(dot(q, k, (1, 1)) * SCALE, i * QB, j * QB, length))
        peak = functools.reduce(jnp.maximum, [jnp.max(p, axis=-1, keepdims=True) for p in parts])
        total = jnp.zeros((QB, 1), F32)
        acc = jnp.zeros((QB, HD), F32)
        for j in range(i + 1):
            e = jnp.exp(parts[j] - peak)
            total += jnp.sum(e, axis=-1, keepdims=True)
            acc += dot(e.astype(BF), qkv_ref[j * QB : (j + 1) * QB, 2 * HD :], (1, 0))
        out = (acc / total).astype(BF)
        for b in range(QB // HD):
            block = i * (QB // HD) + b
            out_ref[block % 8, block // 8] = out[b * HD : (b + 1) * HD]
        total_ref[i * QB : (i + 1) * QB] = peak + jnp.log(total)

def attend(qkv, lengths):
    return pl.pallas_call(
        forward_kernel,
        in_specs=[pl.BlockSpec(memory_space=pltpu.SMEM), pl.BlockSpec(memory_space=pltpu.VMEM)],
        out_specs=[pl.BlockSpec(memory_space=pltpu.VMEM)] * 2,
        out_shape=[jax.ShapeDtypeStruct((8, 2, 128, HD), BF), jax.ShapeDtypeStruct((2048, 1), F32)],
        compiler_params=params(),
        cost_estimate=short(2 * 2 * 2048 * 2048 * 128, 3 << 20),
    )(lengths, qkv)

def backward_kernel(length_ref, qkv_ref, grad_ref, total_ref, out_ref, sent_ref, gk, gv, probs, gprobs):
    length = length_ref[0]
    n = 2048 // QB
    gk[...] = jnp.zeros_like(gk)
    gv[...] = jnp.zeros_like(gv)
    for i in range(n):
        rows = slice(i * QB, (i + 1) * QB)
        q = qkv_ref[rows, :HD]
        blocks = [i * (QB // HD) + b for b in range(QB // HD)]
        g = jnp.concatenate([grad_ref[b % 8, b // 8] for b in blocks], axis=0)
        total = total_ref[rows]
        centre = jnp.zeros((QB, 1), F32)
        for j in range(i + 1):
            keys = slice(j * QB, (j + 1) * QB)
            s = masked(dot(q, qkv_ref[keys, HD : 2 * HD], (1, 1)) * SCALE, i * QB, j * QB, length)
            p = jnp.exp(s - total)
            gp = dot(g, qkv_ref[keys, 2 * HD :], (1, 1))
            centre += jnp.sum(p * gp, axis=-1, keepdims=True)
            probs[:, keys] = p
            gprobs[:, keys] = gp
        gq = jnp.zeros((QB, HD), F32)
        for j in range(i + 1):
            keys = slice(j * QB, (j + 1) * QB)
            p = probs[:, keys]
            gs = (p * (gprobs[:, keys] - centre)).astype(BF)
            gq += dot(gs, qkv_ref[keys, HD : 2 * HD], (1, 0))
            gk[keys] += dot(gs, q, (0, 0))
            gv[keys] += dot(p.astype(BF), g, (0, 0))
        out_ref[rows, :HD] = (gq * SCALE).astype(BF)
    out_ref[:, HD : 2 * HD] = (gk[...] * SCALE).astype(BF)
    out_ref[:, 2 * HD :] = gv[...].astype(BF)

    @pl.when(length_ref[1] == 0)
    def _():
        sent_ref[...] = out_ref[1024:]

    @pl.when(length_ref[1] == 1)
    def _():
        sent_ref[...] = out_ref[:1024]

def attend_back(qkv, grad, totals, lengths):
    return pl.pallas_call(
        backward_kernel,
        in_specs=[pl.BlockSpec(memory_space=pltpu.SMEM)] + [pl.BlockSpec(memory_space=pltpu.VMEM)] * 3,
        out_specs=[pl.BlockSpec(memory_space=pltpu.VMEM)] * 2,
        out_shape=[jax.ShapeDtypeStruct((2048, 3 * HD), BF), jax.ShapeDtypeStruct((1024, 3 * HD), BF)],
        scratch_shapes=[pltpu.VMEM((2048, HD), F32), pltpu.VMEM((2048, HD), F32), pltpu.VMEM((QB, 2048), F32), pltpu.VMEM((QB, 2048), F32)],
        compiler_params=params(),
        cost_estimate=short(5 * 2 * 2048 * 1280 * 128, 4 << 20),
    )(lengths, qkv, grad, totals)


GELU_A = 0.7978845608028654
GELU_B = 0.044715

def front_kernel(place_ref, n_ref, mine_ref, other_ref, uo, up, do, dp, act_ref, gh_ref, part_ref, inc_ref):
    core = place_ref[0]
    inc_ref[0, core] = mine_ref[0]
    inc_ref[0, 1 - core] = other_ref[0]
    n = n_ref[0].reshape(256, 2048)
    inc = inc_ref[0].reshape(256, 2048)
    part = jnp.zeros((256, 2048), F32)
    for h, (u, d) in enumerate(((uo, do), (up, dp))):
        cols = slice(h * 512, (h + 1) * 512)
        hidden = dot(n, u[...], (1, 0))
        square = hidden * hidden
        t = jnp.tanh(GELU_A * (hidden + GELU_B * hidden * square))
        act_ref[:, cols] = (0.5 * hidden * (1 + t)).astype(BF)
        slope = 0.5 * (1 + t) + 0.5 * hidden * (1 - t * t) * (GELU_A * (1 + 3 * GELU_B * square))
        gh = (dot(inc, d[...], (1, 1)) * slope).astype(BF)
        gh_ref[:, cols] = gh
        part += dot(gh, u[...], (1, 1))
    part_ref[0] = part.astype(BF).reshape(2, 128, 2048)

def front(place, normed, mine, other, uo, up, do, dp):
    whole = lambda a: pl.BlockSpec(a.shape, lambda i, p: (0,) * a.ndim)
    blk = pl.BlockSpec((1, 2, 128, 2048), lambda i, p: (i, 0, 0, 0))
    one = pl.BlockSpec((1, 128, 2048), lambda i, p: ((i + 4 - p[1]) % 4, 0, 0))
    col = pl.BlockSpec((256, 1024), lambda i, p: (i, 0))
    return pl.pallas_call(
        front_kernel,
        grid_spec=pltpu.PrefetchScalarGridSpec(
            num_scalar_prefetch=1, grid=(4,),
            in_specs=[blk, one, one, whole(uo), whole(up), whole(do), whole(dp)],
            out_specs=[col, col, blk, blk],
        ),
        out_shape=[jax.ShapeDtypeStruct((1024, 1024), BF)] * 2 + [jax.ShapeDtypeStruct((4, 2, 128, 2048), BF)] * 2,
        compiler_params=params(),
        cost_estimate=short(6 * 1024 * 1024 * 2048, 28 << 20),
    )(place, normed, mine, other, uo, up, do, dp)


def mixed_kernel(act_ref, do, dp, out_ref):
    a = act_ref[...]
    out_ref[...] = (dot(a[:, :512], do[...], (1, 0)) + dot(a[:, 512:], dp[...], (1, 0))).astype(BF)

def mix(act, do, dp):
    whole = lambda a: pl.BlockSpec(a.shape, lambda i: (0,) * a.ndim)
    return pl.pallas_call(
        mixed_kernel, grid=(4,),
        in_specs=[pl.BlockSpec((256, 1024), lambda i: (i, 0)), whole(do), whole(dp)],
        out_specs=pl.BlockSpec((256, 2048), lambda i: (i, 0)),
        out_shape=jax.ShapeDtypeStruct((1024, 2048), BF),
        compiler_params=params(),
        cost_estimate=short(2 * 1024 * 1024 * 2048, 10 << 20, 1),
    )(act, do, dp)


def branch_kernel(place_ref, heads_ref, w_ref, mine_ref, other_ref, left, out):
    @pl.when(pl.program_id(0) == 0)
    def _():
        for h in range(8):
            left[:, h * HD : (h + 1) * HD] = heads_ref[h].reshape(256, HD)

    out[...] = dot(left[...], w_ref[...], (1, 0)).reshape(2, 128, 512)
    mine_ref[...] = out[place_ref[0]]
    other_ref[...] = out[1 - place_ref[0]].astype(BF)

def branch(place, heads, w):
    col = pl.BlockSpec((128, 512), lambda i, p: (0, i))
    return pl.pallas_call(
        branch_kernel,
        grid_spec=pltpu.PrefetchScalarGridSpec(
            num_scalar_prefetch=1, grid=(4,),
            in_specs=[pl.BlockSpec((8, 2, 128, HD), lambda i, p: (0, 0, 0, 0)), pl.BlockSpec((1024, 512), lambda i, p: (0, i))],
            out_specs=[col, col],
            scratch_shapes=[pltpu.VMEM((256, 1024), BF), pltpu.VMEM((2, 128, 512), F32)],
        ),
        out_shape=[jax.ShapeDtypeStruct((128, 2048), F32), jax.ShapeDtypeStruct((128, 2048), BF)],
        compiler_params=params(),
        cost_estimate=short(2 * 256 * 1024 * 2048, 6 << 20),
    )(place, heads, w)

def grads_kernel(place_ref, n_ref, inc_ref, act_ref, gh_ref, mine_ref, partner_ref, keep_ref, send_ref):
    def down(ref):
        ref[...] = dot(act_ref[...], inc_ref[...], (0, 0)).astype(BF)

    @pl.when(pl.program_id(0) < 2)
    def _():
        down(mine_ref)

    @pl.when(pl.program_id(0) >= 2)
    def _():
        down(partner_ref)

    up = dot(gh_ref[...], n_ref[...], (0, 0)).astype(BF)
    even, odd = (
        jnp.concatenate([up[:, (2 * i + low) * 256 : (2 * i + low + 1) * 256] for i in range(4)], axis=1)
        for low in range(2)
    )

    @pl.when(place_ref[0] == 0)
    def _():
        keep_ref[...] = even
        send_ref[...] = odd

    @pl.when(place_ref[0] == 1)
    def _():
        keep_ref[...] = odd
        send_ref[...] = even

def weight_grads(place, n, inc, act, gh):
    rows = pl.BlockSpec((1024, 2048), lambda j, p: (0, 0))
    cols = pl.BlockSpec((1024, 256), lambda j, p: (0, j))
    part = pl.BlockSpec((256, 1024), lambda j, p: (j, 0))
    return pl.pallas_call(
        grads_kernel,
        grid_spec=pltpu.PrefetchScalarGridSpec(
            num_scalar_prefetch=1, grid=(4,),
            in_specs=[rows, rows, cols, cols],
            out_specs=[
                pl.BlockSpec((256, 2048), lambda j, p: (jnp.minimum(j, 1), 0)),
                pl.BlockSpec((256, 2048), lambda j, p: (jnp.maximum(j - 2, 0), 0)),
                part, part,
            ],
        ),
        out_shape=[jax.ShapeDtypeStruct((512, 2048), BF)] * 2 + [jax.ShapeDtypeStruct((1024, 1024), BF)] * 2,
        compiler_params=params(),
        cost_estimate=short(4 * 1024 * 1024 * 2048, 20 << 20),
    )(place, n, inc, act, gh)


def cut_kernel(place_ref, down_ref, down_got_ref, up_ref, up_got_ref, down_keep, down_send, up_keep, up_send):
    down = add(down_ref[...], down_got_ref[...])
    up = add(up_ref[...], up_got_ref[...])
    low = jnp.concatenate([up[:, :256], up[:, 512:768]], axis=1)
    high = jnp.concatenate([up[:, 256:512], up[:, 768:]], axis=1)

    @pl.when(place_ref[0] == 0)
    def _():
        down_keep[...] = down[:, :1024]
        down_send[...] = down[:, 1024:]

    @pl.when(place_ref[0] == 1)
    def _():
        down_keep[...] = down[:, 1024:]
        down_send[...] = down[:, :1024]

    @pl.when(place_ref[1] == 0)
    def _():
        up_keep[...] = low
        up_send[...] = high

    @pl.when(place_ref[1] == 1)
    def _():
        up_keep[...] = high
        up_send[...] = low

def cut(place, down, down_got, up, up_got):
    wide = pl.BlockSpec((128, 2048), lambda i, p: (i, 0))
    half = pl.BlockSpec((128, 1024), lambda i, p: (i, 0))
    four = pl.BlockSpec((256, 1024), lambda i, p: (i, 0))
    two = pl.BlockSpec((256, 512), lambda i, p: (i, 0))
    return pl.pallas_call(
        cut_kernel,
        grid_spec=pltpu.PrefetchScalarGridSpec(
            num_scalar_prefetch=1, grid=(4,),
            in_specs=[wide, wide, four, four],
            out_specs=[half, half, two, two],
        ),
        out_shape=[jax.ShapeDtypeStruct((512, 1024), BF)] * 2 + [jax.ShapeDtypeStruct((1024, 512), BF)] * 2,
        compiler_params=params(),
    )(place, down, down_got, up, up_got)


def cut_again_kernel(place_ref, down_ref, down_got_ref, up_ref, up_got_ref, down_keep, down_send, up_keep, up_send):
    down = add(down_ref[...], down_got_ref[...])
    up = add(up_ref[...], up_got_ref[...])

    def put(halves, at, keep, send):
        @pl.when(at == 0)
        def _():
            keep[...] = halves[0]
            send[...] = halves[1]

        @pl.when(at == 1)
        def _():
            keep[...] = halves[1]
            send[...] = halves[0]

    if up.shape[0] == 1024:
        quarters = [down[:, i * 256 : (i + 1) * 256] for i in range(4)]
        put([jnp.concatenate(quarters[i::2], axis=1) for i in range(2)], place_ref[0], down_keep, down_send)
        up_keep[...] = up[:512]
        up_send[...] = up[512:]
    else:
        put([down[:, :256], down[:, 256:]], place_ref[0], down_keep, down_send)
        put([up[:, :256], up[:, 256:]], place_ref[1], up_keep, up_send)

def cut_again(place, down, down_got, up, up_got):
    size = down.shape[1] // 2
    vmem = pl.BlockSpec(memory_space=pltpu.VMEM)
    return pl.pallas_call(
        cut_again_kernel,
        in_specs=[pl.BlockSpec(memory_space=pltpu.SMEM)] + [vmem] * 4,
        out_specs=[vmem] * 4,
        out_shape=[jax.ShapeDtypeStruct((512, size), BF)] * 4,
        compiler_params=params(),
    )(place, down, down_got, up, up_got)

def finish_kernel(down_ref, down_got_ref, up_ref, up_got_ref, down_out, up_out):
    down_out[...] = down_ref[...].astype(F32) + down_got_ref[...].astype(F32)
    up_out[...] = (up_ref[...].astype(F32) + up_got_ref[...].astype(F32)).T

def finish(*arrays):
    vmem = pl.BlockSpec(memory_space=pltpu.VMEM)
    return pl.pallas_call(
        finish_kernel,
        in_specs=[vmem] * 4,
        out_specs=[vmem] * 2,
        out_shape=[jax.ShapeDtypeStruct((512, 256), F32), jax.ShapeDtypeStruct((256, 512), F32)],
        compiler_params=params(),
    )(*arrays)


def heads_kernel(place_ref, mine_ref, other_ref, w_ref, out_ref, left):
    @pl.when(pl.program_id(0) == 0)
    def _():
        left[place_ref[0]] = mine_ref[...]
        left[1 - place_ref[0]] = other_ref[...]

    part = dot(left[...].reshape(256, 2048), w_ref[...], (1, 1)).astype(BF)
    for h in range(4):
        out_ref[h] = part[:, h * HD : (h + 1) * HD].reshape(2, 128, HD)

def to_heads(place, mine, other, w):
    rows = pl.BlockSpec((128, 2048), lambda i, p: (0, 0))
    return pl.pallas_call(
        heads_kernel,
        grid_spec=pltpu.PrefetchScalarGridSpec(
            num_scalar_prefetch=1, grid=(2,),
            in_specs=[rows, rows, pl.BlockSpec((512, 2048), lambda i, p: (i, 0))],
            out_specs=pl.BlockSpec((4, 2, 128, HD), lambda i, p: (i, 0, 0, 0)),
            scratch_shapes=[pltpu.VMEM((2, 128, 2048), BF)],
        ),
        out_shape=jax.ShapeDtypeStruct((8, 2, 128, HD), BF),
        compiler_params=params(),
    )(place, mine, other, w)


def both_kernel(own_ref, partner_ref, out_ref):
    for c in range(3):
        out_ref[c * HD : (c + 1) * HD] = own_ref[c].T
        out_ref[(c + 3) * HD : (c + 4) * HD] = partner_ref[c].T

def both_weights(own, partner):
    part = pl.BlockSpec((3, 256, HD), lambda i: (0, i, 0))
    return pl.pallas_call(
        both_kernel, grid=(8,),
        in_specs=[part, part],
        out_specs=pl.BlockSpec((6 * HD, 256), lambda i: (0, i)),
        out_shape=jax.ShapeDtypeStruct((6 * HD, 2048), BF),
        compiler_params=params(),
    )(own, partner)


def first_kernel(place_ref, mine_ref, got_ref, w_ref, out_ref, left):
    left[:, : 3 * HD] = mine_ref[...]
    left[:, 3 * HD :] = got_ref[...]
    out_ref[...] = dot(left[...], w_ref[...], (1, 0)).astype(BF)

def first_back(place, mine, got, weights):
    return pl.pallas_call(
        first_kernel,
        grid_spec=pltpu.PrefetchScalarGridSpec(
            num_scalar_prefetch=1, grid=(2,),
            in_specs=[
                pl.BlockSpec((512, 3 * HD), lambda i, p: (p[0] * 2 + i, 0)),
                pl.BlockSpec((512, 3 * HD), lambda i, p: (i, 0)),
                pl.BlockSpec((6 * HD, 2048), lambda i, p: (0, 0)),
            ],
            out_specs=pl.BlockSpec((512, 2048), lambda i, p: (i, 0)),
            scratch_shapes=[pltpu.VMEM((512, 6 * HD), BF)],
        ),
        out_shape=jax.ShapeDtypeStruct((1024, 2048), BF),
        compiler_params=params(),
        cost_estimate=short(2 * 1024 * 2048 * 768, 8 << 20),
    )(place, mine, got, weights)


def stack_kernel(*refs):
    for i, ref in enumerate(refs[:-1]):
        refs[-1][i] = ref[...]

def stack(*arrays):
    return pl.pallas_call(
        stack_kernel,
        in_specs=[pl.BlockSpec(memory_space=pltpu.VMEM)] * len(arrays),
        out_specs=pl.BlockSpec(memory_space=pltpu.VMEM),
        out_shape=jax.ShapeDtypeStruct((len(arrays), *arrays[0].shape), arrays[0].dtype),
        compiler_params=params(),
    )(*arrays)

def out_kernel(place_ref, mine_ref, partner_ref, grad_ref, out_ref):
    grad = grad_ref[...]
    out_ref[0, place_ref[0]] = dot(mine_ref[...], grad, (0, 0)).astype(BF)
    out_ref[0, 1 - place_ref[0]] = dot(partner_ref[...], grad, (0, 0)).astype(BF)

def out_grads(place, mine, partner, grad):
    heads = pl.BlockSpec((1024, HD), lambda i, p: (0, 0))
    return pl.pallas_call(
        out_kernel,
        grid_spec=pltpu.PrefetchScalarGridSpec(
            num_scalar_prefetch=1, grid=(8,),
            in_specs=[heads, heads, pl.BlockSpec((1024, 256), lambda i, p: (0, i))],
            out_specs=pl.BlockSpec((1, 2, HD, 256), lambda i, p: (i, 0, 0, 0)),
        ),
        out_shape=jax.ShapeDtypeStruct((8, 2, HD, 256), BF),
        compiler_params=params(),
        cost_estimate=short(2 * 1024 * 256 * 2048, 6 << 20),
    )(place, mine, partner, grad)


def qkv_grads_kernel(n_ref, gp_ref, w_ref, gain_ref, shift_ref, second_ref, out_ref, left, columns, sums):
    at = pl.program_id(0)

    @pl.when(at == 0)
    def _():
        left[...] = gp_ref[...].T
        columns[...] = jnp.sum(left[...].astype(F32), axis=1, keepdims=True)

    grad = dot(left[...], n_ref[...], (1, 0))
    out_ref[at, : 3 * HD] = grad.astype(BF)
    w = jnp.concatenate([w_ref[c].T for c in range(3)], axis=0).astype(F32)
    shift = jnp.sum(w * columns[...], axis=0, keepdims=True)
    gain = (jnp.sum(w * grad, axis=0, keepdims=True) - shift_ref[...] * shift) / gain_ref[...]
    for i, row in enumerate((gain, second_ref[0], shift, second_ref[1])):
        sums[pl.ds(8 * i + at, 1)] = row

    @pl.when(at == 7)
    def _():
        for i in range(8):
            out_ref[i, 3 * HD :] = sums[...].astype(BF)

def qkv_grads(normed, gp, w, gain, shift, second):
    row = pl.BlockSpec((1, 256), lambda i: (0, i))
    return pl.pallas_call(
        qkv_grads_kernel, grid=(8,),
        in_specs=[
            pl.BlockSpec((2048, 256), lambda i: (0, i)),
            pl.BlockSpec((2048, 384), lambda i: (0, 0)),
            pl.BlockSpec((3, 256, HD), lambda i: (0, i, 0)),
            row, row,
            pl.BlockSpec((2, 1, 256), lambda i: (0, 0, i)),
        ],
        out_specs=pl.BlockSpec((8, 3 * HD + 32, 256), lambda i: (0, 0, 0)),
        out_shape=jax.ShapeDtypeStruct((8, 3 * HD + 32, 256), BF),
        scratch_shapes=[pltpu.VMEM((384, 2048), BF), pltpu.VMEM((384, 1), F32), pltpu.VMEM((32, 256), F32)],
        compiler_params=params(),
        cost_estimate=short(2 * 2048 * 2048 * 384, 12 << 20, 1),
    )(normed, gp, w, gain[None], shift[None], second)


def scatter(values, axes):
    return lax.psum_scatter(values, axes, scatter_dimension=0, tiled=True).astype(F32)


def pick(values, index, axis):
    return lax.dynamic_index_in_dim(values, index, axis, False)


def after(values, *others):
    return lax.optimization_barrier((values, *others))[0]


def sum_over_tensor(values):
    values = values + core_swap(values)
    values = (values + z_far(values)) + (z_up(values) + z_down(values))
    return values + x_pair(values)


def body(
    tokens,
    ln1_gain,
    ln1_shift,
    qkv_weight,
    out_weight,
    ln2_gain,
    ln2_shift,
    up_weight,
    down_weight,
    lengths,
    cotangent,
):
    x_hi, y, x_lo, z, core = (lax.axis_index(axis) for axis in AXES)
    tensor = x_lo * 8 + z * 2 + core
    length = lengths[0]

    place = jnp.stack([core, z, x_lo, y % 2])

    out_own = lax.all_gather(out_weight, ("z", "core"), axis=0, tiled=True)
    live_rows = (tensor * 128 + jnp.arange(128, dtype=jnp.int32) < length).astype(F32)[:, None]
    incoming_rows = cotangent.astype(F32) * live_rows
    sent_rows = incoming_rows.astype(BF)
    later_rows = after(sent_rows, out_own)
    along_z = [z_down(later_rows), z_far(sent_rows), z_up(later_rows)]
    up_partner, down_partner, qkv_partner = x_partner(up_weight), x_partner(down_weight), x_partner(qkv_weight)

    normed_first, projected = project(tokens, ln1_gain, ln1_shift, qkv_weight)
    attended, totals = attend(projected, lengths)
    heads = lax.all_to_all(attended, ("z", "core"), 0, 0)
    branch_mine, branch_other = branch(place[2:], after(heads, up_partner, along_z[1]), out_own)
    branch_other = after(x_pair(branch_other), down_partner, along_z[0], along_z[2])
    token_rows = lax.dynamic_slice_in_dim(tokens, tensor * 128, 128, 0).astype(F32)
    middle_rows = token_rows + (branch_mine + branch_other.astype(F32))
    unit_second, inverse_second = norm_stats(middle_rows)
    normed_rows = (unit_second * ln2_gain + ln2_shift).astype(BF)
    partner_heads = x_pair(pick(after(attended, normed_rows), 1 - x_lo, 1).reshape(1024, HD))
    along_z = stack(after(sent_rows, normed_rows), *along_z)
    from_core = core_swap(along_z)

    normed_second = lax.all_gather(normed_rows, ("z", "core"), axis=0, tiled=True)
    activated, grad_hidden, grad_normed_part, incoming = front(
        place,
        after(normed_second, qkv_partner, partner_heads).reshape(4, 2, 128, 2048),
        along_z,
        from_core,
        up_weight,
        up_partner,
        down_weight,
        down_partner,
    )
    incoming = incoming.reshape(1024, 2048)
    grad_normed_second = scatter(grad_normed_part.reshape(1024, 2048), ("z", "core"))
    down_kept, down_sent, up_kept, up_sent = weight_grads(
        place[3:], normed_second, incoming, activated, grad_hidden
    )
    down_got, up_got = x_partner(down_sent), y_pair(up_sent)
    mixed_part = mix(after(activated, down_sent), down_weight, down_partner)
    qkv_both = both_weights(qkv_weight, after(qkv_partner, mixed_part))
    grad_normed_second = after(grad_normed_second, down_got, up_got, mixed_part, qkv_both)

    grad_middle = incoming_rows + norm_back(grad_normed_second, ln2_gain, unit_second, inverse_second)
    gain_second = jnp.sum(grad_normed_second * unit_second, axis=0)
    shift_second = jnp.sum(grad_normed_second, axis=0)
    grad_branch = grad_middle.astype(BF)
    branch_back = lax.all_gather(grad_branch, ("z", "core"), axis=0, tiled=True)

    branch_got = x_pair(grad_branch)
    down_kept, down_sent, up_kept, up_sent = cut(
        jnp.stack([x_hi, y // 2]), down_kept, after(down_got, grad_branch), up_kept, up_got
    )
    down_got, up_got = x_far(down_sent), y_far(up_sent)
    by_head = to_heads(place[2:], grad_branch, after(branch_got, down_sent), out_own)
    grad_attended = lax.all_to_all(by_head, ("z", "core"), 0, 0)
    mixed_rows = scatter(after(mixed_part, by_head), ("z", "core"))

    out_sent = out_grads(
        x_lo[None], after(pick(attended, x_lo, 1).reshape(1024, HD), by_head), partner_heads, branch_back
    )
    grad_projected, projected_sent = attend_back(
        projected, after(grad_attended, out_sent), totals, jnp.stack([length, x_lo])
    )
    projected_got = x_pair(projected_sent)
    out_got = lax.all_to_all(after(out_sent, projected_sent).reshape(16, HD, 256), ("x_hi", "y", "x_lo"), 0, 0)
    second = jnp.stack([gain_second, shift_second])[:, None]
    qkv_sent = qkv_grads(normed_first, grad_projected, qkv_weight, ln1_gain, ln1_shift, second)
    qkv_got = lax.all_to_all(qkv_sent, BATCH, 0, 0)
    down_kept, down_sent, up_kept, up_sent = cut_again(
        jnp.stack([y % 2, x_hi]), down_kept, after(down_got, qkv_sent), up_kept, up_got
    )
    down_got, up_got = y_pair(down_sent), x_partner(up_sent)
    projected_got = after(projected_got, down_sent, mixed_rows)
    grad_first_part = first_back(place[2:], grad_projected, projected_got, qkv_both)
    grad_normed_first = scatter(after(grad_first_part, down_got, up_got, out_got), ("z", "core"))

    down_kept, down_sent, up_kept, up_sent = cut_again(
        jnp.stack([y // 2, x_hi]), down_kept, after(down_got, grad_first_part), up_kept, up_got
    )
    down_got, up_got = y_far(down_sent), x_far(up_sent)
    grad_down, grad_up = finish(down_kept, down_got, up_kept, up_got)
    qkv_sums = jnp.sum(after(qkv_got, down_got, up_got).astype(F32), axis=0)
    sums = sum_over_tensor(qkv_sums[3 * HD :].reshape(4, 2048))
    grad_qkv = qkv_sums[: 3 * HD].reshape(3, HD, 256).transpose(0, 2, 1)
    output = (middle_rows + mixed_rows).astype(BF)

    unit_rows, inverse_rows = norm_stats(token_rows)
    grad_tokens = (grad_middle + norm_back(grad_normed_first, ln1_gain, unit_rows, inverse_rows)).astype(BF)
    grad_out = jnp.sum(after(out_got, grad_tokens, output).astype(F32), axis=0)
    return (output, grad_tokens, grad_qkv, grad_out, grad_up, grad_down, sums[:2], sums[2:])


def solution(mesh):
    return jax.shard_map(
        body,
        mesh=Mesh(mesh.devices.reshape(2, 4, 2, 4, 2), AXES),
        in_specs=(
            P(BATCH, None),
            P(),
            P(),
            P(None, None, TENSOR),
            P(TENSOR, None),
            P(),
            P(),
            P(None, TENSOR),
            P(TENSOR, None),
            P(BATCH),
            P(AXES, None),
        ),
        out_specs=(
            P(AXES, None),
            P(AXES, None),
            P(None, BATCH, TENSOR),
            P(TENSOR, BATCH),
            P(BATCH, TENSOR),
            P(TENSOR, BATCH),
            P(),
            P(),
        ),
        check_vma=False,
    )
```

```python
import functools

import jax
import jax.numpy as jnp
from jax import lax
from jax.experimental import pallas as pl
from jax.experimental.pallas import tpu as pltpu
from jax.sharding import Mesh
from jax.sharding import PartitionSpec as P

HD = 128
EPS = 1e-05
MASKED_SCORE = -1e30
BF = jnp.bfloat16
F32 = jnp.float32

AXES = ("x_hi", "y", "x_lo", "z", "core")
BATCH, TENSOR = AXES[:2], AXES[2:]


def core_swap(values):
    return lax.ppermute(values, "core", [(0, 1), (1, 0)])


def x_pair(values):
    return lax.ppermute(values, "x_lo", [(0, 1), (1, 0)])


def x_partner(values):
    pairs = [(r * 2 + c, ((r + (1, -1)[c]) % 4) * 2 + c) for r in range(4) for c in range(2)]
    return lax.ppermute(values, ("x_hi", "x_lo", "core"), pairs)


def neighbours(axis):
    pairs = [(i * 2 + c, ((i ^ 1) if c == 0 else 3 - i) * 2 + c) for i in range(4) for c in range(2)]
    return lambda values: lax.ppermute(values, (axis, "core"), pairs)


y_pair = neighbours("y")


def shift(axes, sizes, step):
    return lambda values: lax.ppermute(values, axes, [(i, (i + step) % sizes) for i in range(sizes)])


z_up, z_down, z_far = (shift("z", 4, step) for step in (1, -1, 2))
y_far, x_far = shift("y", 4, 2), shift(("x_hi", "x_lo"), 4, 2)


def norm_stats(values):
    centre = jnp.mean(values, axis=-1, keepdims=True)
    offsets = values - centre
    variance = jnp.mean(offsets * offsets, axis=-1, keepdims=True)
    inverse = lax.rsqrt(variance + EPS)
    return (offsets * inverse, inverse)


def norm_back(grad_normed, gain, unit_rows, inverse):
    scaled = grad_normed * gain
    return inverse * (
        scaled
        - jnp.mean(scaled, axis=-1, keepdims=True)
        - unit_rows * jnp.mean(scaled * unit_rows, axis=-1, keepdims=True)
    )


def dot(left, right, dims):
    return lax.dot_general(left, right, ((dims[:1], dims[1:]), ((), ())), preferred_element_type=F32)


def short(flops, moved, by=64):
    return pl.CostEstimate(flops=flops // by, bytes_accessed=moved // by, transcendentals=0)


def add(left, right):
    return (left.astype(F32) + right.astype(F32)).astype(BF)


def params(limit=60, **kw):
    return pltpu.CompilerParams(vmem_limit_bytes=limit * 2**20, **kw)


def qkv_kernel(x_ref, gain_ref, shift_ref, w_ref, normed_ref, out_ref, weights):
    @pl.when(pl.program_id(0) == 0)
    def _():
        for c in range(3):
            weights[:, c * HD : (c + 1) * HD] = w_ref[c]

    x = x_ref[...].astype(F32)
    offsets = x - jnp.mean(x, axis=-1, keepdims=True)
    inverse = lax.rsqrt(jnp.mean(offsets * offsets, axis=-1, keepdims=True) + EPS)
    normed = (offsets * inverse * gain_ref[...] + shift_ref[...]).astype(BF)
    normed_ref[...] = normed
    out_ref[...] = dot(normed, weights[...], (1, 0)).astype(BF)

def project(tokens, gain, shift, weight):
    rows = 256
    return pl.pallas_call(
        qkv_kernel,
        grid=(2048 // rows,),
        in_specs=[
            pl.BlockSpec((rows, 2048), lambda i: (i, 0)),
            pl.BlockSpec((1, 2048), lambda i: (0, 0)),
            pl.BlockSpec((1, 2048), lambda i: (0, 0)),
            pl.BlockSpec((3, 2048, HD), lambda i: (0, 0, 0)),
        ],
        out_specs=[
            pl.BlockSpec((rows, 2048), lambda i: (i, 0)),
            pl.BlockSpec((rows, 3 * HD), lambda i: (i, 0)),
        ],
        out_shape=[jax.ShapeDtypeStruct((2048, 2048), BF), jax.ShapeDtypeStruct((2048, 3 * HD), BF)],
        scratch_shapes=[pltpu.VMEM((2048, 3 * HD), BF)],
        compiler_params=params(),
        cost_estimate=short(2 * 2048 * 2048 * 384, 20 << 20),
    )(tokens, gain[None], shift[None], weight)


QB = 512
SCALE = HD ** -0.5

def masked(scores, first_query, first_key, length):
    query = first_query + lax.broadcasted_iota(jnp.int32, scores.shape, 0)
    key = first_key + lax.broadcasted_iota(jnp.int32, scores.shape, 1)
    return jnp.where((key <= query) & (key < length), scores, MASKED_SCORE)

def forward_kernel(length_ref, qkv_ref, out_ref, total_ref):
    length = length_ref[0]
    for i in range(2048 // QB):
        q = qkv_ref[i * QB : (i + 1) * QB, :HD]
        parts = []
        for j in range(i + 1):
            k = qkv_ref[j * QB : (j + 1) * QB, HD : 2 * HD]
            parts.append(masked(dot(q, k, (1, 1)) * SCALE, i * QB, j * QB, length))
        peak = functools.reduce(jnp.maximum, [jnp.max(p, axis=-1, keepdims=True) for p in parts])
        total = jnp.zeros((QB, 1), F32)
        acc = jnp.zeros((QB, HD), F32)
        for j in range(i + 1):
            e = jnp.exp(parts[j] - peak)
            total += jnp.sum(e, axis=-1, keepdims=True)
            acc += dot(e.astype(BF), qkv_ref[j * QB : (j + 1) * QB, 2 * HD :], (1, 0))
        out = (acc / total).astype(BF)
        for b in range(QB // HD):
            block = i * (QB // HD) + b
            out_ref[block % 8, block // 8] = out[b * HD : (b + 1) * HD]
        total_ref[i * QB : (i + 1) * QB] = peak + jnp.log(total)

def attend(qkv, lengths):
    return pl.pallas_call(
        forward_kernel,
        in_specs=[pl.BlockSpec(memory_space=pltpu.SMEM), pl.BlockSpec(memory_space=pltpu.VMEM)],
        out_specs=[pl.BlockSpec(memory_space=pltpu.VMEM)] * 2,
        out_shape=[jax.ShapeDtypeStruct((8, 2, 128, HD), BF), jax.ShapeDtypeStruct((2048, 1), F32)],
        compiler_params=params(),
        cost_estimate=short(2 * 2 * 2048 * 2048 * 128, 3 << 20),
    )(lengths, qkv)

def backward_kernel(length_ref, qkv_ref, grad_ref, total_ref, out_ref, sent_ref, gk, gv, probs, gprobs):
    length = length_ref[0]
    n = 2048 // QB
    gk[...] = jnp.zeros_like(gk)
    gv[...] = jnp.zeros_like(gv)
    for i in range(n):
        rows = slice(i * QB, (i + 1) * QB)
        q = qkv_ref[rows, :HD]
        blocks = [i * (QB // HD) + b for b in range(QB // HD)]
        g = jnp.concatenate([grad_ref[b % 8, b // 8] for b in blocks], axis=0)
        total = total_ref[rows]
        centre = jnp.zeros((QB, 1), F32)
        for j in range(i + 1):
            keys = slice(j * QB, (j + 1) * QB)
            s = masked(dot(q, qkv_ref[keys, HD : 2 * HD], (1, 1)) * SCALE, i * QB, j * QB, length)
            p = jnp.exp(s - total)
            gp = dot(g, qkv_ref[keys, 2 * HD :], (1, 1))
            centre += jnp.sum(p * gp, axis=-1, keepdims=True)
            probs[:, keys] = p
            gprobs[:, keys] = gp
        gq = jnp.zeros((QB, HD), F32)
        for j in range(i + 1):
            keys = slice(j * QB, (j + 1) * QB)
            p = probs[:, keys]
            gs = (p * (gprobs[:, keys] - centre)).astype(BF)
            gq += dot(gs, qkv_ref[keys, HD : 2 * HD], (1, 0))
            gk[keys] += dot(gs, q, (0, 0))
            gv[keys] += dot(p.astype(BF), g, (0, 0))
        out_ref[rows, :HD] = (gq * SCALE).astype(BF)
    out_ref[:, HD : 2 * HD] = (gk[...] * SCALE).astype(BF)
    out_ref[:, 2 * HD :] = gv[...].astype(BF)

    @pl.when(length_ref[1] == 0)
    def _():
        sent_ref[...] = out_ref[1024:]

    @pl.when(length_ref[1] == 1)
    def _():
        sent_ref[...] = out_ref[:1024]

def attend_back(qkv, grad, totals, lengths):
    return pl.pallas_call(
        backward_kernel,
        in_specs=[pl.BlockSpec(memory_space=pltpu.SMEM)] + [pl.BlockSpec(memory_space=pltpu.VMEM)] * 3,
        out_specs=[pl.BlockSpec(memory_space=pltpu.VMEM)] * 2,
        out_shape=[jax.ShapeDtypeStruct((2048, 3 * HD), BF), jax.ShapeDtypeStruct((1024, 3 * HD), BF)],
        scratch_shapes=[pltpu.VMEM((2048, HD), F32), pltpu.VMEM((2048, HD), F32), pltpu.VMEM((QB, 2048), F32), pltpu.VMEM((QB, 2048), F32)],
        compiler_params=params(),
        cost_estimate=short(5 * 2 * 2048 * 1280 * 128, 4 << 20),
    )(lengths, qkv, grad, totals)


GELU_A = 0.7978845608028654
GELU_B = 0.044715

def front_kernel(place_ref, n_ref, mine_ref, other_ref, uo, up, do, dp, act_ref, gh_ref, part_ref, inc_ref):
    core = place_ref[0]
    inc_ref[0, core] = mine_ref[0]
    inc_ref[0, 1 - core] = other_ref[0]
    n = n_ref[0].reshape(256, 2048)
    inc = inc_ref[0].reshape(256, 2048)
    part = jnp.zeros((256, 2048), F32)
    for h, (u, d) in enumerate(((uo, do), (up, dp))):
        cols = slice(h * 512, (h + 1) * 512)
        hidden = dot(n, u[...], (1, 0))
        square = hidden * hidden
        t = jnp.tanh(GELU_A * (hidden + GELU_B * hidden * square))
        act_ref[:, cols] = (0.5 * hidden * (1 + t)).astype(BF)
        slope = 0.5 * (1 + t) + 0.5 * hidden * (1 - t * t) * (GELU_A * (1 + 3 * GELU_B * square))
        gh = (dot(inc, d[...], (1, 1)) * slope).astype(BF)
        gh_ref[:, cols] = gh
        part += dot(gh, u[...], (1, 1))
    part_ref[0] = part.astype(BF).reshape(2, 128, 2048)

def front(place, normed, mine, other, uo, up, do, dp):
    whole = lambda a: pl.BlockSpec(a.shape, lambda i, p: (0,) * a.ndim)
    blk = pl.BlockSpec((1, 2, 128, 2048), lambda i, p: (i, 0, 0, 0))
    one = pl.BlockSpec((1, 128, 2048), lambda i, p: ((i + 4 - p[1]) % 4, 0, 0))
    col = pl.BlockSpec((256, 1024), lambda i, p: (i, 0))
    return pl.pallas_call(
        front_kernel,
        grid_spec=pltpu.PrefetchScalarGridSpec(
            num_scalar_prefetch=1, grid=(4,),
            in_specs=[blk, one, one, whole(uo), whole(up), whole(do), whole(dp)],
            out_specs=[col, col, blk, blk],
        ),
        out_shape=[jax.ShapeDtypeStruct((1024, 1024), BF)] * 2 + [jax.ShapeDtypeStruct((4, 2, 128, 2048), BF)] * 2,
        compiler_params=params(),
        cost_estimate=short(6 * 1024 * 1024 * 2048, 28 << 20),
    )(place, normed, mine, other, uo, up, do, dp)


def mixed_kernel(act_ref, do, dp, out_ref):
    a = act_ref[...]
    out_ref[...] = (dot(a[:, :512], do[...], (1, 0)) + dot(a[:, 512:], dp[...], (1, 0))).astype(BF)

def mix(act, do, dp):
    whole = lambda a: pl.BlockSpec(a.shape, lambda i: (0,) * a.ndim)
    return pl.pallas_call(
        mixed_kernel, grid=(4,),
        in_specs=[pl.BlockSpec((256, 1024), lambda i: (i, 0)), whole(do), whole(dp)],
        out_specs=pl.BlockSpec((256, 2048), lambda i: (i, 0)),
        out_shape=jax.ShapeDtypeStruct((1024, 2048), BF),
        compiler_params=params(),
        cost_estimate=short(2 * 1024 * 1024 * 2048, 10 << 20, 1),
    )(act, do, dp)


def branch_kernel(place_ref, heads_ref, w_ref, mine_ref, other_ref, left, out):
    @pl.when(pl.program_id(0) == 0)
    def _():
        for h in range(8):
            left[:, h * HD : (h + 1) * HD] = heads_ref[h].reshape(256, HD)

    out[...] = dot(left[...], w_ref[...], (1, 0)).reshape(2, 128, 512)
    mine_ref[...] = out[place_ref[0]]
    other_ref[...] = out[1 - place_ref[0]].astype(BF)

def branch(place, heads, w):
    col = pl.BlockSpec((128, 512), lambda i, p: (0, i))
    return pl.pallas_call(
        branch_kernel,
        grid_spec=pltpu.PrefetchScalarGridSpec(
            num_scalar_prefetch=1, grid=(4,),
            in_specs=[pl.BlockSpec((8, 2, 128, HD), lambda i, p: (0, 0, 0, 0)), pl.BlockSpec((1024, 512), lambda i, p: (0, i))],
            out_specs=[col, col],
            scratch_shapes=[pltpu.VMEM((256, 1024), BF), pltpu.VMEM((2, 128, 512), F32)],
        ),
        out_shape=[jax.ShapeDtypeStruct((128, 2048), F32), jax.ShapeDtypeStruct((128, 2048), BF)],
        compiler_params=params(),
        cost_estimate=short(2 * 256 * 1024 * 2048, 6 << 20),
    )(place, heads, w)

def grads_kernel(place_ref, n_ref, inc_ref, act_ref, gh_ref, mine_ref, partner_ref, keep_ref, send_ref):
    def down(ref):
        ref[...] = dot(act_ref[...], inc_ref[...], (0, 0)).astype(BF)

    @pl.when(pl.program_id(0) < 2)
    def _():
        down(mine_ref)

    @pl.when(pl.program_id(0) >= 2)
    def _():
        down(partner_ref)

    up = dot(gh_ref[...], n_ref[...], (0, 0)).astype(BF)
    even, odd = (
        jnp.concatenate([up[:, (2 * i + low) * 256 : (2 * i + low + 1) * 256] for i in range(4)], axis=1)
        for low in range(2)
    )

    @pl.when(place_ref[0] == 0)
    def _():
        keep_ref[...] = even
        send_ref[...] = odd

    @pl.when(place_ref[0] == 1)
    def _():
        keep_ref[...] = odd
        send_ref[...] = even

def weight_grads(place, n, inc, act, gh):
    rows = pl.BlockSpec((1024, 2048), lambda j, p: (0, 0))
    cols = pl.BlockSpec((1024, 256), lambda j, p: (0, j))
    part = pl.BlockSpec((256, 1024), lambda j, p: (j, 0))
    return pl.pallas_call(
        grads_kernel,
        grid_spec=pltpu.PrefetchScalarGridSpec(
            num_scalar_prefetch=1, grid=(4,),
            in_specs=[rows, rows, cols, cols],
            out_specs=[
                pl.BlockSpec((256, 2048), lambda j, p: (jnp.minimum(j, 1), 0)),
                pl.BlockSpec((256, 2048), lambda j, p: (jnp.maximum(j - 2, 0), 0)),
                part, part,
            ],
        ),
        out_shape=[jax.ShapeDtypeStruct((512, 2048), BF)] * 2 + [jax.ShapeDtypeStruct((1024, 1024), BF)] * 2,
        compiler_params=params(),
        cost_estimate=short(4 * 1024 * 1024 * 2048, 20 << 20),
    )(place, n, inc, act, gh)


def cut_kernel(place_ref, down_ref, down_got_ref, up_ref, up_got_ref, down_keep, down_send, up_keep, up_send):
    down = add(down_ref[...], down_got_ref[...])
    up = add(up_ref[...], up_got_ref[...])
    low = jnp.concatenate([up[:, :256], up[:, 512:768]], axis=1)
    high = jnp.concatenate([up[:, 256:512], up[:, 768:]], axis=1)

    @pl.when(place_ref[0] == 0)
    def _():
        down_keep[...] = down[:, :1024]
        down_send[...] = down[:, 1024:]

    @pl.when(place_ref[0] == 1)
    def _():
        down_keep[...] = down[:, 1024:]
        down_send[...] = down[:, :1024]

    @pl.when(place_ref[1] == 0)
    def _():
        up_keep[...] = low
        up_send[...] = high

    @pl.when(place_ref[1] == 1)
    def _():
        up_keep[...] = high
        up_send[...] = low

def cut(place, down, down_got, up, up_got):
    wide = pl.BlockSpec((128, 2048), lambda i, p: (i, 0))
    half = pl.BlockSpec((128, 1024), lambda i, p: (i, 0))
    four = pl.BlockSpec((256, 1024), lambda i, p: (i, 0))
    two = pl.BlockSpec((256, 512), lambda i, p: (i, 0))
    return pl.pallas_call(
        cut_kernel,
        grid_spec=pltpu.PrefetchScalarGridSpec(
            num_scalar_prefetch=1, grid=(4,),
            in_specs=[wide, wide, four, four],
            out_specs=[half, half, two, two],
        ),
        out_shape=[jax.ShapeDtypeStruct((512, 1024), BF)] * 2 + [jax.ShapeDtypeStruct((1024, 512), BF)] * 2,
        compiler_params=params(),
    )(place, down, down_got, up, up_got)


def cut_again_kernel(place_ref, down_ref, down_got_ref, up_ref, up_got_ref, down_keep, down_send, up_keep, up_send):
    down = add(down_ref[...], down_got_ref[...])
    up = add(up_ref[...], up_got_ref[...])

    def put(halves, at, keep, send):
        @pl.when(at == 0)
        def _():
            keep[...] = halves[0]
            send[...] = halves[1]

        @pl.when(at == 1)
        def _():
            keep[...] = halves[1]
            send[...] = halves[0]

    if up.shape[0] == 1024:
        quarters = [down[:, i * 256 : (i + 1) * 256] for i in range(4)]
        put([jnp.concatenate(quarters[i::2], axis=1) for i in range(2)], place_ref[0], down_keep, down_send)
        up_keep[...] = up[:512]
        up_send[...] = up[512:]
    else:
        put([down[:, :256], down[:, 256:]], place_ref[0], down_keep, down_send)
        put([up[:, :256], up[:, 256:]], place_ref[1], up_keep, up_send)

def cut_again(place, down, down_got, up, up_got):
    size = down.shape[1] // 2
    vmem = pl.BlockSpec(memory_space=pltpu.VMEM)
    return pl.pallas_call(
        cut_again_kernel,
        in_specs=[pl.BlockSpec(memory_space=pltpu.SMEM)] + [vmem] * 4,
        out_specs=[vmem] * 4,
        out_shape=[jax.ShapeDtypeStruct((512, size), BF)] * 4,
        compiler_params=params(),
    )(place, down, down_got, up, up_got)

def finish_kernel(down_ref, down_got_ref, up_ref, up_got_ref, down_out, up_out):
    down_out[...] = down_ref[...].astype(F32) + down_got_ref[...].astype(F32)
    up_out[...] = (up_ref[...].astype(F32) + up_got_ref[...].astype(F32)).T

def finish(*arrays):
    vmem = pl.BlockSpec(memory_space=pltpu.VMEM)
    return pl.pallas_call(
        finish_kernel,
        in_specs=[vmem] * 4,
        out_specs=[vmem] * 2,
        out_shape=[jax.ShapeDtypeStruct((512, 256), F32), jax.ShapeDtypeStruct((256, 512), F32)],
        compiler_params=params(),
    )(*arrays)


def heads_kernel(place_ref, mine_ref, other_ref, w_ref, out_ref, left):
    @pl.when(pl.program_id(0) == 0)
    def _():
        left[place_ref[0]] = mine_ref[...]
        left[1 - place_ref[0]] = other_ref[...]

    part = dot(left[...].reshape(256, 2048), w_ref[...], (1, 1)).astype(BF)
    for h in range(4):
        out_ref[h] = part[:, h * HD : (h + 1) * HD].reshape(2, 128, HD)

def to_heads(place, mine, other, w):
    rows = pl.BlockSpec((128, 2048), lambda i, p: (0, 0))
    return pl.pallas_call(
        heads_kernel,
        grid_spec=pltpu.PrefetchScalarGridSpec(
            num_scalar_prefetch=1, grid=(2,),
            in_specs=[rows, rows, pl.BlockSpec((512, 2048), lambda i, p: (i, 0))],
            out_specs=pl.BlockSpec((4, 2, 128, HD), lambda i, p: (i, 0, 0, 0)),
            scratch_shapes=[pltpu.VMEM((2, 128, 2048), BF)],
        ),
        out_shape=jax.ShapeDtypeStruct((8, 2, 128, HD), BF),
        compiler_params=params(),
    )(place, mine, other, w)


def both_kernel(own_ref, partner_ref, out_ref):
    for c in range(3):
        out_ref[c * HD : (c + 1) * HD] = own_ref[c].T
        out_ref[(c + 3) * HD : (c + 4) * HD] = partner_ref[c].T

def both_weights(own, partner):
    part = pl.BlockSpec((3, 256, HD), lambda i: (0, i, 0))
    return pl.pallas_call(
        both_kernel, grid=(8,),
        in_specs=[part, part],
        out_specs=pl.BlockSpec((6 * HD, 256), lambda i: (0, i)),
        out_shape=jax.ShapeDtypeStruct((6 * HD, 2048), BF),
        compiler_params=params(),
    )(own, partner)


def first_kernel(place_ref, mine_ref, got_ref, w_ref, out_ref, left):
    left[:, : 3 * HD] = mine_ref[...]
    left[:, 3 * HD :] = got_ref[...]
    out_ref[...] = dot(left[...], w_ref[...], (1, 0)).astype(BF)

def first_back(place, mine, got, weights):
    return pl.pallas_call(
        first_kernel,
        grid_spec=pltpu.PrefetchScalarGridSpec(
            num_scalar_prefetch=1, grid=(2,),
            in_specs=[
                pl.BlockSpec((512, 3 * HD), lambda i, p: (p[0] * 2 + i, 0)),
                pl.BlockSpec((512, 3 * HD), lambda i, p: (i, 0)),
                pl.BlockSpec((6 * HD, 2048), lambda i, p: (0, 0)),
            ],
            out_specs=pl.BlockSpec((512, 2048), lambda i, p: (i, 0)),
            scratch_shapes=[pltpu.VMEM((512, 6 * HD), BF)],
        ),
        out_shape=jax.ShapeDtypeStruct((1024, 2048), BF),
        compiler_params=params(),
        cost_estimate=short(2 * 1024 * 2048 * 768, 8 << 20),
    )(place, mine, got, weights)


def stack_kernel(*refs):
    for i, ref in enumerate(refs[:-1]):
        refs[-1][i] = ref[...]

def stack(*arrays):
    return pl.pallas_call(
        stack_kernel,
        in_specs=[pl.BlockSpec(memory_space=pltpu.VMEM)] * len(arrays),
        out_specs=pl.BlockSpec(memory_space=pltpu.VMEM),
        out_shape=jax.ShapeDtypeStruct((len(arrays), *arrays[0].shape), arrays[0].dtype),
        compiler_params=params(),
    )(*arrays)

def out_kernel(place_ref, mine_ref, partner_ref, grad_ref, out_ref):
    grad = grad_ref[...]
    out_ref[0, place_ref[0]] = dot(mine_ref[...], grad, (0, 0)).astype(BF)
    out_ref[0, 1 - place_ref[0]] = dot(partner_ref[...], grad, (0, 0)).astype(BF)

def out_grads(place, mine, partner, grad):
    heads = pl.BlockSpec((1024, HD), lambda i, p: (0, 0))
    return pl.pallas_call(
        out_kernel,
        grid_spec=pltpu.PrefetchScalarGridSpec(
            num_scalar_prefetch=1, grid=(8,),
            in_specs=[heads, heads, pl.BlockSpec((1024, 256), lambda i, p: (0, i))],
            out_specs=pl.BlockSpec((1, 2, HD, 256), lambda i, p: (i, 0, 0, 0)),
        ),
        out_shape=jax.ShapeDtypeStruct((8, 2, HD, 256), BF),
        compiler_params=params(),
        cost_estimate=short(2 * 1024 * 256 * 2048, 6 << 20),
    )(place, mine, partner, grad)


def qkv_grads_kernel(n_ref, gp_ref, w_ref, gain_ref, shift_ref, second_ref, out_ref, left, columns, sums):
    at = pl.program_id(0)

    @pl.when(at == 0)
    def _():
        left[...] = gp_ref[...].T
        columns[...] = jnp.sum(left[...].astype(F32), axis=1, keepdims=True)

    grad = dot(left[...], n_ref[...], (1, 0))
    out_ref[at, : 3 * HD] = grad.astype(BF)
    w = jnp.concatenate([w_ref[c].T for c in range(3)], axis=0).astype(F32)
    shift = jnp.sum(w * columns[...], axis=0, keepdims=True)
    gain = (jnp.sum(w * grad, axis=0, keepdims=True) - shift_ref[...] * shift) / gain_ref[...]
    for i, row in enumerate((gain, second_ref[0], shift, second_ref[1])):
        sums[pl.ds(8 * i + at, 1)] = row

    @pl.when(at == 7)
    def _():
        for i in range(8):
            out_ref[i, 3 * HD :] = sums[...].astype(BF)

def qkv_grads(normed, gp, w, gain, shift, second):
    row = pl.BlockSpec((1, 256), lambda i: (0, i))
    return pl.pallas_call(
        qkv_grads_kernel, grid=(8,),
        in_specs=[
            pl.BlockSpec((2048, 256), lambda i: (0, i)),
            pl.BlockSpec((2048, 384), lambda i: (0, 0)),
            pl.BlockSpec((3, 256, HD), lambda i: (0, i, 0)),
            row, row,
            pl.BlockSpec((2, 1, 256), lambda i: (0, 0, i)),
        ],
        out_specs=pl.BlockSpec((8, 3 * HD + 32, 256), lambda i: (0, 0, 0)),
        out_shape=jax.ShapeDtypeStruct((8, 3 * HD + 32, 256), BF),
        scratch_shapes=[pltpu.VMEM((384, 2048), BF), pltpu.VMEM((384, 1), F32), pltpu.VMEM((32, 256), F32)],
        compiler_params=params(),
        cost_estimate=short(2 * 2048 * 2048 * 384, 12 << 20, 1),
    )(normed, gp, w, gain[None], shift[None], second)


def scatter(values, axes):
    return lax.psum_scatter(values, axes, scatter_dimension=0, tiled=True).astype(F32)


def pick(values, index, axis):
    return lax.dynamic_index_in_dim(values, index, axis, False)


def after(values, *others):
    return lax.optimization_barrier((values, *others))[0]


def sum_over_tensor(values, last_gate):
    values = values + core_swap(values)
    values = (values + z_far(values)) + (z_up(values) + z_down(values))
    return values + after(x_pair(values), last_gate)


def body(
    tokens,
    ln1_gain,
    ln1_shift,
    qkv_weight,
    out_weight,
    ln2_gain,
    ln2_shift,
    up_weight,
    down_weight,
    lengths,
    cotangent,
):
    x_hi, y, x_lo, z, core = (lax.axis_index(axis) for axis in AXES)
    tensor = x_lo * 8 + z * 2 + core
    length = lengths[0]

    place = jnp.stack([core, z, x_lo, y % 2])

    out_own = lax.all_gather(out_weight, ("z", "core"), axis=0, tiled=True)
    live_rows = (tensor * 128 + jnp.arange(128, dtype=jnp.int32) < length).astype(F32)[:, None]
    incoming_rows = cotangent.astype(F32) * live_rows
    sent_rows = incoming_rows.astype(BF)
    later_rows = after(sent_rows, out_own)
    along_z = [z_down(later_rows), z_far(sent_rows), z_up(later_rows)]
    up_partner, down_partner, qkv_partner = x_partner(up_weight), x_partner(down_weight), x_partner(qkv_weight)

    normed_first, projected = project(tokens, ln1_gain, ln1_shift, qkv_weight)
    attended, totals = attend(projected, lengths)
    heads = lax.all_to_all(attended, ("z", "core"), 0, 0)
    branch_mine, branch_other = branch(place[2:], after(heads, up_partner, along_z[1]), out_own)
    branch_other = after(x_pair(branch_other), down_partner, along_z[0], along_z[2])
    token_rows = lax.dynamic_slice_in_dim(tokens, tensor * 128, 128, 0).astype(F32)
    middle_rows = token_rows + (branch_mine + branch_other.astype(F32))
    unit_second, inverse_second = norm_stats(middle_rows)
    normed_rows = (unit_second * ln2_gain + ln2_shift).astype(BF)
    partner_heads = x_pair(pick(after(attended, normed_rows), 1 - x_lo, 1).reshape(1024, HD))
    along_z = stack(after(sent_rows, normed_rows), *along_z)
    from_core = core_swap(along_z)

    normed_second = lax.all_gather(normed_rows, ("z", "core"), axis=0, tiled=True)
    activated, grad_hidden, grad_normed_part, incoming = front(
        place,
        after(normed_second, qkv_partner, partner_heads).reshape(4, 2, 128, 2048),
        along_z,
        from_core,
        up_weight,
        up_partner,
        down_weight,
        down_partner,
    )
    incoming = incoming.reshape(1024, 2048)
    grad_normed_second = scatter(grad_normed_part.reshape(1024, 2048), ("z", "core"))
    down_kept, down_sent, up_kept, up_sent = weight_grads(
        place[3:], normed_second, incoming, activated, grad_hidden
    )
    down_got, up_got = x_partner(down_sent), y_pair(up_sent)
    mixed_part = mix(after(activated, down_sent), down_weight, down_partner)
    qkv_both = both_weights(qkv_weight, after(qkv_partner, mixed_part))
    grad_normed_second = after(grad_normed_second, mixed_part, qkv_both)

    grad_middle = incoming_rows + norm_back(grad_normed_second, ln2_gain, unit_second, inverse_second)
    gain_second = jnp.sum(grad_normed_second * unit_second, axis=0)
    shift_second = jnp.sum(grad_normed_second, axis=0)
    grad_branch = after(grad_middle.astype(BF), down_got, up_got)
    branch_back = lax.all_gather(grad_branch, ("z", "core"), axis=0, tiled=True)

    branch_got = x_pair(grad_branch)
    down_kept, down_sent, up_kept, up_sent = cut(
        jnp.stack([x_hi, y // 2]), down_kept, after(down_got, grad_branch), up_kept, up_got
    )
    down_got, up_got = x_far(down_sent), y_far(up_sent)
    by_head = to_heads(place[2:], grad_branch, after(branch_got, down_sent), out_own)
    grad_attended = lax.all_to_all(by_head, ("z", "core"), 0, 0)
    mixed_rows = scatter(after(mixed_part, by_head), ("z", "core"))

    grad_projected, projected_sent = attend_back(
        projected, grad_attended, totals, jnp.stack([length, x_lo])
    )
    projected_got = x_pair(projected_sent)
    second = jnp.stack([gain_second, shift_second])[:, None]
    qkv_sent = qkv_grads(normed_first, grad_projected, qkv_weight, ln1_gain, ln1_shift, second)
    qkv_got = lax.all_to_all(qkv_sent, BATCH, 0, 0)
    down_kept, down_sent, up_kept, up_sent = cut_again(
        jnp.stack([y % 2, x_hi]), down_kept, after(down_got, qkv_sent), up_kept, up_got
    )
    down_got, up_got = y_pair(down_sent), x_partner(up_sent)
    projected_got = after(projected_got, down_sent, mixed_rows)
    grad_first_part = first_back(place[2:], grad_projected, projected_got, qkv_both)
    grad_normed_first = scatter(after(grad_first_part, down_got, up_got), ("z", "core"))

    down_kept, down_sent, up_kept, up_sent = cut_again(
        jnp.stack([y // 2, x_hi]), down_kept, after(down_got, grad_first_part), up_kept, up_got
    )
    out_sent = out_grads(
        x_lo[None], after(pick(attended, x_lo, 1).reshape(1024, HD), down_sent), partner_heads, branch_back
    )
    down_got, up_got = y_far(down_sent), x_far(up_sent)
    grad_down, grad_up = finish(down_kept, down_got, up_kept, up_got)
    out_got = lax.all_to_all(after(out_sent, qkv_got).reshape(16, HD, 256), ("x_hi", "y", "x_lo"), 0, 0)
    qkv_sums = jnp.sum(after(qkv_got, out_sent, down_got, up_got).astype(F32), axis=0)
    sums = sum_over_tensor(qkv_sums[3 * HD :].reshape(4, 2048), out_got)
    grad_qkv = qkv_sums[: 3 * HD].reshape(3, HD, 256).transpose(0, 2, 1)
    output = (middle_rows + mixed_rows).astype(BF)
    grad_out = jnp.sum(out_got.astype(F32), axis=0)

    unit_rows, inverse_rows = norm_stats(token_rows)
    grad_tokens = (grad_middle + norm_back(grad_normed_first, ln1_gain, unit_rows, inverse_rows)).astype(BF)
    return (output, grad_tokens, grad_qkv, grad_out, grad_up, grad_down, sums[:2], sums[2:])


def solution(mesh):
    return jax.shard_map(
        body,
        mesh=Mesh(mesh.devices.reshape(2, 4, 2, 4, 2), AXES),
        in_specs=(
            P(BATCH, None),
            P(),
            P(),
            P(None, None, TENSOR),
            P(TENSOR, None),
            P(),
            P(),
            P(None, TENSOR),
            P(TENSOR, None),
            P(BATCH),
            P(AXES, None),
        ),
        out_specs=(
            P(AXES, None),
            P(AXES, None),
            P(None, BATCH, TENSOR),
            P(TENSOR, BATCH),
            P(BATCH, TENSOR),
            P(TENSOR, BATCH),
            P(),
            P(),
        ),
        check_vma=False,
    )
```
